32 devices in a mesh: dp: 8 (over y, x, core), tensor: 4 (over z).
Axes of the slice: x: 2, y: 2, z: 4, core: 2. Of those that a mesh axis runs over, the one named last changes fastest.
Arguments:
- hidden: bfloat16 [4096, 2048], P(('dp', 'tensor')), may hold values from -6 to 6
- cotangent: bfloat16 [4096, 2048], P(('dp', 'tensor')), may hold values from -6 to 6
- routes: int32 [4096, 6], P('dp'), may hold values from 0 to 15, all different within a row; in each aligned block of 512 rows (0 to 511, 512 to 1023, ...) at most 256 rows name the same one
- route_gates: float32 [4096, 6], P('dp'), may hold values from 0.08 to 0.32
- doc_lengths: int32 [8, 3], P('dp'), may hold values from 1 to 448, 512 in all within a row
- attn_gain: float32 [2048], replicated, may hold values from 0.25 to 1.75
- query_weight: bfloat16 [2048, 3072], P('dp', 'tensor'), may hold values from -0.125 to 0.125
- latent_weight: bfloat16 [2048, 576], replicated, may hold values from -0.125 to 0.125
- latent_gain: float32 [512], replicated, may hold values from 0.25 to 1.75
- expand_weight: bfloat16 [512, 4096], P('dp', 'tensor'), may hold values from -0.25 to 0.25
- output_weight: bfloat16 [2048, 2048], P('tensor', 'dp'), may hold values from -2 to 2
- mlp_gain: float32 [2048], replicated, may hold values from 0.25 to 1.75
- shared_gate: bfloat16 [2048, 2816], P('dp', 'tensor'), may hold values from -0.125 to 0.125
- shared_up: bfloat16 [2048, 2816], P('dp', 'tensor'), may hold values from -0.125 to 0.125
- shared_down: bfloat16 [2816, 2048], P('tensor', 'dp'), may hold values from -0.109375 to 0.109375
- expert_gate: bfloat16 [16, 2048, 1408], P('dp', None, 'tensor'), may hold values from -0.125 to 0.125
- expert_up: bfloat16 [16, 2048, 1408], P('dp', None, 'tensor'), may hold values from -0.125 to 0.125
- expert_down: bfloat16 [16, 1408, 2048], P('dp', 'tensor'), may hold values from -0.15625 to 0.15625
Outputs:
- layer_out: bfloat16 [4096, 2048], P(('dp', 'tensor'))
- hidden_grad: float32 [4096, 2048], P(('dp', 'tensor'))
- attngain_grad: float32 [2048], replicated
- query_grad: float32 [2048, 3072], P('dp', 'tensor')
- latent_grad: float32 [2048, 576], replicated
- latgain_grad: float32 [512], replicated
- expand_grad: float32 [512, 4096], P('dp', 'tensor')
- output_grad: float32 [2048, 2048], P('tensor', 'dp')
- mlpgain_grad: float32 [2048], replicated
- sgate_grad: float32 [2048, 2816], P('dp', 'tensor')
- sup_grad: float32 [2048, 2816], P('dp', 'tensor')
- sdown_grad: float32 [2816, 2048], P('tensor', 'dp')
- egate_grad: float32 [16, 2048, 1408], P('dp', None, 'tensor')
- eup_grad: float32 [16, 2048, 1408], P('dp', None, 'tensor')
- edown_grad: float32 [16, 1408, 2048], P('dp', 'tensor')
The draws below stay inside these ranges and needn't reach their ends.
Inputs may be any that keep to these rules, and one draw needn't show every extreme that they name: `routes`: the 6 experts of a token differ. Within each group of 512 rows no expert is named by more than 256 rows, a bound that some block reaches. `doc_lengths`: each row sums to 512; its longest document has exactly 448 tokens.
All inputs are finite; a program needn't handle non-finite values.
Results may differ from the reference program's by a relative error of at most 0.018.
Values may be sent and summed in bfloat16 or wider, within the bound.
A program may use at most 448 MiB of HBM per device.

```python
import math
import jax
import jax.numpy as jnp
import numpy as np
from jax import lax

D = 2048
HEADS = 16
NOPE = 128
ROPE = 64
VDIM = 128
LATENT = 512
FFE = 1408
SHARED = 2816
TOPK = 6
DOCS = 3
EXPERTS = 16
GROUP = 512
TOKENS = 4096
DOC_MOST = 448
CAP = 256
N_DP = 8


def block_levels(stream_key, extent, split, least, largest):
    def one(dim, shards_of):
        steps = jax.random.uniform(jax.random.fold_in(jax.random.fold_in(stream_key, 6), dim), (shards_of,), jnp.float32, least / len(split), largest / len(split))
        return jnp.repeat(jnp.exp(steps), extent[dim] // shards_of).reshape((-1,) + (1,) * (len(extent) - dim - 1))

    loudness = one(*split[0])
    for cut in split[1:]:
        loudness = loudness * one(*cut)
    return loudness


def profile(number_of, total, reach, skew):
    loads = [(1 << 20) // math.isqrt(standing ** skew) + 1 for standing in range(2, number_of + 1)]
    surplus, counts = total - reach - (number_of - 1), [1] * (number_of - 1)
    while surplus > 0:
        candidates = [i for i in range(number_of - 1) if counts[i] < reach]
        mass, budget = sum([loads[i] for i in candidates]), surplus
        for i in candidates:
            more = min(reach - counts[i], max(1, budget * loads[i] // mass), surplus)
            counts[i] = counts[i] + more
            surplus = surplus - more
    return np.array([reach] + counts)


def uneven(rng, count, total, reach, slope):
    if count == 2:
        one = jax.random.randint(rng, (), max(1, total - reach), min(reach, total - 1) + 1)
        return jnp.stack([one, total - one])
    tallies = jnp.asarray(profile(count, total, reach, slope), jnp.int32)
    couples = (count - 1) // 2
    donor, sink = tallies[1:1 + 2 * couples:2], tallies[2:2 + 2 * couples:2]
    slack = jnp.minimum(donor - 1, reach - sink)
    moved = jax.random.randint(jax.random.fold_in(rng, 1), (couples,), 0, 1 << 20) % (slack + 1)
    tallies = tallies.at[1:1 + 2 * couples:2].set(donor - moved).at[2:2 + 2 * couples:2].set(sink + moved)
    return tallies[jax.random.permutation(jax.random.fold_in(rng, 2), count)]


def deal_out(key, own, number, rows, number_of, top, most, lean):
    ranking = jax.random.permutation(key, number_of)
    packed, ordinary = portions_of(number_of, rows * top, most, lean, True), portions_of(number_of, rows * top, most, lean, False)
    places = jnp.arange(number_of)

    def named(sizes, rotation):
        used = int((sizes > 0).sum())
        fixed = max(1, used // 4)
        moved = fixed + (places - fixed + rotation * (used - fixed)) % max(1, number_of - fixed)
        return jnp.zeros((number_of,), jnp.int32).at[ranking[jnp.where(places < fixed, places, moved)]].set(jnp.asarray(sizes, jnp.int32))

    sizes = jnp.where(number % 4 == 0, named(packed, number // 4), named(ordinary, number - number // 4 - 1))
    mixed = jax.random.permutation(jax.random.fold_in(own, 3), number_of)
    donor, sink = mixed[0:number_of // 2 * 2:2], mixed[1:number_of // 2 * 2:2]
    room = jnp.minimum(sizes[donor] - 1, most - sizes[sink]) // 2
    room = jnp.where((donor == ranking[0]) | (sink == ranking[0]) | (sizes[sink] == 0), 0, jnp.maximum(room, 0))
    moved = jax.random.randint(jax.random.fold_in(own, 4), (number_of // 2,), 0, 1 << 20) % (room + 1)
    sizes = sizes.at[donor].add(-moved).at[sink].add(moved)
    members = jnp.searchsorted(jnp.cumsum(sizes), jnp.arange(rows * top), side="right").astype(jnp.int32)
    listing = members.reshape(top, rows).T
    listing = listing[jax.random.permutation(jax.random.fold_in(own, 1), rows)]
    rotation = jax.random.randint(jax.random.fold_in(own, 2), (rows, 1), 0, top)
    return jnp.take_along_axis(listing, (jnp.arange(top)[None, :] + rotation) % top, axis=1)


def portions_of(count, total, reach, skew, full):
    loads = [(1 << 20) // math.isqrt(rank ** skew) + 1 for rank in range(1, count + 1)]
    largest = reach if full else min(reach, max(-(-total // count), total * loads[0] // sum(loads)))
    least = 1 if total - largest >= count - 1 else 0
    given, spare = [largest] + [least] * (count - 1), total - largest - least * (count - 1)
    while spare > 0:
        free = [i for i in range(1, count) if given[i] < largest] or [i for i in range(1, count) if given[i] < reach]
        mass, remaining = sum([loads[i] for i in free]), spare
        for i in free:
            extra = min(reach - given[i], max(1, remaining * loads[i] // mass), spare)
            given[i] = given[i] + extra
            spare = spare - extra
    return np.array(given)


def noise(rng, extent, deviation, reach, split=(), held_as=jnp.bfloat16):
    array = deviation * jax.random.normal(rng, extent, jnp.float32)
    if split:
        array = array * block_levels(rng, extent, split, -0.22, 0.18)
    return jnp.clip(array, -reach, reach).astype(held_as)


def setup_inputs(seed: int = 0) -> dict:
    keys = jax.random.split(jax.random.key(seed), 19)
    hidden = noise(keys[0], (TOKENS, D), 1.0, 6.0, ((0, 32),))
    cotangent = noise(keys[1], (TOKENS, D), 1.0, 6.0, ((0, 32),))
    routes_keys = jax.random.split(jax.random.fold_in(keys[2], 1), TOKENS // GROUP)
    routes_turns = jax.random.permutation(jax.random.fold_in(keys[2], 3), TOKENS // GROUP)
    routes = jax.vmap(lambda own, number: deal_out(jax.random.fold_in(keys[2], 2), own, number, GROUP, EXPERTS, TOPK, CAP, 1))(routes_keys, routes_turns).reshape((TOKENS, TOPK))
    route_gates = jnp.clip(jnp.exp(math.log(0.32) - 1.3862944 * jax.random.uniform(keys[3], (TOKENS, TOPK), jnp.float32) ** block_levels(keys[3], (TOKENS, TOPK), ((0, 8),), -0.2, 0.2)), 0.08, 0.32)
    doc_lengths = jax.vmap(lambda own: uneven(own, DOCS, GROUP, DOC_MOST, 0))(jax.random.split(keys[4], N_DP)).reshape((N_DP, DOCS)).astype(jnp.int32)
    attn_gain = jnp.clip(1.0 + 0.15 * jax.random.normal(keys[5], (D,), jnp.float32), 0.25, 1.75)
    query_weight = noise(keys[6], (D, HEADS * (NOPE + ROPE)), D ** -0.5, 0.125, ((0, 8), (1, 4)))
    latent_weight = noise(keys[7], (D, LATENT + ROPE), D ** -0.5, 0.125)
    latent_gain = jnp.clip(1.0 + 0.15 * jax.random.normal(keys[8], (LATENT,), jnp.float32), 0.25, 1.75)
    expand_weight = noise(keys[9], (LATENT, HEADS * (NOPE + VDIM)), LATENT ** -0.5, 0.25, ((0, 8), (1, 4)))
    output_weight = noise(keys[10], (HEADS * VDIM, D), (HEADS * VDIM * 2 // DOC_MOST) ** -0.5, 2.0, ((0, 4), (1, 8)))
    mlp_gain = jnp.clip(1.0 + 0.15 * jax.random.normal(keys[11], (D,), jnp.float32), 0.25, 1.75)
    shared_gate = noise(keys[12], (D, SHARED), D ** -0.5, 0.125, ((0, 8), (1, 4)))
    shared_up = noise(keys[13], (D, SHARED), D ** -0.5, 0.125, ((0, 8), (1, 4)))
    shared_down = noise(keys[14], (SHARED, D), SHARED ** -0.5, 0.109375, ((0, 4), (1, 8)))
    expert_gate = noise(keys[15], (EXPERTS, D, FFE), D ** -0.5, 0.125, ((0, 8), (2, 4)))
    expert_up = noise(keys[16], (EXPERTS, D, FFE), D ** -0.5, 0.125, ((0, 8), (2, 4)))
    expert_down = noise(keys[17], (EXPERTS, FFE, D), FFE ** -0.5, 0.15625, ((0, 8), (1, 4)))
    return dict(hidden=hidden, cotangent=cotangent, routes=routes, route_gates=route_gates, doc_lengths=doc_lengths, attn_gain=attn_gain, query_weight=query_weight, latent_weight=latent_weight, latent_gain=latent_gain, expand_weight=expand_weight, output_weight=output_weight, mlp_gain=mlp_gain, shared_gate=shared_gate, shared_up=shared_up, shared_down=shared_down, expert_gate=expert_gate, expert_up=expert_up, expert_down=expert_down)


epsilon = 1e-06
rope_base = 10000.0

@jax.custom_vjp
def low(v):
    return lax.optimization_barrier(v.astype(jnp.bfloat16)).astype(jnp.float32)

@jax.custom_vjp
def low_back(v):
    return v

def low_keep(v):
    return (low(v), None)

def low_pass(kept, grad):
    return (grad,)

def back_keep(v):
    return (v, None)

def back_low(kept, grad):
    return (low(grad),)
low.defvjp(low_keep, low_pass)
low_back.defvjp(back_keep, back_low)

def matmul(left_op, right_op):
    return jnp.dot(left_op, right_op, precision=lax.Precision.HIGHEST)

def rms_norm(values, gain_vec):
    return values * lax.rsqrt(lax.optimization_barrier(jnp.mean(values * values, axis=-1, keepdims=True)) + epsilon) * gain_vec

def rope_tables(positions, rot_width):
    middle = rot_width // 2
    frequency = rope_base ** (-jnp.arange(middle, dtype=jnp.float32) * 2.0 / rot_width)
    angles = positions.astype(jnp.float32)[:, None] * frequency[None, :]
    return (jnp.cos(angles), jnp.sin(angles))

def rotate(values, cos_table, sin_table):
    middle = values.shape[-1] // 2
    first_half = values[..., :middle]
    second_half = values[..., middle:]
    return jnp.concatenate([first_half * cos_table - second_half * sin_table, second_half * cos_table + first_half * sin_table], axis=-1)

def doc_layout(lengths, row_count):
    doc_ends = jnp.cumsum(lengths).astype(jnp.int32)
    tok_index = jnp.arange(row_count, dtype=jnp.int32)
    before = (doc_ends[None, :] <= tok_index[:, None]).astype(jnp.int32)
    doc_ids = lax.optimization_barrier(jnp.sum(before, axis=1))
    starts = lax.optimization_barrier(jnp.sum(before * lengths[None, :], axis=1))
    return (doc_ids, tok_index - starts)

def slot_tables(routes, experts, capacity):
    row_count = routes.shape[0] * routes.shape[1]
    flat_routes = routes.reshape(row_count)
    onehot = (flat_routes[:, None] == jnp.arange(experts, dtype=jnp.int32)[None, :]).astype(jnp.int32)
    earlier = jnp.cumsum(onehot, axis=0) - onehot
    position = lax.optimization_barrier(jnp.sum(earlier * onehot, axis=1))
    slot_ids = flat_routes * capacity + position
    tok_rows = jnp.arange(row_count, dtype=jnp.int32) // routes.shape[1]
    owner_tok = jnp.zeros((experts * capacity,), jnp.int32).at[slot_ids].set(tok_rows)
    return (slot_ids.reshape(routes.shape), owner_tok)

def group_forward(params, pieces):
    attn_gain, query_weight, latent_weight, latent_gain, expand_weight, output_weight, mlp_gain, shared_gate, shared_up, shared_down, expert_gate, expert_up, expert_down = params
    hidden_f, routes, gate_rows, lengths = pieces
    normed_one = low(rms_norm(hidden_f, attn_gain))
    latent_full = low_back(matmul(normed_one, latent_weight))
    latent_norm = low(rms_norm(latent_full[:, :LATENT], latent_gain))
    doc_ids, positions = doc_layout(lengths, GROUP)
    cos_table, sin_table = rope_tables(positions, ROPE)
    key_rot = rotate(latent_full[:, LATENT:], cos_table, sin_table)
    query_raw = low_back(matmul(normed_one, query_weight)).reshape(GROUP, HEADS, NOPE + ROPE)
    query_rot = rotate(query_raw[..., NOPE:], cos_table[:, None, :], sin_table[:, None, :])
    query_all = low(low_back(jnp.concatenate([query_raw[..., :NOPE], query_rot], axis=-1)))
    expanded = matmul(latent_norm, expand_weight).reshape(GROUP, HEADS, NOPE + VDIM)
    key_shared = jnp.broadcast_to(key_rot[:, None, :], (GROUP, HEADS, ROPE))
    key_all = low(low_back(jnp.concatenate([expanded[..., :NOPE], key_shared], axis=-1)))
    value_all = low(low_back(expanded[..., NOPE:]))
    scores = jnp.einsum('qhd,khd->hqk', query_all, key_all, precision=lax.Precision.HIGHEST)
    scores = low_back(scores * (NOPE + ROPE) ** (-0.5))
    row_index = jnp.arange(GROUP, dtype=jnp.int32)
    allowed = (row_index[None, :] <= row_index[:, None]) & (doc_ids[None, :] == doc_ids[:, None])
    scores = jnp.where(allowed[None], scores, -jnp.inf)
    exp_scores = jnp.exp(scores - lax.optimization_barrier(jnp.max(scores, axis=-1, keepdims=True)))
    probability = low(exp_scores / lax.optimization_barrier(jnp.sum(exp_scores, axis=-1, keepdims=True)))
    attended = jnp.einsum('hqk,khd->qhd', probability, value_all, precision=lax.Precision.HIGHEST)
    attended = low(low_back(attended)).reshape(GROUP, HEADS * VDIM)
    residual = hidden_f + low_back(matmul(attended, output_weight))
    mlp_rows = low(rms_norm(residual, mlp_gain))
    shared_pre = low_back(matmul(mlp_rows, shared_gate))
    shared_lin = low_back(matmul(mlp_rows, shared_up))
    shared_hidden = low(jax.nn.silu(shared_pre) * shared_lin)
    shared_out = matmul(shared_hidden, shared_down)
    slot_ids, owner_tok = slot_tables(routes, EXPERTS, CAP)
    expert_in = mlp_rows[owner_tok].reshape(EXPERTS, CAP, D)
    gate_pre = low_back(jnp.einsum('ecd,edf->ecf', expert_in, expert_gate, precision=lax.Precision.HIGHEST))
    up_pre = low_back(jnp.einsum('ecd,edf->ecf', expert_in, expert_up, precision=lax.Precision.HIGHEST))
    expert_hidden = low(jax.nn.silu(gate_pre) * up_pre)
    expert_out = jnp.einsum('ecf,efd->ecd', expert_hidden, expert_down, precision=lax.Precision.HIGHEST)
    expert_out = low_back(expert_out).reshape(EXPERTS * CAP, D)
    routed = lax.optimization_barrier(jnp.sum(gate_rows[:, :, None] * expert_out[slot_ids], axis=1))
    return residual + low_back(shared_out + routed)

def reference(hidden, cotangent, routes, route_gates, doc_lengths, attn_gain, query_weight, latent_weight, latent_gain, expand_weight, output_weight, mlp_gain, shared_gate, shared_up, shared_down, expert_gate, expert_up, expert_down):
    params = tuple((weight.astype(jnp.float32) for weight in (attn_gain, query_weight, latent_weight, latent_gain, expand_weight, output_weight, mlp_gain, shared_gate, shared_up, shared_down, expert_gate, expert_up, expert_down)))
    group_step = jax.checkpoint(group_forward)

    def forward(hidden_all, params_all):
        pieces = (hidden_all.reshape(N_DP, GROUP, D), routes.reshape(N_DP, GROUP, TOPK), route_gates.astype(jnp.float32).reshape(N_DP, GROUP, TOPK), doc_lengths)
        outputs = lax.map(lambda group_pieces: group_step(params_all, group_pieces), pieces)
        return outputs.reshape(TOKENS, D)
    layer_out, pullback = jax.vjp(forward, hidden.astype(jnp.float32), params)
    hidden_grad, weight_grads = pullback(cotangent.astype(jnp.float32))
    return (layer_out.astype(jnp.bfloat16), hidden_grad, weight_grads[0], weight_grads[1], weight_grads[2], weight_grads[3], weight_grads[4], weight_grads[5], weight_grads[6], weight_grads[7], weight_grads[8], weight_grads[9], weight_grads[10], weight_grads[11], weight_grads[12])
```

```python
import functools
from types import SimpleNamespace

import jax
import jax.numpy as jnp
from jax import lax
from jax.experimental import pallas as pl
from jax.experimental.pallas import tpu as pltpu
from jax.sharding import PartitionSpec as P

DP = "dp"
TENSOR = "tensor"
NOPE = 128
ROPE = 64
VDIM = 128
LATENT = 512
TOPK = 6


epsilon = 1e-06
rope_base = 10000.0


def bfloat(values):
    return values.astype(jnp.bfloat16)


def plain_dot(left_op, right_op):
    return jnp.dot(left_op, right_op, preferred_element_type=jnp.float32)


def first_dot(left_op, right_op):
    return lax.dot_general(
        left_op, right_op, (((0,), (0,)), ((), ())), preferred_element_type=jnp.float32
    )


def last_dot(left_op, right_op):
    return lax.dot_general(
        left_op, right_op, (((1,), (1,)), ((), ())), preferred_element_type=jnp.float32
    )


def rms_scale(values):
    return lax.rsqrt(jnp.mean(values * values, axis=-1, keepdims=True) + epsilon)


def rms_back(grad_out, values, scaling, gain_vec):
    scaled_grad = grad_out * gain_vec
    inner_sum = jnp.mean(scaled_grad * values, axis=-1, keepdims=True)
    grad_in = scaling * scaled_grad - values * (scaling * scaling * scaling) * inner_sum
    return (grad_in, jnp.sum(grad_out * values * scaling, axis=0))


def silu_parts(values):
    sigmoid = jax.nn.sigmoid(values)
    return (values * sigmoid, sigmoid * (1.0 + values * (1.0 - sigmoid)))


def rope_tables(positions, rot_width):
    middle = rot_width // 2
    frequency = rope_base ** (-jnp.arange(middle, dtype=jnp.float32) * 2.0 / rot_width)
    angles = positions.astype(jnp.float32)[:, None] * frequency[None, :]
    return (jnp.cos(angles), jnp.sin(angles))


def rotate(values, cos_table, sin_table):
    middle = values.shape[-1] // 2
    first_half = values[..., :middle]
    second_half = values[..., middle:]
    return jnp.concatenate(
        [
            first_half * cos_table - second_half * sin_table,
            second_half * cos_table + first_half * sin_table,
        ],
        axis=-1,
    )


def doc_layout(lengths, row_count):
    doc_ends = jnp.cumsum(lengths)
    tok_index = jnp.arange(row_count, dtype=jnp.int32)
    before = (doc_ends[None, :] <= tok_index[:, None]).astype(jnp.int32)
    doc_ids = jnp.sum(before, axis=1)
    starts = jnp.sum(before * lengths[None, :], axis=1)
    return (doc_ids, tok_index - starts)


def slot_tables(routes, experts, capacity):
    row_count = routes.shape[0] * routes.shape[1]
    flat_routes = routes.reshape(row_count)
    onehot = (flat_routes[:, None] == jnp.arange(experts, dtype=jnp.int32)[None, :]).astype(
        jnp.int32
    )
    earlier = jnp.cumsum(onehot, axis=0) - onehot
    position = jnp.sum(earlier * onehot, axis=1)
    slot_ids = flat_routes * capacity + position
    tok_rows = jnp.arange(row_count, dtype=jnp.int32) // routes.shape[1]
    owner_tok = jnp.zeros((experts * capacity,), jnp.int32).at[slot_ids].set(tok_rows)
    return (slot_ids.reshape(routes.shape), owner_tok)


def slot_share(capacity):
    return (0, capacity)


def route_rows(outgoing, apply_fn):
    arrived = lax.all_to_all(outgoing, DP, split_axis=1, concat_axis=1, tiled=True)
    result, extra = apply_fn(arrived)
    back = lax.all_to_all(
        result.astype(jnp.bfloat16), DP, split_axis=1, concat_axis=1, tiled=True
    ).astype(result.dtype)
    return (back, extra)


def block_mask(doc_ids, row_start, block_rows):
    group_rows = doc_ids.shape[0]
    key_index = jnp.arange(group_rows, dtype=jnp.int32)
    query_index = row_start + jnp.arange(block_rows, dtype=jnp.int32)
    return (key_index[None, :] <= query_index[:, None]) & (doc_ids[None, :] == doc_ids[:, None])


def attend(query_all, key_all, value_all, doc_ids, scaling):
    group_rows = query_all.shape[0]
    block_rows = min(512, group_rows)
    block_count = group_rows // block_rows

    def one_block(block_id):
        row_start = block_id * block_rows
        allowed = block_mask(doc_ids, row_start, block_rows)
        scores = (
            jnp.einsum("qhd,khd->hqk", query_all, key_all, preferred_element_type=jnp.float32)
            * scaling
        )
        scores = jnp.where(allowed[None], scores, -jnp.inf)
        row_max = jnp.max(scores, axis=-1, keepdims=True)
        exp_scores = jnp.exp(scores - row_max)
        row_total = jnp.sum(exp_scores, axis=-1, keepdims=True)
        probability = bfloat(exp_scores / row_total)
        output = jnp.einsum(
            "hqk,khd->qhd", probability, value_all, preferred_element_type=jnp.float32
        )
        return (output, (row_max + jnp.log(row_total))[..., 0])

    outputs, log_total = lax.map(one_block, jnp.arange(block_count, dtype=jnp.int32))
    return (outputs.reshape(group_rows, outputs.shape[2], outputs.shape[3]), log_total)


def attend_back(query_all, key_all, value_all, doc_ids, scaling, log_total, grad_out):
    group_rows = query_all.shape[0]
    block_rows = min(512, group_rows)
    block_count = group_rows // block_rows

    def one_block(carried, inputs):
        key_grad, value_grad = carried
        block_id, block_lse = inputs
        row_start = block_id * block_rows
        allowed = block_mask(doc_ids, row_start, block_rows)
        scores = (
            jnp.einsum("qhd,khd->hqk", query_all, key_all, preferred_element_type=jnp.float32)
            * scaling
        )
        scores = jnp.where(allowed[None], scores, -jnp.inf)
        probability = jnp.exp(scores - block_lse[..., None])
        value_grad = value_grad + jnp.einsum(
            "hqk,qhd->khd", bfloat(probability), grad_out, preferred_element_type=jnp.float32
        )
        prob_grad = jnp.einsum(
            "qhd,khd->hqk", grad_out, value_all, preferred_element_type=jnp.float32
        )
        row_dot = jnp.sum(prob_grad * probability, axis=-1, keepdims=True)
        score_grad = bfloat(probability * (prob_grad - row_dot))
        query_grad = (
            jnp.einsum("hqk,khd->qhd", score_grad, key_all, preferred_element_type=jnp.float32)
            * scaling
        )
        key_grad = (
            key_grad
            + jnp.einsum("hqk,qhd->khd", score_grad, query_all, preferred_element_type=jnp.float32)
            * scaling
        )
        return ((key_grad, value_grad), query_grad)

    start_state = (jnp.zeros(key_all.shape, jnp.float32), jnp.zeros(value_all.shape, jnp.float32))
    (key_grad, value_grad), query_blocks = lax.scan(
        one_block, start_state, (jnp.arange(block_count, dtype=jnp.int32), log_total)
    )
    query_grad = query_blocks.reshape(group_rows, query_blocks.shape[2], query_blocks.shape[3])
    return (query_grad, key_grad, value_grad)


def forward_pass(
    hidden,
    cotangent,
    routes,
    route_gates,
    doc_lengths,
    attn_gain,
    query_weight,
    latent_weight,
    latent_gain,
    expand_weight,
    output_weight,
    mlp_gain,
    shared_gate,
    shared_up,
    shared_down,
    expert_gate,
    expert_up,
    expert_down,
):
    tensor_count = lax.axis_size(TENSOR)
    dp_count = lax.axis_size(DP)
    local_rows = hidden.shape[0]
    group_rows = local_rows * tensor_count
    query_full, expand_full, output_full, sgate_full, sup_full, sdown_full = (
        lax.all_gather(query_weight, DP, axis=0, tiled=True),
        lax.all_gather(expand_weight, DP, axis=0, tiled=True),
        lax.all_gather(output_weight, DP, axis=1, tiled=True),
        lax.all_gather(shared_gate, DP, axis=0, tiled=True),
        lax.all_gather(shared_up, DP, axis=0, tiled=True),
        lax.all_gather(shared_down, DP, axis=1, tiled=True),
    )
    hidden_f = hidden.astype(jnp.float32)
    scale_one = rms_scale(hidden_f)
    normed_one = bfloat(hidden_f * scale_one * attn_gain)
    latent_full = plain_dot(normed_one, latent_weight)
    latent_part = latent_full[:, :LATENT]
    scale_latent = rms_scale(latent_part)
    latent_norm = bfloat(latent_part * scale_latent * latent_gain)
    doc_ids, positions = doc_layout(doc_lengths[0], group_rows)
    cos_group, sin_group = rope_tables(positions, ROPE)
    local_start = lax.axis_index(TENSOR) * local_rows
    cos_local = lax.dynamic_slice_in_dim(cos_group, local_start, local_rows, 0)
    sin_local = lax.dynamic_slice_in_dim(sin_group, local_start, local_rows, 0)
    key_rot = bfloat(rotate(latent_full[:, LATENT:], cos_local, sin_local))
    normed_group, latent_group, keyrot_group = (
        lax.all_gather(normed_one, TENSOR, axis=0, tiled=True),
        lax.all_gather(latent_norm, TENSOR, axis=0, tiled=True),
        lax.all_gather(key_rot, TENSOR, axis=0, tiled=True),
    )
    local_heads = query_full.shape[1] // (NOPE + ROPE)
    query_raw = plain_dot(normed_group, query_full).reshape(group_rows, local_heads, NOPE + ROPE)
    query_rot = rotate(query_raw[..., NOPE:], cos_group[:, None, :], sin_group[:, None, :])
    query_all = bfloat(jnp.concatenate([query_raw[..., :NOPE], query_rot], axis=-1))
    expanded = plain_dot(latent_group, expand_full).reshape(group_rows, local_heads, NOPE + VDIM)
    key_shared = jnp.broadcast_to(keyrot_group[:, None, :], (group_rows, local_heads, ROPE))
    key_all = jnp.concatenate([bfloat(expanded[..., :NOPE]), key_shared], axis=-1)
    value_all = bfloat(expanded[..., NOPE:])
    scaling = (NOPE + ROPE) ** (-0.5)
    attended, log_total = attend(query_all, key_all, value_all, doc_ids, scaling)
    attended_low = bfloat(attended).reshape(group_rows, local_heads * VDIM)
    attn_local = lax.psum_scatter(
        plain_dot(attended_low, output_full), TENSOR, scatter_dimension=0, tiled=True
    )
    residual = hidden_f + attn_local
    scale_two = rms_scale(residual)
    normed_two = bfloat(residual * scale_two * mlp_gain)
    mlp_rows, cotan_rows = (
        lax.all_gather(normed_two, TENSOR, axis=0, tiled=True),
        lax.all_gather(cotangent, TENSOR, axis=0, tiled=True),
    )
    shared_gpre = plain_dot(mlp_rows, sgate_full)
    shared_upre = plain_dot(mlp_rows, sup_full)
    shared_silu, shared_dsilu = silu_parts(shared_gpre)
    shared_hidden = bfloat(shared_silu * shared_upre)
    shared_out = plain_dot(shared_hidden, sdown_full)
    local_experts = expert_gate.shape[0]
    experts = local_experts * dp_count
    capacity = group_rows * TOPK * 4 // (3 * experts)
    slot_ids, owner_tok = slot_tables(routes, experts, capacity)
    slot_start, slot_count = slot_share(capacity)
    all_tok = owner_tok.reshape(dp_count, local_experts, capacity).transpose(1, 0, 2)
    send_rows = mlp_rows[all_tok]

    def expert_apply(received):
        gate_pre = jnp.einsum(
            "jscd,jdf->jscf", received, expert_gate, preferred_element_type=jnp.float32
        )
        up_pre = jnp.einsum(
            "jscd,jdf->jscf", received, expert_up, preferred_element_type=jnp.float32
        )
        gate_silu, gate_dsilu = silu_parts(gate_pre)
        activated = bfloat(gate_silu * up_pre)
        result = jnp.einsum(
            "jscf,jfd->jscd", activated, expert_down, preferred_element_type=jnp.float32
        )
        return (result, (received, up_pre, gate_silu, gate_dsilu, activated))

    returned, expert_state = route_rows(send_rows, expert_apply)
    received, up_pre, gate_silu, gate_dsilu, activated = expert_state
    position = slot_ids % capacity - slot_start
    slot_mask = ((position >= 0) & (position < slot_count)).astype(jnp.float32)
    flat_index = (
        routes % local_experts * dp_count + routes // local_experts
    ) * slot_count + jnp.clip(position, 0, slot_count - 1)
    returned_flat = returned.reshape(local_experts * dp_count * slot_count, returned.shape[-1])
    routed = jnp.sum((route_gates * slot_mask)[:, :, None] * returned_flat[flat_index], axis=1)
    moe_local = lax.psum_scatter(
        (shared_out + routed).astype(jnp.bfloat16), TENSOR, scatter_dimension=0, tiled=True
    ).astype(jnp.float32)
    layer_out = bfloat(residual + moe_local)
    return SimpleNamespace(
        layer_out=layer_out,
        hidden_f=hidden_f,
        scale_one=scale_one,
        normed_one=normed_one,
        latent_part=latent_part,
        scale_latent=scale_latent,
        cos_local=cos_local,
        sin_local=sin_local,
        cos_group=cos_group,
        sin_group=sin_group,
        doc_ids=doc_ids,
        normed_group=normed_group,
        latent_group=latent_group,
        query_all=query_all,
        key_all=key_all,
        value_all=value_all,
        log_total=log_total,
        attended_low=attended_low,
        residual=residual,
        scale_two=scale_two,
        mlp_rows=mlp_rows,
        cotan_rows=cotan_rows,
        shared_upre=shared_upre,
        shared_silu=shared_silu,
        shared_dsilu=shared_dsilu,
        shared_hidden=shared_hidden,
        slot_ids=slot_ids,
        send_tok=all_tok,
        flat_index=flat_index,
        slot_mask=slot_mask,
        received=received,
        up_pre=up_pre,
        gate_silu=gate_silu,
        gate_dsilu=gate_dsilu,
        activated=activated,
        query_full=query_full,
        expand_full=expand_full,
        output_full=output_full,
        sgate_full=sgate_full,
        sup_full=sup_full,
        sdown_full=sdown_full,
    )


def general_shards(
    hidden,
    cotangent,
    routes,
    route_gates,
    doc_lengths,
    attn_gain,
    query_weight,
    latent_weight,
    latent_gain,
    expand_weight,
    output_weight,
    mlp_gain,
    shared_gate,
    shared_up,
    shared_down,
    expert_gate,
    expert_up,
    expert_down,
):
    kept_state = forward_pass(
        hidden,
        cotangent,
        routes,
        route_gates,
        doc_lengths,
        attn_gain,
        query_weight,
        latent_weight,
        latent_gain,
        expand_weight,
        output_weight,
        mlp_gain,
        shared_gate,
        shared_up,
        shared_down,
        expert_gate,
        expert_up,
        expert_down,
    )
    dp_count = lax.axis_size(DP)
    local_experts = expert_gate.shape[0]
    experts = local_experts * dp_count
    group_rows = kept_state.mlp_rows.shape[0]
    capacity = group_rows * TOPK * 4 // (3 * experts)
    cotan_rows = kept_state.cotan_rows
    mlp_rows = kept_state.mlp_rows
    sdown_wgrad = first_dot(kept_state.shared_hidden, cotan_rows)
    shared_hgrad = last_dot(cotan_rows, kept_state.sdown_full)
    sgate_pgrad = bfloat(shared_hgrad * kept_state.shared_upre * kept_state.shared_dsilu)
    sup_pgrad = bfloat(shared_hgrad * kept_state.shared_silu)
    sgate_wgrad = first_dot(mlp_rows, sgate_pgrad)
    sup_wgrad = first_dot(mlp_rows, sup_pgrad)
    mlp_partial = last_dot(sgate_pgrad, kept_state.sgate_full) + last_dot(
        sup_pgrad, kept_state.sup_full
    )
    slot_start, slot_count = slot_share(capacity)
    slot_gate = (
        jnp.zeros((experts * capacity,), jnp.float32)
        .at[kept_state.slot_ids.reshape(-1)]
        .set(route_gates.reshape(-1))
    )
    all_gate = slot_gate.reshape(dp_count, local_experts, capacity).transpose(1, 0, 2)
    grad_send = bfloat(all_gate[..., None] * cotan_rows[kept_state.send_tok].astype(jnp.float32))
    received = kept_state.received

    def expert_back(grad_recv):
        expert_down_partial = jnp.einsum(
            "jscf,jscd->jfd", kept_state.activated, grad_recv, preferred_element_type=jnp.float32
        )
        act_grad = jnp.einsum(
            "jscd,jfd->jscf", grad_recv, expert_down, preferred_element_type=jnp.float32
        )
        gate_pgrad = bfloat(act_grad * kept_state.up_pre * kept_state.gate_dsilu)
        up_pgrad = bfloat(act_grad * kept_state.gate_silu)
        row_gradient = jnp.einsum(
            "jscf,jdf->jscd", gate_pgrad, expert_gate, preferred_element_type=jnp.float32
        )
        row_gradient = row_gradient + jnp.einsum(
            "jscf,jdf->jscd", up_pgrad, expert_up, preferred_element_type=jnp.float32
        )
        expert_gate_partial = jnp.einsum(
            "jscd,jscf->jdf", received, gate_pgrad, preferred_element_type=jnp.float32
        )
        expert_up_partial = jnp.einsum(
            "jscd,jscf->jdf", received, up_pgrad, preferred_element_type=jnp.float32
        )
        return (row_gradient, (expert_gate_partial, expert_up_partial, expert_down_partial))

    rows_back, expert_weight_gradients = route_rows(grad_send, expert_back)
    expert_gate_weight_gradient, expert_up_weight_gradient, expert_down_weight_gradient = (
        expert_weight_gradients
    )
    back_flat = rows_back.reshape(local_experts * dp_count * slot_count, rows_back.shape[-1])
    mlp_partial = mlp_partial + jnp.sum(
        kept_state.slot_mask[:, :, None] * back_flat[kept_state.flat_index], axis=1
    )
    mlp_grad = lax.psum_scatter(mlp_partial, TENSOR, scatter_dimension=0, tiled=True)
    resid_from, mlpgain_part = rms_back(
        mlp_grad, kept_state.residual, kept_state.scale_two, mlp_gain
    )
    resid_grad = cotangent.astype(jnp.float32) + resid_from
    attn_rows = lax.all_gather(bfloat(resid_grad), TENSOR, axis=0, tiled=True)
    output_wgrad = first_dot(kept_state.attended_low, attn_rows)
    local_heads = kept_state.query_all.shape[1]
    attended_grad = bfloat(last_dot(attn_rows, kept_state.output_full)).reshape(
        group_rows, local_heads, VDIM
    )
    query_g, key_g, value_g = attend_back(
        kept_state.query_all,
        kept_state.key_all,
        kept_state.value_all,
        kept_state.doc_ids,
        (NOPE + ROPE) ** (-0.5),
        kept_state.log_total,
        attended_grad,
    )
    query_low = bfloat(query_g)
    key_low = bfloat(key_g)
    value_low = bfloat(value_g)
    query_unrot = rotate(
        query_low[..., NOPE:].astype(jnp.float32),
        kept_state.cos_group[:, None, :],
        -kept_state.sin_group[:, None, :],
    )
    qraw_grad = bfloat(
        jnp.concatenate([query_low[..., :NOPE].astype(jnp.float32), query_unrot], axis=-1)
    )
    qraw_grad = qraw_grad.reshape(group_rows, local_heads * (NOPE + ROPE))
    query_wgrad = first_dot(kept_state.normed_group, qraw_grad)
    normed_partial = last_dot(qraw_grad, kept_state.query_full)
    expand_rows = jnp.concatenate([key_low[..., :NOPE], value_low], axis=-1).reshape(
        group_rows, local_heads * (NOPE + VDIM)
    )
    expand_wgrad = first_dot(kept_state.latent_group, expand_rows)
    latent_partial = last_dot(expand_rows, kept_state.expand_full)
    keyrot_partial = jnp.sum(key_low[..., NOPE:].astype(jnp.float32), axis=1)
    normed_back, latent_back, keyrot_back = (
        lax.psum_scatter(
            normed_partial.astype(jnp.bfloat16), TENSOR, scatter_dimension=0, tiled=True
        ).astype(jnp.float32),
        lax.psum_scatter(
            latent_partial.astype(jnp.bfloat16), TENSOR, scatter_dimension=0, tiled=True
        ).astype(jnp.float32),
        lax.psum_scatter(
            keyrot_partial.astype(jnp.bfloat16), TENSOR, scatter_dimension=0, tiled=True
        ).astype(jnp.float32),
    )
    keyraw_back = rotate(keyrot_back, kept_state.cos_local, -kept_state.sin_local)
    latent_in, latgain_part = rms_back(
        latent_back, kept_state.latent_part, kept_state.scale_latent, latent_gain
    )
    latent_low = bfloat(jnp.concatenate([latent_in, keyraw_back], axis=-1))
    latent_wgrad = first_dot(kept_state.normed_one, latent_low)
    normed_total = normed_back + last_dot(latent_low, latent_weight)
    hidden_back, attngain_part = rms_back(
        normed_total, kept_state.hidden_f, kept_state.scale_one, attn_gain
    )
    hidden_grad = resid_grad + hidden_back
    fsdp_sums = (
        lax.psum_scatter(
            query_wgrad.astype(jnp.bfloat16), DP, scatter_dimension=0, tiled=True
        ).astype(jnp.float32),
        lax.psum_scatter(
            expand_wgrad.astype(jnp.bfloat16), DP, scatter_dimension=0, tiled=True
        ).astype(jnp.float32),
        lax.psum_scatter(
            output_wgrad.astype(jnp.bfloat16), DP, scatter_dimension=1, tiled=True
        ).astype(jnp.float32),
        lax.psum_scatter(
            sgate_wgrad.astype(jnp.bfloat16), DP, scatter_dimension=0, tiled=True
        ).astype(jnp.float32),
        lax.psum_scatter(
            sup_wgrad.astype(jnp.bfloat16), DP, scatter_dimension=0, tiled=True
        ).astype(jnp.float32),
        lax.psum_scatter(
            sdown_wgrad.astype(jnp.bfloat16), DP, scatter_dimension=1, tiled=True
        ).astype(jnp.float32),
    )
    small_sums = lax.psum(
        (latent_wgrad, attngain_part, mlpgain_part, latgain_part), (DP, TENSOR)
    )
    return (
        kept_state.layer_out,
        hidden_grad,
        small_sums[1],
        fsdp_sums[0],
        small_sums[0],
        small_sums[3],
        fsdp_sums[1],
        fsdp_sums[2],
        small_sums[2],
        fsdp_sums[3],
        fsdp_sums[4],
        fsdp_sums[5],
        expert_gate_weight_gradient,
        expert_up_weight_gradient,
        expert_down_weight_gradient,
    )


MESH = pl.DeviceIdType.MESH


def flip(index, bit):
    return index + bit - 2 * bit * ((index // bit) % 2)


def remote(src, dst, send_sem, recv_sem, peer):
    return pltpu.make_async_remote_copy(
        src_ref=src,
        dst_ref=dst,
        send_sem=send_sem,
        recv_sem=recv_sem,
        device_id=peer,
        device_id_type=MESH,
    )


def greet(peers):
    barrier = pltpu.get_barrier_semaphore()
    for peer in peers:
        pl.semaphore_signal(barrier, inc=1, device_id=peer, device_id_type=MESH)
    pl.semaphore_wait(barrier, len(peers))


(
    K_RING,
    K_X,
    K_Y,
    K_CORE,
    K_FAR_Y,
    K_FAR_X,
    K_CORE_X,
    K_CORE_Y,
    K_CORE_FAR,
    K_CORE_OWN,
    K_X_FIRST,
    K_X_LAST,
    K_Y_FIRST,
    K_Y_LAST,
) = range(14)

SLOTS = (0, 1, 2, 4, 3, 5, 6, 7)


def moe_kernel(
    rows,
    back,
    gates,
    expert_gate,
    expert_up,
    shared_all,
    rows_all,
    act_all,
    gpre_all,
    upre_all,
    grad_out,
    gate_rows,
    up_rows,
    row_buf,
    back_buf,
    out_buf,
    blocks,
    core_buf,
    far_buf,
    x_buf,
    y_buf,
    ring_buf,
    ring_out,
    weight_sem,
    load_sem,
    back_sem,
    store_sem,
    ag_send,
    ag_recv,
    rs_send,
    rs_recv,
    ring_send,
    ring_recv,
    *,
    expert_width,
    routed_width,
):
    me, rank = lax.axis_index(DP), lax.axis_index(TENSOR)
    ranks = lax.axis_size(TENSOR)
    right = (me, lax.rem(rank + 1, ranks))
    left = (me, lax.rem(rank + ranks - 1, ranks))
    by_core, by_x, by_y = [(flip(me, bit), rank) for bit in (1, 2, 4)]
    count = rows.shape[0]
    half = count // 2
    first, last = pl.ds(0, half), pl.ds(half, half)
    hidden_width = gate_rows.shape[0]
    shared_pad = shared_all.shape[1]
    greet([by_core, by_x, by_y, right, left])

    def ag(kind, j, src, dst, peer):
        return remote(src, dst, ag_send.at[kind, j], ag_recv.at[kind, j], peer)

    def rs(kind, j, src, dst, peer):
        return remote(src, dst, rs_send.at[kind, j], rs_recv.at[kind, j], peer)

    def row_copy(kind, j):
        at = rows_all.at
        return {
            K_RING: lambda: ag(0, j, at[0, j - 1], at[0, j], right),
            K_X: lambda: ag(1, j, at[0, j], at[2, j], by_x),
            K_Y: lambda: ag(2, j, at[0, j], at[3, j], by_y),
            K_CORE: lambda: ag(3, j, at[0, j], at[1, j], by_core),
            K_FAR_Y: lambda: ag(4, j, at[2, j, last], at[6, j, last], by_y),
            K_FAR_X: lambda: ag(5, j, at[3, j, first], at[6, j, first], by_x),
            K_CORE_X: lambda: ag(6, j, at[2, j], at[4, j], by_core),
            K_CORE_Y: lambda: ag(7, j, at[3, j], at[5, j], by_core),
            K_CORE_FAR: lambda: ag(8, j, at[6, j], at[7, j], by_core),
        }[kind]()

    def sum_copy(kind, j):
        at = blocks.at[lax.rem(j, 2)].at
        return {
            K_CORE_OWN: lambda: rs(0, j, at[1], core_buf.at[j, 0], by_core),
            K_CORE_X: lambda: rs(1, j, at[4], core_buf.at[j, 1], by_core),
            K_CORE_Y: lambda: rs(2, j, at[5], core_buf.at[j, 2], by_core),
            K_CORE_FAR: lambda: rs(3, j, at[7], core_buf.at[j, 3], by_core),
            K_FAR_X: lambda: rs(4, j, at[6, first], far_buf.at[j, 0], by_x),
            K_FAR_Y: lambda: rs(5, j, at[6, last], far_buf.at[j, 1], by_y),
            K_X_FIRST: lambda: rs(6, j, at[2, first], x_buf.at[j, 0], by_x),
            K_X_LAST: lambda: rs(7, j, at[2, last], x_buf.at[j, 1], by_x),
            K_Y_FIRST: lambda: rs(8, j, at[3, first], y_buf.at[j, 0], by_y),
            K_Y_LAST: lambda: rs(9, j, at[3, last], y_buf.at[j, 1], by_y),
        }[kind]()

    def ring_copy(step):
        return remote(
            ring_out.at[step], ring_buf.at[step], ring_send.at[step], ring_recv.at[step], right
        )

    def add_rows(target, size, *terms, store=None):
        step = 16

        def one(i, carry):
            at = pl.ds(pl.multiple_of(i * step, step), step)
            total = target[at, :].astype(jnp.float32)
            for term in terms:
                total = total + term[at, :].astype(jnp.float32)
            to = target if store is None else store
            to[at, :] = total.astype(to.dtype)
            return carry

        lax.fori_loop(0, size // step, one, 0)

    def loads(j, p, parity):
        return (
            pltpu.make_async_copy(
                back.at[pl.ds(2 * p, 2), j], back_buf.at[parity], back_sem.at[parity]
            ),
        )

    def stores(j, p, parity):
        return [
            pltpu.make_async_copy(
                out_buf.at[parity, n], to.at[pl.ds(2 * p, 2), j], store_sem.at[parity, n]
            )
            for n, to in enumerate((act_all, gpre_all, upre_all))
        ]

    def compute(j, p):
        parity = p % 2
        load = pltpu.make_async_copy(rows_all.at[pl.ds(2 * p, 2), j], row_buf, load_sem)
        load.start()
        if p < 3:
            for copy in loads(j, p + 1, 1 - parity):
                copy.start()
        else:

            @pl.when(j < ranks - 1)
            def _():
                for copy in loads(j + 1, 0, 0):
                    copy.start()

        for copy in loads(j, p, parity):
            copy.wait()
        if p >= 2:
            for copy in stores(j, p - 2, parity):
                copy.wait()
        else:

            @pl.when(j > 0)
            def _():
                for copy in stores(j - 1, p + 2, parity):
                    copy.wait()

        load.wait()
        wide = row_buf[...].reshape(2 * count, row_buf.shape[2])
        gate_pre = last_dot(wide, gate_rows[...])
        up_pre = last_dot(wide, up_rows[...])
        column = lax.broadcasted_iota(jnp.int32, (1, hidden_width), 1)
        lanes = pl.ds(pl.multiple_of(j * count, count), count)
        gate = jnp.concatenate([gates[2 * p + i, :, lanes].T for i in range(2)], axis=0)
        scaled = jnp.where(
            column < expert_width,
            gate[:, 0:1],
            jnp.where(column < routed_width, gate[:, 1:2], 1.0),
        )
        sigmoid = 1.0 / (1.0 + jnp.exp(-gate_pre))
        silu = gate_pre * sigmoid
        dsilu = sigmoid * (1.0 + gate_pre * (1.0 - sigmoid))
        back_pre = back_buf[parity].reshape(2 * count, hidden_width).astype(jnp.float32) * scaled
        act = bfloat(silu * up_pre * scaled)
        gate_grad = bfloat(back_pre * up_pre * dsilu)
        up_grad = bfloat(back_pre * silu)
        out_buf[parity, 0] = act.reshape(2, count, hidden_width)
        out_buf[parity, 1] = gate_grad.reshape(2, count, hidden_width)
        out_buf[parity, 2] = up_grad.reshape(2, count, hidden_width)
        for copy in stores(j, p, parity):
            copy.start()
        grad = plain_dot(gate_grad, gate_rows[...]) + plain_dot(up_grad, up_rows[...])
        blocks[lax.rem(j, 2), pl.ds(2 * p, 2)] = bfloat(grad).reshape(2, count, grad.shape[1])

    own = pltpu.make_async_copy(rows, rows_all.at[0, 0], load_sem)
    own.start()
    assembled = []
    for n, (routed, target) in enumerate(((expert_gate, gate_rows), (expert_up, up_rows))):
        for i, (src, at) in enumerate(
            ((routed, pl.ds(0, routed_width)), (shared_all.at[n], pl.ds(routed_width, shared_pad)))
        ):
            copy = pltpu.make_async_copy(src, target.at[at], weight_sem.at[n, i])
            copy.start()
            assembled.append(copy)
        target[routed_width + shared_pad :] = jnp.zeros(
            (hidden_width - routed_width - shared_pad, target.shape[1]), jnp.bfloat16
        )
    for copy in loads(0, 0, 0):
        copy.start()
    own.wait()
    ring0 = row_copy(K_RING, 1)
    ring0.start()
    for kind in (K_X, K_Y, K_CORE):
        row_copy(kind, 0).start()
    for copy in assembled:
        copy.wait()

    def body(j, carry):
        before = j - 1

        @pl.when(j < ranks)
        def _():
            row_copy(K_CORE, j).wait_recv()
            compute(j, 0)
            sum_copy(K_CORE_OWN, j).start()

        @pl.when(j > 0)
        def _():
            par = lax.rem(before, 2)
            sum_copy(K_CORE_FAR, before).wait_recv()
            add_rows(blocks.at[par, 6], count, core_buf.at[before, 3])
            sum_copy(K_FAR_X, before).start()
            sum_copy(K_FAR_Y, before).start()

        @pl.when(j < ranks)
        def _():
            row_copy(K_X, j).wait_recv()
            row_copy(K_FAR_Y, j).start()
            row_copy(K_CORE_X, j).start()
            row_copy(K_Y, j).wait_recv()
            row_copy(K_FAR_X, j).start()
            row_copy(K_CORE_Y, j).start()

            @pl.when(j < ranks - 1)
            def _():
                row_copy(K_RING, j + 1).wait_recv()

                @pl.when(j < ranks - 2)
                def _():
                    row_copy(K_RING, j + 2).start()

                for kind in (K_X, K_Y, K_CORE):
                    row_copy(kind, j + 1).start()

            compute(j, 1)

        @pl.when(j > 0)
        def _():
            par = lax.rem(before, 2)
            sum_copy(K_FAR_X, before).wait_recv()
            add_rows(
                blocks.at[par, 3, first],
                half,
                core_buf.at[before, 2, first],
                far_buf.at[before, 0],
            )
            sum_copy(K_Y_FIRST, before).start()
            sum_copy(K_FAR_Y, before).wait_recv()
            add_rows(
                blocks.at[par, 2, last],
                half,
                core_buf.at[before, 1, last],
                far_buf.at[before, 1],
            )
            sum_copy(K_X_LAST, before).start()

        @pl.when(j < ranks)
        def _():
            row_copy(K_FAR_X, j).wait_recv()
            row_copy(K_FAR_Y, j).wait_recv()
            row_copy(K_CORE_FAR, j).start()
            row_copy(K_CORE_X, j).wait_recv()
            row_copy(K_CORE_Y, j).wait_recv()
            compute(j, 2)
            sum_copy(K_CORE_X, j).start()
            sum_copy(K_CORE_Y, j).start()
            row_copy(K_CORE_FAR, j).wait_recv()
            compute(j, 3)
            sum_copy(K_CORE_FAR, j).start()
            par = lax.rem(j, 2)
            sum_copy(K_CORE_X, j).wait_recv()
            add_rows(blocks.at[par, 2, first], half, core_buf.at[j, 1, first])
            sum_copy(K_X_FIRST, j).start()
            sum_copy(K_CORE_Y, j).wait_recv()
            add_rows(blocks.at[par, 3, last], half, core_buf.at[j, 2, last])
            sum_copy(K_Y_LAST, j).start()

        @pl.when(j > 0)
        def _():
            par = lax.rem(before, 2)
            for kind in (K_CORE_OWN, K_X_FIRST, K_X_LAST, K_Y_FIRST, K_Y_LAST):
                sum_copy(kind, before).wait_recv()
            terms = [
                (core_buf.at[before, 0, part], x_buf.at[before, n], y_buf.at[before, n])
                for n, part in enumerate((first, last))
            ]

            @pl.when(before == 0)
            def _():
                for part, more in zip((first, last), terms):
                    add_rows(blocks.at[par, 0, part], half, *more, store=grad_out.at[part])

            @pl.when(before == 1)
            def _():
                for part, more in zip((first, last), terms):
                    add_rows(blocks.at[par, 0, part], half, *more, store=ring_out.at[0, part])
                ring_copy(0).start()

            @pl.when(before > 1)
            def _():
                ring_copy(before - 2).wait_recv()
                for part, more in zip((first, last), terms):
                    add_rows(
                        blocks.at[par, 0, part],
                        half,
                        *more,
                        ring_buf.at[before - 2, part],
                        store=ring_out.at[before - 1, part],
                    )
                ring_copy(before - 1).start()

            for kind in (
                K_CORE_OWN,
                K_CORE_X,
                K_CORE_Y,
                K_CORE_FAR,
                K_FAR_X,
                K_FAR_Y,
                K_X_FIRST,
                K_X_LAST,
                K_Y_FIRST,
                K_Y_LAST,
            ):
                sum_copy(kind, before).wait_send()

        return carry

    lax.fori_loop(0, ranks + 1, body, 0)
    ring_copy(ranks - 2).wait_recv()
    add_rows(grad_out, count, ring_buf.at[ranks - 2])
    for step in range(ranks - 1):
        ring_copy(step).wait_send()
        row_copy(K_RING, step + 1).wait_send()
    for p in (2, 3):
        for copy in stores(ranks - 1, p, p % 2):
            copy.wait()

    def drain(j, carry):
        for kind in (K_X, K_Y, K_CORE, K_FAR_Y, K_FAR_X, K_CORE_X, K_CORE_Y, K_CORE_FAR):
            row_copy(kind, j).wait_send()
        return carry

    lax.fori_loop(0, ranks, drain, 0)


def moe_pass(rows, back, gates, expert_gate, expert_up, shared_all, expert_width):
    ranks = lax.axis_size(TENSOR)
    groups = lax.axis_size(DP)
    count, width = rows.shape
    hidden_width = back.shape[-1]
    anywhere = pl.BlockSpec(memory_space=pl.ANY)
    in_vmem = pl.BlockSpec(memory_space=pltpu.VMEM)
    low = jnp.bfloat16
    hidden_shape = jax.ShapeDtypeStruct((groups, ranks, count, hidden_width), low)
    dma = pltpu.SemaphoreType.DMA
    return pl.pallas_call(
        functools.partial(
            moe_kernel, expert_width=expert_width, routed_width=expert_gate.shape[0]
        ),
        out_shape=(
            jax.ShapeDtypeStruct((groups, ranks, count, width), low),
            hidden_shape,
            hidden_shape,
            hidden_shape,
            jax.ShapeDtypeStruct((count, width), jnp.float32),
        ),
        in_specs=[anywhere, anywhere, in_vmem, anywhere, anywhere, anywhere],
        out_specs=(anywhere, anywhere, anywhere, anywhere, in_vmem),
        scratch_shapes=[
            pltpu.VMEM((hidden_width, width), low),
            pltpu.VMEM((hidden_width, width), low),
            pltpu.VMEM((2, count, width), low),
            pltpu.VMEM((2, 2, count, hidden_width), low),
            pltpu.VMEM((2, 3, 2, count, hidden_width), low),
            pltpu.VMEM((2, groups, count, width), low),
            pltpu.VMEM((ranks, 4, count, width), low),
            pltpu.VMEM((ranks, 2, count // 2, width), low),
            pltpu.VMEM((ranks, 2, count // 2, width), low),
            pltpu.VMEM((ranks, 2, count // 2, width), low),
            pltpu.VMEM((ranks - 1, count, width), low),
            pltpu.VMEM((ranks - 1, count, width), low),
            dma((2, 2)),
            dma,
            dma((2,)),
            dma((2, 3)),
            dma((9, ranks)),
            dma((9, ranks)),
            dma((10, ranks)),
            dma((10, ranks)),
            dma((ranks - 1,)),
            dma((ranks - 1,)),
        ],
        compiler_params=pltpu.CompilerParams(
            collective_id=2, has_side_effects=True, vmem_limit_bytes=60 * 1024 * 1024
        ),
        name="moe_pass",
    )(rows, back, gates, expert_gate, expert_up, shared_all)


def cube_copies(gathered, sends, recvs, by_core, by_x, by_y):
    half = gathered.shape[2] // 2
    first, last = pl.ds(0, half), pl.ds(half, half)
    at = gathered.at

    def copy(kind, j):
        src, dst, peer = {
            K_X: lambda: (at[0, j], at[2, j], by_x),
            K_Y: lambda: (at[0, j], at[3, j], by_y),
            K_CORE: lambda: (at[0, j], at[1, j], by_core),
            K_FAR_Y: lambda: (at[2, j, last], at[6, j, last], by_y),
            K_FAR_X: lambda: (at[3, j, first], at[6, j, first], by_x),
            K_CORE_X: lambda: (at[2, j], at[4, j], by_core),
            K_CORE_Y: lambda: (at[3, j], at[5, j], by_core),
            K_CORE_FAR: lambda: (at[6, j], at[7, j], by_core),
        }[kind]()
        return remote(src, dst, sends.at[kind, j], recvs.at[kind, j], peer)

    return copy


def swap_halves(values):
    lane = lax.broadcasted_iota(jnp.int32, values.shape, 1)
    middle = ROPE // 2
    lanes = values.shape[1]
    ahead, behind = pltpu.roll(values, lanes - middle, 1), pltpu.roll(values, middle, 1)
    return jnp.where((lane // middle) % 2 == 0, ahead, behind)


def turn(values, cos_table, sin_table):
    return values * cos_table + swap_halves(values) * sin_table


def front_kernel(
    lengths,
    hidden,
    cotangent,
    query,
    expand,
    output,
    shared,
    expert_down,
    routes,
    route_gates,
    latent_rows,
    attn_gain,
    latent_gain,
    mlp_gain,
    frequency,
    normed_out,
    latent_out,
    own_latent,
    query_out,
    expand_out,
    output_out,
    qcat_out,
    kcat_out,
    value_out,
    prob_out,
    attended_out,
    cos_out,
    sin_out,
    residual_out,
    normed_two,
    shared_all,
    gates_all,
    cotan_all,
    back_all,
    hidden_all,
    query_all,
    expand_all,
    output_all,
    down_rows,
    normed,
    latent_low,
    q_cat,
    k_cat,
    value,
    mask,
    prob,
    attended,
    gate_abs,
    gate_rel,
    gate_send,
    row_buf,
    back_buf,
    ring_out,
    ring_buf,
    local_sem,
    prob_sem,
    row_sem,
    back_sem,
    ring_send,
    ring_recv,
    w_send,
    w_recv,
    deal_send,
    deal_recv,
    gates_send,
    gates_recv,
    cring_send,
    cring_recv,
    c_send,
    c_recv,
    sum_send,
    sum_recv,
):
    me, rank = lax.axis_index(DP), lax.axis_index(TENSOR)
    ranks, count = lax.axis_size(TENSOR), lax.axis_size(DP)
    right = (me, lax.rem(rank + 1, ranks))
    left = (me, lax.rem(rank + ranks - 1, ranks))
    by_core, by_x, by_y = [(flip(me, bit), rank) for bit in (1, 2, 4)]
    partners = []
    for k in range(1, count):
        other = me
        for bit in (1, 2, 4):
            other = flip(other, bit) if k & bit else other
        partners.append((k, (other, rank)))
    rows, width = hidden.shape
    group_rows = rows * ranks
    heads = q_cat.shape[0]
    local_experts = gate_abs.shape[0] // count
    q_rows, e_rows, o_cols = query.shape[0], expand.shape[0], output.shape[1]
    routed_width = expert_down.shape[0]
    shared_pad = shared.shape[2]
    piece = shared.shape[3]

    def query_at(owner, half=None):
        size = q_rows if half is None else q_rows // 2
        start = owner * q_rows + (0 if half is None else half * size)
        return query_all.at[pl.ds(pl.multiple_of(start, size), size)]

    def expand_at(owner, half=None):
        size = e_rows if half is None else e_rows // 2
        start = owner * e_rows + (0 if half is None else half * size)
        return expand_all.at[pl.ds(pl.multiple_of(start, size), size)]

    def output_at(owner, half=None):
        size = output.shape[0] if half is None else output.shape[0] // 2
        start = 0 if half is None else half * size
        return output_all.at[
            pl.ds(start, size), pl.ds(pl.multiple_of(owner * o_cols, o_cols), o_cols)
        ]

    greet([peer for _, peer in partners] + [right, left])

    ring = {}

    def ring_step(step):
        src = hidden if step == 0 else hidden_all.at[step]
        ring[step] = remote(
            src, hidden_all.at[step + 1], ring_send.at[step], ring_recv.at[step], right
        )
        ring[step].start()

    weights = ((query, query_at), (expand, expand_at), (output, output_at))
    copies = {}

    def send(i, kind, src, dst, peer):
        copies[i, kind] = remote(src, dst, w_send.at[i, kind], w_recv.at[i, kind], peer)
        copies[i, kind].start()

    def weight_first(i):
        own, at = weights[i]
        send(i, 0, own, at(me), by_x)
        send(i, 1, own, at(me), by_y)
        send(i, 2, own, at(me), by_core)

    def weight_forward(i):
        _, at = weights[i]
        copies[i, 0].wait_recv()
        send(i, 3, at(flip(me, 2), 1), at(flip(me, 2), 1), by_y)
        send(i, 4, at(flip(me, 2)), at(flip(me, 2)), by_core)
        copies[i, 1].wait_recv()
        send(i, 5, at(flip(me, 4), 0), at(flip(me, 4), 0), by_x)
        send(i, 6, at(flip(me, 4)), at(flip(me, 4)), by_core)

    def weight_far(i):
        _, at = weights[i]
        far = flip(flip(me, 2), 4)
        copies[i, 3].wait_recv()
        copies[i, 5].wait_recv()
        send(i, 7, at(far), at(far), by_core)

    def weight_last(i):
        for kind in (2, 4, 6, 7):
            copies[i, kind].wait_recv()

    cube = cube_copies(cotan_all, c_send, c_recv, by_core, by_x, by_y)

    def cotan_ring(j):
        src = cotan_all.at[0, j - 1]
        return remote(src, cotan_all.at[0, j], cring_send.at[j - 1], cring_recv.at[j - 1], right)

    def cotan_send(j):
        for kind in (K_X, K_Y, K_CORE):
            cube(kind, j).start()

    def cotan_forward(j):
        cube(K_X, j).wait_recv()
        cube(K_FAR_Y, j).start()
        cube(K_CORE_X, j).start()
        cube(K_Y, j).wait_recv()
        cube(K_FAR_X, j).start()
        cube(K_CORE_Y, j).start()

    def cotan_far(j):
        cube(K_FAR_X, j).wait_recv()
        cube(K_FAR_Y, j).wait_recv()
        cube(K_CORE_FAR, j).start()

    def cotan_next(j):
        cotan_ring(j).wait_recv()
        if j + 1 < ranks:
            cotan_ring(j + 1).start()
        cotan_send(j)

    def down_back(j):
        for kind in (K_CORE, K_CORE_X, K_CORE_Y, K_CORE_FAR):
            cube(kind, j).wait_recv()

        def load(p, parity):
            return pltpu.make_async_copy(
                cotan_all.at[pl.ds(2 * p, 2), j], row_buf.at[parity], row_sem.at[parity]
            )

        def store(p, parity):
            return pltpu.make_async_copy(
                back_buf.at[parity], back_all.at[pl.ds(2 * p, 2), j], back_sem.at[parity]
            )

        load(0, 0).start()

        def one(p, carry):
            parity = lax.rem(p, 2)
            load(p, parity).wait()

            @pl.when(p < 3)
            def _():
                load(p + 1, 1 - parity).start()

            @pl.when(p > 1)
            def _():
                store(p - 2, parity).wait()

            wide = row_buf[parity].reshape(2 * rows, width)
            back = bfloat(last_dot(wide, down_rows[...]))
            back_buf[parity] = back.reshape(2, rows, back.shape[1])
            store(p, parity).start()
            return carry

        lax.fori_loop(0, 4, one, 0)
        store(2, 0).wait()
        store(3, 1).wait()

    ring_step(0)
    weight_first(0)
    weight_first(1)
    dealt = []
    for n, (k, peer) in enumerate(partners):
        copy = remote(
            shared.at[peer[0]],
            shared_all.at[:, :, pl.ds(pl.multiple_of(me * piece, piece), piece)],
            deal_send.at[n],
            deal_recv.at[n],
            peer,
        )
        dealt.append(copy)
    local = [
        pltpu.make_async_copy(hidden, hidden_all.at[0], local_sem.at[0]),
        pltpu.make_async_copy(query, query_at(me), local_sem.at[1]),
        pltpu.make_async_copy(expand, expand_at(me), local_sem.at[2]),
        pltpu.make_async_copy(output, output_at(me), local_sem.at[3]),
        pltpu.make_async_copy(
            shared.at[me],
            shared_all.at[:, :, pl.ds(pl.multiple_of(me * piece, piece), piece)],
            local_sem.at[4],
        ),
        pltpu.make_async_copy(cotangent, cotan_all.at[0, 0], local_sem.at[5]),
        pltpu.make_async_copy(expert_down, down_rows.at[pl.ds(0, routed_width)], local_sem.at[6]),
    ]
    for copy in local:
        copy.start()

    def absolute(index):
        block = index // rows
        return ((rank + ranks - block) % ranks) * rows + index % rows

    def starts_of(token):
        start, total = jnp.zeros_like(token), 0
        for n in range(lengths.shape[1]):
            total = total + lengths[0, n]
            start = jnp.where(token >= total, total, start)
        return start

    token = absolute(lax.broadcasted_iota(jnp.int32, (group_rows, cos_out.shape[1]), 0))
    angle = (token - starts_of(token)).astype(jnp.float32) * frequency[...]
    lane = lax.broadcasted_iota(jnp.int32, angle.shape, 1)
    cos_out[...] = jnp.cos(angle)
    sine = jnp.sin(angle)
    sin_out[...] = jnp.where((lane // (ROPE // 2)) % 2 == 0, -sine, sine)
    row_token = absolute(lax.broadcasted_iota(jnp.int32, mask.shape, 0))
    column_token = absolute(lax.broadcasted_iota(jnp.int32, mask.shape, 1))
    allowed = (column_token <= row_token) & (column_token >= starts_of(row_token))
    mask[...] = jnp.where(allowed, 0.0, -jnp.inf)

    expert = lax.broadcasted_iota(jnp.int32, gate_abs.shape, 0)
    dense = jnp.zeros(gate_abs.shape, jnp.float32)
    for k in range(routes.shape[0]):
        dense = dense + jnp.where(routes[k : k + 1, :] == expert, route_gates[k : k + 1, :], 0.0)
    gate_abs[...] = dense
    for r in range(ranks):
        start = pl.multiple_of(((rank + ranks - r) % ranks) * rows, rows)
        gate_rel[:, r * rows : (r + 1) * rows] = gate_abs[:, pl.ds(start, rows)]
    gate_send[...] = jnp.zeros_like(gate_send)
    for p in range(count):
        gate_send[p, 0:local_experts] = gate_rel[p * local_experts : (p + 1) * local_experts]
    down_rows[routed_width + shared_pad :] = jnp.zeros(
        (down_rows.shape[0] - routed_width - shared_pad, width), jnp.bfloat16
    )
    gate_copies = []
    for n, (k, peer) in enumerate(partners):
        gate_copies.append(
            remote(
                gate_send.at[peer[0]],
                gates_all.at[SLOTS.index(k)],
                gates_send.at[n],
                gates_recv.at[n],
                peer,
            )
        )
    own_gates = pltpu.make_async_copy(gate_send.at[me], gates_all.at[0], local_sem.at[7])
    own_gates.start()

    def norm_piece(r):
        at = pl.ds(r * rows, rows)
        values = hidden_all[r].astype(jnp.float32)
        scale = lax.rsqrt(jnp.mean(values * values, axis=-1, keepdims=True) + epsilon)
        normed[at, :] = bfloat(values * scale * attn_gain[...])

    def project_piece(r):
        at = pl.ds(r * rows, rows)
        values = normed[at, :]
        cos_table, sin_table = cos_out[at, :], sin_out[at, :]
        lanes = cos_table.shape[1]
        raw = plain_dot(values, query_all[...])
        for h in range(heads):
            q_cat[h, at, 0:NOPE] = bfloat(raw[:, h * NOPE : (h + 1) * NOPE])
        for pair in range(heads // 2):
            start = heads * NOPE + pair * lanes
            turned = bfloat(turn(raw[:, start : start + lanes], cos_table, sin_table))
            q_cat[2 * pair, at, NOPE : NOPE + lanes] = turned
            q_cat[2 * pair + 1, at, NOPE : NOPE + lanes] = turned
        latent = last_dot(values, latent_rows[...])
        part = latent[:, :LATENT]
        if r == 0:
            own_latent[...] = part
        scale = lax.rsqrt(jnp.mean(part * part, axis=-1, keepdims=True) + epsilon)
        low_part = bfloat(part * scale * latent_gain[...])
        latent_low[at, :] = low_part
        turned = turn(latent[:, LATENT:], cos_table, sin_table)
        lane = lax.broadcasted_iota(jnp.int32, turned.shape, 1)
        even = bfloat(jnp.where(lane < ROPE, turned, 0.0))
        odd = bfloat(jnp.where(lane < ROPE, 0.0, turned))
        expanded = plain_dot(low_part, expand_all[...])
        step = NOPE + VDIM
        for h in range(heads):
            k_cat[h, at, 0:NOPE] = bfloat(expanded[:, h * step : h * step + NOPE])
            k_cat[h, at, NOPE : NOPE + lanes] = even if h % 2 == 0 else odd
            value[h, at, :] = bfloat(expanded[:, h * step + NOPE : (h + 1) * step])

    def prob_store(h, parity):
        return pltpu.make_async_copy(prob.at[parity], prob_out.at[h], prob_sem.at[parity])

    def head(h):
        parity = h % 2
        if h >= 2:
            prob_store(h - 2, parity).wait()
        scores = last_dot(q_cat[h], k_cat[h]) * (NOPE + ROPE) ** (-0.5) + mask[...]
        exp_scores = jnp.exp(scores - jnp.max(scores, axis=-1, keepdims=True))
        ratio = exp_scores / jnp.sum(exp_scores, axis=-1, keepdims=True)
        prob[parity] = ratio
        prob_store(h, parity).start()
        attended[:, h * VDIM : (h + 1) * VDIM] = bfloat(plain_dot(bfloat(ratio), value[h]))

    norm_piece_wait = [local[0].wait] + [lambda s=s: ring[s].wait_recv() for s in range(ranks - 1)]
    norm_piece_wait[0]()
    norm_piece(0)
    for copy in dealt:
        copy.start()
    for copy in gate_copies:
        copy.start()
    weight_first(2)
    weight_forward(0)
    norm_piece_wait[1]()
    ring_step(1)
    weight_forward(1)
    norm_piece(1)
    weight_far(0)
    weight_far(1)
    local[5].wait()
    cotan_send(0)
    norm_piece_wait[2]()
    ring_step(2)
    cotan_ring(1).start()
    norm_piece(2)
    weight_forward(2)
    weight_last(0)
    weight_last(1)
    local[1].wait()
    local[2].wait()
    project_piece(0)
    project_piece(1)
    weight_far(2)
    project_piece(2)
    norm_piece_wait[3]()
    norm_piece(3)
    cotan_forward(0)
    project_piece(3)
    cotan_next(1)
    head(0)
    cotan_far(0)
    cotan_forward(1)
    head(1)
    cotan_next(2)
    head(2)
    cotan_far(1)
    head(3)
    weight_last(2)
    local[3].wait()

    def attn_block(r):
        return plain_dot(attended[r * rows : (r + 1) * rows, :], output_all[...])

    def sum_step(step):
        return remote(
            ring_out.at[step], ring_buf.at[step], sum_send.at[step], sum_recv.at[step], right
        )

    ring_out[0] = bfloat(attn_block(1))
    sum_step(0).start()
    cotan_forward(2)
    cotan_next(3)
    for copy in dealt:
        copy.wait_recv()
    local[4].wait()
    local[6].wait()
    shared_down = pltpu.make_async_copy(
        shared_all.at[2], down_rows.at[pl.ds(routed_width, shared_pad)], local_sem.at[8]
    )
    shared_down.start()
    shared_down.wait()
    down_back(0)
    sum_step(0).wait_recv()
    ring_out[1] = bfloat(attn_block(2) + ring_buf[0].astype(jnp.float32))
    sum_step(1).start()
    cotan_far(2)
    cotan_forward(3)
    down_back(1)
    sum_step(1).wait_recv()
    ring_out[2] = bfloat(attn_block(3) + ring_buf[1].astype(jnp.float32))
    sum_step(2).start()
    outs = [
        pltpu.make_async_copy(src, dst, local_sem.at[9 + n])
        for n, (src, dst) in enumerate(
            (
                (normed, normed_out),
                (latent_low, latent_out),
                (query_all, query_out),
                (expand_all, expand_out),
                (output_all, output_out),
                (q_cat, qcat_out),
                (k_cat, kcat_out),
                (value, value_out),
                (attended, attended_out),
            )
        )
    ]
    for copy in outs:
        copy.start()
    down_back(2)
    cotan_far(3)
    sum_step(2).wait_recv()
    residual = (
        hidden_all[0].astype(jnp.float32) + attn_block(0) + ring_buf[2].astype(jnp.float32)
    )
    residual_out[...] = residual
    scale = lax.rsqrt(jnp.mean(residual * residual, axis=-1, keepdims=True) + epsilon)
    normed_two[...] = bfloat(residual * scale * mlp_gain[...])
    down_back(3)

    for h in (heads - 2, heads - 1):
        prob_store(h, h % 2).wait()
    for copy in outs:
        copy.wait()
    own_gates.wait()
    for copy in gate_copies:
        copy.wait()
    for copy in dealt:
        copy.wait_send()
    for i in range(len(weights)):
        for kind in range(8):
            copies[i, kind].wait_send()
    for step in range(ranks - 1):
        ring[step].wait_send()
        cotan_ring(step + 1).wait_send()
        sum_step(step).wait_send()
    for j in range(ranks):
        for kind in (
            K_X,
            K_Y,
            K_CORE,
            K_FAR_Y,
            K_FAR_X,
            K_CORE_X,
            K_CORE_Y,
            K_CORE_FAR,
        ):
            cube(kind, j).wait_send()


def front_pass(
    lengths,
    hidden,
    cotangent,
    query,
    expand,
    output,
    shared,
    expert_down,
    routes,
    route_gates,
    latent_rows,
    attn_gain,
    latent_gain,
    mlp_gain,
    hidden_width,
    experts,
):
    count, ranks = lax.axis_size(DP), lax.axis_size(TENSOR)
    rows, width = hidden.shape
    group_rows = rows * ranks
    heads = query.shape[1] // (NOPE + ROPE)
    lanes = 2 * ROPE
    low, full = jnp.bfloat16, jnp.float32
    frequency = rope_base ** (-jnp.arange(ROPE // 2, dtype=full) * 2.0 / ROPE)
    frequency = jnp.tile(frequency, lanes // (ROPE // 2))[None, :]
    anywhere = pl.BlockSpec(memory_space=pl.ANY)
    in_vmem = pl.BlockSpec(memory_space=pltpu.VMEM)
    dma = pltpu.SemaphoreType.DMA
    by_slot = (count, ranks, rows)

    def array(*shape, dtype=low):
        return jax.ShapeDtypeStruct(shape, dtype)

    def full_query():
        return (count * query.shape[0], query.shape[1])

    def full_expand():
        return (count * expand.shape[0], expand.shape[1])

    def full_output():
        return (output.shape[0], count * output.shape[1])

    return pl.pallas_call(
        front_kernel,
        out_shape=(
            array(group_rows, width),
            array(group_rows, LATENT),
            array(rows, LATENT, dtype=full),
            array(*full_query()),
            array(*full_expand()),
            array(*full_output()),
            array(heads, group_rows, NOPE + lanes),
            array(heads, group_rows, NOPE + lanes),
            array(heads, group_rows, VDIM),
            array(heads, group_rows, group_rows, dtype=full),
            array(group_rows, heads * VDIM),
            array(group_rows, lanes, dtype=full),
            array(group_rows, lanes, dtype=full),
            array(rows, width, dtype=full),
            array(rows, width),
            array(*shared.shape[1:3], count * shared.shape[3]),
            array(count, 8, group_rows, dtype=full),
            array(*by_slot, width),
            array(*by_slot, hidden_width),
        ),
        in_specs=[pl.BlockSpec(memory_space=pltpu.SMEM)] + [anywhere] * 7 + [in_vmem] * 7,
        out_specs=(anywhere, anywhere, in_vmem)
        + (anywhere,) * 8
        + (in_vmem,) * 4
        + (anywhere,) * 4,
        scratch_shapes=[
            pltpu.VMEM((ranks, rows, width), low),
            pltpu.VMEM(full_query(), low),
            pltpu.VMEM(full_expand(), low),
            pltpu.VMEM(full_output(), low),
            pltpu.VMEM((hidden_width, width), low),
            pltpu.VMEM((group_rows, width), low),
            pltpu.VMEM((group_rows, LATENT), low),
            pltpu.VMEM((heads, group_rows, NOPE + lanes), low),
            pltpu.VMEM((heads, group_rows, NOPE + lanes), low),
            pltpu.VMEM((heads, group_rows, VDIM), low),
            pltpu.VMEM((group_rows, group_rows), full),
            pltpu.VMEM((2, group_rows, group_rows), full),
            pltpu.VMEM((group_rows, heads * VDIM), low),
            pltpu.VMEM((experts, group_rows), full),
            pltpu.VMEM((experts, group_rows), full),
            pltpu.VMEM((count, 8, group_rows), full),
            pltpu.VMEM((2, 2, rows, width), low),
            pltpu.VMEM((2, 2, rows, hidden_width), low),
            pltpu.VMEM((ranks - 1, rows, width), low),
            pltpu.VMEM((ranks - 1, rows, width), low),
            dma((18,)),
            dma((2,)),
            dma((2,)),
            dma((2,)),
            dma((ranks - 1,)),
            dma((ranks - 1,)),
            dma((3, 8)),
            dma((3, 8)),
            dma((count - 1,)),
            dma((count - 1,)),
            dma((count - 1,)),
            dma((count - 1,)),
            dma((ranks - 1,)),
            dma((ranks - 1,)),
            dma((9, ranks)),
            dma((9, ranks)),
            dma((ranks - 1,)),
            dma((ranks - 1,)),
        ],
        compiler_params=pltpu.CompilerParams(
            collective_id=1, has_side_effects=True, vmem_limit_bytes=60 * 1024 * 1024
        ),
        name="front_pass",
    )(
        lengths,
        hidden,
        cotangent,
        query,
        expand,
        output,
        shared,
        expert_down,
        routes,
        route_gates,
        latent_rows,
        attn_gain,
        latent_gain,
        mlp_gain,
        frequency,
    )


def swap(values, bit):
    return lax.ppermute(values, DP, [(i, i ^ bit) for i in range(lax.axis_size(DP))])


def shift(values, steps):
    count = lax.axis_size(TENSOR)
    return lax.ppermute(values, TENSOR, [(i, (i + steps) % count) for i in range(count)])


def add_low(left_op, right_op):
    return bfloat(left_op.astype(jnp.float32) + right_op.astype(jnp.float32))


def ring_gather(values):
    blocks = [values]
    for _ in range(lax.axis_size(TENSOR) - 1):
        blocks.append(shift(blocks[-1], 1))
    return blocks


def ring_scatter(blocks):
    count = len(blocks)
    total = blocks[1]
    for r in list(range(2, count)) + [0]:
        moved = shift(total, 1)
        if r:
            total = add_low(blocks[r], moved)
        else:
            total = blocks[0].astype(jnp.float32) + moved.astype(jnp.float32)
    return total


def cube_gather(values, axis=0):
    half = values.shape[axis] // 2
    first = lax.slice_in_dim(values, 0, half, axis=axis)
    last = lax.slice_in_dim(values, half, 2 * half, axis=axis)
    by_x, by_y, by_core = swap(values, 2), swap(values, 4), swap(values, 1)
    far_first = swap(lax.slice_in_dim(by_y, 0, half, axis=axis), 2)
    far_last = swap(lax.slice_in_dim(by_x, half, 2 * half, axis=axis), 4)
    far = jnp.concatenate([far_first, far_last], axis=axis)
    return [values, by_core, by_x, swap(by_x, 1), by_y, swap(by_y, 1), far, swap(far, 1)]


def cube_scatter(blocks):
    half = blocks[0].shape[0] // 2
    sums = {k: add_low(blocks[k], swap(blocks[k ^ 1], 1)) for k in (6, 2, 4, 0)}
    far_y = add_low(sums[4][:half], swap(sums[6][:half], 2))
    far_x = add_low(sums[2][half:], swap(sums[6][half:], 4))
    x_first, x_last = swap(sums[2][:half], 2), swap(far_x, 2)
    y_first, y_last = swap(far_y, 4), swap(sums[4][half:], 4)
    own = sums[0].astype(jnp.float32)
    first = own[:half] + x_first.astype(jnp.float32) + y_first.astype(jnp.float32)
    last = own[half:] + x_last.astype(jnp.float32) + y_last.astype(jnp.float32)
    return jnp.concatenate([first, last], axis=0)


def place(blocks, axis):
    me = lax.axis_index(DP)
    size = blocks[0].shape[axis]
    shape = list(blocks[0].shape)
    shape[axis] = size * len(blocks)
    whole = jnp.zeros(shape, blocks[0].dtype)
    for k, block in enumerate(blocks):
        whole = lax.dynamic_update_slice_in_dim(whole, block, (me ^ k) * size, axis)
    return whole


def pick(values, axis):
    me = lax.axis_index(DP)
    size = values.shape[axis] // lax.axis_size(DP)
    return [
        lax.dynamic_slice_in_dim(values, (me ^ k) * size, size, axis)
        for k in range(lax.axis_size(DP))
    ]


def part_heads(values, heads):
    split = values.reshape(-1, heads, NOPE + ROPE)
    parts = (split[:, :, :NOPE], split[:, :, NOPE:])
    return jnp.concatenate([part.reshape(values.shape[0], -1) for part in parts], axis=1)


def join_heads(values, heads):
    plain = values[:, : heads * NOPE].reshape(-1, heads, NOPE)
    turned = values[:, heads * NOPE :].reshape(-1, heads, ROPE)
    return jnp.concatenate([plain, turned], axis=2).reshape(values.shape)


def sum_all(values):
    for bit in (1, 2, 4):
        values = values + swap(values, bit)
    for bit in (1, 2):
        count = lax.axis_size(TENSOR)
        values = values + lax.ppermute(values, TENSOR, [(i, i ^ bit) for i in range(count)])
    return values


def cube_shards(
    hidden,
    cotangent,
    routes,
    route_gates,
    doc_lengths,
    attn_gain,
    query_weight,
    latent_weight,
    latent_gain,
    expand_weight,
    output_weight,
    mlp_gain,
    shared_gate,
    shared_up,
    shared_down,
    expert_gate,
    expert_up,
    expert_down,
):
    ranks = lax.axis_size(TENSOR)
    groups = lax.axis_size(DP)
    me_dp, me_tensor = lax.axis_index(DP), lax.axis_index(TENSOR)
    rows = hidden.shape[0]
    group_rows = rows * ranks
    width = hidden.shape[1]
    local_experts, _, expert_width = expert_gate.shape
    experts = local_experts * groups

    shared_width = shared_gate.shape[1] // groups
    shared_pad = -(-shared_width // 16) * 16
    shared_stack = jnp.stack(
        [
            jnp.pad(
                weight.reshape(groups, shared_width, weight.shape[1]),
                ((0, 0), (0, shared_pad - shared_width), (0, 0)),
            )
            for weight in (shared_gate.T, shared_up.T, shared_down)
        ],
        axis=1,
    )
    routed_width = local_experts * expert_width
    hidden_width = -(-(routed_width + shared_pad) // 128) * 128
    local_heads = query_weight.shape[1] // (NOPE + ROPE)
    latent_columns = latent_weight.T

    (
        normed_group,
        latent_group,
        own_latent,
        query_full,
        expand_full,
        output_full,
        q_cat,
        k_cat,
        value_all,
        probability,
        attended_low,
        cos_group,
        sin_group,
        residual,
        normed_two,
        shared_all,
        slot_gates,
        cotan_all,
        back_all,
    ) = front_pass(
        doc_lengths,
        hidden,
        cotangent,
        part_heads(query_weight, local_heads),
        expand_weight,
        output_weight,
        shared_stack,
        expert_down.reshape(-1, width),
        routes.T,
        route_gates.T,
        jnp.concatenate([latent_columns, latent_columns[LATENT:]], axis=0),
        attn_gain[None],
        latent_gain[None],
        mlp_gain[None],
        hidden_width,
        experts,
    )
    row_all, act_all, gate_all, up_all, mlp_grad = moe_pass(
        normed_two,
        back_all,
        slot_gates,
        expert_gate.transpose(0, 2, 1).reshape(-1, width),
        expert_up.transpose(0, 2, 1).reshape(-1, width),
        shared_all,
        expert_width,
    )
    hidden_f = hidden.astype(jnp.float32)
    scale_one = rms_scale(hidden_f)
    normed_one = bfloat(hidden_f * scale_one * attn_gain)
    scale_latent = rms_scale(own_latent)
    scale_two = rms_scale(residual)
    scaling = (NOPE + ROPE) ** (-0.5)
    cotan_all = cotan_all.reshape(-1, width)
    spare = jnp.zeros((hidden_width - routed_width - shared_pad, width), jnp.bfloat16)
    down_rows = jnp.concatenate([expert_down.reshape(-1, width), shared_all[2], spare], axis=0)
    row_all = row_all.reshape(-1, width)
    act_all, gate_all, up_all = (
        values.reshape(-1, hidden_width) for values in (act_all, gate_all, up_all)
    )
    out_all = bfloat(plain_dot(act_all, down_rows)).reshape(groups, group_rows, width)
    out_sum = cube_scatter([out_all[SLOTS.index(k)] for k in range(groups)])
    out_low = bfloat(out_sum)
    moe_local = ring_scatter([out_low[r * rows : (r + 1) * rows] for r in range(ranks)])
    layer_out = bfloat(residual + moe_local)
    gate_wgrad = first_dot(gate_all, row_all)
    up_wgrad = first_dot(up_all, row_all)
    down_wgrad = first_dot(act_all, cotan_all)

    def expert_part(values):
        return values[:routed_width].reshape(local_experts, expert_width, width)

    shared_wgrad = bfloat(
        jnp.stack(
            [
                values[routed_width : routed_width + shared_width]
                for values in (gate_wgrad, up_wgrad, down_wgrad)
            ]
        )
    )
    shared_back = [
        swap(block, k) if k else block for k, block in enumerate(pick(shared_wgrad, 2))
    ]
    shared_total = place(shared_back, 1).astype(jnp.float32)

    resid_from, mlpgain_part = rms_back(mlp_grad, residual, scale_two, mlp_gain)
    resid_grad = cotangent.astype(jnp.float32) + resid_from
    resid_low = bfloat(resid_grad)
    resid_rows = jnp.concatenate(ring_gather(resid_low), axis=0)
    attended_grad = bfloat(last_dot(resid_rows, output_full)).reshape(
        group_rows, local_heads, VDIM
    )
    output_wgrad = first_dot(attended_low, resid_rows)

    value_g = jnp.einsum(
        "hqk,qhd->khd", bfloat(probability), attended_grad, preferred_element_type=jnp.float32
    )
    prob_grad = jnp.einsum(
        "qhd,hkd->hqk", attended_grad, value_all, preferred_element_type=jnp.float32
    )
    row_dot = jnp.sum(prob_grad * probability, axis=-1, keepdims=True)
    score_grad = bfloat(probability * (prob_grad - row_dot))
    query_g = jnp.einsum("hqk,hkd->qhd", score_grad, k_cat, preferred_element_type=jnp.float32)
    key_g = jnp.einsum("hqk,hqd->khd", score_grad, q_cat, preferred_element_type=jnp.float32)
    query_low, key_low = bfloat(query_g * scaling), bfloat(key_g * scaling)
    value_low = bfloat(value_g)
    expand_rows = jnp.concatenate([key_low[..., :NOPE], value_low], axis=-1).reshape(
        group_rows, local_heads * (NOPE + VDIM)
    )
    latent_partial = last_dot(expand_rows, expand_full)
    keyrot_partial = sum(
        key_low[:, h, NOPE + h % 2 * ROPE : NOPE + (h % 2 + 1) * ROPE].astype(jnp.float32)
        for h in range(local_heads)
    )
    latent_cat = bfloat(jnp.concatenate([latent_partial, keyrot_partial], axis=1))
    latent_back = ring_scatter([latent_cat[r * rows : (r + 1) * rows] for r in range(ranks)])
    cos_own, sin_own = cos_group[:rows, : ROPE // 2], sin_group[:rows, ROPE // 2 : ROPE]
    keyraw_back = rotate(latent_back[:, LATENT:], cos_own, -sin_own)
    latent_in, latgain_part = rms_back(
        latent_back[:, :LATENT], own_latent, scale_latent, latent_gain
    )
    latent_low = bfloat(jnp.concatenate([latent_in, keyraw_back], axis=-1))

    query_rope = jnp.stack(
        [
            query_low[:, h, NOPE + h % 2 * ROPE : NOPE + (h % 2 + 1) * ROPE]
            for h in range(local_heads)
        ],
        axis=1,
    ).astype(jnp.float32)
    query_unrot = rotate(
        query_rope,
        cos_group[:, None, : ROPE // 2],
        -sin_group[:, None, ROPE // 2 : ROPE],
    )
    qraw_grad = jnp.concatenate(
        [
            query_low[..., :NOPE].reshape(group_rows, -1),
            bfloat(query_unrot).reshape(group_rows, -1),
        ],
        axis=1,
    )
    normed_partial = bfloat(last_dot(qraw_grad, query_full))
    normed_back = ring_scatter([normed_partial[r * rows : (r + 1) * rows] for r in range(ranks)])

    normed_total = normed_back + last_dot(latent_low, latent_weight)
    hidden_back, attngain_part = rms_back(normed_total, hidden_f, scale_one, attn_gain)
    hidden_grad = resid_grad + hidden_back

    query_wgrad = bfloat(first_dot(normed_group, qraw_grad))
    expand_wgrad = bfloat(first_dot(latent_group, expand_rows))
    query_total = cube_scatter(pick(query_wgrad, 0))
    expand_total = cube_scatter(pick(expand_wgrad, 0))
    output_total = cube_scatter(pick(bfloat(output_wgrad), 1))

    latent_rows = jnp.concatenate(
        [latent_low] + [shift(latent_low, r) for r in range(1, ranks)], axis=0
    )
    part_width = width // ranks
    normed_part = lax.dynamic_slice_in_dim(normed_group, me_tensor * part_width, part_width, 1)
    latent_wgrad = bfloat(first_dot(latent_rows, normed_part))
    latent_piece = 0.0
    for k, block in enumerate(pick(latent_wgrad, 0)):
        latent_piece = latent_piece + (swap(block, k) if k else block).astype(jnp.float32)
    latent_piece = bfloat(latent_piece)
    order = jnp.stack([latent_piece] + [shift(latent_piece, r) for r in range(1, ranks)])
    parts = jnp.stack(cube_gather(order.reshape(-1, part_width)))
    parts = parts.reshape((groups, ranks) + latent_piece.shape)
    parts = jnp.take(parts, me_dp ^ jnp.arange(groups), axis=0)
    parts = jnp.take(parts, (me_tensor - jnp.arange(ranks)) % ranks, axis=1)
    latent_total = parts.transpose(0, 2, 1, 3).reshape(-1, width).T.astype(jnp.float32)

    small = sum_all(jnp.concatenate([attngain_part, mlpgain_part, latgain_part]))
    return (
        layer_out,
        hidden_grad,
        small[:width],
        join_heads(query_total, local_heads),
        latent_total,
        small[2 * width :],
        expand_total,
        output_total,
        small[width : 2 * width],
        shared_total[0].T,
        shared_total[1].T,
        shared_total[2],
        expert_part(gate_wgrad).transpose(0, 2, 1),
        expert_part(up_wgrad).transpose(0, 2, 1),
        expert_part(down_wgrad),
    )


def solution(mesh):
    in_specs = (
        P((DP, TENSOR), None),
        P((DP, TENSOR), None),
        P(DP, None),
        P(DP, None),
        P(DP, None),
        P(),
        P(DP, TENSOR),
        P(),
        P(),
        P(DP, TENSOR),
        P(TENSOR, DP),
        P(),
        P(DP, TENSOR),
        P(DP, TENSOR),
        P(TENSOR, DP),
        P(DP, None, TENSOR),
        P(DP, None, TENSOR),
        P(DP, TENSOR, None),
    )
    out_specs = (
        P((DP, TENSOR), None),
        P((DP, TENSOR), None),
        P(),
        P(DP, TENSOR),
        P(),
        P(),
        P(DP, TENSOR),
        P(TENSOR, DP),
        P(),
        P(DP, TENSOR),
        P(DP, TENSOR),
        P(TENSOR, DP),
        P(DP, None, TENSOR),
        P(DP, None, TENSOR),
        P(DP, TENSOR, None),
    )
    cube = dict(mesh.shape) == {DP: 8, TENSOR: 4}
    shards = cube_shards if cube else general_shards
    return jax.shard_map(shards, mesh=mesh, in_specs=in_specs, out_specs=out_specs, check_vma=False)
```

```python
import functools
from types import SimpleNamespace

import jax
import jax.numpy as jnp
from jax import lax
from jax.experimental import pallas as pl
from jax.experimental.pallas import tpu as pltpu
from jax.sharding import PartitionSpec as P

DP = "dp"
TENSOR = "tensor"
NOPE = 128
ROPE = 64
VDIM = 128
LATENT = 512
TOPK = 6


epsilon = 1e-06
rope_base = 10000.0


def bfloat(values):
    return values.astype(jnp.bfloat16)


def plain_dot(left_op, right_op):
    return jnp.dot(left_op, right_op, preferred_element_type=jnp.float32)


def first_dot(left_op, right_op):
    return lax.dot_general(
        left_op, right_op, (((0,), (0,)), ((), ())), preferred_element_type=jnp.float32
    )


def last_dot(left_op, right_op):
    return lax.dot_general(
        left_op, right_op, (((1,), (1,)), ((), ())), preferred_element_type=jnp.float32
    )


def rms_scale(values):
    return lax.rsqrt(jnp.mean(values * values, axis=-1, keepdims=True) + epsilon)


def rms_back(grad_out, values, scaling, gain_vec):
    scaled_grad = grad_out * gain_vec
    inner_sum = jnp.mean(scaled_grad * values, axis=-1, keepdims=True)
    grad_in = scaling * scaled_grad - values * (scaling * scaling * scaling) * inner_sum
    return (grad_in, jnp.sum(grad_out * values * scaling, axis=0))


def silu_parts(values):
    sigmoid = jax.nn.sigmoid(values)
    return (values * sigmoid, sigmoid * (1.0 + values * (1.0 - sigmoid)))


def rope_tables(positions, rot_width):
    middle = rot_width // 2
    frequency = rope_base ** (-jnp.arange(middle, dtype=jnp.float32) * 2.0 / rot_width)
    angles = positions.astype(jnp.float32)[:, None] * frequency[None, :]
    return (jnp.cos(angles), jnp.sin(angles))


def rotate(values, cos_table, sin_table):
    middle = values.shape[-1] // 2
    first_half = values[..., :middle]
    second_half = values[..., middle:]
    return jnp.concatenate(
        [
            first_half * cos_table - second_half * sin_table,
            second_half * cos_table + first_half * sin_table,
        ],
        axis=-1,
    )


def doc_layout(lengths, row_count):
    doc_ends = jnp.cumsum(lengths)
    tok_index = jnp.arange(row_count, dtype=jnp.int32)
    before = (doc_ends[None, :] <= tok_index[:, None]).astype(jnp.int32)
    doc_ids = jnp.sum(before, axis=1)
    starts = jnp.sum(before * lengths[None, :], axis=1)
    return (doc_ids, tok_index - starts)


def slot_tables(routes, experts, capacity):
    row_count = routes.shape[0] * routes.shape[1]
    flat_routes = routes.reshape(row_count)
    onehot = (flat_routes[:, None] == jnp.arange(experts, dtype=jnp.int32)[None, :]).astype(
        jnp.int32
    )
    earlier = jnp.cumsum(onehot, axis=0) - onehot
    position = jnp.sum(earlier * onehot, axis=1)
    slot_ids = flat_routes * capacity + position
    tok_rows = jnp.arange(row_count, dtype=jnp.int32) // routes.shape[1]
    owner_tok = jnp.zeros((experts * capacity,), jnp.int32).at[slot_ids].set(tok_rows)
    return (slot_ids.reshape(routes.shape), owner_tok)


def slot_share(capacity):
    return (0, capacity)


def route_rows(outgoing, apply_fn):
    arrived = lax.all_to_all(outgoing, DP, split_axis=1, concat_axis=1, tiled=True)
    result, extra = apply_fn(arrived)
    back = lax.all_to_all(
        result.astype(jnp.bfloat16), DP, split_axis=1, concat_axis=1, tiled=True
    ).astype(result.dtype)
    return (back, extra)


def block_mask(doc_ids, row_start, block_rows):
    group_rows = doc_ids.shape[0]
    key_index = jnp.arange(group_rows, dtype=jnp.int32)
    query_index = row_start + jnp.arange(block_rows, dtype=jnp.int32)
    return (key_index[None, :] <= query_index[:, None]) & (doc_ids[None, :] == doc_ids[:, None])


def attend(query_all, key_all, value_all, doc_ids, scaling):
    group_rows = query_all.shape[0]
    block_rows = min(512, group_rows)
    block_count = group_rows // block_rows

    def one_block(block_id):
        row_start = block_id * block_rows
        allowed = block_mask(doc_ids, row_start, block_rows)
        scores = (
            jnp.einsum("qhd,khd->hqk", query_all, key_all, preferred_element_type=jnp.float32)
            * scaling
        )
        scores = jnp.where(allowed[None], scores, -jnp.inf)
        row_max = jnp.max(scores, axis=-1, keepdims=True)
        exp_scores = jnp.exp(scores - row_max)
        row_total = jnp.sum(exp_scores, axis=-1, keepdims=True)
        probability = bfloat(exp_scores / row_total)
        output = jnp.einsum(
            "hqk,khd->qhd", probability, value_all, preferred_element_type=jnp.float32
        )
        return (output, (row_max + jnp.log(row_total))[..., 0])

    outputs, log_total = lax.map(one_block, jnp.arange(block_count, dtype=jnp.int32))
    return (outputs.reshape(group_rows, outputs.shape[2], outputs.shape[3]), log_total)


def attend_back(query_all, key_all, value_all, doc_ids, scaling, log_total, grad_out):
    group_rows = query_all.shape[0]
    block_rows = min(512, group_rows)
    block_count = group_rows // block_rows

    def one_block(carried, inputs):
        key_grad, value_grad = carried
        block_id, block_lse = inputs
        row_start = block_id * block_rows
        allowed = block_mask(doc_ids, row_start, block_rows)
        scores = (
            jnp.einsum("qhd,khd->hqk", query_all, key_all, preferred_element_type=jnp.float32)
            * scaling
        )
        scores = jnp.where(allowed[None], scores, -jnp.inf)
        probability = jnp.exp(scores - block_lse[..., None])
        value_grad = value_grad + jnp.einsum(
            "hqk,qhd->khd", bfloat(probability), grad_out, preferred_element_type=jnp.float32
        )
        prob_grad = jnp.einsum(
            "qhd,khd->hqk", grad_out, value_all, preferred_element_type=jnp.float32
        )
        row_dot = jnp.sum(prob_grad * probability, axis=-1, keepdims=True)
        score_grad = bfloat(probability * (prob_grad - row_dot))
        query_grad = (
            jnp.einsum("hqk,khd->qhd", score_grad, key_all, preferred_element_type=jnp.float32)
            * scaling
        )
        key_grad = (
            key_grad
            + jnp.einsum("hqk,qhd->khd", score_grad, query_all, preferred_element_type=jnp.float32)
            * scaling
        )
        return ((key_grad, value_grad), query_grad)

    start_state = (jnp.zeros(key_all.shape, jnp.float32), jnp.zeros(value_all.shape, jnp.float32))
    (key_grad, value_grad), query_blocks = lax.scan(
        one_block, start_state, (jnp.arange(block_count, dtype=jnp.int32), log_total)
    )
    query_grad = query_blocks.reshape(group_rows, query_blocks.shape[2], query_blocks.shape[3])
    return (query_grad, key_grad, value_grad)


def forward_pass(
    hidden,
    cotangent,
    routes,
    route_gates,
    doc_lengths,
    attn_gain,
    query_weight,
    latent_weight,
    latent_gain,
    expand_weight,
    output_weight,
    mlp_gain,
    shared_gate,
    shared_up,
    shared_down,
    expert_gate,
    expert_up,
    expert_down,
):
    tensor_count = lax.axis_size(TENSOR)
    dp_count = lax.axis_size(DP)
    local_rows = hidden.shape[0]
    group_rows = local_rows * tensor_count
    query_full, expand_full, output_full, sgate_full, sup_full, sdown_full = (
        lax.all_gather(query_weight, DP, axis=0, tiled=True),
        lax.all_gather(expand_weight, DP, axis=0, tiled=True),
        lax.all_gather(output_weight, DP, axis=1, tiled=True),
        lax.all_gather(shared_gate, DP, axis=0, tiled=True),
        lax.all_gather(shared_up, DP, axis=0, tiled=True),
        lax.all_gather(shared_down, DP, axis=1, tiled=True),
    )
    hidden_f = hidden.astype(jnp.float32)
    scale_one = rms_scale(hidden_f)
    normed_one = bfloat(hidden_f * scale_one * attn_gain)
    latent_full = plain_dot(normed_one, latent_weight)
    latent_part = latent_full[:, :LATENT]
    scale_latent = rms_scale(latent_part)
    latent_norm = bfloat(latent_part * scale_latent * latent_gain)
    doc_ids, positions = doc_layout(doc_lengths[0], group_rows)
    cos_group, sin_group = rope_tables(positions, ROPE)
    local_start = lax.axis_index(TENSOR) * local_rows
    cos_local = lax.dynamic_slice_in_dim(cos_group, local_start, local_rows, 0)
    sin_local = lax.dynamic_slice_in_dim(sin_group, local_start, local_rows, 0)
    key_rot = bfloat(rotate(latent_full[:, LATENT:], cos_local, sin_local))
    normed_group, latent_group, keyrot_group = (
        lax.all_gather(normed_one, TENSOR, axis=0, tiled=True),
        lax.all_gather(latent_norm, TENSOR, axis=0, tiled=True),
        lax.all_gather(key_rot, TENSOR, axis=0, tiled=True),
    )
    local_heads = query_full.shape[1] // (NOPE + ROPE)
    query_raw = plain_dot(normed_group, query_full).reshape(group_rows, local_heads, NOPE + ROPE)
    query_rot = rotate(query_raw[..., NOPE:], cos_group[:, None, :], sin_group[:, None, :])
    query_all = bfloat(jnp.concatenate([query_raw[..., :NOPE], query_rot], axis=-1))
    expanded = plain_dot(latent_group, expand_full).reshape(group_rows, local_heads, NOPE + VDIM)
    key_shared = jnp.broadcast_to(keyrot_group[:, None, :], (group_rows, local_heads, ROPE))
    key_all = jnp.concatenate([bfloat(expanded[..., :NOPE]), key_shared], axis=-1)
    value_all = bfloat(expanded[..., NOPE:])
    scaling = (NOPE + ROPE) ** (-0.5)
    attended, log_total = attend(query_all, key_all, value_all, doc_ids, scaling)
    attended_low = bfloat(attended).reshape(group_rows, local_heads * VDIM)
    attn_local = lax.psum_scatter(
        plain_dot(attended_low, output_full), TENSOR, scatter_dimension=0, tiled=True
    )
    residual = hidden_f + attn_local
    scale_two = rms_scale(residual)
    normed_two = bfloat(residual * scale_two * mlp_gain)
    mlp_rows, cotan_rows = (
        lax.all_gather(normed_two, TENSOR, axis=0, tiled=True),
        lax.all_gather(cotangent, TENSOR, axis=0, tiled=True),
    )
    shared_gpre = plain_dot(mlp_rows, sgate_full)
    shared_upre = plain_dot(mlp_rows, sup_full)
    shared_silu, shared_dsilu = silu_parts(shared_gpre)
    shared_hidden = bfloat(shared_silu * shared_upre)
    shared_out = plain_dot(shared_hidden, sdown_full)
    local_experts = expert_gate.shape[0]
    experts = local_experts * dp_count
    capacity = group_rows * TOPK * 4 // (3 * experts)
    slot_ids, owner_tok = slot_tables(routes, experts, capacity)
    slot_start, slot_count = slot_share(capacity)
    all_tok = owner_tok.reshape(dp_count, local_experts, capacity).transpose(1, 0, 2)
    send_rows = mlp_rows[all_tok]

    def expert_apply(received):
        gate_pre = jnp.einsum(
            "jscd,jdf->jscf", received, expert_gate, preferred_element_type=jnp.float32
        )
        up_pre = jnp.einsum(
            "jscd,jdf->jscf", received, expert_up, preferred_element_type=jnp.float32
        )
        gate_silu, gate_dsilu = silu_parts(gate_pre)
        activated = bfloat(gate_silu * up_pre)
        result = jnp.einsum(
            "jscf,jfd->jscd", activated, expert_down, preferred_element_type=jnp.float32
        )
        return (result, (received, up_pre, gate_silu, gate_dsilu, activated))

    returned, expert_state = route_rows(send_rows, expert_apply)
    received, up_pre, gate_silu, gate_dsilu, activated = expert_state
    position = slot_ids % capacity - slot_start
    slot_mask = ((position >= 0) & (position < slot_count)).astype(jnp.float32)
    flat_index = (
        routes % local_experts * dp_count + routes // local_experts
    ) * slot_count + jnp.clip(position, 0, slot_count - 1)
    returned_flat = returned.reshape(local_experts * dp_count * slot_count, returned.shape[-1])
    routed = jnp.sum((route_gates * slot_mask)[:, :, None] * returned_flat[flat_index], axis=1)
    moe_local = lax.psum_scatter(
        (shared_out + routed).astype(jnp.bfloat16), TENSOR, scatter_dimension=0, tiled=True
    ).astype(jnp.float32)
    layer_out = bfloat(residual + moe_local)
    return SimpleNamespace(
        layer_out=layer_out,
        hidden_f=hidden_f,
        scale_one=scale_one,
        normed_one=normed_one,
        latent_part=latent_part,
        scale_latent=scale_latent,
        cos_local=cos_local,
        sin_local=sin_local,
        cos_group=cos_group,
        sin_group=sin_group,
        doc_ids=doc_ids,
        normed_group=normed_group,
        latent_group=latent_group,
        query_all=query_all,
        key_all=key_all,
        value_all=value_all,
        log_total=log_total,
        attended_low=attended_low,
        residual=residual,
        scale_two=scale_two,
        mlp_rows=mlp_rows,
        cotan_rows=cotan_rows,
        shared_upre=shared_upre,
        shared_silu=shared_silu,
        shared_dsilu=shared_dsilu,
        shared_hidden=shared_hidden,
        slot_ids=slot_ids,
        send_tok=all_tok,
        flat_index=flat_index,
        slot_mask=slot_mask,
        received=received,
        up_pre=up_pre,
        gate_silu=gate_silu,
        gate_dsilu=gate_dsilu,
        activated=activated,
        query_full=query_full,
        expand_full=expand_full,
        output_full=output_full,
        sgate_full=sgate_full,
        sup_full=sup_full,
        sdown_full=sdown_full,
    )


def general_shards(
    hidden,
    cotangent,
    routes,
    route_gates,
    doc_lengths,
    attn_gain,
    query_weight,
    latent_weight,
    latent_gain,
    expand_weight,
    output_weight,
    mlp_gain,
    shared_gate,
    shared_up,
    shared_down,
    expert_gate,
    expert_up,
    expert_down,
):
    kept_state = forward_pass(
        hidden,
        cotangent,
        routes,
        route_gates,
        doc_lengths,
        attn_gain,
        query_weight,
        latent_weight,
        latent_gain,
        expand_weight,
        output_weight,
        mlp_gain,
        shared_gate,
        shared_up,
        shared_down,
        expert_gate,
        expert_up,
        expert_down,
    )
    dp_count = lax.axis_size(DP)
    local_experts = expert_gate.shape[0]
    experts = local_experts * dp_count
    group_rows = kept_state.mlp_rows.shape[0]
    capacity = group_rows * TOPK * 4 // (3 * experts)
    cotan_rows = kept_state.cotan_rows
    mlp_rows = kept_state.mlp_rows
    sdown_wgrad = first_dot(kept_state.shared_hidden, cotan_rows)
    shared_hgrad = last_dot(cotan_rows, kept_state.sdown_full)
    sgate_pgrad = bfloat(shared_hgrad * kept_state.shared_upre * kept_state.shared_dsilu)
    sup_pgrad = bfloat(shared_hgrad * kept_state.shared_silu)
    sgate_wgrad = first_dot(mlp_rows, sgate_pgrad)
    sup_wgrad = first_dot(mlp_rows, sup_pgrad)
    mlp_partial = last_dot(sgate_pgrad, kept_state.sgate_full) + last_dot(
        sup_pgrad, kept_state.sup_full
    )
    slot_start, slot_count = slot_share(capacity)
    slot_gate = (
        jnp.zeros((experts * capacity,), jnp.float32)
        .at[kept_state.slot_ids.reshape(-1)]
        .set(route_gates.reshape(-1))
    )
    all_gate = slot_gate.reshape(dp_count, local_experts, capacity).transpose(1, 0, 2)
    grad_send = bfloat(all_gate[..., None] * cotan_rows[kept_state.send_tok].astype(jnp.float32))
    received = kept_state.received

    def expert_back(grad_recv):
        expert_down_partial = jnp.einsum(
            "jscf,jscd->jfd", kept_state.activated, grad_recv, preferred_element_type=jnp.float32
        )
        act_grad = jnp.einsum(
            "jscd,jfd->jscf", grad_recv, expert_down, preferred_element_type=jnp.float32
        )
        gate_pgrad = bfloat(act_grad * kept_state.up_pre * kept_state.gate_dsilu)
        up_pgrad = bfloat(act_grad * kept_state.gate_silu)
        row_gradient = jnp.einsum(
            "jscf,jdf->jscd", gate_pgrad, expert_gate, preferred_element_type=jnp.float32
        )
        row_gradient = row_gradient + jnp.einsum(
            "jscf,jdf->jscd", up_pgrad, expert_up, preferred_element_type=jnp.float32
        )
        expert_gate_partial = jnp.einsum(
            "jscd,jscf->jdf", received, gate_pgrad, preferred_element_type=jnp.float32
        )
        expert_up_partial = jnp.einsum(
            "jscd,jscf->jdf", received, up_pgrad, preferred_element_type=jnp.float32
        )
        return (row_gradient, (expert_gate_partial, expert_up_partial, expert_down_partial))

    rows_back, expert_weight_gradients = route_rows(grad_send, expert_back)
    expert_gate_weight_gradient, expert_up_weight_gradient, expert_down_weight_gradient = (
        expert_weight_gradients
    )
    back_flat = rows_back.reshape(local_experts * dp_count * slot_count, rows_back.shape[-1])
    mlp_partial = mlp_partial + jnp.sum(
        kept_state.slot_mask[:, :, None] * back_flat[kept_state.flat_index], axis=1
    )
    mlp_grad = lax.psum_scatter(mlp_partial, TENSOR, scatter_dimension=0, tiled=True)
    resid_from, mlpgain_part = rms_back(
        mlp_grad, kept_state.residual, kept_state.scale_two, mlp_gain
    )
    resid_grad = cotangent.astype(jnp.float32) + resid_from
    attn_rows = lax.all_gather(bfloat(resid_grad), TENSOR, axis=0, tiled=True)
    output_wgrad = first_dot(kept_state.attended_low, attn_rows)
    local_heads = kept_state.query_all.shape[1]
    attended_grad = bfloat(last_dot(attn_rows, kept_state.output_full)).reshape(
        group_rows, local_heads, VDIM
    )
    query_g, key_g, value_g = attend_back(
        kept_state.query_all,
        kept_state.key_all,
        kept_state.value_all,
        kept_state.doc_ids,
        (NOPE + ROPE) ** (-0.5),
        kept_state.log_total,
        attended_grad,
    )
    query_low = bfloat(query_g)
    key_low = bfloat(key_g)
    value_low = bfloat(value_g)
    query_unrot = rotate(
        query_low[..., NOPE:].astype(jnp.float32),
        kept_state.cos_group[:, None, :],
        -kept_state.sin_group[:, None, :],
    )
    qraw_grad = bfloat(
        jnp.concatenate([query_low[..., :NOPE].astype(jnp.float32), query_unrot], axis=-1)
    )
    qraw_grad = qraw_grad.reshape(group_rows, local_heads * (NOPE + ROPE))
    query_wgrad = first_dot(kept_state.normed_group, qraw_grad)
    normed_partial = last_dot(qraw_grad, kept_state.query_full)
    expand_rows = jnp.concatenate([key_low[..., :NOPE], value_low], axis=-1).reshape(
        group_rows, local_heads * (NOPE + VDIM)
    )
    expand_wgrad = first_dot(kept_state.latent_group, expand_rows)
    latent_partial = last_dot(expand_rows, kept_state.expand_full)
    keyrot_partial = jnp.sum(key_low[..., NOPE:].astype(jnp.float32), axis=1)
    normed_back, latent_back, keyrot_back = (
        lax.psum_scatter(
            normed_partial.astype(jnp.bfloat16), TENSOR, scatter_dimension=0, tiled=True
        ).astype(jnp.float32),
        lax.psum_scatter(
            latent_partial.astype(jnp.bfloat16), TENSOR, scatter_dimension=0, tiled=True
        ).astype(jnp.float32),
        lax.psum_scatter(
            keyrot_partial.astype(jnp.bfloat16), TENSOR, scatter_dimension=0, tiled=True
        ).astype(jnp.float32),
    )
    keyraw_back = rotate(keyrot_back, kept_state.cos_local, -kept_state.sin_local)
    latent_in, latgain_part = rms_back(
        latent_back, kept_state.latent_part, kept_state.scale_latent, latent_gain
    )
    latent_low = bfloat(jnp.concatenate([latent_in, keyraw_back], axis=-1))
    latent_wgrad = first_dot(kept_state.normed_one, latent_low)
    normed_total = normed_back + last_dot(latent_low, latent_weight)
    hidden_back, attngain_part = rms_back(
        normed_total, kept_state.hidden_f, kept_state.scale_one, attn_gain
    )
    hidden_grad = resid_grad + hidden_back
    fsdp_sums = (
        lax.psum_scatter(
            query_wgrad.astype(jnp.bfloat16), DP, scatter_dimension=0, tiled=True
        ).astype(jnp.float32),
        lax.psum_scatter(
            expand_wgrad.astype(jnp.bfloat16), DP, scatter_dimension=0, tiled=True
        ).astype(jnp.float32),
        lax.psum_scatter(
            output_wgrad.astype(jnp.bfloat16), DP, scatter_dimension=1, tiled=True
        ).astype(jnp.float32),
        lax.psum_scatter(
            sgate_wgrad.astype(jnp.bfloat16), DP, scatter_dimension=0, tiled=True
        ).astype(jnp.float32),
        lax.psum_scatter(
            sup_wgrad.astype(jnp.bfloat16), DP, scatter_dimension=0, tiled=True
        ).astype(jnp.float32),
        lax.psum_scatter(
            sdown_wgrad.astype(jnp.bfloat16), DP, scatter_dimension=1, tiled=True
        ).astype(jnp.float32),
    )
    small_sums = lax.psum(
        (latent_wgrad, attngain_part, mlpgain_part, latgain_part), (DP, TENSOR)
    )
    return (
        kept_state.layer_out,
        hidden_grad,
        small_sums[1],
        fsdp_sums[0],
        small_sums[0],
        small_sums[3],
        fsdp_sums[1],
        fsdp_sums[2],
        small_sums[2],
        fsdp_sums[3],
        fsdp_sums[4],
        fsdp_sums[5],
        expert_gate_weight_gradient,
        expert_up_weight_gradient,
        expert_down_weight_gradient,
    )


MESH = pl.DeviceIdType.MESH


def flip(index, bit):
    return index + bit - 2 * bit * ((index // bit) % 2)


def remote(src, dst, send_sem, recv_sem, peer):
    return pltpu.make_async_remote_copy(
        src_ref=src,
        dst_ref=dst,
        send_sem=send_sem,
        recv_sem=recv_sem,
        device_id=peer,
        device_id_type=MESH,
    )


def greet(peers):
    barrier = pltpu.get_barrier_semaphore()
    for peer in peers:
        pl.semaphore_signal(barrier, inc=1, device_id=peer, device_id_type=MESH)
    pl.semaphore_wait(barrier, len(peers))


(
    K_RING,
    K_X,
    K_Y,
    K_CORE,
    K_FAR_Y,
    K_FAR_X,
    K_CORE_X,
    K_CORE_Y,
    K_CORE_FAR,
    K_CORE_OWN,
    K_X_FIRST,
    K_X_LAST,
    K_Y_FIRST,
    K_Y_LAST,
) = range(14)

SLOTS = (0, 1, 2, 4, 3, 5, 6, 7)


def moe_kernel(
    rows,
    back,
    gates,
    expert_gate,
    expert_up,
    shared_all,
    rows_all,
    act_all,
    gpre_all,
    upre_all,
    grad_out,
    gate_rows,
    up_rows,
    row_buf,
    back_buf,
    out_buf,
    blocks,
    core_buf,
    far_buf,
    x_buf,
    y_buf,
    ring_buf,
    ring_out,
    weight_sem,
    load_sem,
    back_sem,
    store_sem,
    ag_send,
    ag_recv,
    rs_send,
    rs_recv,
    ring_send,
    ring_recv,
    *,
    expert_width,
    routed_width,
):
    me, rank = lax.axis_index(DP), lax.axis_index(TENSOR)
    ranks = lax.axis_size(TENSOR)
    right = (me, lax.rem(rank + 1, ranks))
    left = (me, lax.rem(rank + ranks - 1, ranks))
    by_core, by_x, by_y = [(flip(me, bit), rank) for bit in (1, 2, 4)]
    count = rows.shape[0]
    half = count // 2
    first, last = pl.ds(0, half), pl.ds(half, half)
    hidden_width = gate_rows.shape[0]
    shared_pad = shared_all.shape[1]
    greet([by_core, by_x, by_y, right, left])

    def ag(kind, j, src, dst, peer):
        return remote(src, dst, ag_send.at[kind, j], ag_recv.at[kind, j], peer)

    def rs(kind, j, src, dst, peer):
        return remote(src, dst, rs_send.at[kind, j], rs_recv.at[kind, j], peer)

    def row_copy(kind, j):
        at = rows_all.at
        return {
            K_RING: lambda: ag(0, j, at[0, j - 1], at[0, j], right),
            K_X: lambda: ag(1, j, at[0, j], at[2, j], by_x),
            K_Y: lambda: ag(2, j, at[0, j], at[3, j], by_y),
            K_CORE: lambda: ag(3, j, at[0, j], at[1, j], by_core),
            K_FAR_Y: lambda: ag(4, j, at[2, j, last], at[6, j, last], by_y),
            K_FAR_X: lambda: ag(5, j, at[3, j, first], at[6, j, first], by_x),
            K_CORE_X: lambda: ag(6, j, at[2, j], at[4, j], by_core),
            K_CORE_Y: lambda: ag(7, j, at[3, j], at[5, j], by_core),
            K_CORE_FAR: lambda: ag(8, j, at[6, j], at[7, j], by_core),
        }[kind]()

    def sum_copy(kind, j):
        at = blocks.at[lax.rem(j, 2)].at
        return {
            K_CORE_OWN: lambda: rs(0, j, at[1], core_buf.at[j, 0], by_core),
            K_CORE_X: lambda: rs(1, j, at[4], core_buf.at[j, 1], by_core),
            K_CORE_Y: lambda: rs(2, j, at[5], core_buf.at[j, 2], by_core),
            K_CORE_FAR: lambda: rs(3, j, at[7], core_buf.at[j, 3], by_core),
            K_FAR_X: lambda: rs(4, j, at[6, first], far_buf.at[j, 0], by_x),
            K_FAR_Y: lambda: rs(5, j, at[6, last], far_buf.at[j, 1], by_y),
            K_X_FIRST: lambda: rs(6, j, at[2, first], x_buf.at[j, 0], by_x),
            K_X_LAST: lambda: rs(7, j, at[2, last], x_buf.at[j, 1], by_x),
            K_Y_FIRST: lambda: rs(8, j, at[3, first], y_buf.at[j, 0], by_y),
            K_Y_LAST: lambda: rs(9, j, at[3, last], y_buf.at[j, 1], by_y),
        }[kind]()

    def ring_copy(step):
        return remote(
            ring_out.at[step], ring_buf.at[step], ring_send.at[step], ring_recv.at[step], right
        )

    def add_rows(target, size, *terms, store=None):
        step = 16

        def one(i, carry):
            at = pl.ds(pl.multiple_of(i * step, step), step)
            total = target[at, :].astype(jnp.float32)
            for term in terms:
                total = total + term[at, :].astype(jnp.float32)
            to = target if store is None else store
            to[at, :] = total.astype(to.dtype)
            return carry

        lax.fori_loop(0, size // step, one, 0)

    def loads(j, p, parity):
        return (
            pltpu.make_async_copy(
                back.at[pl.ds(2 * p, 2), j], back_buf.at[parity], back_sem.at[parity]
            ),
        )

    def stores(j, p, parity):
        return [
            pltpu.make_async_copy(
                out_buf.at[parity, n], to.at[pl.ds(2 * p, 2), j], store_sem.at[parity, n]
            )
            for n, to in enumerate((act_all, gpre_all, upre_all))
        ]

    def compute(j, p):
        parity = p % 2
        load = pltpu.make_async_copy(rows_all.at[pl.ds(2 * p, 2), j], row_buf, load_sem)
        load.start()
        if p < 3:
            for copy in loads(j, p + 1, 1 - parity):
                copy.start()
        else:

            @pl.when(j < ranks - 1)
            def _():
                for copy in loads(j + 1, 0, 0):
                    copy.start()

        for copy in loads(j, p, parity):
            copy.wait()
        if p >= 2:
            for copy in stores(j, p - 2, parity):
                copy.wait()
        else:

            @pl.when(j > 0)
            def _():
                for copy in stores(j - 1, p + 2, parity):
                    copy.wait()

        load.wait()
        wide = row_buf[...].reshape(2 * count, row_buf.shape[2])
        gate_pre = last_dot(wide, gate_rows[...])
        up_pre = last_dot(wide, up_rows[...])
        column = lax.broadcasted_iota(jnp.int32, (1, hidden_width), 1)
        lanes = pl.ds(pl.multiple_of(j * count, count), count)
        gate = jnp.concatenate([gates[2 * p + i, :, lanes].T for i in range(2)], axis=0)
        scaled = jnp.where(
            column < expert_width,
            gate[:, 0:1],
            jnp.where(column < routed_width, gate[:, 1:2], 1.0),
        )
        sigmoid = 1.0 / (1.0 + jnp.exp(-gate_pre))
        silu = gate_pre * sigmoid
        dsilu = sigmoid * (1.0 + gate_pre * (1.0 - sigmoid))
        back_pre = back_buf[parity].reshape(2 * count, hidden_width).astype(jnp.float32) * scaled
        act = bfloat(silu * up_pre * scaled)
        gate_grad = bfloat(back_pre * up_pre * dsilu)
        up_grad = bfloat(back_pre * silu)
        out_buf[parity, 0] = act.reshape(2, count, hidden_width)
        out_buf[parity, 1] = gate_grad.reshape(2, count, hidden_width)
        out_buf[parity, 2] = up_grad.reshape(2, count, hidden_width)
        for copy in stores(j, p, parity):
            copy.start()
        grad = plain_dot(gate_grad, gate_rows[...]) + plain_dot(up_grad, up_rows[...])
        blocks[lax.rem(j, 2), pl.ds(2 * p, 2)] = bfloat(grad).reshape(2, count, grad.shape[1])

    own = pltpu.make_async_copy(rows, rows_all.at[0, 0], load_sem)
    own.start()
    assembled = []
    for n, (routed, target) in enumerate(((expert_gate, gate_rows), (expert_up, up_rows))):
        for i, (src, at) in enumerate(
            ((routed, pl.ds(0, routed_width)), (shared_all.at[n], pl.ds(routed_width, shared_pad)))
        ):
            copy = pltpu.make_async_copy(src, target.at[at], weight_sem.at[n, i])
            copy.start()
            assembled.append(copy)
        target[routed_width + shared_pad :] = jnp.zeros(
            (hidden_width - routed_width - shared_pad, target.shape[1]), jnp.bfloat16
        )
    for copy in loads(0, 0, 0):
        copy.start()
    own.wait()
    ring0 = row_copy(K_RING, 1)
    ring0.start()
    for kind in (K_X, K_Y, K_CORE):
        row_copy(kind, 0).start()
    for copy in assembled:
        copy.wait()

    def body(j, carry):
        before = j - 1

        @pl.when(j < ranks)
        def _():
            row_copy(K_CORE, j).wait_recv()
            compute(j, 0)
            sum_copy(K_CORE_OWN, j).start()

        @pl.when(j > 0)
        def _():
            par = lax.rem(before, 2)
            sum_copy(K_CORE_FAR, before).wait_recv()
            add_rows(blocks.at[par, 6], count, core_buf.at[before, 3])
            sum_copy(K_FAR_X, before).start()
            sum_copy(K_FAR_Y, before).start()

        @pl.when(j < ranks)
        def _():
            row_copy(K_X, j).wait_recv()
            row_copy(K_FAR_Y, j).start()
            row_copy(K_CORE_X, j).start()
            row_copy(K_Y, j).wait_recv()
            row_copy(K_FAR_X, j).start()
            row_copy(K_CORE_Y, j).start()

            @pl.when(j < ranks - 1)
            def _():
                row_copy(K_RING, j + 1).wait_recv()

                @pl.when(j < ranks - 2)
                def _():
                    row_copy(K_RING, j + 2).start()

                for kind in (K_X, K_Y, K_CORE):
                    row_copy(kind, j + 1).start()

            compute(j, 1)

        @pl.when(j > 0)
        def _():
            par = lax.rem(before, 2)
            sum_copy(K_FAR_X, before).wait_recv()
            add_rows(
                blocks.at[par, 3, first],
                half,
                core_buf.at[before, 2, first],
                far_buf.at[before, 0],
            )
            sum_copy(K_Y_FIRST, before).start()
            sum_copy(K_FAR_Y, before).wait_recv()
            add_rows(
                blocks.at[par, 2, last],
                half,
                core_buf.at[before, 1, last],
                far_buf.at[before, 1],
            )
            sum_copy(K_X_LAST, before).start()

        @pl.when(j < ranks)
        def _():
            row_copy(K_FAR_X, j).wait_recv()
            row_copy(K_FAR_Y, j).wait_recv()
            row_copy(K_CORE_FAR, j).start()
            row_copy(K_CORE_X, j).wait_recv()
            row_copy(K_CORE_Y, j).wait_recv()
            compute(j, 2)
            sum_copy(K_CORE_X, j).start()
            sum_copy(K_CORE_Y, j).start()
            row_copy(K_CORE_FAR, j).wait_recv()
            compute(j, 3)
            sum_copy(K_CORE_FAR, j).start()
            par = lax.rem(j, 2)
            sum_copy(K_CORE_X, j).wait_recv()
            add_rows(blocks.at[par, 2, first], half, core_buf.at[j, 1, first])
            sum_copy(K_X_FIRST, j).start()
            sum_copy(K_CORE_Y, j).wait_recv()
            add_rows(blocks.at[par, 3, last], half, core_buf.at[j, 2, last])
            sum_copy(K_Y_LAST, j).start()

        @pl.when(j > 0)
        def _():
            par = lax.rem(before, 2)
            for kind in (K_CORE_OWN, K_X_FIRST, K_X_LAST, K_Y_FIRST, K_Y_LAST):
                sum_copy(kind, before).wait_recv()
            terms = [
                (core_buf.at[before, 0, part], x_buf.at[before, n], y_buf.at[before, n])
                for n, part in enumerate((first, last))
            ]

            @pl.when(before == 0)
            def _():
                for part, more in zip((first, last), terms):
                    add_rows(blocks.at[par, 0, part], half, *more, store=grad_out.at[part])

            @pl.when(before == 1)
            def _():
                for part, more in zip((first, last), terms):
                    add_rows(blocks.at[par, 0, part], half, *more, store=ring_out.at[0, part])
                ring_copy(0).start()

            @pl.when(before > 1)
            def _():
                ring_copy(before - 2).wait_recv()
                for part, more in zip((first, last), terms):
                    add_rows(
                        blocks.at[par, 0, part],
                        half,
                        *more,
                        ring_buf.at[before - 2, part],
                        store=ring_out.at[before - 1, part],
                    )
                ring_copy(before - 1).start()

            for kind in (
                K_CORE_OWN,
                K_CORE_X,
                K_CORE_Y,
                K_CORE_FAR,
                K_FAR_X,
                K_FAR_Y,
                K_X_FIRST,
                K_X_LAST,
                K_Y_FIRST,
                K_Y_LAST,
            ):
                sum_copy(kind, before).wait_send()

        return carry

    lax.fori_loop(0, ranks + 1, body, 0)
    ring_copy(ranks - 2).wait_recv()
    add_rows(grad_out, count, ring_buf.at[ranks - 2])
    for step in range(ranks - 1):
        ring_copy(step).wait_send()
        row_copy(K_RING, step + 1).wait_send()
    for p in (2, 3):
        for copy in stores(ranks - 1, p, p % 2):
            copy.wait()

    def drain(j, carry):
        for kind in (K_X, K_Y, K_CORE, K_FAR_Y, K_FAR_X, K_CORE_X, K_CORE_Y, K_CORE_FAR):
            row_copy(kind, j).wait_send()
        return carry

    lax.fori_loop(0, ranks, drain, 0)


def moe_pass(rows, back, gates, expert_gate, expert_up, shared_all, expert_width):
    ranks = lax.axis_size(TENSOR)
    groups = lax.axis_size(DP)
    count, width = rows.shape
    hidden_width = back.shape[-1]
    anywhere = pl.BlockSpec(memory_space=pl.ANY)
    in_vmem = pl.BlockSpec(memory_space=pltpu.VMEM)
    low = jnp.bfloat16
    hidden_shape = jax.ShapeDtypeStruct((groups, ranks, count, hidden_width), low)
    dma = pltpu.SemaphoreType.DMA
    return pl.pallas_call(
        functools.partial(
            moe_kernel, expert_width=expert_width, routed_width=expert_gate.shape[0]
        ),
        out_shape=(
            jax.ShapeDtypeStruct((groups, ranks, count, width), low),
            hidden_shape,
            hidden_shape,
            hidden_shape,
            jax.ShapeDtypeStruct((count, width), jnp.float32),
        ),
        in_specs=[anywhere, anywhere, in_vmem, anywhere, anywhere, anywhere],
        out_specs=(anywhere, anywhere, anywhere, anywhere, in_vmem),
        scratch_shapes=[
            pltpu.VMEM((hidden_width, width), low),
            pltpu.VMEM((hidden_width, width), low),
            pltpu.VMEM((2, count, width), low),
            pltpu.VMEM((2, 2, count, hidden_width), low),
            pltpu.VMEM((2, 3, 2, count, hidden_width), low),
            pltpu.VMEM((2, groups, count, width), low),
            pltpu.VMEM((ranks, 4, count, width), low),
            pltpu.VMEM((ranks, 2, count // 2, width), low),
            pltpu.VMEM((ranks, 2, count // 2, width), low),
            pltpu.VMEM((ranks, 2, count // 2, width), low),
            pltpu.VMEM((ranks - 1, count, width), low),
            pltpu.VMEM((ranks - 1, count, width), low),
            dma((2, 2)),
            dma,
            dma((2,)),
            dma((2, 3)),
            dma((9, ranks)),
            dma((9, ranks)),
            dma((10, ranks)),
            dma((10, ranks)),
            dma((ranks - 1,)),
            dma((ranks - 1,)),
        ],
        compiler_params=pltpu.CompilerParams(
            collective_id=2, has_side_effects=True, vmem_limit_bytes=60 * 1024 * 1024
        ),
        name="moe_pass",
    )(rows, back, gates, expert_gate, expert_up, shared_all)


def cube_copies(gathered, sends, recvs, by_core, by_x, by_y):
    half = gathered.shape[2] // 2
    first, last = pl.ds(0, half), pl.ds(half, half)
    at = gathered.at

    def copy(kind, j):
        src, dst, peer = {
            K_X: lambda: (at[0, j], at[2, j], by_x),
            K_Y: lambda: (at[0, j], at[3, j], by_y),
            K_CORE: lambda: (at[0, j], at[1, j], by_core),
            K_FAR_Y: lambda: (at[2, j, last], at[6, j, last], by_y),
            K_FAR_X: lambda: (at[3, j, first], at[6, j, first], by_x),
            K_CORE_X: lambda: (at[2, j], at[4, j], by_core),
            K_CORE_Y: lambda: (at[3, j], at[5, j], by_core),
            K_CORE_FAR: lambda: (at[6, j], at[7, j], by_core),
        }[kind]()
        return remote(src, dst, sends.at[kind, j], recvs.at[kind, j], peer)

    return copy


def swap_halves(values):
    lane = lax.broadcasted_iota(jnp.int32, values.shape, 1)
    middle = ROPE // 2
    lanes = values.shape[1]
    ahead, behind = pltpu.roll(values, lanes - middle, 1), pltpu.roll(values, middle, 1)
    return jnp.where((lane // middle) % 2 == 0, ahead, behind)


def turn(values, cos_table, sin_table):
    return values * cos_table + swap_halves(values) * sin_table


def front_kernel(
    lengths,
    hidden,
    cotangent,
    query,
    expand,
    output,
    shared,
    expert_down,
    routes,
    route_gates,
    latent_rows,
    attn_gain,
    latent_gain,
    mlp_gain,
    frequency,
    normed_out,
    latent_out,
    own_latent,
    query_out,
    expand_out,
    output_out,
    qcat_out,
    kcat_out,
    value_out,
    prob_out,
    attended_out,
    cos_out,
    sin_out,
    residual_out,
    normed_two,
    shared_all,
    gates_all,
    cotan_all,
    back_all,
    hidden_all,
    query_all,
    expand_all,
    output_all,
    down_rows,
    normed,
    latent_low,
    q_cat,
    k_cat,
    value,
    mask,
    prob,
    attended,
    gate_abs,
    gate_rel,
    gate_send,
    row_buf,
    back_buf,
    ring_out,
    ring_buf,
    local_sem,
    prob_sem,
    row_sem,
    back_sem,
    ring_send,
    ring_recv,
    w_send,
    w_recv,
    deal_send,
    deal_recv,
    gates_send,
    gates_recv,
    cring_send,
    cring_recv,
    c_send,
    c_recv,
    sum_send,
    sum_recv,
):
    me, rank = lax.axis_index(DP), lax.axis_index(TENSOR)
    ranks, count = lax.axis_size(TENSOR), lax.axis_size(DP)
    right = (me, lax.rem(rank + 1, ranks))
    left = (me, lax.rem(rank + ranks - 1, ranks))
    by_core, by_x, by_y = [(flip(me, bit), rank) for bit in (1, 2, 4)]
    partners = []
    for k in range(1, count):
        other = me
        for bit in (1, 2, 4):
            other = flip(other, bit) if k & bit else other
        partners.append((k, (other, rank)))
    rows, width = hidden.shape
    group_rows = rows * ranks
    heads = q_cat.shape[0]
    local_experts = gate_abs.shape[0] // count
    q_rows, e_rows, o_cols = query.shape[0], expand.shape[0], output.shape[1]
    routed_width = expert_down.shape[0]
    shared_pad = shared.shape[2]
    piece = shared.shape[3]

    def query_at(owner, half=None):
        size = q_rows if half is None else q_rows // 2
        start = owner * q_rows + (0 if half is None else half * size)
        return query_all.at[pl.ds(pl.multiple_of(start, size), size)]

    def expand_at(owner, half=None):
        size = e_rows if half is None else e_rows // 2
        start = owner * e_rows + (0 if half is None else half * size)
        return expand_all.at[pl.ds(pl.multiple_of(start, size), size)]

    def output_at(owner, half=None):
        size = output.shape[0] if half is None else output.shape[0] // 2
        start = 0 if half is None else half * size
        return output_all.at[
            pl.ds(start, size), pl.ds(pl.multiple_of(owner * o_cols, o_cols), o_cols)
        ]

    greet([peer for _, peer in partners] + [right, left])

    ring = {}

    def ring_step(step):
        src = hidden if step == 0 else hidden_all.at[step]
        ring[step] = remote(
            src, hidden_all.at[step + 1], ring_send.at[step], ring_recv.at[step], right
        )
        ring[step].start()

    weights = ((query, query_at), (expand, expand_at), (output, output_at))
    copies = {}

    def send(i, kind, src, dst, peer):
        copies[i, kind] = remote(src, dst, w_send.at[i, kind], w_recv.at[i, kind], peer)
        copies[i, kind].start()

    def weight_first(i):
        own, at = weights[i]
        send(i, 0, own, at(me), by_x)
        send(i, 1, own, at(me), by_y)
        send(i, 2, own, at(me), by_core)

    def weight_forward(i):
        _, at = weights[i]
        copies[i, 0].wait_recv()
        send(i, 3, at(flip(me, 2), 1), at(flip(me, 2), 1), by_y)
        send(i, 4, at(flip(me, 2)), at(flip(me, 2)), by_core)
        copies[i, 1].wait_recv()
        send(i, 5, at(flip(me, 4), 0), at(flip(me, 4), 0), by_x)
        send(i, 6, at(flip(me, 4)), at(flip(me, 4)), by_core)

    def weight_far(i):
        _, at = weights[i]
        far = flip(flip(me, 2), 4)
        copies[i, 3].wait_recv()
        copies[i, 5].wait_recv()
        send(i, 7, at(far), at(far), by_core)

    def weight_last(i):
        for kind in (2, 4, 6, 7):
            copies[i, kind].wait_recv()

    cube = cube_copies(cotan_all, c_send, c_recv, by_core, by_x, by_y)

    def cotan_ring(j):
        src = cotan_all.at[0, j - 1]
        return remote(src, cotan_all.at[0, j], cring_send.at[j - 1], cring_recv.at[j - 1], right)

    def cotan_send(j):
        for kind in (K_X, K_Y, K_CORE):
            cube(kind, j).start()

    def cotan_forward(j):
        cube(K_X, j).wait_recv()
        cube(K_FAR_Y, j).start()
        cube(K_CORE_X, j).start()
        cube(K_Y, j).wait_recv()
        cube(K_FAR_X, j).start()
        cube(K_CORE_Y, j).start()

    def cotan_far(j):
        cube(K_FAR_X, j).wait_recv()
        cube(K_FAR_Y, j).wait_recv()
        cube(K_CORE_FAR, j).start()

    def cotan_next(j):
        cotan_ring(j).wait_recv()
        if j + 1 < ranks:
            cotan_ring(j + 1).start()
        cotan_send(j)

    def down_back(j):
        for kind in (K_CORE, K_CORE_X, K_CORE_Y, K_CORE_FAR):
            cube(kind, j).wait_recv()

        def load(p, parity):
            return pltpu.make_async_copy(
                cotan_all.at[pl.ds(2 * p, 2), j], row_buf.at[parity], row_sem.at[parity]
            )

        def store(p, parity):
            return pltpu.make_async_copy(
                back_buf.at[parity], back_all.at[pl.ds(2 * p, 2), j], back_sem.at[parity]
            )

        load(0, 0).start()

        def one(p, carry):
            parity = lax.rem(p, 2)
            load(p, parity).wait()

            @pl.when(p < 3)
            def _():
                load(p + 1, 1 - parity).start()

            @pl.when(p > 1)
            def _():
                store(p - 2, parity).wait()

            wide = row_buf[parity].reshape(2 * rows, width)
            back = bfloat(last_dot(wide, down_rows[...]))
            back_buf[parity] = back.reshape(2, rows, back.shape[1])
            store(p, parity).start()
            return carry

        lax.fori_loop(0, 4, one, 0)
        store(2, 0).wait()
        store(3, 1).wait()

    ring_step(0)
    weight_first(0)
    weight_first(1)
    dealt = []
    for n, (k, peer) in enumerate(partners):
        copy = remote(
            shared.at[peer[0]],
            shared_all.at[:, :, pl.ds(pl.multiple_of(me * piece, piece), piece)],
            deal_send.at[n],
            deal_recv.at[n],
            peer,
        )
        dealt.append(copy)
    local = [
        pltpu.make_async_copy(hidden, hidden_all.at[0], local_sem.at[0]),
        pltpu.make_async_copy(query, query_at(me), local_sem.at[1]),
        pltpu.make_async_copy(expand, expand_at(me), local_sem.at[2]),
        pltpu.make_async_copy(output, output_at(me), local_sem.at[3]),
        pltpu.make_async_copy(
            shared.at[me],
            shared_all.at[:, :, pl.ds(pl.multiple_of(me * piece, piece), piece)],
            local_sem.at[4],
        ),
        pltpu.make_async_copy(cotangent, cotan_all.at[0, 0], local_sem.at[5]),
        pltpu.make_async_copy(expert_down, down_rows.at[pl.ds(0, routed_width)], local_sem.at[6]),
    ]
    for copy in local:
        copy.start()

    def absolute(index):
        block = index // rows
        return ((rank + ranks - block) % ranks) * rows + index % rows

    def starts_of(token):
        start, total = jnp.zeros_like(token), 0
        for n in range(lengths.shape[1]):
            total = total + lengths[0, n]
            start = jnp.where(token >= total, total, start)
        return start

    token = absolute(lax.broadcasted_iota(jnp.int32, (group_rows, cos_out.shape[1]), 0))
    angle = (token - starts_of(token)).astype(jnp.float32) * frequency[...]
    lane = lax.broadcasted_iota(jnp.int32, angle.shape, 1)
    cos_out[...] = jnp.cos(angle)
    sine = jnp.sin(angle)
    sin_out[...] = jnp.where((lane // (ROPE // 2)) % 2 == 0, -sine, sine)
    row_token = absolute(lax.broadcasted_iota(jnp.int32, mask.shape, 0))
    column_token = absolute(lax.broadcasted_iota(jnp.int32, mask.shape, 1))
    allowed = (column_token <= row_token) & (column_token >= starts_of(row_token))
    mask[...] = jnp.where(allowed, 0.0, -jnp.inf)

    expert = lax.broadcasted_iota(jnp.int32, gate_abs.shape, 0)
    dense = jnp.zeros(gate_abs.shape, jnp.float32)
    for k in range(routes.shape[0]):
        dense = dense + jnp.where(routes[k : k + 1, :] == expert, route_gates[k : k + 1, :], 0.0)
    gate_abs[...] = dense
    for r in range(ranks):
        start = pl.multiple_of(((rank + ranks - r) % ranks) * rows, rows)
        gate_rel[:, r * rows : (r + 1) * rows] = gate_abs[:, pl.ds(start, rows)]
    gate_send[...] = jnp.zeros_like(gate_send)
    for p in range(count):
        gate_send[p, 0:local_experts] = gate_rel[p * local_experts : (p + 1) * local_experts]
    down_rows[routed_width + shared_pad :] = jnp.zeros(
        (down_rows.shape[0] - routed_width - shared_pad, width), jnp.bfloat16
    )
    gate_copies = []
    for n, (k, peer) in enumerate(partners):
        gate_copies.append(
            remote(
                gate_send.at[peer[0]],
                gates_all.at[SLOTS.index(k)],
                gates_send.at[n],
                gates_recv.at[n],
                peer,
            )
        )
    own_gates = pltpu.make_async_copy(gate_send.at[me], gates_all.at[0], local_sem.at[7])
    own_gates.start()

    def norm_piece(r):
        at = pl.ds(r * rows, rows)
        values = hidden_all[r].astype(jnp.float32)
        scale = lax.rsqrt(jnp.mean(values * values, axis=-1, keepdims=True) + epsilon)
        normed[at, :] = bfloat(values * scale * attn_gain[...])

    def project_piece(r):
        at = pl.ds(r * rows, rows)
        values = normed[at, :]
        cos_table, sin_table = cos_out[at, :], sin_out[at, :]
        lanes = cos_table.shape[1]
        raw = plain_dot(values, query_all[...])
        for h in range(heads):
            q_cat[h, at, 0:NOPE] = bfloat(raw[:, h * NOPE : (h + 1) * NOPE])
        for pair in range(heads // 2):
            start = heads * NOPE + pair * lanes
            turned = bfloat(turn(raw[:, start : start + lanes], cos_table, sin_table))
            q_cat[2 * pair, at, NOPE : NOPE + lanes] = turned
            q_cat[2 * pair + 1, at, NOPE : NOPE + lanes] = turned
        latent = last_dot(values, latent_rows[...])
        part = latent[:, :LATENT]
        if r == 0:
            own_latent[...] = part
        scale = lax.rsqrt(jnp.mean(part * part, axis=-1, keepdims=True) + epsilon)
        low_part = bfloat(part * scale * latent_gain[...])
        latent_low[at, :] = low_part
        turned = turn(latent[:, LATENT:], cos_table, sin_table)
        lane = lax.broadcasted_iota(jnp.int32, turned.shape, 1)
        even = bfloat(jnp.where(lane < ROPE, turned, 0.0))
        odd = bfloat(jnp.where(lane < ROPE, 0.0, turned))
        expanded = plain_dot(low_part, expand_all[...])
        step = NOPE + VDIM
        for h in range(heads):
            k_cat[h, at, 0:NOPE] = bfloat(expanded[:, h * step : h * step + NOPE])
            k_cat[h, at, NOPE : NOPE + lanes] = even if h % 2 == 0 else odd
            value[h, at, :] = bfloat(expanded[:, h * step + NOPE : (h + 1) * step])

    def prob_store(h, parity):
        return pltpu.make_async_copy(prob.at[parity], prob_out.at[h], prob_sem.at[parity])

    def head(h):
        parity = h % 2
        if h >= 2:
            prob_store(h - 2, parity).wait()
        scores = last_dot(q_cat[h], k_cat[h]) * (NOPE + ROPE) ** (-0.5) + mask[...]
        exp_scores = jnp.exp(scores - jnp.max(scores, axis=-1, keepdims=True))
        ratio = exp_scores / jnp.sum(exp_scores, axis=-1, keepdims=True)
        prob[parity] = ratio
        prob_store(h, parity).start()
        attended[:, h * VDIM : (h + 1) * VDIM] = bfloat(plain_dot(bfloat(ratio), value[h]))

    norm_piece_wait = [local[0].wait] + [lambda s=s: ring[s].wait_recv() for s in range(ranks - 1)]
    norm_piece_wait[0]()
    norm_piece(0)
    for copy in dealt:
        copy.start()
    for copy in gate_copies:
        copy.start()
    weight_first(2)
    weight_forward(0)
    norm_piece_wait[1]()
    ring_step(1)
    weight_forward(1)
    norm_piece(1)
    weight_far(0)
    weight_far(1)
    local[5].wait()
    cotan_send(0)
    norm_piece_wait[2]()
    ring_step(2)
    cotan_ring(1).start()
    norm_piece(2)
    weight_forward(2)
    weight_last(0)
    weight_last(1)
    local[1].wait()
    local[2].wait()
    project_piece(0)
    project_piece(1)
    weight_far(2)
    project_piece(2)
    norm_piece_wait[3]()
    norm_piece(3)
    cotan_forward(0)
    project_piece(3)
    cotan_next(1)
    head(0)
    cotan_far(0)
    cotan_forward(1)
    head(1)
    cotan_next(2)
    head(2)
    cotan_far(1)
    head(3)
    weight_last(2)
    local[3].wait()

    def attn_block(r):
        return plain_dot(attended[r * rows : (r + 1) * rows, :], output_all[...])

    def sum_step(step):
        return remote(
            ring_out.at[step], ring_buf.at[step], sum_send.at[step], sum_recv.at[step], right
        )

    ring_out[0] = bfloat(attn_block(1))
    sum_step(0).start()
    cotan_forward(2)
    cotan_next(3)
    for copy in dealt:
        copy.wait_recv()
    local[4].wait()
    local[6].wait()
    shared_down = pltpu.make_async_copy(
        shared_all.at[2], down_rows.at[pl.ds(routed_width, shared_pad)], local_sem.at[8]
    )
    shared_down.start()
    shared_down.wait()
    down_back(0)
    sum_step(0).wait_recv()
    ring_out[1] = bfloat(attn_block(2) + ring_buf[0].astype(jnp.float32))
    sum_step(1).start()
    cotan_far(2)
    cotan_forward(3)
    down_back(1)
    sum_step(1).wait_recv()
    ring_out[2] = bfloat(attn_block(3) + ring_buf[1].astype(jnp.float32))
    sum_step(2).start()
    outs = [
        pltpu.make_async_copy(src, dst, local_sem.at[9 + n])
        for n, (src, dst) in enumerate(
            (
                (normed, normed_out),
                (latent_low, latent_out),
                (query_all, query_out),
                (expand_all, expand_out),
                (output_all, output_out),
                (q_cat, qcat_out),
                (k_cat, kcat_out),
                (value, value_out),
                (attended, attended_out),
            )
        )
    ]
    for copy in outs:
        copy.start()
    down_back(2)
    cotan_far(3)
    sum_step(2).wait_recv()
    residual = (
        hidden_all[0].astype(jnp.float32) + attn_block(0) + ring_buf[2].astype(jnp.float32)
    )
    residual_out[...] = residual
    scale = lax.rsqrt(jnp.mean(residual * residual, axis=-1, keepdims=True) + epsilon)
    normed_two[...] = bfloat(residual * scale * mlp_gain[...])
    down_back(3)

    for h in (heads - 2, heads - 1):
        prob_store(h, h % 2).wait()
    for copy in outs:
        copy.wait()
    own_gates.wait()
    for copy in gate_copies:
        copy.wait()
    for copy in dealt:
        copy.wait_send()
    for i in range(len(weights)):
        for kind in range(8):
            copies[i, kind].wait_send()
    for step in range(ranks - 1):
        ring[step].wait_send()
        cotan_ring(step + 1).wait_send()
        sum_step(step).wait_send()
    for j in range(ranks):
        for kind in (
            K_X,
            K_Y,
            K_CORE,
            K_FAR_Y,
            K_FAR_X,
            K_CORE_X,
            K_CORE_Y,
            K_CORE_FAR,
        ):
            cube(kind, j).wait_send()


def front_pass(
    lengths,
    hidden,
    cotangent,
    query,
    expand,
    output,
    shared,
    expert_down,
    routes,
    route_gates,
    latent_rows,
    attn_gain,
    latent_gain,
    mlp_gain,
    hidden_width,
    experts,
):
    count, ranks = lax.axis_size(DP), lax.axis_size(TENSOR)
    rows, width = hidden.shape
    group_rows = rows * ranks
    heads = query.shape[1] // (NOPE + ROPE)
    lanes = 2 * ROPE
    low, full = jnp.bfloat16, jnp.float32
    frequency = rope_base ** (-jnp.arange(ROPE // 2, dtype=full) * 2.0 / ROPE)
    frequency = jnp.tile(frequency, lanes // (ROPE // 2))[None, :]
    anywhere = pl.BlockSpec(memory_space=pl.ANY)
    in_vmem = pl.BlockSpec(memory_space=pltpu.VMEM)
    dma = pltpu.SemaphoreType.DMA
    by_slot = (count, ranks, rows)

    def array(*shape, dtype=low):
        return jax.ShapeDtypeStruct(shape, dtype)

    def full_query():
        return (count * query.shape[0], query.shape[1])

    def full_expand():
        return (count * expand.shape[0], expand.shape[1])

    def full_output():
        return (output.shape[0], count * output.shape[1])

    return pl.pallas_call(
        front_kernel,
        out_shape=(
            array(group_rows, width),
            array(group_rows, LATENT),
            array(rows, LATENT, dtype=full),
            array(*full_query()),
            array(*full_expand()),
            array(*full_output()),
            array(heads, group_rows, NOPE + lanes),
            array(heads, group_rows, NOPE + lanes),
            array(heads, group_rows, VDIM),
            array(heads, group_rows, group_rows, dtype=full),
            array(group_rows, heads * VDIM),
            array(group_rows, lanes, dtype=full),
            array(group_rows, lanes, dtype=full),
            array(rows, width, dtype=full),
            array(rows, width),
            array(*shared.shape[1:3], count * shared.shape[3]),
            array(count, 8, group_rows, dtype=full),
            array(*by_slot, width),
            array(*by_slot, hidden_width),
        ),
        in_specs=[pl.BlockSpec(memory_space=pltpu.SMEM)] + [anywhere] * 7 + [in_vmem] * 7,
        out_specs=(anywhere, anywhere, in_vmem)
        + (anywhere,) * 8
        + (in_vmem,) * 4
        + (anywhere,) * 4,
        scratch_shapes=[
            pltpu.VMEM((ranks, rows, width), low),
            pltpu.VMEM(full_query(), low),
            pltpu.VMEM(full_expand(), low),
            pltpu.VMEM(full_output(), low),
            pltpu.VMEM((hidden_width, width), low),
            pltpu.VMEM((group_rows, width), low),
            pltpu.VMEM((group_rows, LATENT), low),
            pltpu.VMEM((heads, group_rows, NOPE + lanes), low),
            pltpu.VMEM((heads, group_rows, NOPE + lanes), low),
            pltpu.VMEM((heads, group_rows, VDIM), low),
            pltpu.VMEM((group_rows, group_rows), full),
            pltpu.VMEM((2, group_rows, group_rows), full),
            pltpu.VMEM((group_rows, heads * VDIM), low),
            pltpu.VMEM((experts, group_rows), full),
            pltpu.VMEM((experts, group_rows), full),
            pltpu.VMEM((count, 8, group_rows), full),
            pltpu.VMEM((2, 2, rows, width), low),
            pltpu.VMEM((2, 2, rows, hidden_width), low),
            pltpu.VMEM((ranks - 1, rows, width), low),
            pltpu.VMEM((ranks - 1, rows, width), low),
            dma((18,)),
            dma((2,)),
            dma((2,)),
            dma((2,)),
            dma((ranks - 1,)),
            dma((ranks - 1,)),
            dma((3, 8)),
            dma((3, 8)),
            dma((count - 1,)),
            dma((count - 1,)),
            dma((count - 1,)),
            dma((count - 1,)),
            dma((ranks - 1,)),
            dma((ranks - 1,)),
            dma((9, ranks)),
            dma((9, ranks)),
            dma((ranks - 1,)),
            dma((ranks - 1,)),
        ],
        compiler_params=pltpu.CompilerParams(
            collective_id=1, has_side_effects=True, vmem_limit_bytes=60 * 1024 * 1024
        ),
        name="front_pass",
    )(
        lengths,
        hidden,
        cotangent,
        query,
        expand,
        output,
        shared,
        expert_down,
        routes,
        route_gates,
        latent_rows,
        attn_gain,
        latent_gain,
        mlp_gain,
        frequency,
    )


def add_rows(target, size, *terms, store=None):
    step = 16

    def one(i, carry):
        at = pl.ds(pl.multiple_of(i * step, step), step)
        total = target[at, :].astype(jnp.float32)
        for term in terms:
            total = total + term[at, :].astype(jnp.float32)
        to = target if store is None else store
        to[at, :] = total.astype(to.dtype)
        return carry

    lax.fori_loop(0, size // step, one, 0)


def sum_copies(blocks, core_buf, far_buf, x_buf, y_buf, sends, recvs, by_core, by_x, by_y):
    half = blocks.shape[2] // 2
    first, last = pl.ds(0, half), pl.ds(half, half)

    def copy(kind, j):
        at = blocks.at[lax.rem(j, 2)].at
        n, src, dst, peer = {
            K_CORE_OWN: lambda: (0, at[1], core_buf.at[j, 0], by_core),
            K_CORE_X: lambda: (1, at[4], core_buf.at[j, 1], by_core),
            K_CORE_Y: lambda: (2, at[5], core_buf.at[j, 2], by_core),
            K_CORE_FAR: lambda: (3, at[7], core_buf.at[j, 3], by_core),
            K_FAR_X: lambda: (4, at[6, first], far_buf.at[j, 0], by_x),
            K_FAR_Y: lambda: (5, at[6, last], far_buf.at[j, 1], by_y),
            K_X_FIRST: lambda: (6, at[2, first], x_buf.at[j, 0], by_x),
            K_X_LAST: lambda: (7, at[2, last], x_buf.at[j, 1], by_x),
            K_Y_FIRST: lambda: (8, at[3, first], y_buf.at[j, 0], by_y),
            K_Y_LAST: lambda: (9, at[3, last], y_buf.at[j, 1], by_y),
        }[kind]()
        return remote(src, dst, sends.at[n, j], recvs.at[n, j], peer)

    return copy


SUM_KINDS = (
    K_CORE_OWN,
    K_CORE_X,
    K_CORE_Y,
    K_CORE_FAR,
    K_FAR_X,
    K_FAR_Y,
    K_X_FIRST,
    K_X_LAST,
    K_Y_FIRST,
    K_Y_LAST,
)


def back_kernel(
    resid,
    acts,
    expert_down,
    shared_all,
    output,
    query,
    expand,
    q_cat,
    k_cat,
    value,
    prob_all,
    cos_table,
    sin_table,
    resid_all,
    moe_out,
    normed_back,
    latent_back,
    query_grad,
    expand_grad,
    down_rows,
    act_buf,
    resid_buf,
    attended_grad,
    prob,
    pair,
    key_rot,
    blocks,
    core_buf,
    far_buf,
    x_buf,
    y_buf,
    ring_out,
    ring_buf,
    moe_ring_out,
    moe_ring_buf,
    local_sem,
    act_sem,
    prob_sem,
    resid_send,
    resid_recv,
    s_send,
    s_recv,
    ring_send,
    ring_recv,
    moe_send,
    moe_recv,
):
    me, rank = lax.axis_index(DP), lax.axis_index(TENSOR)
    ranks = lax.axis_size(TENSOR)
    right = (me, lax.rem(rank + 1, ranks))
    left = (me, lax.rem(rank + ranks - 1, ranks))
    by_core, by_x, by_y = [(flip(me, bit), rank) for bit in (1, 2, 4)]
    rows, width = resid.shape
    half = rows // 2
    first, last = pl.ds(0, half), pl.ds(half, half)
    heads = q_cat.shape[0]
    lanes = cos_table.shape[1]
    routed_width, shared_pad = expert_down.shape[0], shared_all.shape[1]
    scaling = (NOPE + ROPE) ** (-0.5)
    greet([by_core, by_x, by_y, right, left])

    local = [
        pltpu.make_async_copy(resid, resid_buf.at[0], local_sem.at[0]),
        pltpu.make_async_copy(expert_down, down_rows.at[pl.ds(0, routed_width)], local_sem.at[1]),
        pltpu.make_async_copy(
            shared_all.at[2], down_rows.at[pl.ds(routed_width, shared_pad)], local_sem.at[2]
        ),
    ]

    def resid_step(step):
        src = resid if step == 0 else resid_buf.at[step]
        return remote(
            src, resid_buf.at[step + 1], resid_send.at[step], resid_recv.at[step], right
        )

    resid_step(0).start()
    for copy in local:
        copy.start()
    down_rows[routed_width + shared_pad :] = jnp.zeros(
        (down_rows.shape[0] - routed_width - shared_pad, width), jnp.bfloat16
    )
    key_rot[...] = jnp.zeros_like(key_rot)

    copy_of = sum_copies(
        blocks, core_buf, far_buf, x_buf, y_buf, s_send, s_recv, by_core, by_x, by_y
    )

    def act_load(j, p, parity):
        return pltpu.make_async_copy(
            acts.at[pl.ds(2 * p, 2), j], act_buf.at[parity], act_sem.at[parity]
        )

    def outputs(j):
        if j == 0:
            act_load(0, 0, 0).start()

        def one(p, carry):
            parity = lax.rem(p, 2)
            act_load(j, p, parity).wait()

            @pl.when(p < 3)
            def _():
                act_load(j, p + 1, 1 - parity).start()

            if j + 1 < ranks:

                @pl.when(p == 3)
                def _():
                    act_load(j + 1, 0, 0).start()

            wide = act_buf[parity].reshape(2 * rows, act_buf.shape[3])
            out = plain_dot(wide, down_rows[...])
            blocks[j % 2, pl.ds(2 * p, 2)] = bfloat(out).reshape(2, rows, width)
            return carry

        lax.fori_loop(0, 4, one, 0)
        for kind in (K_CORE_FAR, K_CORE_X, K_CORE_Y, K_CORE_OWN):
            copy_of(kind, j).start()

    def sums_first(j):
        at = blocks.at[j % 2].at
        copy_of(K_CORE_FAR, j).wait_recv()
        add_rows(at[6], rows, core_buf.at[j, 3])
        copy_of(K_FAR_X, j).start()
        copy_of(K_FAR_Y, j).start()
        copy_of(K_CORE_X, j).wait_recv()
        add_rows(at[2, first], half, core_buf.at[j, 1, first])
        copy_of(K_X_FIRST, j).start()
        copy_of(K_CORE_Y, j).wait_recv()
        add_rows(at[3, last], half, core_buf.at[j, 2, last])
        copy_of(K_Y_LAST, j).start()

    def sums_next(j):
        at = blocks.at[j % 2].at
        copy_of(K_FAR_X, j).wait_recv()
        add_rows(at[3, first], half, core_buf.at[j, 2, first], far_buf.at[j, 0])
        copy_of(K_Y_FIRST, j).start()
        copy_of(K_FAR_Y, j).wait_recv()
        add_rows(at[2, last], half, core_buf.at[j, 1, last], far_buf.at[j, 1])
        copy_of(K_X_LAST, j).start()

    def moe_step(step):
        return remote(
            moe_ring_out.at[step],
            moe_ring_buf.at[step],
            moe_send.at[step],
            moe_recv.at[step],
            right,
        )

    def sums_last(j):
        at = blocks.at[j % 2].at
        for kind in (K_CORE_OWN, K_X_FIRST, K_X_LAST, K_Y_FIRST, K_Y_LAST):
            copy_of(kind, j).wait_recv()
        if j > 1:
            moe_step(j - 2).wait_recv()
        for n, part in enumerate((first, last)):
            terms = [core_buf.at[j, 0, part], x_buf.at[j, n], y_buf.at[j, n]]
            if j > 1:
                terms.append(moe_ring_buf.at[j - 2, part])
            store = moe_out.at[part] if j == 0 else moe_ring_out.at[j - 1, part]
            add_rows(at[0, part], half, *terms, store=store)
        if j > 0:
            moe_step(j - 1).start()
        for kind in SUM_KINDS:
            copy_of(kind, j).wait_send()

    def attended_piece(r):
        attended_grad[r * rows : (r + 1) * rows, :] = bfloat(
            last_dot(resid_buf[r], output[...])
        )

    def prob_load(h):
        return pltpu.make_async_copy(prob_all.at[h], prob.at[h % 2], prob_sem.at[h % 2])

    def head(h):
        prob_load(h).wait()
        ratio = prob[h % 2]
        back = attended_grad[:, h * VDIM : (h + 1) * VDIM]
        prob_back = last_dot(back, value[h])
        row_dot = jnp.sum(prob_back * ratio, axis=-1, keepdims=True)
        score_back = bfloat(ratio * (prob_back - row_dot))
        value_back = first_dot(bfloat(ratio), back)
        query_back = bfloat(plain_dot(score_back, k_cat[h]) * scaling)
        key_back = bfloat(first_dot(score_back, q_cat[h]) * scaling)
        step = NOPE + VDIM
        expand_grad[:, h * step : h * step + NOPE] = key_back[:, :NOPE]
        expand_grad[:, h * step + NOPE : (h + 1) * step] = bfloat(value_back)
        query_grad[:, h * NOPE : (h + 1) * NOPE] = query_back[:, :NOPE]
        turned = key_back[:, NOPE:].astype(jnp.float32)
        lane = lax.broadcasted_iota(jnp.int32, turned.shape, 1)
        own = (lane < ROPE) if h % 2 == 0 else (lane >= ROPE)
        key_rot[...] += jnp.where(own, turned, 0.0)
        rope_part = query_back[:, NOPE:].astype(jnp.float32)
        if h % 2 == 0:
            pair[...] = rope_part
        else:
            whole = pair[...] + rope_part
            start = heads * NOPE + h // 2 * lanes
            query_grad[:, start : start + lanes] = bfloat(
                turn(whole, cos_table[...], -sin_table[...])
            )
        if h + 2 < heads:
            prob_load(h + 2).start()

    prob_load(0).start()
    prob_load(1).start()
    for copy in local[1:]:
        copy.wait()
    outputs(0)
    local[0].wait()
    attended_piece(0)
    sums_first(0)
    resid_step(0).wait_recv()
    resid_step(1).start()
    attended_piece(1)
    outputs(1)
    sums_next(0)
    resid_step(1).wait_recv()
    resid_step(2).start()
    attended_piece(2)
    sums_first(1)
    sums_last(0)
    outputs(2)
    resid_step(2).wait_recv()
    attended_piece(3)
    sums_next(1)
    sums_first(2)
    save = pltpu.make_async_copy(resid_buf, resid_all, local_sem.at[3])
    save.start()
    head(0)
    sums_last(1)
    sums_next(2)
    head(1)
    outputs(3)
    sums_first(3)
    head(2)
    sums_last(2)
    sums_next(3)
    head(3)

    folded = key_rot[...] + pltpu.roll(key_rot[...], ROPE, 1)
    key_rot[...] = folded

    def partial(r):
        at = slice(r * rows, (r + 1) * rows)
        latent = last_dot(expand_grad[at, :], expand[...])
        normed = last_dot(query_grad[at, :], query[...])
        return normed, latent, key_rot[at, :]

    splits = ((0, width), (width, width + LATENT), (width + LATENT, width + LATENT + lanes))

    def ring_step(step):
        return remote(
            ring_out.at[step], ring_buf.at[step], ring_send.at[step], ring_recv.at[step], right
        )

    for step in range(ranks - 1):
        parts = partial(step + 1)
        if step:
            ring_step(step - 1).wait_recv()
        for (start, stop), part in zip(splits, parts):
            if step:
                part = part + ring_buf[step - 1, :, start:stop].astype(jnp.float32)
            ring_out[step, :, start:stop] = bfloat(part)
        ring_step(step).start()
        if step == 0:
            sums_last(3)
    parts = partial(0)
    moe_step(ranks - 2).wait_recv()
    add_rows(moe_out, rows, moe_ring_buf.at[ranks - 2])
    ring_step(ranks - 2).wait_recv()
    normed_back[...] = parts[0] + ring_buf[ranks - 2, :, :width].astype(jnp.float32)
    latent_back[:, :LATENT] = parts[1] + ring_buf[
        ranks - 2, :, width : width + LATENT
    ].astype(jnp.float32)
    latent_back[:, LATENT:] = parts[2] + ring_buf[ranks - 2, :, width + LATENT :].astype(
        jnp.float32
    )
    save.wait()
    for step in range(ranks - 1):
        resid_step(step).wait_send()
        ring_step(step).wait_send()
        moe_step(step).wait_send()


def back_pass(
    resid,
    acts,
    expert_down,
    shared_all,
    output,
    query,
    expand,
    q_cat,
    k_cat,
    value,
    prob_all,
    cos_table,
    sin_table,
):
    ranks, groups = lax.axis_size(TENSOR), lax.axis_size(DP)
    rows, width = resid.shape
    group_rows = rows * ranks
    heads = q_cat.shape[0]
    lanes = cos_table.shape[1]
    hidden_width = acts.shape[-1]
    low, full = jnp.bfloat16, jnp.float32
    anywhere = pl.BlockSpec(memory_space=pl.ANY)
    in_vmem = pl.BlockSpec(memory_space=pltpu.VMEM)
    dma = pltpu.SemaphoreType.DMA

    def array(*shape, dtype=low):
        return jax.ShapeDtypeStruct(shape, dtype)

    return pl.pallas_call(
        back_kernel,
        out_shape=(
            array(ranks, rows, width),
            array(rows, width, dtype=full),
            array(rows, width, dtype=full),
            array(rows, LATENT + lanes, dtype=full),
            array(group_rows, query.shape[1]),
            array(group_rows, expand.shape[1]),
        ),
        in_specs=[anywhere] * 4 + [in_vmem] * 6 + [anywhere] + [in_vmem] * 2,
        out_specs=(anywhere,) + (in_vmem,) * 5,
        scratch_shapes=[
            pltpu.VMEM((hidden_width, width), low),
            pltpu.VMEM((2, 2, rows, hidden_width), low),
            pltpu.VMEM((ranks, rows, width), low),
            pltpu.VMEM((group_rows, heads * VDIM), low),
            pltpu.VMEM((2, group_rows, group_rows), full),
            pltpu.VMEM((group_rows, lanes), full),
            pltpu.VMEM((group_rows, lanes), full),
            pltpu.VMEM((2, groups, rows, width), low),
            pltpu.VMEM((ranks, 4, rows, width), low),
            pltpu.VMEM((ranks, 2, rows // 2, width), low),
            pltpu.VMEM((ranks, 2, rows // 2, width), low),
            pltpu.VMEM((ranks, 2, rows // 2, width), low),
            pltpu.VMEM((ranks - 1, rows, width + LATENT + lanes), low),
            pltpu.VMEM((ranks - 1, rows, width + LATENT + lanes), low),
            pltpu.VMEM((ranks - 1, rows, width), low),
            pltpu.VMEM((ranks - 1, rows, width), low),
            dma((4,)),
            dma((2,)),
            dma((2,)),
            dma((ranks - 1,)),
            dma((ranks - 1,)),
            dma((10, ranks)),
            dma((10, ranks)),
            dma((ranks - 1,)),
            dma((ranks - 1,)),
            dma((ranks - 1,)),
            dma((ranks - 1,)),
        ],
        compiler_params=pltpu.CompilerParams(
            collective_id=3, has_side_effects=True, vmem_limit_bytes=60 * 1024 * 1024
        ),
        name="back_pass",
    )(
        resid,
        acts,
        expert_down,
        shared_all,
        output,
        query,
        expand,
        q_cat,
        k_cat,
        value,
        prob_all,
        cos_table,
        sin_table,
    )


def weight_kernel(
    normed,
    latent_group,
    attended,
    resid,
    query_grad,
    expand_grad,
    latent_own,
    gains,
    gate_all,
    up_all,
    act_all,
    row_all,
    cotan_all,
    query_out,
    expand_out,
    output_out,
    gains_out,
    gate_out,
    up_out,
    down_out,
    shared_back,
    latent_all,
    query_full,
    expand_full,
    output_full,
    core_q,
    core_e,
    core_o,
    far_q,
    far_e,
    far_o,
    x_q,
    x_e,
    x_o,
    y_q,
    y_e,
    y_o,
    latent_rows,
    latent_full,
    latent_buf,
    latent_piece,
    gains_buf,
    gains_sum,
    gains_rank,
    gate_buf,
    up_buf,
    row_buf,
    gate_acc,
    up_acc,
    shared_low,
    load_sem,
    local_sem,
    out_sem,
    s_send,
    s_recv,
    lz_send,
    lz_recv,
    ld_send,
    ld_recv,
    lp_send,
    lp_recv,
    lc_send,
    lc_recv,
    gd_send,
    gd_recv,
    gz_send,
    gz_recv,
    h_send,
    h_recv,
):
    me, rank = lax.axis_index(DP), lax.axis_index(TENSOR)
    ranks, count = lax.axis_size(TENSOR), lax.axis_size(DP)
    by_core, by_x, by_y = [(flip(me, bit), rank) for bit in (1, 2, 4)]

    def owner(k):
        other = me
        for bit in (1, 2, 4):
            other = flip(other, bit) if k & bit else other
        return other

    partners = [(owner(k), rank) for k in range(1, count)]
    beside = [(me, lax.rem(rank + r, ranks)) for r in range(1, ranks)]
    width = normed.shape[1]
    routed_width = gate_out.shape[0]
    shared_pad = shared_low.shape[1]
    greet(partners + beside)

    own_latent = pltpu.make_async_copy(latent_own, latent_rows.at[0], local_sem.at[0])
    own_latent.start()
    latent_sends = [
        remote(latent_own, latent_rows.at[r], lz_send.at[r - 1], lz_recv.at[r - 1], peer)
        for r, peer in enumerate(beside, 1)
    ]
    gains_sends = [
        remote(gains, gains_buf.at[me], gd_send.at[n], gd_recv.at[n], peer)
        for n, peer in enumerate(partners)
    ]
    for copy in latent_sends + gains_sends:
        copy.start()
    gains_buf[me] = gains[...]

    sets = (
        (query_full, core_q, far_q, x_q, y_q, query_out),
        (expand_full, core_e, far_e, x_e, y_e, expand_out),
        (output_full, core_o, far_o, x_o, y_o, output_out),
    )

    def copy_of(i, kind):
        whole, core, far, x_buf, y_buf, _ = sets[i]
        half = whole.shape[1] // 2
        first, last = pl.ds(0, half), pl.ds(half, half)
        at = whole.at
        n, src, dst, peer = {
            K_CORE_OWN: lambda: (0, at[owner(1)], core.at[0], by_core),
            K_CORE_X: lambda: (1, at[owner(3)], core.at[1], by_core),
            K_CORE_Y: lambda: (2, at[owner(5)], core.at[2], by_core),
            K_CORE_FAR: lambda: (3, at[owner(7)], core.at[3], by_core),
            K_FAR_X: lambda: (4, at[owner(6), first], far.at[0], by_x),
            K_FAR_Y: lambda: (5, at[owner(6), last], far.at[1], by_y),
            K_X_FIRST: lambda: (6, at[owner(2), first], x_buf.at[0], by_x),
            K_X_LAST: lambda: (7, at[owner(2), last], x_buf.at[1], by_x),
            K_Y_FIRST: lambda: (8, at[owner(4), first], y_buf.at[0], by_y),
            K_Y_LAST: lambda: (9, at[owner(4), last], y_buf.at[1], by_y),
        }[kind]()
        return remote(src, dst, s_send.at[i, n], s_recv.at[i, n], peer)

    def sums_start(i):
        for kind in (K_CORE_FAR, K_CORE_X, K_CORE_Y, K_CORE_OWN):
            copy_of(i, kind).start()

    def sums_first(i):
        whole, core, _, _, _, _ = sets[i]
        half = whole.shape[1] // 2
        first, last = pl.ds(0, half), pl.ds(half, half)
        copy_of(i, K_CORE_FAR).wait_recv()
        add_rows(whole.at[owner(6)], 2 * half, core.at[3])
        copy_of(i, K_FAR_X).start()
        copy_of(i, K_FAR_Y).start()
        copy_of(i, K_CORE_X).wait_recv()
        add_rows(whole.at[owner(2), first], half, core.at[1, first])
        copy_of(i, K_X_FIRST).start()
        copy_of(i, K_CORE_Y).wait_recv()
        add_rows(whole.at[owner(4), last], half, core.at[2, last])
        copy_of(i, K_Y_LAST).start()

    def sums_next(i):
        whole, core, far, _, _, _ = sets[i]
        half = whole.shape[1] // 2
        first, last = pl.ds(0, half), pl.ds(half, half)
        copy_of(i, K_FAR_X).wait_recv()
        add_rows(whole.at[owner(4), first], half, core.at[2, first], far.at[0])
        copy_of(i, K_Y_FIRST).start()
        copy_of(i, K_FAR_Y).wait_recv()
        add_rows(whole.at[owner(2), last], half, core.at[1, last], far.at[1])
        copy_of(i, K_X_LAST).start()

    def sums_last(i):
        whole, core, _, x_buf, y_buf, out = sets[i]
        half = whole.shape[1] // 2
        for kind in (K_CORE_OWN, K_X_FIRST, K_X_LAST, K_Y_FIRST, K_Y_LAST):
            copy_of(i, kind).wait_recv()
        for n in range(2):
            part = pl.ds(n * half, half)
            add_rows(
                whole.at[me, part],
                half,
                core.at[0, part],
                x_buf.at[n],
                y_buf.at[n],
                store=out.at[part],
            )

    q_rows, o_cols = query_full.shape[1], output_full.shape[2]
    for o in range(count):
        at = slice(o * q_rows, (o + 1) * q_rows)
        query_full[o] = bfloat(first_dot(normed[:, at], query_grad[...]))
    sums_start(0)
    for o in range(count):
        at = slice(o * o_cols, (o + 1) * o_cols)
        output_full[o] = bfloat(first_dot(attended[...], resid[:, at]))
    sums_start(2)
    expanded = bfloat(first_dot(latent_group[...], expand_grad[...]))
    expand_full[...] = expanded.reshape(expand_full.shape)
    sums_start(1)

    part_width = latent_full.shape[2]
    latent_count = latent_full.shape[1]
    own_latent.wait()
    for copy in latent_sends:
        copy.wait_recv()
    columns = pl.ds(pl.multiple_of(rank * part_width, part_width), part_width)
    rows_low = latent_rows[...].reshape(-1, latent_rows.shape[2])
    latent_full[...] = bfloat(first_dot(rows_low, normed[:, columns])).reshape(latent_full.shape)
    dealt = [
        remote(
            latent_full.at[peer[0]], latent_buf.at[me], ld_send.at[n], ld_recv.at[n], peer
        )
        for n, peer in enumerate(partners)
    ]
    for copy in dealt:
        copy.start()
    latent_buf[me] = latent_full[me]

    pieces = [
        remote(
            latent_piece, latent_all.at[me, rank], lp_send.at[r - 1], lp_recv.at[r - 1], peer
        )
        for r, peer in enumerate(beside, 1)
    ]
    own_piece = pltpu.make_async_copy(latent_piece, latent_all.at[me, rank], local_sem.at[1])

    def latent_sum():
        for copy in dealt:
            copy.wait_recv()
        total = latent_buf[0].astype(jnp.float32)
        for o in range(1, count):
            total = total + latent_buf[o].astype(jnp.float32)
        latent_piece[...] = bfloat(total)
        for copy in pieces + [own_piece]:
            copy.start()

    def latent_copy(kind):
        half = ranks // 2
        first, last = pl.ds(0, half), pl.ds(half, half)
        at = latent_all.at
        n, block, peer = {
            K_X: lambda: (0, at[me], by_x),
            K_Y: lambda: (1, at[me], by_y),
            K_CORE: lambda: (2, at[me], by_core),
            K_FAR_Y: lambda: (3, at[owner(2), last], by_y),
            K_FAR_X: lambda: (4, at[owner(4), first], by_x),
            K_CORE_X: lambda: (5, at[owner(2)], by_core),
            K_CORE_Y: lambda: (6, at[owner(4)], by_core),
            K_CORE_FAR: lambda: (7, at[owner(6)], by_core),
        }[kind]()
        return remote(block, block, lc_send.at[n], lc_recv.at[n], peer)

    def latent_cube():
        own_piece.wait()
        for copy in pieces:
            copy.wait_recv()
        for kind in (K_X, K_Y, K_CORE):
            latent_copy(kind).start()

    def latent_forward():
        latent_copy(K_X).wait_recv()
        latent_copy(K_FAR_Y).start()
        latent_copy(K_CORE_X).start()
        latent_copy(K_Y).wait_recv()
        latent_copy(K_FAR_X).start()
        latent_copy(K_CORE_Y).start()

    def latent_far():
        latent_copy(K_FAR_X).wait_recv()
        latent_copy(K_FAR_Y).wait_recv()
        latent_copy(K_CORE_FAR).start()

    gains_beside = [
        remote(gains_sum, gains_rank.at[rank], gz_send.at[r - 1], gz_recv.at[r - 1], peer)
        for r, peer in enumerate(beside, 1)
    ]

    def gains_first():
        for copy in gains_sends:
            copy.wait_recv()
        total = gains_buf[0]
        for o in range(1, count):
            total = total + gains_buf[o]
        gains_sum[...] = total
        gains_rank[rank] = total
        for copy in gains_beside:
            copy.start()

    def gains_last():
        for copy in gains_beside:
            copy.wait_recv()
        total = gains_rank[0]
        for r in range(1, ranks):
            total = total + gains_rank[r]
        gains_out[...] = total

    chunk = row_buf.shape[1]
    chunks = row_all.shape[0] // chunk

    def loads(sources, i, parity):
        at = pl.ds(pl.multiple_of(i * chunk, chunk), chunk)
        return [
            pltpu.make_async_copy(src.at[at], buf.at[parity], load_sem.at[parity, n])
            for n, (src, buf) in enumerate(sources)
        ]

    def products(sources, totals, then, following):
        def one(i, carry):
            parity = lax.rem(i, 2)

            @pl.when(i < chunks - 1)
            def _():
                for copy in loads(sources, i + 1, 1 - parity):
                    copy.start()

            @pl.when(i == chunks - 1)
            def _():
                for copy in following(1 - parity):
                    copy.start()

            for copy in loads(sources, i, parity):
                copy.wait()
            right = sources[-1][1]
            for (_, left), total in zip(sources, totals):
                part = first_dot(left[parity], right[parity])

                @pl.when(i == 0)
                def _(part=part, total=total):
                    total[...] = part

                @pl.when(i > 0)
                def _(part=part, total=total):
                    total[...] += part

            for n, step in enumerate(then):
                pl.when(i == n)(step)
            return carry

        lax.fori_loop(0, chunks, one, 0)

    def shared_copies(at, n):
        size = shared_back.shape[3]
        return [
            remote(
                shared_low.at[at, :, pl.ds(pl.multiple_of(peer[0] * size, size), size)],
                shared_back.at[me, at],
                h_send.at[n, m],
                h_recv.at[n, m],
                peer,
            )
            for m, peer in enumerate(partners)
        ]

    def own_shared(at, n):
        size = shared_back.shape[3]
        return pltpu.make_async_copy(
            shared_low.at[at, :, pl.ds(pl.multiple_of(me * size, size), size)],
            shared_back.at[me, at],
            local_sem.at[2 + n],
        )

    two = ((gate_all, gate_buf), (up_all, up_buf), (row_all, row_buf))
    one = ((act_all, gate_buf), (cotan_all, row_buf))
    for copy in loads(two, 0, 0):
        copy.start()

    def step_a():
        for i in (0, 2, 1):
            sums_first(i)
        latent_sum()
        gains_first()

    def step_b():
        for i in (0, 2, 1):
            sums_next(i)
        latent_cube()
        gains_last()

    def step_c():
        latent_forward()
        for i in (0, 2, 1):
            sums_last(i)

    def step_d():
        latent_far()

    def after_two(parity):
        return loads(one, 0, parity)

    products(two, (gate_acc, up_acc), (step_a, step_b, step_c, step_d), after_two)
    outs = [
        pltpu.make_async_copy(
            total.at[pl.ds(0, routed_width)], out, out_sem.at[n]
        )
        for n, (total, out) in enumerate(((gate_acc, gate_out), (up_acc, up_out)))
    ]
    for copy in outs:
        copy.start()
    for n, total in enumerate((gate_acc, up_acc)):
        shared_low[n] = bfloat(total[routed_width : routed_width + shared_pad, :])
    pair = pl.ds(0, 2)
    for copy in shared_copies(pair, 0) + [own_shared(pair, 0)]:
        copy.start()
    outs[0].wait()
    products(one, (gate_acc,), (), lambda parity: [])
    down = pltpu.make_async_copy(
        gate_acc.at[pl.ds(0, routed_width)], down_out, out_sem.at[0]
    )
    down.start()
    shared_low[2] = bfloat(gate_acc[routed_width : routed_width + shared_pad, :])
    single = pl.ds(2, 1)
    for copy in shared_copies(single, 1) + [own_shared(single, 1)]:
        copy.start()

    for kind in (K_CORE, K_CORE_X, K_CORE_Y, K_CORE_FAR):
        latent_copy(kind).wait_recv()
    for kind in (K_X, K_Y, K_CORE, K_FAR_Y, K_FAR_X, K_CORE_X, K_CORE_Y, K_CORE_FAR):
        latent_copy(kind).wait_send()
    for copy in latent_sends + gains_sends + dealt + pieces + gains_beside:
        copy.wait_send()
    for i in range(len(sets)):
        for kind in SUM_KINDS:
            copy_of(i, kind).wait_send()
    outs[1].wait()
    down.wait()
    for at, n in ((pair, 0), (single, 1)):
        own_shared(at, n).wait()
        for copy in shared_copies(at, n):
            copy.wait()


def weight_pass(
    normed,
    latent_group,
    attended,
    resid,
    query_grad,
    expand_grad,
    latent_own,
    gains,
    gate_all,
    up_all,
    act_all,
    row_all,
    cotan_all,
    routed_width,
    shared_pad,
):
    ranks, count = lax.axis_size(TENSOR), lax.axis_size(DP)
    rows = latent_own.shape[0]
    width = normed.shape[1]
    hidden_width = act_all.shape[1]
    low, full = jnp.bfloat16, jnp.float32
    anywhere = pl.BlockSpec(memory_space=pl.ANY)
    in_vmem = pl.BlockSpec(memory_space=pltpu.VMEM)
    dma = pltpu.SemaphoreType.DMA
    chunk = 1024
    q_shape = (width // count, query_grad.shape[1])
    e_shape = (latent_group.shape[1] // count, expand_grad.shape[1])
    o_shape = (attended.shape[1], width // count)
    l_shape = (latent_own.shape[1] // count, width // ranks)
    shapes = (q_shape, e_shape, o_shape)

    def array(*shape, dtype=low):
        return jax.ShapeDtypeStruct(shape, dtype)

    def halves(n):
        return [pltpu.VMEM((n, shape[0] // 2, shape[1]), low) for shape in shapes]

    return pl.pallas_call(
        weight_kernel,
        out_shape=(
            array(*q_shape, dtype=full),
            array(*e_shape, dtype=full),
            array(*o_shape, dtype=full),
            array(*gains.shape, dtype=full),
            array(routed_width, width, dtype=full),
            array(routed_width, width, dtype=full),
            array(routed_width, width, dtype=full),
            array(count, 3, shared_pad, width // count),
            array(count, ranks, *l_shape),
        ),
        in_specs=[in_vmem] * 6 + [anywhere, in_vmem] + [anywhere] * 5,
        out_specs=(in_vmem,) * 4 + (anywhere,) * 5,
        scratch_shapes=[pltpu.VMEM((count,) + shape, low) for shape in shapes]
        + [pltpu.VMEM((4,) + shape, low) for shape in shapes]
        + halves(2)
        + halves(2)
        + halves(2)
        + [
            pltpu.VMEM((ranks, rows, latent_own.shape[1]), low),
            pltpu.VMEM((count,) + l_shape, low),
            pltpu.VMEM((count,) + l_shape, low),
            pltpu.VMEM(l_shape, low),
            pltpu.VMEM((count,) + gains.shape, full),
            pltpu.VMEM(gains.shape, full),
            pltpu.VMEM((ranks,) + gains.shape, full),
            pltpu.VMEM((2, chunk, hidden_width), low),
            pltpu.VMEM((2, chunk, hidden_width), low),
            pltpu.VMEM((2, chunk, width), low),
            pltpu.VMEM((hidden_width, width), full),
            pltpu.VMEM((hidden_width, width), full),
            pltpu.VMEM((3, shared_pad, width), low),
            dma((2, 3)),
            dma((4,)),
            dma((2,)),
            dma((3, 10)),
            dma((3, 10)),
            dma((ranks - 1,)),
            dma((ranks - 1,)),
            dma((count - 1,)),
            dma((count - 1,)),
            dma((ranks - 1,)),
            dma((ranks - 1,)),
            dma((8,)),
            dma((8,)),
            dma((count - 1,)),
            dma((count - 1,)),
            dma((ranks - 1,)),
            dma((ranks - 1,)),
            dma((2, count - 1)),
            dma((2, count - 1)),
        ],
        compiler_params=pltpu.CompilerParams(
            collective_id=4, has_side_effects=True, vmem_limit_bytes=62 * 1024 * 1024
        ),
        name="weight_pass",
    )(
        normed,
        latent_group,
        attended,
        resid,
        query_grad,
        expand_grad,
        latent_own,
        gains,
        gate_all,
        up_all,
        act_all,
        row_all,
        cotan_all,
    )


def part_heads(values, heads):
    split = values.reshape(-1, heads, NOPE + ROPE)
    parts = (split[:, :, :NOPE], split[:, :, NOPE:])
    return jnp.concatenate([part.reshape(values.shape[0], -1) for part in parts], axis=1)


def join_heads(values, heads):
    plain = values[:, : heads * NOPE].reshape(-1, heads, NOPE)
    turned = values[:, heads * NOPE :].reshape(-1, heads, ROPE)
    return jnp.concatenate([plain, turned], axis=2).reshape(values.shape)


def cube_shards(
    hidden,
    cotangent,
    routes,
    route_gates,
    doc_lengths,
    attn_gain,
    query_weight,
    latent_weight,
    latent_gain,
    expand_weight,
    output_weight,
    mlp_gain,
    shared_gate,
    shared_up,
    shared_down,
    expert_gate,
    expert_up,
    expert_down,
):
    ranks = lax.axis_size(TENSOR)
    groups = lax.axis_size(DP)
    rows = hidden.shape[0]
    group_rows = rows * ranks
    width = hidden.shape[1]
    local_experts, _, expert_width = expert_gate.shape
    experts = local_experts * groups

    shared_width = shared_gate.shape[1] // groups
    shared_pad = -(-shared_width // 16) * 16
    shared_stack = jnp.stack(
        [
            jnp.pad(
                weight.reshape(groups, shared_width, weight.shape[1]),
                ((0, 0), (0, shared_pad - shared_width), (0, 0)),
            )
            for weight in (shared_gate.T, shared_up.T, shared_down)
        ],
        axis=1,
    )
    routed_width = local_experts * expert_width
    hidden_width = -(-(routed_width + shared_pad) // 128) * 128
    local_heads = query_weight.shape[1] // (NOPE + ROPE)
    latent_columns = latent_weight.T

    (
        normed_group,
        latent_group,
        own_latent,
        query_full,
        expand_full,
        output_full,
        q_cat,
        k_cat,
        value_all,
        probability,
        attended_low,
        cos_group,
        sin_group,
        residual,
        normed_two,
        shared_all,
        slot_gates,
        cotan_all,
        back_all,
    ) = front_pass(
        doc_lengths,
        hidden,
        cotangent,
        part_heads(query_weight, local_heads),
        expand_weight,
        output_weight,
        shared_stack,
        expert_down.reshape(-1, width),
        routes.T,
        route_gates.T,
        jnp.concatenate([latent_columns, latent_columns[LATENT:]], axis=0),
        attn_gain[None],
        latent_gain[None],
        mlp_gain[None],
        hidden_width,
        experts,
    )
    row_all, act_all, gate_all, up_all, mlp_grad = moe_pass(
        normed_two,
        back_all,
        slot_gates,
        expert_gate.transpose(0, 2, 1).reshape(-1, width),
        expert_up.transpose(0, 2, 1).reshape(-1, width),
        shared_all,
        expert_width,
    )
    hidden_f = hidden.astype(jnp.float32)
    scale_one = rms_scale(hidden_f)
    normed_one = bfloat(hidden_f * scale_one * attn_gain)
    scale_latent = rms_scale(own_latent)
    scale_two = rms_scale(residual)
    cotan_all = cotan_all.reshape(-1, width)
    resid_from, mlpgain_part = rms_back(mlp_grad, residual, scale_two, mlp_gain)
    resid_grad = cotangent.astype(jnp.float32) + resid_from
    resid_low = bfloat(resid_grad)
    resid_all, moe_local, normed_back, latent_back, qraw_grad, expand_rows = back_pass(
        resid_low,
        act_all,
        expert_down.reshape(-1, width),
        shared_all,
        output_full,
        query_full,
        expand_full,
        q_cat,
        k_cat,
        value_all,
        probability,
        cos_group,
        sin_group,
    )
    layer_out = bfloat(residual + moe_local)
    cos_own, sin_own = cos_group[:rows, : ROPE // 2], sin_group[:rows, ROPE // 2 : ROPE]
    keyraw_back = rotate(latent_back[:, LATENT : LATENT + ROPE], cos_own, -sin_own)
    latent_in, latgain_part = rms_back(
        latent_back[:, :LATENT], own_latent, scale_latent, latent_gain
    )
    latent_low = bfloat(jnp.concatenate([latent_in, keyraw_back], axis=-1))

    normed_total = normed_back + last_dot(latent_low, latent_weight)
    hidden_back, attngain_part = rms_back(normed_total, hidden_f, scale_one, attn_gain)
    hidden_grad = resid_grad + hidden_back

    gains_part = jnp.concatenate([attngain_part, mlpgain_part, latgain_part])
    gains_rows = -(-gains_part.shape[0] // 1024) * 8
    gains_part = jnp.pad(gains_part, (0, gains_rows * 128 - gains_part.shape[0]))
    (
        query_total,
        expand_total,
        output_total,
        small,
        gate_wgrad,
        up_wgrad,
        down_wgrad,
        shared_back,
        latent_blocks,
    ) = weight_pass(
        normed_group,
        latent_group,
        attended_low,
        resid_all.reshape(group_rows, width),
        qraw_grad,
        expand_rows,
        jnp.concatenate([latent_low, latent_low[:, LATENT:]], axis=1),
        gains_part.reshape(gains_rows, 128),
        gate_all.reshape(-1, hidden_width),
        up_all.reshape(-1, hidden_width),
        act_all.reshape(-1, hidden_width),
        row_all.reshape(-1, width),
        cotan_all,
        routed_width,
        shared_pad,
    )
    small = small.reshape(-1)
    shared_total = shared_back[:, :, :shared_width].transpose(1, 0, 2, 3).reshape(
        3, groups * shared_width, -1
    ).astype(jnp.float32)
    latent_total = latent_blocks.transpose(0, 2, 1, 3).reshape(-1, width)
    latent_total = latent_total[: LATENT + ROPE].T.astype(jnp.float32)

    def expert_part(values):
        return values.reshape(local_experts, expert_width, width)

    return (
        layer_out,
        hidden_grad,
        small[:width],
        join_heads(query_total, local_heads),
        latent_total,
        small[2 * width : 2 * width + LATENT],
        expand_total,
        output_total,
        small[width : 2 * width],
        shared_total[0].T,
        shared_total[1].T,
        shared_total[2],
        expert_part(gate_wgrad).transpose(0, 2, 1),
        expert_part(up_wgrad).transpose(0, 2, 1),
        expert_part(down_wgrad),
    )


def solution(mesh):
    in_specs = (
        P((DP, TENSOR), None),
        P((DP, TENSOR), None),
        P(DP, None),
        P(DP, None),
        P(DP, None),
        P(),
        P(DP, TENSOR),
        P(),
        P(),
        P(DP, TENSOR),
        P(TENSOR, DP),
        P(),
        P(DP, TENSOR),
        P(DP, TENSOR),
        P(TENSOR, DP),
        P(DP, None, TENSOR),
        P(DP, None, TENSOR),
        P(DP, TENSOR, None),
    )
    out_specs = (
        P((DP, TENSOR), None),
        P((DP, TENSOR), None),
        P(),
        P(DP, TENSOR),
        P(),
        P(),
        P(DP, TENSOR),
        P(TENSOR, DP),
        P(),
        P(DP, TENSOR),
        P(DP, TENSOR),
        P(TENSOR, DP),
        P(DP, None, TENSOR),
        P(DP, None, TENSOR),
        P(DP, TENSOR, None),
    )
    cube = dict(mesh.shape) == {DP: 8, TENSOR: 4}
    shards = cube_shards if cube else general_shards
    return jax.shard_map(shards, mesh=mesh, in_specs=in_specs, out_specs=out_specs, check_vma=False)
```

```python
import functools
from types import SimpleNamespace

import jax
import jax.numpy as jnp
from jax import lax
from jax.experimental import pallas as pl
from jax.experimental.pallas import tpu as pltpu
from jax.sharding import PartitionSpec as P

DP = "dp"
TENSOR = "tensor"
NOPE = 128
ROPE = 64
VDIM = 128
LATENT = 512
TOPK = 6

(
    K_RING,
    K_X,
    K_Y,
    K_CORE,
    K_FAR_Y,
    K_FAR_X,
    K_CORE_X,
    K_CORE_Y,
    K_CORE_FAR,
    K_CORE_OWN,
    K_X_FIRST,
    K_X_LAST,
    K_Y_FIRST,
    K_Y_LAST,
    K_FAR_RING,
) = range(15)


epsilon = 1e-06
rope_base = 10000.0


def bfloat(values):
    return values.astype(jnp.bfloat16)


def plain_dot(left_op, right_op):
    return jnp.dot(left_op, right_op, preferred_element_type=jnp.float32)


def first_dot(left_op, right_op):
    return lax.dot_general(
        left_op, right_op, (((0,), (0,)), ((), ())), preferred_element_type=jnp.float32
    )


def last_dot(left_op, right_op):
    return lax.dot_general(
        left_op, right_op, (((1,), (1,)), ((), ())), preferred_element_type=jnp.float32
    )


def rms_scale(values):
    return lax.rsqrt(jnp.mean(values * values, axis=-1, keepdims=True) + epsilon)


def rms_back(grad_out, values, scaling, gain_vec):
    scaled_grad = grad_out * gain_vec
    inner_sum = jnp.mean(scaled_grad * values, axis=-1, keepdims=True)
    grad_in = scaling * scaled_grad - values * (scaling * scaling * scaling) * inner_sum
    return (grad_in, jnp.sum(grad_out * values * scaling, axis=0))


def silu_parts(values):
    sigmoid = jax.nn.sigmoid(values)
    return (values * sigmoid, sigmoid * (1.0 + values * (1.0 - sigmoid)))


def rope_tables(positions, rot_width):
    middle = rot_width // 2
    frequency = rope_base ** (-jnp.arange(middle, dtype=jnp.float32) * 2.0 / rot_width)
    angles = positions.astype(jnp.float32)[:, None] * frequency[None, :]
    return (jnp.cos(angles), jnp.sin(angles))


def rotate(values, cos_table, sin_table):
    middle = values.shape[-1] // 2
    first_half = values[..., :middle]
    second_half = values[..., middle:]
    return jnp.concatenate(
        [
            first_half * cos_table - second_half * sin_table,
            second_half * cos_table + first_half * sin_table,
        ],
        axis=-1,
    )


def doc_layout(lengths, row_count):
    doc_ends = jnp.cumsum(lengths)
    tok_index = jnp.arange(row_count, dtype=jnp.int32)
    before = (doc_ends[None, :] <= tok_index[:, None]).astype(jnp.int32)
    doc_ids = jnp.sum(before, axis=1)
    starts = jnp.sum(before * lengths[None, :], axis=1)
    return (doc_ids, tok_index - starts)


def slot_tables(routes, experts, capacity):
    row_count = routes.shape[0] * routes.shape[1]
    flat_routes = routes.reshape(row_count)
    onehot = (flat_routes[:, None] == jnp.arange(experts, dtype=jnp.int32)[None, :]).astype(
        jnp.int32
    )
    earlier = jnp.cumsum(onehot, axis=0) - onehot
    position = jnp.sum(earlier * onehot, axis=1)
    slot_ids = flat_routes * capacity + position
    tok_rows = jnp.arange(row_count, dtype=jnp.int32) // routes.shape[1]
    owner_tok = jnp.zeros((experts * capacity,), jnp.int32).at[slot_ids].set(tok_rows)
    return (slot_ids.reshape(routes.shape), owner_tok)


def slot_share(capacity):
    return (0, capacity)


def route_rows(outgoing, apply_fn):
    arrived = lax.all_to_all(outgoing, DP, split_axis=1, concat_axis=1, tiled=True)
    result, extra = apply_fn(arrived)
    back = lax.all_to_all(
        result.astype(jnp.bfloat16), DP, split_axis=1, concat_axis=1, tiled=True
    ).astype(result.dtype)
    return (back, extra)


def block_mask(doc_ids, row_start, block_rows):
    group_rows = doc_ids.shape[0]
    key_index = jnp.arange(group_rows, dtype=jnp.int32)
    query_index = row_start + jnp.arange(block_rows, dtype=jnp.int32)
    return (key_index[None, :] <= query_index[:, None]) & (doc_ids[None, :] == doc_ids[:, None])


def attend(query_all, key_all, value_all, doc_ids, scaling):
    group_rows = query_all.shape[0]
    block_rows = min(512, group_rows)
    block_count = group_rows // block_rows

    def one_block(block_id):
        row_start = block_id * block_rows
        allowed = block_mask(doc_ids, row_start, block_rows)
        scores = (
            jnp.einsum("qhd,khd->hqk", query_all, key_all, preferred_element_type=jnp.float32)
            * scaling
        )
        scores = jnp.where(allowed[None], scores, -jnp.inf)
        row_max = jnp.max(scores, axis=-1, keepdims=True)
        exp_scores = jnp.exp(scores - row_max)
        row_total = jnp.sum(exp_scores, axis=-1, keepdims=True)
        probability = bfloat(exp_scores / row_total)
        output = jnp.einsum(
            "hqk,khd->qhd", probability, value_all, preferred_element_type=jnp.float32
        )
        return (output, (row_max + jnp.log(row_total))[..., 0])

    outputs, log_total = lax.map(one_block, jnp.arange(block_count, dtype=jnp.int32))
    return (outputs.reshape(group_rows, outputs.shape[2], outputs.shape[3]), log_total)


def attend_back(query_all, key_all, value_all, doc_ids, scaling, log_total, grad_out):
    group_rows = query_all.shape[0]
    block_rows = min(512, group_rows)
    block_count = group_rows // block_rows

    def one_block(carried, inputs):
        key_grad, value_grad = carried
        block_id, block_lse = inputs
        row_start = block_id * block_rows
        allowed = block_mask(doc_ids, row_start, block_rows)
        scores = (
            jnp.einsum("qhd,khd->hqk", query_all, key_all, preferred_element_type=jnp.float32)
            * scaling
        )
        scores = jnp.where(allowed[None], scores, -jnp.inf)
        probability = jnp.exp(scores - block_lse[..., None])
        value_grad = value_grad + jnp.einsum(
            "hqk,qhd->khd", bfloat(probability), grad_out, preferred_element_type=jnp.float32
        )
        prob_grad = jnp.einsum(
            "qhd,khd->hqk", grad_out, value_all, preferred_element_type=jnp.float32
        )
        row_dot = jnp.sum(prob_grad * probability, axis=-1, keepdims=True)
        score_grad = bfloat(probability * (prob_grad - row_dot))
        query_grad = (
            jnp.einsum("hqk,khd->qhd", score_grad, key_all, preferred_element_type=jnp.float32)
            * scaling
        )
        key_grad = (
            key_grad
            + jnp.einsum("hqk,qhd->khd", score_grad, query_all, preferred_element_type=jnp.float32)
            * scaling
        )
        return ((key_grad, value_grad), query_grad)

    start_state = (jnp.zeros(key_all.shape, jnp.float32), jnp.zeros(value_all.shape, jnp.float32))
    (key_grad, value_grad), query_blocks = lax.scan(
        one_block, start_state, (jnp.arange(block_count, dtype=jnp.int32), log_total)
    )
    query_grad = query_blocks.reshape(group_rows, query_blocks.shape[2], query_blocks.shape[3])
    return (query_grad, key_grad, value_grad)


def forward_pass(
    hidden,
    cotangent,
    routes,
    route_gates,
    doc_lengths,
    attn_gain,
    query_weight,
    latent_weight,
    latent_gain,
    expand_weight,
    output_weight,
    mlp_gain,
    shared_gate,
    shared_up,
    shared_down,
    expert_gate,
    expert_up,
    expert_down,
):
    tensor_count = lax.axis_size(TENSOR)
    dp_count = lax.axis_size(DP)
    local_rows = hidden.shape[0]
    group_rows = local_rows * tensor_count
    query_full, expand_full, output_full, sgate_full, sup_full, sdown_full = (
        lax.all_gather(query_weight, DP, axis=0, tiled=True),
        lax.all_gather(expand_weight, DP, axis=0, tiled=True),
        lax.all_gather(output_weight, DP, axis=1, tiled=True),
        lax.all_gather(shared_gate, DP, axis=0, tiled=True),
        lax.all_gather(shared_up, DP, axis=0, tiled=True),
        lax.all_gather(shared_down, DP, axis=1, tiled=True),
    )
    hidden_f = hidden.astype(jnp.float32)
    scale_one = rms_scale(hidden_f)
    normed_one = bfloat(hidden_f * scale_one * attn_gain)
    latent_full = plain_dot(normed_one, latent_weight)
    latent_part = latent_full[:, :LATENT]
    scale_latent = rms_scale(latent_part)
    latent_norm = bfloat(latent_part * scale_latent * latent_gain)
    doc_ids, positions = doc_layout(doc_lengths[0], group_rows)
    cos_group, sin_group = rope_tables(positions, ROPE)
    local_start = lax.axis_index(TENSOR) * local_rows
    cos_local = lax.dynamic_slice_in_dim(cos_group, local_start, local_rows, 0)
    sin_local = lax.dynamic_slice_in_dim(sin_group, local_start, local_rows, 0)
    key_rot = bfloat(rotate(latent_full[:, LATENT:], cos_local, sin_local))
    normed_group, latent_group, keyrot_group = (
        lax.all_gather(normed_one, TENSOR, axis=0, tiled=True),
        lax.all_gather(latent_norm, TENSOR, axis=0, tiled=True),
        lax.all_gather(key_rot, TENSOR, axis=0, tiled=True),
    )
    local_heads = query_full.shape[1] // (NOPE + ROPE)
    query_raw = plain_dot(normed_group, query_full).reshape(group_rows, local_heads, NOPE + ROPE)
    query_rot = rotate(query_raw[..., NOPE:], cos_group[:, None, :], sin_group[:, None, :])
    query_all = bfloat(jnp.concatenate([query_raw[..., :NOPE], query_rot], axis=-1))
    expanded = plain_dot(latent_group, expand_full).reshape(group_rows, local_heads, NOPE + VDIM)
    key_shared = jnp.broadcast_to(keyrot_group[:, None, :], (group_rows, local_heads, ROPE))
    key_all = jnp.concatenate([bfloat(expanded[..., :NOPE]), key_shared], axis=-1)
    value_all = bfloat(expanded[..., NOPE:])
    scaling = (NOPE + ROPE) ** (-0.5)
    attended, log_total = attend(query_all, key_all, value_all, doc_ids, scaling)
    attended_low = bfloat(attended).reshape(group_rows, local_heads * VDIM)
    attn_local = lax.psum_scatter(
        plain_dot(attended_low, output_full), TENSOR, scatter_dimension=0, tiled=True
    )
    residual = hidden_f + attn_local
    scale_two = rms_scale(residual)
    normed_two = bfloat(residual * scale_two * mlp_gain)
    mlp_rows, cotan_rows = (
        lax.all_gather(normed_two, TENSOR, axis=0, tiled=True),
        lax.all_gather(cotangent, TENSOR, axis=0, tiled=True),
    )
    shared_gpre = plain_dot(mlp_rows, sgate_full)
    shared_upre = plain_dot(mlp_rows, sup_full)
    shared_silu, shared_dsilu = silu_parts(shared_gpre)
    shared_hidden = bfloat(shared_silu * shared_upre)
    shared_out = plain_dot(shared_hidden, sdown_full)
    local_experts = expert_gate.shape[0]
    experts = local_experts * dp_count
    capacity = group_rows * TOPK * 4 // (3 * experts)
    slot_ids, owner_tok = slot_tables(routes, experts, capacity)
    slot_start, slot_count = slot_share(capacity)
    all_tok = owner_tok.reshape(dp_count, local_experts, capacity).transpose(1, 0, 2)
    send_rows = mlp_rows[all_tok]

    def expert_apply(received):
        gate_pre = jnp.einsum(
            "jscd,jdf->jscf", received, expert_gate, preferred_element_type=jnp.float32
        )
        up_pre = jnp.einsum(
            "jscd,jdf->jscf", received, expert_up, preferred_element_type=jnp.float32
        )
        gate_silu, gate_dsilu = silu_parts(gate_pre)
        activated = bfloat(gate_silu * up_pre)
        result = jnp.einsum(
            "jscf,jfd->jscd", activated, expert_down, preferred_element_type=jnp.float32
        )
        return (result, (received, up_pre, gate_silu, gate_dsilu, activated))

    returned, expert_state = route_rows(send_rows, expert_apply)
    received, up_pre, gate_silu, gate_dsilu, activated = expert_state
    position = slot_ids % capacity - slot_start
    slot_mask = ((position >= 0) & (position < slot_count)).astype(jnp.float32)
    flat_index = (
        routes % local_experts * dp_count + routes // local_experts
    ) * slot_count + jnp.clip(position, 0, slot_count - 1)
    returned_flat = returned.reshape(local_experts * dp_count * slot_count, returned.shape[-1])
    routed = jnp.sum((route_gates * slot_mask)[:, :, None] * returned_flat[flat_index], axis=1)
    moe_local = lax.psum_scatter(
        (shared_out + routed).astype(jnp.bfloat16), TENSOR, scatter_dimension=0, tiled=True
    ).astype(jnp.float32)
    layer_out = bfloat(residual + moe_local)
    return SimpleNamespace(
        layer_out=layer_out,
        hidden_f=hidden_f,
        scale_one=scale_one,
        normed_one=normed_one,
        latent_part=latent_part,
        scale_latent=scale_latent,
        cos_local=cos_local,
        sin_local=sin_local,
        cos_group=cos_group,
        sin_group=sin_group,
        doc_ids=doc_ids,
        normed_group=normed_group,
        latent_group=latent_group,
        query_all=query_all,
        key_all=key_all,
        value_all=value_all,
        log_total=log_total,
        attended_low=attended_low,
        residual=residual,
        scale_two=scale_two,
        mlp_rows=mlp_rows,
        cotan_rows=cotan_rows,
        shared_upre=shared_upre,
        shared_silu=shared_silu,
        shared_dsilu=shared_dsilu,
        shared_hidden=shared_hidden,
        slot_ids=slot_ids,
        send_tok=all_tok,
        flat_index=flat_index,
        slot_mask=slot_mask,
        received=received,
        up_pre=up_pre,
        gate_silu=gate_silu,
        gate_dsilu=gate_dsilu,
        activated=activated,
        query_full=query_full,
        expand_full=expand_full,
        output_full=output_full,
        sgate_full=sgate_full,
        sup_full=sup_full,
        sdown_full=sdown_full,
    )


def general_shards(
    hidden,
    cotangent,
    routes,
    route_gates,
    doc_lengths,
    attn_gain,
    query_weight,
    latent_weight,
    latent_gain,
    expand_weight,
    output_weight,
    mlp_gain,
    shared_gate,
    shared_up,
    shared_down,
    expert_gate,
    expert_up,
    expert_down,
):
    kept_state = forward_pass(
        hidden,
        cotangent,
        routes,
        route_gates,
        doc_lengths,
        attn_gain,
        query_weight,
        latent_weight,
        latent_gain,
        expand_weight,
        output_weight,
        mlp_gain,
        shared_gate,
        shared_up,
        shared_down,
        expert_gate,
        expert_up,
        expert_down,
    )
    dp_count = lax.axis_size(DP)
    local_experts = expert_gate.shape[0]
    experts = local_experts * dp_count
    group_rows = kept_state.mlp_rows.shape[0]
    capacity = group_rows * TOPK * 4 // (3 * experts)
    cotan_rows = kept_state.cotan_rows
    mlp_rows = kept_state.mlp_rows
    sdown_wgrad = first_dot(kept_state.shared_hidden, cotan_rows)
    shared_hgrad = last_dot(cotan_rows, kept_state.sdown_full)
    sgate_pgrad = bfloat(shared_hgrad * kept_state.shared_upre * kept_state.shared_dsilu)
    sup_pgrad = bfloat(shared_hgrad * kept_state.shared_silu)
    sgate_wgrad = first_dot(mlp_rows, sgate_pgrad)
    sup_wgrad = first_dot(mlp_rows, sup_pgrad)
    mlp_partial = last_dot(sgate_pgrad, kept_state.sgate_full) + last_dot(
        sup_pgrad, kept_state.sup_full
    )
    slot_start, slot_count = slot_share(capacity)
    slot_gate = (
        jnp.zeros((experts * capacity,), jnp.float32)
        .at[kept_state.slot_ids.reshape(-1)]
        .set(route_gates.reshape(-1))
    )
    all_gate = slot_gate.reshape(dp_count, local_experts, capacity).transpose(1, 0, 2)
    grad_send = bfloat(all_gate[..., None] * cotan_rows[kept_state.send_tok].astype(jnp.float32))
    received = kept_state.received

    def expert_back(grad_recv):
        expert_down_partial = jnp.einsum(
            "jscf,jscd->jfd", kept_state.activated, grad_recv, preferred_element_type=jnp.float32
        )
        act_grad = jnp.einsum(
            "jscd,jfd->jscf", grad_recv, expert_down, preferred_element_type=jnp.float32
        )
        gate_pgrad = bfloat(act_grad * kept_state.up_pre * kept_state.gate_dsilu)
        up_pgrad = bfloat(act_grad * kept_state.gate_silu)
        row_gradient = jnp.einsum(
            "jscf,jdf->jscd", gate_pgrad, expert_gate, preferred_element_type=jnp.float32
        )
        row_gradient = row_gradient + jnp.einsum(
            "jscf,jdf->jscd", up_pgrad, expert_up, preferred_element_type=jnp.float32
        )
        expert_gate_partial = jnp.einsum(
            "jscd,jscf->jdf", received, gate_pgrad, preferred_element_type=jnp.float32
        )
        expert_up_partial = jnp.einsum(
            "jscd,jscf->jdf", received, up_pgrad, preferred_element_type=jnp.float32
        )
        return (row_gradient, (expert_gate_partial, expert_up_partial, expert_down_partial))

    rows_back, expert_weight_gradients = route_rows(grad_send, expert_back)
    expert_gate_weight_gradient, expert_up_weight_gradient, expert_down_weight_gradient = (
        expert_weight_gradients
    )
    back_flat = rows_back.reshape(local_experts * dp_count * slot_count, rows_back.shape[-1])
    mlp_partial = mlp_partial + jnp.sum(
        kept_state.slot_mask[:, :, None] * back_flat[kept_state.flat_index], axis=1
    )
    mlp_grad = lax.psum_scatter(mlp_partial, TENSOR, scatter_dimension=0, tiled=True)
    resid_from, mlpgain_part = rms_back(
        mlp_grad, kept_state.residual, kept_state.scale_two, mlp_gain
    )
    resid_grad = cotangent.astype(jnp.float32) + resid_from
    attn_rows = lax.all_gather(bfloat(resid_grad), TENSOR, axis=0, tiled=True)
    output_wgrad = first_dot(kept_state.attended_low, attn_rows)
    local_heads = kept_state.query_all.shape[1]
    attended_grad = bfloat(last_dot(attn_rows, kept_state.output_full)).reshape(
        group_rows, local_heads, VDIM
    )
    query_g, key_g, value_g = attend_back(
        kept_state.query_all,
        kept_state.key_all,
        kept_state.value_all,
        kept_state.doc_ids,
        (NOPE + ROPE) ** (-0.5),
        kept_state.log_total,
        attended_grad,
    )
    query_low = bfloat(query_g)
    key_low = bfloat(key_g)
    value_low = bfloat(value_g)
    query_unrot = rotate(
        query_low[..., NOPE:].astype(jnp.float32),
        kept_state.cos_group[:, None, :],
        -kept_state.sin_group[:, None, :],
    )
    qraw_grad = bfloat(
        jnp.concatenate([query_low[..., :NOPE].astype(jnp.float32), query_unrot], axis=-1)
    )
    qraw_grad = qraw_grad.reshape(group_rows, local_heads * (NOPE + ROPE))
    query_wgrad = first_dot(kept_state.normed_group, qraw_grad)
    normed_partial = last_dot(qraw_grad, kept_state.query_full)
    expand_rows = jnp.concatenate([key_low[..., :NOPE], value_low], axis=-1).reshape(
        group_rows, local_heads * (NOPE + VDIM)
    )
    expand_wgrad = first_dot(kept_state.latent_group, expand_rows)
    latent_partial = last_dot(expand_rows, kept_state.expand_full)
    keyrot_partial = jnp.sum(key_low[..., NOPE:].astype(jnp.float32), axis=1)
    normed_back, latent_back, keyrot_back = (
        lax.psum_scatter(
            normed_partial.astype(jnp.bfloat16), TENSOR, scatter_dimension=0, tiled=True
        ).astype(jnp.float32),
        lax.psum_scatter(
            latent_partial.astype(jnp.bfloat16), TENSOR, scatter_dimension=0, tiled=True
        ).astype(jnp.float32),
        lax.psum_scatter(
            keyrot_partial.astype(jnp.bfloat16), TENSOR, scatter_dimension=0, tiled=True
        ).astype(jnp.float32),
    )
    keyraw_back = rotate(keyrot_back, kept_state.cos_local, -kept_state.sin_local)
    latent_in, latgain_part = rms_back(
        latent_back, kept_state.latent_part, kept_state.scale_latent, latent_gain
    )
    latent_low = bfloat(jnp.concatenate([latent_in, keyraw_back], axis=-1))
    latent_wgrad = first_dot(kept_state.normed_one, latent_low)
    normed_total = normed_back + last_dot(latent_low, latent_weight)
    hidden_back, attngain_part = rms_back(
        normed_total, kept_state.hidden_f, kept_state.scale_one, attn_gain
    )
    hidden_grad = resid_grad + hidden_back
    fsdp_sums = (
        lax.psum_scatter(
            query_wgrad.astype(jnp.bfloat16), DP, scatter_dimension=0, tiled=True
        ).astype(jnp.float32),
        lax.psum_scatter(
            expand_wgrad.astype(jnp.bfloat16), DP, scatter_dimension=0, tiled=True
        ).astype(jnp.float32),
        lax.psum_scatter(
            output_wgrad.astype(jnp.bfloat16), DP, scatter_dimension=1, tiled=True
        ).astype(jnp.float32),
        lax.psum_scatter(
            sgate_wgrad.astype(jnp.bfloat16), DP, scatter_dimension=0, tiled=True
        ).astype(jnp.float32),
        lax.psum_scatter(
            sup_wgrad.astype(jnp.bfloat16), DP, scatter_dimension=0, tiled=True
        ).astype(jnp.float32),
        lax.psum_scatter(
            sdown_wgrad.astype(jnp.bfloat16), DP, scatter_dimension=1, tiled=True
        ).astype(jnp.float32),
    )
    small_sums = lax.psum(
        (latent_wgrad, attngain_part, mlpgain_part, latgain_part), (DP, TENSOR)
    )
    return (
        kept_state.layer_out,
        hidden_grad,
        small_sums[1],
        fsdp_sums[0],
        small_sums[0],
        small_sums[3],
        fsdp_sums[1],
        fsdp_sums[2],
        small_sums[2],
        fsdp_sums[3],
        fsdp_sums[4],
        fsdp_sums[5],
        expert_gate_weight_gradient,
        expert_up_weight_gradient,
        expert_down_weight_gradient,
    )


MESH = pl.DeviceIdType.MESH


def flip(index, bit):
    return index + bit - 2 * bit * ((index // bit) % 2)


def remote(src, dst, send_sem, recv_sem, peer):
    return pltpu.make_async_remote_copy(
        src_ref=src,
        dst_ref=dst,
        send_sem=send_sem,
        recv_sem=recv_sem,
        device_id=peer,
        device_id_type=MESH,
    )


def greet(peers):
    barrier = pltpu.get_barrier_semaphore()
    for peer in peers:
        pl.semaphore_signal(barrier, inc=1, device_id=peer, device_id_type=MESH)
    pl.semaphore_wait(barrier, len(peers))


def add_rows(target, size, *terms, store=None):
    step = 16
    while step * target.shape[1] < 65536 and size % (2 * step) == 0:
        step *= 2

    def one(i, carry):
        at = pl.ds(pl.multiple_of(i * step, step), step)
        total = target[at, :].astype(jnp.float32)
        for term in terms:
            total = total + term[at, :].astype(jnp.float32)
        to = target if store is None else store
        to[at, :] = total.astype(to.dtype)
        return carry

    lax.fori_loop(0, size // step, one, 0)


def sum_copies(blocks, core_buf, far_buf, x_buf, y_buf, sends, recvs, by_core, by_x, by_y):
    half = blocks.shape[2] // 2
    first, last = pl.ds(0, half), pl.ds(half, half)

    def copy(kind, j):
        at = blocks.at[lax.rem(j, 2)].at
        n, src, dst, peer = {
            K_CORE_OWN: lambda: (0, at[1], core_buf.at[j, 0], by_core),
            K_CORE_X: lambda: (1, at[4], core_buf.at[j, 1], by_core),
            K_CORE_Y: lambda: (2, at[5], core_buf.at[j, 2], by_core),
            K_CORE_FAR: lambda: (3, at[7], core_buf.at[j, 3], by_core),
            K_FAR_X: lambda: (4, at[6, first], far_buf.at[j, 0], by_x),
            K_FAR_Y: lambda: (5, at[6, last], far_buf.at[j, 1], by_y),
            K_X_FIRST: lambda: (6, at[2, first], x_buf.at[j, 0], by_x),
            K_X_LAST: lambda: (7, at[2, last], x_buf.at[j, 1], by_x),
            K_Y_FIRST: lambda: (8, at[3, first], y_buf.at[j, 0], by_y),
            K_Y_LAST: lambda: (9, at[3, last], y_buf.at[j, 1], by_y),
        }[kind]()
        return remote(src, dst, sends.at[n, j], recvs.at[n, j], peer)

    return copy


SUM_KINDS = (
    K_CORE_OWN,
    K_CORE_X,
    K_CORE_Y,
    K_CORE_FAR,
    K_FAR_X,
    K_FAR_Y,
    K_X_FIRST,
    K_X_LAST,
    K_Y_FIRST,
    K_Y_LAST,
)


SLOTS = (0, 1, 2, 4, 3, 5, 6, 7)


def moe_kernel(
    rows,
    back,
    gates,
    expert_gate,
    expert_up,
    shared_all,
    residual,
    cotangent,
    gain,
    rows_all,
    act_all,
    gpre_all,
    upre_all,
    resid_grad,
    resid_low,
    gain_grad,
    grad_out,
    gate_rows,
    up_rows,
    row_buf,
    back_buf,
    out_buf,
    blocks,
    core_buf,
    far_buf,
    x_buf,
    y_buf,
    ring_buf,
    ring_out,
    weight_sem,
    load_sem,
    back_sem,
    store_sem,
    ag_send,
    ag_recv,
    rs_send,
    rs_recv,
    ring_send,
    ring_recv,
    *,
    expert_width,
    routed_width,
):
    me, rank = lax.axis_index(DP), lax.axis_index(TENSOR)
    ranks = lax.axis_size(TENSOR)
    right = (me, lax.rem(rank + 1, ranks))
    left = (me, lax.rem(rank + ranks - 1, ranks))
    by_core, by_x, by_y = [(flip(me, bit), rank) for bit in (1, 2, 4)]
    count = rows.shape[0]
    half = count // 2
    first, last = pl.ds(0, half), pl.ds(half, half)
    hidden_width = gate_rows.shape[0]
    shared_pad = shared_all.shape[1]
    greet([by_core, by_x, by_y, right, left])

    def ag(kind, j, src, dst, peer):
        return remote(src, dst, ag_send.at[kind, j], ag_recv.at[kind, j], peer)

    def rs(kind, j, src, dst, peer):
        return remote(src, dst, rs_send.at[kind, j], rs_recv.at[kind, j], peer)

    def row_copy(kind, j):
        at = rows_all.at
        return {
            K_RING: lambda: ag(0, j, at[0, j - 1], at[0, j], right),
            K_X: lambda: ag(1, j, at[0, j], at[2, j], by_x),
            K_Y: lambda: ag(2, j, at[0, j], at[3, j], by_y),
            K_CORE: lambda: ag(3, j, at[0, j], at[1, j], by_core),
            K_FAR_Y: lambda: ag(4, j, at[2, j, last], at[6, j, last], by_y),
            K_FAR_X: lambda: ag(5, j, at[3, j, first], at[6, j, first], by_x),
            K_CORE_X: lambda: ag(6, j, at[2, j], at[4, j], by_core),
            K_CORE_Y: lambda: ag(7, j, at[3, j], at[5, j], by_core),
            K_CORE_FAR: lambda: ag(8, j, at[6, j], at[7, j], by_core),
            K_FAR_RING: lambda: ag(4, j, at[6, j - 1], at[6, j], right),
        }[kind]()

    def sum_copy(kind, j):
        at = blocks.at[lax.rem(j, 2)].at
        return {
            K_CORE_OWN: lambda: rs(0, j, at[1], core_buf.at[j, 0], by_core),
            K_CORE_X: lambda: rs(1, j, at[4], core_buf.at[j, 1], by_core),
            K_CORE_Y: lambda: rs(2, j, at[5], core_buf.at[j, 2], by_core),
            K_CORE_FAR: lambda: rs(3, j, at[7], core_buf.at[j, 3], by_core),
            K_FAR_X: lambda: rs(4, j, at[6, first], far_buf.at[j, 0], by_x),
            K_FAR_Y: lambda: rs(5, j, at[6, last], far_buf.at[j, 1], by_y),
            K_X_FIRST: lambda: rs(6, j, at[2, first], x_buf.at[j, 0], by_x),
            K_X_LAST: lambda: rs(7, j, at[2, last], x_buf.at[j, 1], by_x),
            K_Y_FIRST: lambda: rs(8, j, at[3, first], y_buf.at[j, 0], by_y),
            K_Y_LAST: lambda: rs(9, j, at[3, last], y_buf.at[j, 1], by_y),
        }[kind]()

    def ring_copy(step):
        return remote(
            ring_out.at[step], ring_buf.at[step], ring_send.at[step], ring_recv.at[step], right
        )

    def back_load(j, p, parity):
        return pltpu.make_async_copy(
            back.at[pl.ds(2 * p, 2), j], back_buf.at[parity], back_sem.at[parity]
        )

    def row_load(j, p, parity):
        return pltpu.make_async_copy(
            rows_all.at[pl.ds(2 * p, 2), j], row_buf.at[parity], load_sem.at[parity]
        )

    def stores(j, p, parity):
        return [
            pltpu.make_async_copy(
                out_buf.at[parity, n], to.at[pl.ds(2 * p, 2), j], store_sem.at[parity, n]
            )
            for n, to in enumerate((act_all, gpre_all, upre_all))
        ]

    def compute(j, p, place, following, used):
        parity = place % 2
        if following is not None:
            back_load(*following, 1 - parity).start()
        back_load(j, p, parity).wait()
        for copy in stores(*used, parity) if used is not None else ():
            copy.wait()
        row_load(j, p, parity).wait()
        wide = row_buf[parity].reshape(2 * count, row_buf.shape[3])
        gate_pre = last_dot(wide, gate_rows[...])
        up_pre = last_dot(wide, up_rows[...])
        column = lax.broadcasted_iota(jnp.int32, (1, hidden_width), 1)
        lanes = pl.ds(pl.multiple_of(j * count, count), count)
        gate = jnp.concatenate([gates[2 * p + i, :, lanes].T for i in range(2)], axis=0)
        scaled = jnp.where(
            column < expert_width,
            gate[:, 0:1],
            jnp.where(column < routed_width, gate[:, 1:2], 1.0),
        )
        sigmoid = 1.0 / (1.0 + jnp.exp(-gate_pre))
        silu = gate_pre * sigmoid
        dsilu = sigmoid * (1.0 + gate_pre * (1.0 - sigmoid))
        back_pre = back_buf[parity].reshape(2 * count, hidden_width).astype(jnp.float32) * scaled
        act = bfloat(silu * up_pre * scaled)
        gate_grad = bfloat(back_pre * up_pre * dsilu)
        up_grad = bfloat(back_pre * silu)
        out_buf[parity, 0] = act.reshape(2, count, hidden_width)
        out_buf[parity, 1] = gate_grad.reshape(2, count, hidden_width)
        out_buf[parity, 2] = up_grad.reshape(2, count, hidden_width)
        for copy in stores(j, p, parity):
            copy.start()
        grad = plain_dot(gate_grad, gate_rows[...]) + plain_dot(up_grad, up_rows[...])
        blocks[lax.rem(j, 2), pl.ds(2 * p, 2)] = bfloat(grad).reshape(2, count, grad.shape[1])

    own = pltpu.make_async_copy(rows, rows_all.at[0, 0], load_sem.at[0])
    own.start()
    assembled = []
    for n, (routed, target) in enumerate(((expert_gate, gate_rows), (expert_up, up_rows))):
        for i, (src, at) in enumerate(
            ((routed, pl.ds(0, routed_width)), (shared_all.at[n], pl.ds(routed_width, shared_pad)))
        ):
            copy = pltpu.make_async_copy(src, target.at[at], weight_sem.at[n, i])
            copy.start()
            assembled.append(copy)
        target[routed_width + shared_pad :] = jnp.zeros(
            (hidden_width - routed_width - shared_pad, target.shape[1]), jnp.bfloat16
        )
    back_load(0, 0, 0).start()
    own.wait()
    ring0 = row_copy(K_RING, 1)
    ring0.start()
    for kind in (K_X, K_Y, K_CORE):
        row_copy(kind, 0).start()
    for copy in assembled:
        copy.wait()

    def send_piece(j):
        for kind in (K_X, K_Y, K_CORE):
            row_copy(kind, j).start()

    def forward_piece(j):
        row_copy(K_X, j).wait_recv()
        row_copy(K_CORE_X, j).start()
        row_copy(K_Y, j).wait_recv()
        row_copy(K_CORE_Y, j).start()

    def sums_far(j):
        sum_copy(K_CORE_FAR, j).wait_recv()
        add_rows(blocks.at[lax.rem(j, 2), 6], count, core_buf.at[j, 3])
        sum_copy(K_FAR_X, j).start()
        sum_copy(K_FAR_Y, j).start()

    def sums_near(j):
        at = blocks.at[lax.rem(j, 2)].at
        sum_copy(K_CORE_X, j).wait_recv()
        add_rows(at[2, first], half, core_buf.at[j, 1, first])
        sum_copy(K_X_FIRST, j).start()
        sum_copy(K_CORE_Y, j).wait_recv()
        add_rows(at[3, last], half, core_buf.at[j, 2, last])
        sum_copy(K_Y_LAST, j).start()

    def sums_next(j):
        at = blocks.at[lax.rem(j, 2)].at
        sum_copy(K_FAR_X, j).wait_recv()
        add_rows(at[3, first], half, core_buf.at[j, 2, first], far_buf.at[j, 0])
        sum_copy(K_Y_FIRST, j).start()
        sum_copy(K_FAR_Y, j).wait_recv()
        add_rows(at[2, last], half, core_buf.at[j, 1, last], far_buf.at[j, 1])
        sum_copy(K_X_LAST, j).start()

    def sums_last(j):
        at = blocks.at[lax.rem(j, 2)].at
        for kind in (K_CORE_OWN, K_X_FIRST, K_X_LAST, K_Y_FIRST, K_Y_LAST):
            sum_copy(kind, j).wait_recv()
        terms = [
            (core_buf.at[j, 0, part], x_buf.at[j, n], y_buf.at[j, n])
            for n, part in enumerate((first, last))
        ]

        @pl.when(j == 0)
        def _():
            for part, more in zip((first, last), terms):
                add_rows(at[0, part], half, *more, store=grad_out.at[part])

        @pl.when(j == 1)
        def _():
            for part, more in zip((first, last), terms):
                add_rows(at[0, part], half, *more, store=ring_out.at[0, part])
            ring_copy(0).start()

        @pl.when(j > 1)
        def _():
            ring_copy(j - 2).wait_recv()
            for part, more in zip((first, last), terms):
                add_rows(
                    at[0, part],
                    half,
                    *more,
                    ring_buf.at[j - 2, part],
                    store=ring_out.at[j - 1, part],
                )
            ring_copy(j - 1).start()

        for kind in SUM_KINDS:
            sum_copy(kind, j).wait_send()

    row_copy(K_CORE, 0).wait_recv()
    row_load(0, 0, 0).start()
    compute(0, 0, 0, (0, 1), None)
    sum_copy(K_CORE_OWN, 0).start()
    row_copy(K_RING, 1).wait_recv()
    row_copy(K_RING, 2).start()
    send_piece(1)
    row_copy(K_X, 0).wait_recv()
    row_copy(K_FAR_Y, 0).start()
    row_copy(K_CORE_X, 0).start()
    row_copy(K_Y, 0).wait_recv()
    row_copy(K_FAR_X, 0).start()
    row_copy(K_CORE_Y, 0).start()
    row_load(0, 1, 1).start()
    compute(0, 1, 1, (0, 2), None)
    row_copy(K_RING, 2).wait_recv()
    row_copy(K_RING, 3).start()
    send_piece(2)
    row_copy(K_CORE_X, 0).wait_recv()
    row_copy(K_CORE_Y, 0).wait_recv()
    row_load(0, 2, 0).start()
    row_copy(K_FAR_X, 0).wait_recv()
    row_copy(K_FAR_Y, 0).wait_recv()
    row_copy(K_CORE_FAR, 0).start()
    row_copy(K_FAR_RING, 1).start()
    compute(0, 2, 0, (0, 3), (0, 0))
    sum_copy(K_CORE_X, 0).start()
    sum_copy(K_CORE_Y, 0).start()
    row_copy(K_CORE_FAR, 0).wait_recv()
    row_load(0, 3, 1).start()
    row_copy(K_RING, 3).wait_recv()
    send_piece(3)
    forward_piece(1)
    row_copy(K_CORE, 1).wait_recv()
    compute(0, 3, 1, (1, 3), (0, 1))
    sum_copy(K_CORE_FAR, 0).start()
    sums_near(0)
    sums_far(0)
    row_copy(K_FAR_RING, 1).wait_recv()
    row_copy(K_CORE_FAR, 1).start()
    row_copy(K_FAR_RING, 2).start()
    row_copy(K_CORE_FAR, 1).wait_recv()
    row_load(1, 3, 0).start()

    def body(j, carry):
        before = j - 1
        row_copy(K_CORE_X, j).wait_recv()
        row_copy(K_CORE_Y, j).wait_recv()
        row_load(j, 2, 1).start()

        @pl.when(j == 1)
        def _():
            for copy in stores(0, 2, 0):
                copy.wait()

        @pl.when(j > 1)
        def _():
            for copy in stores(before, 1, 0):
                copy.wait()

        compute(j, 3, 0, (j, 2), None)
        sum_copy(K_CORE_FAR, j).start()

        @pl.when(j == 1)
        def _():
            sums_next(0)
            for copy in stores(0, 3, 1):
                copy.wait()

        @pl.when(j > 1)
        def _():
            for copy in stores(before, 0, 1):
                copy.wait()

        row_load(j, 1, 0).start()
        compute(j, 2, 1, (j, 1), None)
        sum_copy(K_CORE_X, j).start()
        sum_copy(K_CORE_Y, j).start()
        sums_far(j)

        @pl.when(j < ranks - 1)
        def _():
            row_copy(K_FAR_RING, j + 1).wait_recv()
            row_copy(K_CORE_FAR, j + 1).start()

            @pl.when(j < ranks - 2)
            def _():
                row_copy(K_FAR_RING, j + 2).start()

        row_load(j, 0, 1).start()
        compute(j, 1, 0, (j, 0), (j, 3))
        sums_near(j)

        @pl.when(j < ranks - 1)
        def _():
            forward_piece(j + 1)
            row_copy(K_CORE, j + 1).wait_recv()
            row_copy(K_CORE_FAR, j + 1).wait_recv()
            row_load(j + 1, 3, 0).start()
            back_load(j + 1, 3, 0).start()

        compute(j, 0, 1, None, (j, 2))
        sum_copy(K_CORE_OWN, j).start()
        sums_last(before)
        sums_next(j)
        return carry

    lax.fori_loop(1, ranks, body, 0)
    sums_last(ranks - 1)
    ring_copy(ranks - 2).wait_recv()
    grad = grad_out[...] + ring_buf[ranks - 2].astype(jnp.float32)
    values = residual[...]
    scale = lax.rsqrt(jnp.mean(values * values, axis=-1, keepdims=True) + epsilon)
    scaled_grad = grad * gain[...]
    inner = jnp.mean(scaled_grad * values, axis=-1, keepdims=True)
    through = scale * scaled_grad - values * (scale * scale * scale) * inner
    total = cotangent[...].astype(jnp.float32) + through
    resid_grad[...] = total
    resid_low[...] = bfloat(total)
    gain_grad[...] = jnp.sum(grad * values * scale, axis=0, keepdims=True)
    for step in range(ranks - 1):
        ring_copy(step).wait_send()
        row_copy(K_RING, step + 1).wait_send()
    for p in (1, 0):
        for copy in stores(ranks - 1, p, 1 - p):
            copy.wait()

    def drain(j, carry):
        for kind in (K_X, K_Y, K_CORE, K_CORE_X, K_CORE_Y, K_CORE_FAR):
            row_copy(kind, j).wait_send()
        return carry

    row_copy(K_FAR_X, 0).wait_send()
    row_copy(K_FAR_Y, 0).wait_send()
    for j in range(1, ranks):
        row_copy(K_FAR_RING, j).wait_send()
    lax.fori_loop(0, ranks, drain, 0)


def moe_pass(
    rows,
    back,
    gates,
    expert_gate,
    expert_up,
    shared_all,
    residual,
    cotangent,
    gain,
    expert_width,
):
    ranks = lax.axis_size(TENSOR)
    groups = lax.axis_size(DP)
    count, width = rows.shape
    hidden_width = back.shape[-1]
    anywhere = pl.BlockSpec(memory_space=pl.ANY)
    in_vmem = pl.BlockSpec(memory_space=pltpu.VMEM)
    low = jnp.bfloat16
    hidden_shape = jax.ShapeDtypeStruct((groups, ranks, count, hidden_width), low)
    dma = pltpu.SemaphoreType.DMA
    return pl.pallas_call(
        functools.partial(
            moe_kernel, expert_width=expert_width, routed_width=expert_gate.shape[0]
        ),
        out_shape=(
            jax.ShapeDtypeStruct((groups, ranks, count, width), low),
            hidden_shape,
            hidden_shape,
            hidden_shape,
            jax.ShapeDtypeStruct((count, width), jnp.float32),
            jax.ShapeDtypeStruct((count, width), low),
            jax.ShapeDtypeStruct((1, width), jnp.float32),
        ),
        in_specs=[anywhere, anywhere, in_vmem] + [anywhere] * 3 + [in_vmem] * 3,
        out_specs=(anywhere,) * 4 + (in_vmem,) * 3,
        scratch_shapes=[
            pltpu.VMEM((count, width), jnp.float32),
            pltpu.VMEM((hidden_width, width), low),
            pltpu.VMEM((hidden_width, width), low),
            pltpu.VMEM((2, 2, count, width), low),
            pltpu.VMEM((2, 2, count, hidden_width), low),
            pltpu.VMEM((2, 3, 2, count, hidden_width), low),
            pltpu.VMEM((2, groups, count, width), low),
            pltpu.VMEM((ranks, 4, count, width), low),
            pltpu.VMEM((ranks, 2, count // 2, width), low),
            pltpu.VMEM((ranks, 2, count // 2, width), low),
            pltpu.VMEM((ranks, 2, count // 2, width), low),
            pltpu.VMEM((ranks - 1, count, width), low),
            pltpu.VMEM((ranks - 1, count, width), low),
            dma((2, 2)),
            dma((2,)),
            dma((2,)),
            dma((2, 3)),
            dma((9, ranks)),
            dma((9, ranks)),
            dma((10, ranks)),
            dma((10, ranks)),
            dma((ranks - 1,)),
            dma((ranks - 1,)),
        ],
        compiler_params=pltpu.CompilerParams(
            collective_id=2, has_side_effects=True, vmem_limit_bytes=60 * 1024 * 1024
        ),
        name="moe_pass",
    )(
        rows,
        back,
        gates,
        expert_gate,
        expert_up,
        shared_all,
        residual,
        cotangent,
        gain,
    )


def cube_copies(gathered, sends, recvs, by_core, by_x, by_y):
    half = gathered.shape[2] // 2
    first, last = pl.ds(0, half), pl.ds(half, half)
    at = gathered.at

    def copy(kind, j):
        src, dst, peer = {
            K_X: lambda: (at[0, j], at[2, j], by_x),
            K_Y: lambda: (at[0, j], at[3, j], by_y),
            K_CORE: lambda: (at[0, j], at[1, j], by_core),
            K_FAR_Y: lambda: (at[2, j, last], at[6, j, last], by_y),
            K_FAR_X: lambda: (at[3, j, first], at[6, j, first], by_x),
            K_CORE_X: lambda: (at[2, j], at[4, j], by_core),
            K_CORE_Y: lambda: (at[3, j], at[5, j], by_core),
            K_CORE_FAR: lambda: (at[6, j], at[7, j], by_core),
        }[kind]()
        return remote(src, dst, sends.at[kind, j], recvs.at[kind, j], peer)

    return copy


def swap_halves(values):
    lane = lax.broadcasted_iota(jnp.int32, values.shape, 1)
    middle = ROPE // 2
    lanes = values.shape[1]
    ahead, behind = pltpu.roll(values, lanes - middle, 1), pltpu.roll(values, middle, 1)
    return jnp.where((lane // middle) % 2 == 0, ahead, behind)


def turn(values, cos_table, sin_table):
    return values * cos_table + swap_halves(values) * sin_table


def front_kernel(
    lengths,
    hidden,
    cotangent,
    query,
    expand,
    output,
    shared,
    expert_down,
    routes,
    route_gates,
    latent_rows,
    attn_gain,
    latent_gain,
    mlp_gain,
    frequency,
    normed_out,
    latent_out,
    own_latent,
    query_out,
    expand_out,
    output_out,
    qcat_out,
    kcat_out,
    value_out,
    prob_out,
    attended_out,
    cos_out,
    sin_out,
    residual_out,
    normed_two,
    shared_all,
    gates_all,
    cotan_all,
    back_all,
    hidden_all,
    query_all,
    expand_all,
    output_all,
    down_rows,
    normed,
    latent_low,
    q_cat,
    k_cat,
    value,
    mask,
    prob,
    attended,
    gate_abs,
    gate_rel,
    gate_send,
    row_buf,
    back_buf,
    ring_out,
    ring_buf,
    local_sem,
    prob_sem,
    row_sem,
    back_sem,
    ring_send,
    ring_recv,
    w_send,
    w_recv,
    deal_send,
    deal_recv,
    gates_send,
    gates_recv,
    cring_send,
    cring_recv,
    c_send,
    c_recv,
    sum_send,
    sum_recv,
):
    me, rank = lax.axis_index(DP), lax.axis_index(TENSOR)
    ranks, count = lax.axis_size(TENSOR), lax.axis_size(DP)
    right = (me, lax.rem(rank + 1, ranks))
    left = (me, lax.rem(rank + ranks - 1, ranks))
    by_core, by_x, by_y = [(flip(me, bit), rank) for bit in (1, 2, 4)]
    partners = []
    for k in range(1, count):
        other = me
        for bit in (1, 2, 4):
            other = flip(other, bit) if k & bit else other
        partners.append((k, (other, rank)))
    rows, width = hidden.shape
    group_rows = rows * ranks
    heads = q_cat.shape[0]
    local_experts = gate_abs.shape[0] // count
    q_rows, e_rows, o_cols = query.shape[0], expand.shape[0], output.shape[1]
    routed_width = expert_down.shape[0]
    shared_pad = shared.shape[2]
    piece = shared.shape[3]

    def query_at(owner, half=None):
        size = q_rows if half is None else q_rows // 2
        start = owner * q_rows + (0 if half is None else half * size)
        return query_all.at[pl.ds(pl.multiple_of(start, size), size)]

    def expand_at(owner, half=None):
        size = e_rows if half is None else e_rows // 2
        start = owner * e_rows + (0 if half is None else half * size)
        return expand_all.at[pl.ds(pl.multiple_of(start, size), size)]

    def output_at(owner, half=None):
        size = output.shape[0] if half is None else output.shape[0] // 2
        start = 0 if half is None else half * size
        return output_all.at[
            pl.ds(start, size), pl.ds(pl.multiple_of(owner * o_cols, o_cols), o_cols)
        ]

    greet([peer for _, peer in partners] + [right, left])

    ring = {}

    def ring_step(step):
        src = hidden if step == 0 else hidden_all.at[step]
        ring[step] = remote(
            src, hidden_all.at[step + 1], ring_send.at[step], ring_recv.at[step], right
        )
        ring[step].start()

    weights = ((query, query_at), (expand, expand_at), (output, output_at))
    copies = {}

    def send(i, kind, src, dst, peer):
        copies[i, kind] = remote(src, dst, w_send.at[i, kind], w_recv.at[i, kind], peer)
        copies[i, kind].start()

    def weight_first(i):
        own, at = weights[i]
        send(i, 0, own, at(me), by_x)
        send(i, 1, own, at(me), by_y)
        send(i, 2, own, at(me), by_core)

    def weight_forward(i):
        _, at = weights[i]
        copies[i, 0].wait_recv()
        send(i, 3, at(flip(me, 2), 1), at(flip(me, 2), 1), by_y)
        send(i, 4, at(flip(me, 2)), at(flip(me, 2)), by_core)
        copies[i, 1].wait_recv()
        send(i, 5, at(flip(me, 4), 0), at(flip(me, 4), 0), by_x)
        send(i, 6, at(flip(me, 4)), at(flip(me, 4)), by_core)

    def weight_far(i):
        _, at = weights[i]
        far = flip(flip(me, 2), 4)
        copies[i, 3].wait_recv()
        copies[i, 5].wait_recv()
        send(i, 7, at(far), at(far), by_core)

    def weight_last(i):
        for kind in (2, 4, 6, 7):
            copies[i, kind].wait_recv()

    cube = cube_copies(cotan_all, c_send, c_recv, by_core, by_x, by_y)

    def cotan_ring(j):
        src = cotan_all.at[0, j - 1]
        return remote(src, cotan_all.at[0, j], cring_send.at[j - 1], cring_recv.at[j - 1], right)

    def cotan_send(j):
        for kind in (K_X, K_Y, K_CORE):
            cube(kind, j).start()

    def cotan_forward(j):
        cube(K_X, j).wait_recv()
        cube(K_FAR_Y, j).start()
        cube(K_CORE_X, j).start()
        cube(K_Y, j).wait_recv()
        cube(K_FAR_X, j).start()
        cube(K_CORE_Y, j).start()

    def cotan_far(j):
        cube(K_FAR_X, j).wait_recv()
        cube(K_FAR_Y, j).wait_recv()
        cube(K_CORE_FAR, j).start()

    def cotan_next(j):
        cotan_ring(j).wait_recv()
        if j + 1 < ranks:
            cotan_ring(j + 1).start()
        cotan_send(j)

    def down_back(j, begin=0, end=4):
        needs = ((K_CORE,), (), (K_CORE_X, K_CORE_Y), (K_CORE_FAR,))
        for p in range(begin, end):
            for kind in needs[p]:
                cube(kind, j).wait_recv()

        def load(p, parity):
            return pltpu.make_async_copy(
                cotan_all.at[pl.ds(2 * p, 2), j], row_buf.at[parity], row_sem.at[parity]
            )

        def store(p, parity):
            return pltpu.make_async_copy(
                back_buf.at[parity], back_all.at[pl.ds(2 * p, 2), j], back_sem.at[parity]
            )

        load(begin, begin % 2).start()

        def one(p, carry):
            parity = lax.rem(p, 2)
            load(p, parity).wait()

            @pl.when(p + 1 < end)
            def _():
                load(p + 1, 1 - parity).start()

            @pl.when(p > begin + 1)
            def _():
                store(p - 2, parity).wait()

            wide = row_buf[parity].reshape(2 * rows, width)
            back = bfloat(last_dot(wide, down_rows[...]))
            back_buf[parity] = back.reshape(2, rows, back.shape[1])
            store(p, parity).start()
            return carry

        lax.fori_loop(begin, end, one, 0)
        for p in range(max(begin, end - 2), end):
            store(p, p % 2).wait()

    ring_step(0)
    weight_first(0)
    weight_first(1)
    dealt = []
    for n, (k, peer) in enumerate(partners):
        copy = remote(
            shared.at[peer[0]],
            shared_all.at[:, :, pl.ds(pl.multiple_of(me * piece, piece), piece)],
            deal_send.at[n],
            deal_recv.at[n],
            peer,
        )
        dealt.append(copy)
    local = [
        pltpu.make_async_copy(hidden, hidden_all.at[0], local_sem.at[0]),
        pltpu.make_async_copy(query, query_at(me), local_sem.at[1]),
        pltpu.make_async_copy(expand, expand_at(me), local_sem.at[2]),
        pltpu.make_async_copy(output, output_at(me), local_sem.at[3]),
        pltpu.make_async_copy(
            shared.at[me],
            shared_all.at[:, :, pl.ds(pl.multiple_of(me * piece, piece), piece)],
            local_sem.at[4],
        ),
        pltpu.make_async_copy(cotangent, cotan_all.at[0, 0], local_sem.at[5]),
        pltpu.make_async_copy(expert_down, down_rows.at[pl.ds(0, routed_width)], local_sem.at[6]),
    ]
    for copy in local:
        copy.start()

    def absolute(index):
        block = index // rows
        return ((rank + ranks - block) % ranks) * rows + index % rows

    def starts_of(token):
        start, total = jnp.zeros_like(token), 0
        for n in range(lengths.shape[1]):
            total = total + lengths[0, n]
            start = jnp.where(token >= total, total, start)
        return start

    token = absolute(lax.broadcasted_iota(jnp.int32, (group_rows, cos_out.shape[1]), 0))
    angle = (token - starts_of(token)).astype(jnp.float32) * frequency[...]
    lane = lax.broadcasted_iota(jnp.int32, angle.shape, 1)
    cos_out[...] = jnp.cos(angle)
    sine = jnp.sin(angle)
    sin_out[...] = jnp.where((lane // (ROPE // 2)) % 2 == 0, -sine, sine)
    row_token = absolute(lax.broadcasted_iota(jnp.int32, mask.shape, 0))
    column_token = absolute(lax.broadcasted_iota(jnp.int32, mask.shape, 1))
    allowed = (column_token <= row_token) & (column_token >= starts_of(row_token))
    mask[...] = jnp.where(allowed, 0.0, -jnp.inf)

    expert = lax.broadcasted_iota(jnp.int32, gate_abs.shape, 0)
    dense = jnp.zeros(gate_abs.shape, jnp.float32)
    for k in range(routes.shape[0]):
        dense = dense + jnp.where(routes[k : k + 1, :] == expert, route_gates[k : k + 1, :], 0.0)
    gate_abs[...] = dense
    for r in range(ranks):
        start = pl.multiple_of(((rank + ranks - r) % ranks) * rows, rows)
        gate_rel[:, r * rows : (r + 1) * rows] = gate_abs[:, pl.ds(start, rows)]
    gate_send[...] = jnp.zeros_like(gate_send)
    for p in range(count):
        gate_send[p, 0:local_experts] = gate_rel[p * local_experts : (p + 1) * local_experts]
    down_rows[routed_width + shared_pad :] = jnp.zeros(
        (down_rows.shape[0] - routed_width - shared_pad, width), jnp.bfloat16
    )
    gate_copies = []
    for n, (k, peer) in enumerate(partners):
        gate_copies.append(
            remote(
                gate_send.at[peer[0]],
                gates_all.at[SLOTS.index(k)],
                gates_send.at[n],
                gates_recv.at[n],
                peer,
            )
        )
    own_gates = pltpu.make_async_copy(gate_send.at[me], gates_all.at[0], local_sem.at[7])
    own_gates.start()

    def norm_piece(r):
        at = pl.ds(r * rows, rows)
        values = hidden_all[r].astype(jnp.float32)
        scale = lax.rsqrt(jnp.mean(values * values, axis=-1, keepdims=True) + epsilon)
        normed[at, :] = bfloat(values * scale * attn_gain[...])

    def project_piece(r):
        at = pl.ds(r * rows, rows)
        values = normed[at, :]
        cos_table, sin_table = cos_out[at, :], sin_out[at, :]
        lanes = cos_table.shape[1]
        raw = plain_dot(values, query_all[...])
        for h in range(heads):
            q_cat[h, at, 0:NOPE] = bfloat(raw[:, h * NOPE : (h + 1) * NOPE])
        for pair in range(heads // 2):
            start = heads * NOPE + pair * lanes
            turned = bfloat(turn(raw[:, start : start + lanes], cos_table, sin_table))
            q_cat[2 * pair, at, NOPE : NOPE + lanes] = turned
            q_cat[2 * pair + 1, at, NOPE : NOPE + lanes] = turned
        latent = last_dot(values, latent_rows[...])
        part = latent[:, :LATENT]
        if r == 0:
            own_latent[...] = part
        scale = lax.rsqrt(jnp.mean(part * part, axis=-1, keepdims=True) + epsilon)
        low_part = bfloat(part * scale * latent_gain[...])
        latent_low[at, :] = low_part
        turned = turn(latent[:, LATENT:], cos_table, sin_table)
        lane = lax.broadcasted_iota(jnp.int32, turned.shape, 1)
        even = bfloat(jnp.where(lane < ROPE, turned, 0.0))
        odd = bfloat(jnp.where(lane < ROPE, 0.0, turned))
        expanded = plain_dot(low_part, expand_all[...])
        step = NOPE + VDIM
        for h in range(heads):
            k_cat[h, at, 0:NOPE] = bfloat(expanded[:, h * step : h * step + NOPE])
            k_cat[h, at, NOPE : NOPE + lanes] = even if h % 2 == 0 else odd
            value[h, at, :] = bfloat(expanded[:, h * step + NOPE : (h + 1) * step])

    def prob_store(h, parity):
        return pltpu.make_async_copy(prob.at[parity], prob_out.at[h], prob_sem.at[parity])

    def head(h):
        parity = h % 2
        if h >= 2:
            prob_store(h - 2, parity).wait()
        scores = last_dot(q_cat[h], k_cat[h]) * (NOPE + ROPE) ** (-0.5) + mask[...]
        exp_scores = jnp.exp(scores - jnp.max(scores, axis=-1, keepdims=True))
        ratio = exp_scores / jnp.sum(exp_scores, axis=-1, keepdims=True)
        prob[parity] = ratio
        prob_store(h, parity).start()
        attended[:, h * VDIM : (h + 1) * VDIM] = bfloat(plain_dot(bfloat(ratio), value[h]))

    norm_piece_wait = [local[0].wait] + [lambda s=s: ring[s].wait_recv() for s in range(ranks - 1)]
    norm_piece_wait[0]()
    norm_piece(0)
    weight_first(2)
    weight_forward(0)
    norm_piece_wait[1]()
    ring_step(1)
    weight_forward(1)
    norm_piece(1)
    weight_far(0)
    weight_far(1)
    local[5].wait()
    cotan_send(0)
    norm_piece_wait[2]()
    ring_step(2)
    cotan_ring(1).start()
    norm_piece(2)
    weight_forward(2)
    weight_last(0)
    weight_last(1)
    local[1].wait()
    local[2].wait()
    project_piece(0)
    project_piece(1)
    weight_far(2)
    project_piece(2)
    norm_piece_wait[3]()
    norm_piece(3)
    cotan_forward(0)
    for copy in gate_copies:
        copy.start()
    for copy in dealt:
        copy.start()
    project_piece(3)
    cotan_next(1)
    for h in range(heads):
        head(h)
    weight_last(2)
    local[3].wait()

    def attn_block(r):
        return plain_dot(attended[r * rows : (r + 1) * rows, :], output_all[...])

    def sum_step(step):
        return remote(
            ring_out.at[step], ring_buf.at[step], sum_send.at[step], sum_recv.at[step], right
        )

    ring_out[0] = bfloat(attn_block(1))
    sum_step(0).start()
    cotan_far(0)
    for copy in dealt:
        copy.wait_recv()
    local[4].wait()
    local[6].wait()
    shared_down = pltpu.make_async_copy(
        shared_all.at[2], down_rows.at[pl.ds(routed_width, shared_pad)], local_sem.at[8]
    )
    shared_down.start()
    shared_down.wait()
    down_back(0)
    cotan_next(2)
    sum_step(0).wait_recv()
    ring_out[1] = bfloat(attn_block(2) + ring_buf[0].astype(jnp.float32))
    sum_step(1).start()
    outs = [
        pltpu.make_async_copy(src, dst, local_sem.at[9 + n])
        for n, (src, dst) in enumerate(
            (
                (normed, normed_out),
                (latent_low, latent_out),
                (query_all, query_out),
                (expand_all, expand_out),
                (output_all, output_out),
                (q_cat, qcat_out),
                (k_cat, kcat_out),
                (value, value_out),
                (attended, attended_out),
            )
        )
    ]
    for copy in outs:
        copy.start()
    cotan_forward(1)
    cotan_far(1)
    cotan_next(3)
    sum_step(1).wait_recv()
    ring_out[2] = bfloat(attn_block(3) + ring_buf[1].astype(jnp.float32))
    sum_step(2).start()
    down_back(1)
    cotan_forward(2)
    cotan_far(2)
    cotan_forward(3)
    sum_step(2).wait_recv()
    residual = (
        hidden_all[0].astype(jnp.float32) + attn_block(0) + ring_buf[2].astype(jnp.float32)
    )
    residual_out[...] = residual
    scale = lax.rsqrt(jnp.mean(residual * residual, axis=-1, keepdims=True) + epsilon)
    normed_two[...] = bfloat(residual * scale * mlp_gain[...])
    down_back(2)
    cotan_far(3)
    down_back(3, 0, 3)
    down_back(3, 3, 4)

    for h in (heads - 2, heads - 1):
        prob_store(h, h % 2).wait()
    for copy in outs:
        copy.wait()
    own_gates.wait()
    for copy in gate_copies:
        copy.wait()
    for copy in dealt:
        copy.wait_send()
    for i in range(len(weights)):
        for kind in range(8):
            copies[i, kind].wait_send()
    for step in range(ranks - 1):
        ring[step].wait_send()
        cotan_ring(step + 1).wait_send()
        sum_step(step).wait_send()
    for j in range(ranks):
        for kind in (
            K_X,
            K_Y,
            K_CORE,
            K_FAR_Y,
            K_FAR_X,
            K_CORE_X,
            K_CORE_Y,
            K_CORE_FAR,
        ):
            cube(kind, j).wait_send()


def front_pass(
    lengths,
    hidden,
    cotangent,
    query,
    expand,
    output,
    shared,
    expert_down,
    routes,
    route_gates,
    latent_rows,
    attn_gain,
    latent_gain,
    mlp_gain,
    hidden_width,
    experts,
):
    count, ranks = lax.axis_size(DP), lax.axis_size(TENSOR)
    rows, width = hidden.shape
    group_rows = rows * ranks
    heads = query.shape[1] // (NOPE + ROPE)
    lanes = 2 * ROPE
    low, full = jnp.bfloat16, jnp.float32
    frequency = rope_base ** (-jnp.arange(ROPE // 2, dtype=full) * 2.0 / ROPE)
    frequency = jnp.tile(frequency, lanes // (ROPE // 2))[None, :]
    anywhere = pl.BlockSpec(memory_space=pl.ANY)
    in_vmem = pl.BlockSpec(memory_space=pltpu.VMEM)
    dma = pltpu.SemaphoreType.DMA
    by_slot = (count, ranks, rows)

    def array(*shape, dtype=low):
        return jax.ShapeDtypeStruct(shape, dtype)

    def full_query():
        return (count * query.shape[0], query.shape[1])

    def full_expand():
        return (count * expand.shape[0], expand.shape[1])

    def full_output():
        return (output.shape[0], count * output.shape[1])

    return pl.pallas_call(
        front_kernel,
        out_shape=(
            array(group_rows, width),
            array(group_rows, LATENT),
            array(rows, LATENT, dtype=full),
            array(*full_query()),
            array(*full_expand()),
            array(*full_output()),
            array(heads, group_rows, NOPE + lanes),
            array(heads, group_rows, NOPE + lanes),
            array(heads, group_rows, VDIM),
            array(heads, group_rows, group_rows, dtype=full),
            array(group_rows, heads * VDIM),
            array(group_rows, lanes, dtype=full),
            array(group_rows, lanes, dtype=full),
            array(rows, width, dtype=full),
            array(rows, width),
            array(*shared.shape[1:3], count * shared.shape[3]),
            array(count, 8, group_rows, dtype=full),
            array(*by_slot, width),
            array(*by_slot, hidden_width),
        ),
        in_specs=[pl.BlockSpec(memory_space=pltpu.SMEM)] + [anywhere] * 7 + [in_vmem] * 7,
        out_specs=(anywhere, anywhere, in_vmem)
        + (anywhere,) * 8
        + (in_vmem,) * 4
        + (anywhere,) * 4,
        scratch_shapes=[
            pltpu.VMEM((ranks, rows, width), low),
            pltpu.VMEM(full_query(), low),
            pltpu.VMEM(full_expand(), low),
            pltpu.VMEM(full_output(), low),
            pltpu.VMEM((hidden_width, width), low),
            pltpu.VMEM((group_rows, width), low),
            pltpu.VMEM((group_rows, LATENT), low),
            pltpu.VMEM((heads, group_rows, NOPE + lanes), low),
            pltpu.VMEM((heads, group_rows, NOPE + lanes), low),
            pltpu.VMEM((heads, group_rows, VDIM), low),
            pltpu.VMEM((group_rows, group_rows), full),
            pltpu.VMEM((2, group_rows, group_rows), full),
            pltpu.VMEM((group_rows, heads * VDIM), low),
            pltpu.VMEM((experts, group_rows), full),
            pltpu.VMEM((experts, group_rows), full),
            pltpu.VMEM((count, 8, group_rows), full),
            pltpu.VMEM((2, 2, rows, width), low),
            pltpu.VMEM((2, 2, rows, hidden_width), low),
            pltpu.VMEM((ranks - 1, rows, width), low),
            pltpu.VMEM((ranks - 1, rows, width), low),
            dma((18,)),
            dma((2,)),
            dma((2,)),
            dma((2,)),
            dma((ranks - 1,)),
            dma((ranks - 1,)),
            dma((3, 8)),
            dma((3, 8)),
            dma((count - 1,)),
            dma((count - 1,)),
            dma((count - 1,)),
            dma((count - 1,)),
            dma((ranks - 1,)),
            dma((ranks - 1,)),
            dma((9, ranks)),
            dma((9, ranks)),
            dma((ranks - 1,)),
            dma((ranks - 1,)),
        ],
        compiler_params=pltpu.CompilerParams(
            collective_id=1, has_side_effects=True, vmem_limit_bytes=60 * 1024 * 1024
        ),
        name="front_pass",
    )(
        lengths,
        hidden,
        cotangent,
        query,
        expand,
        output,
        shared,
        expert_down,
        routes,
        route_gates,
        latent_rows,
        attn_gain,
        latent_gain,
        mlp_gain,
        frequency,
    )


def back_kernel(
    resid,
    acts,
    expert_down,
    shared_all,
    output,
    query,
    expand,
    q_cat,
    k_cat,
    value,
    prob_all,
    cos_table,
    sin_table,
    gate_all,
    up_all,
    row_all,
    resid_all,
    moe_sums,
    gate_out,
    up_out,
    shared_rows,
    normed_back,
    latent_back,
    query_grad,
    expand_grad,
    down_rows,
    act_buf,
    resid_buf,
    attended_grad,
    prob,
    pair,
    key_rot,
    blocks,
    core_buf,
    far_buf,
    x_buf,
    y_buf,
    ring_out,
    ring_buf,
    left_buf,
    right_buf,
    acc,
    local_sem,
    act_sem,
    prob_sem,
    sums_sem,
    load_sem,
    acc_sem,
    resid_send,
    resid_recv,
    s_send,
    s_recv,
    ring_send,
    ring_recv,
):
    me, rank = lax.axis_index(DP), lax.axis_index(TENSOR)
    ranks = lax.axis_size(TENSOR)
    right = (me, lax.rem(rank + 1, ranks))
    left = (me, lax.rem(rank + ranks - 1, ranks))
    by_core, by_x, by_y = [(flip(me, bit), rank) for bit in (1, 2, 4)]
    rows, width = resid.shape
    half = rows // 2
    first, last = pl.ds(0, half), pl.ds(half, half)
    heads = q_cat.shape[0]
    lanes = cos_table.shape[1]
    routed_width, shared_pad = expert_down.shape[0], shared_all.shape[1]
    scaling = (NOPE + ROPE) ** (-0.5)
    greet([by_core, by_x, by_y, right, left])

    local = [
        pltpu.make_async_copy(resid, resid_buf.at[0], local_sem.at[0]),
        pltpu.make_async_copy(expert_down, down_rows.at[pl.ds(0, routed_width)], local_sem.at[1]),
        pltpu.make_async_copy(
            shared_all.at[2], down_rows.at[pl.ds(routed_width, shared_pad)], local_sem.at[2]
        ),
    ]

    def resid_step(step):
        src = resid if step == 0 else resid_buf.at[step]
        return remote(
            src, resid_buf.at[step + 1], resid_send.at[step], resid_recv.at[step], right
        )

    resid_step(0).start()
    for copy in local:
        copy.start()
    down_rows[routed_width + shared_pad :] = jnp.zeros(
        (down_rows.shape[0] - routed_width - shared_pad, width), jnp.bfloat16
    )
    key_rot[...] = jnp.zeros_like(key_rot)

    copy_of = sum_copies(
        blocks, core_buf, far_buf, x_buf, y_buf, s_send, s_recv, by_core, by_x, by_y
    )

    def act_load(j, p, parity):
        return pltpu.make_async_copy(
            acts.at[pl.ds(2 * p, 2), j], act_buf.at[parity], act_sem.at[parity]
        )

    def outputs(j):
        if j == 0:
            act_load(0, 0, 0).start()

        def one(p, carry):
            parity = lax.rem(p, 2)
            act_load(j, p, parity).wait()

            @pl.when(p < 3)
            def _():
                act_load(j, p + 1, 1 - parity).start()

            if j + 1 < ranks:

                @pl.when(p == 3)
                def _():
                    act_load(j + 1, 0, 0).start()

            wide = act_buf[parity].reshape(2 * rows, act_buf.shape[3])
            out = plain_dot(wide, down_rows[...])
            blocks[j % 2, pl.ds(2 * p, 2)] = bfloat(out).reshape(2, rows, width)
            return carry

        lax.fori_loop(0, 4, one, 0)
        for kind in (K_CORE_FAR, K_CORE_X, K_CORE_Y, K_CORE_OWN):
            copy_of(kind, j).start()

    def sums_first(j):
        at = blocks.at[j % 2].at
        copy_of(K_CORE_FAR, j).wait_recv()
        add_rows(at[6], rows, core_buf.at[j, 3])
        copy_of(K_FAR_X, j).start()
        copy_of(K_FAR_Y, j).start()
        copy_of(K_CORE_X, j).wait_recv()
        add_rows(at[2, first], half, core_buf.at[j, 1, first])
        copy_of(K_X_FIRST, j).start()
        copy_of(K_CORE_Y, j).wait_recv()
        add_rows(at[3, last], half, core_buf.at[j, 2, last])
        copy_of(K_Y_LAST, j).start()

    def sums_next(j):
        at = blocks.at[j % 2].at
        copy_of(K_FAR_X, j).wait_recv()
        add_rows(at[3, first], half, core_buf.at[j, 2, first], far_buf.at[j, 0])
        copy_of(K_Y_FIRST, j).start()
        copy_of(K_FAR_Y, j).wait_recv()
        add_rows(at[2, last], half, core_buf.at[j, 1, last], far_buf.at[j, 1])
        copy_of(K_X_LAST, j).start()

    def sums_store(j):
        return pltpu.make_async_copy(
            blocks.at[j % 2, 0], moe_sums.at[j], sums_sem.at[j % 2]
        )

    def sums_last(j):
        at = blocks.at[j % 2].at
        for kind in (K_CORE_OWN, K_X_FIRST, K_X_LAST, K_Y_FIRST, K_Y_LAST):
            copy_of(kind, j).wait_recv()
        for n, part in enumerate((first, last)):
            add_rows(at[0, part], half, core_buf.at[j, 0, part], x_buf.at[j, n], y_buf.at[j, n])
        sums_store(j).start()
        for kind in SUM_KINDS:
            copy_of(kind, j).wait_send()
        sums_store(j).wait()

    chunk, columns = right_buf.shape[1:]
    chunks, parts = row_all.shape[0] // chunk, width // columns
    kinds = ((gate_all, gate_out), (up_all, up_out))

    def chunk_loads(w, unit, parity):
        at = pl.ds(pl.multiple_of(lax.rem(unit, chunks) * chunk, chunk), chunk)
        part = pl.ds(pl.multiple_of(lax.div(unit, chunks) * columns, columns), columns)
        return (
            pltpu.make_async_copy(kinds[w][0].at[at], left_buf.at[parity], load_sem.at[parity, 0]),
            pltpu.make_async_copy(
                row_all.at[at, part], right_buf.at[parity], load_sem.at[parity, 1]
            ),
        )

    def acc_store(w, unit):
        part = pl.ds(pl.multiple_of(lax.div(unit, chunks) * columns, columns), columns)
        return (
            pltpu.make_async_copy(
                acc.at[pl.ds(0, routed_width)], kinds[w][1].at[:, part], acc_sem.at[0]
            ),
            pltpu.make_async_copy(
                acc.at[pl.ds(routed_width, shared_pad)], shared_rows.at[w, :, part], acc_sem.at[1]
            ),
        )

    units = chunks * parts

    def products(w, begin, end):
        def one(unit, carry):
            parity = lax.rem(unit, 2)

            @pl.when(unit + 1 < units)
            def _():
                for copy in chunk_loads(w, unit + 1, 1 - parity):
                    copy.start()

            if w + 1 < len(kinds):

                @pl.when(unit + 1 == units)
                def _():
                    for copy in chunk_loads(w + 1, 0, 0):
                        copy.start()

            for copy in chunk_loads(w, unit, parity):
                copy.wait()
            part = first_dot(left_buf[parity], right_buf[parity])
            place = lax.rem(unit, chunks)

            @pl.when(place == 0)
            def _():
                acc[...] = part

            @pl.when(place > 0)
            def _():
                acc[...] += part

            @pl.when(place == chunks - 1)
            def _():
                for copy in acc_store(w, unit):
                    copy.start()
                for copy in acc_store(w, unit):
                    copy.wait()

            return carry

        lax.fori_loop(begin, end, one, 0)

    def attended_piece(r):
        attended_grad[r * rows : (r + 1) * rows, :] = bfloat(
            last_dot(resid_buf[r], output[...])
        )

    def prob_load(h):
        return pltpu.make_async_copy(prob_all.at[h], prob.at[h % 2], prob_sem.at[h % 2])

    def head(h):
        prob_load(h).wait()
        ratio = prob[h % 2]
        back = attended_grad[:, h * VDIM : (h + 1) * VDIM]
        prob_back = last_dot(back, value[h])
        row_dot = jnp.sum(prob_back * ratio, axis=-1, keepdims=True)
        score_back = bfloat(ratio * (prob_back - row_dot))
        value_back = first_dot(bfloat(ratio), back)
        query_back = bfloat(plain_dot(score_back, k_cat[h]) * scaling)
        key_back = bfloat(first_dot(score_back, q_cat[h]) * scaling)
        step = NOPE + VDIM
        expand_grad[:, h * step : h * step + NOPE] = key_back[:, :NOPE]
        expand_grad[:, h * step + NOPE : (h + 1) * step] = bfloat(value_back)
        query_grad[:, h * NOPE : (h + 1) * NOPE] = query_back[:, :NOPE]
        turned = key_back[:, NOPE:].astype(jnp.float32)
        lane = lax.broadcasted_iota(jnp.int32, turned.shape, 1)
        own = (lane < ROPE) if h % 2 == 0 else (lane >= ROPE)
        key_rot[...] += jnp.where(own, turned, 0.0)
        rope_part = query_back[:, NOPE:].astype(jnp.float32)
        if h % 2 == 0:
            pair[...] = rope_part
        else:
            whole = pair[...] + rope_part
            start = heads * NOPE + h // 2 * lanes
            query_grad[:, start : start + lanes] = bfloat(
                turn(whole, cos_table[...], -sin_table[...])
            )
        if h + 2 < heads:
            prob_load(h + 2).start()

    prob_load(0).start()
    prob_load(1).start()
    for copy in chunk_loads(0, 0, 0):
        copy.start()
    for copy in local[1:]:
        copy.wait()
    outputs(0)
    local[0].wait()
    attended_piece(0)
    sums_first(0)
    resid_step(0).wait_recv()
    resid_step(1).start()
    attended_piece(1)
    outputs(1)
    sums_next(0)
    sums_first(1)
    products(0, 0, 3)
    resid_step(1).wait_recv()
    resid_step(2).start()
    attended_piece(2)
    sums_last(0)
    outputs(2)
    sums_next(1)
    sums_first(2)
    products(0, 3, 5)
    resid_step(2).wait_recv()
    save = pltpu.make_async_copy(resid_buf, resid_all, local_sem.at[3])
    save.start()
    attended_piece(3)
    for h in range(heads):
        head(h)

    folded = key_rot[...] + pltpu.roll(key_rot[...], ROPE, 1)
    key_rot[...] = folded

    def partial(r):
        at = slice(r * rows, (r + 1) * rows)
        latent = last_dot(expand_grad[at, :], expand[...])
        normed = last_dot(query_grad[at, :], query[...])
        return normed, latent, key_rot[at, :]

    splits = ((0, width), (width, width + LATENT), (width + LATENT, width + LATENT + lanes))

    def ring_step(step):
        return remote(
            ring_out.at[step], ring_buf.at[step], ring_send.at[step], ring_recv.at[step], right
        )

    def between_0():
        sums_last(1)
        outputs(3)
        sums_next(2)
        sums_first(3)
        products(0, 5, 8)

    def between_1():
        sums_last(2)
        sums_next(3)
        products(0, 8, 16)

    def between_2():
        sums_last(3)
        products(1, 0, 8)

    for step, between in enumerate((between_0, between_1, between_2)):
        values = partial(step + 1)
        if step:
            ring_step(step - 1).wait_recv()
        for (start, stop), part in zip(splits, values):
            if step:
                part = part + ring_buf[step - 1, :, start:stop].astype(jnp.float32)
            ring_out[step, :, start:stop] = bfloat(part)
        ring_step(step).start()
        between()
    parts = partial(0)
    ring_step(ranks - 2).wait_recv()
    normed_back[...] = parts[0] + ring_buf[ranks - 2, :, :width].astype(jnp.float32)
    latent_back[:, :LATENT] = parts[1] + ring_buf[
        ranks - 2, :, width : width + LATENT
    ].astype(jnp.float32)
    latent_back[:, LATENT:] = parts[2] + ring_buf[ranks - 2, :, width + LATENT :].astype(
        jnp.float32
    )
    products(1, 8, 16)
    save.wait()
    for step in range(ranks - 1):
        resid_step(step).wait_send()
        ring_step(step).wait_send()


def back_pass(
    resid,
    acts,
    expert_down,
    shared_all,
    output,
    query,
    expand,
    q_cat,
    k_cat,
    value,
    prob_all,
    cos_table,
    sin_table,
    gate_all,
    up_all,
    row_all,
):
    ranks, groups = lax.axis_size(TENSOR), lax.axis_size(DP)
    rows, width = resid.shape
    group_rows = rows * ranks
    heads = q_cat.shape[0]
    lanes = cos_table.shape[1]
    hidden_width = acts.shape[-1]
    low, full = jnp.bfloat16, jnp.float32
    anywhere = pl.BlockSpec(memory_space=pl.ANY)
    in_vmem = pl.BlockSpec(memory_space=pltpu.VMEM)
    dma = pltpu.SemaphoreType.DMA

    def array(*shape, dtype=low):
        return jax.ShapeDtypeStruct(shape, dtype)

    return pl.pallas_call(
        back_kernel,
        out_shape=(
            array(ranks, rows, width),
            array(ranks, rows, width),
            array(expert_down.shape[0], width, dtype=full),
            array(expert_down.shape[0], width, dtype=full),
            array(2, shared_all.shape[1], width, dtype=full),
            array(rows, width, dtype=full),
            array(rows, LATENT + lanes, dtype=full),
            array(group_rows, query.shape[1]),
            array(group_rows, expand.shape[1]),
        ),
        in_specs=[anywhere] * 4 + [in_vmem] * 6 + [anywhere] + [in_vmem] * 2 + [anywhere] * 3,
        out_specs=(anywhere,) * 5 + (in_vmem,) * 4,
        scratch_shapes=[
            pltpu.VMEM((hidden_width, width), low),
            pltpu.VMEM((2, 2, rows, hidden_width), low),
            pltpu.VMEM((ranks, rows, width), low),
            pltpu.VMEM((group_rows, heads * VDIM), low),
            pltpu.VMEM((2, group_rows, group_rows), full),
            pltpu.VMEM((group_rows, lanes), full),
            pltpu.VMEM((group_rows, lanes), full),
            pltpu.VMEM((2, groups, rows, width), low),
            pltpu.VMEM((ranks, 4, rows, width), low),
            pltpu.VMEM((ranks, 2, rows // 2, width), low),
            pltpu.VMEM((ranks, 2, rows // 2, width), low),
            pltpu.VMEM((ranks, 2, rows // 2, width), low),
            pltpu.VMEM((ranks - 1, rows, width + LATENT + lanes), low),
            pltpu.VMEM((ranks - 1, rows, width + LATENT + lanes), low),
            pltpu.VMEM((2, 512, hidden_width), low),
            pltpu.VMEM((2, 512, width // 2), low),
            pltpu.VMEM((hidden_width, width // 2), full),
            dma((4,)),
            dma((2,)),
            dma((2,)),
            dma((2,)),
            dma((2, 2)),
            dma((2,)),
            dma((ranks - 1,)),
            dma((ranks - 1,)),
            dma((10, ranks)),
            dma((10, ranks)),
            dma((ranks - 1,)),
            dma((ranks - 1,)),
        ],
        compiler_params=pltpu.CompilerParams(
            collective_id=3, has_side_effects=True, vmem_limit_bytes=63 * 1024 * 1024
        ),
        name="back_pass",
    )(
        resid,
        acts,
        expert_down,
        shared_all,
        output,
        query,
        expand,
        q_cat,
        k_cat,
        value,
        prob_all,
        cos_table,
        sin_table,
        gate_all,
        up_all,
        row_all,
    )


def weight_kernel(
    normed_in,
    latent_group_in,
    attended_in,
    resid_in,
    query_grad_in,
    expand_grad_in,
    normed_back,
    latent_back,
    own_latent,
    hidden_in,
    resid_grad_in,
    residual_in,
    cos_table,
    sin_table,
    attn_gain,
    latent_gain,
    mlp_grad,
    latent_columns_in,
    moe_sums,
    shared_rows,
    act_all,
    cotan_all,
    layer_out,
    hidden_grad,
    query_out,
    expand_out,
    output_out,
    gains_out,
    latent_all,
    shared_gate_out,
    shared_up_out,
    shared_down_out,
    down_out,
    query_full,
    expand_full,
    output_full,
    core_q,
    core_e,
    core_o,
    far_q,
    far_e,
    far_o,
    x_q,
    x_e,
    x_o,
    y_q,
    y_e,
    y_o,
    gains,
    latent_own,
    latent_rows,
    latent_full,
    latent_buf,
    latent_piece,
    gains_buf,
    gains_sum,
    gains_rank,
    act_buf,
    cotan_buf,
    acc,
    shared_full,
    shared_low,
    shared_back,
    moe_first,
    moe_out,
    moe_in,
    normed,
    attended,
    resid,
    query_grad,
    expand_grad,
    latent_group,
    hidden,
    resid_grad,
    residual,
    latent_columns,
    stage_sem,
    load_sem,
    local_sem,
    out_sem,
    s_send,
    s_recv,
    lz_send,
    lz_recv,
    ld_send,
    ld_recv,
    lp_send,
    lp_recv,
    lc_send,
    lc_recv,
    gd_send,
    gd_recv,
    gz_send,
    gz_recv,
    h_send,
    h_recv,
    m_send,
    m_recv,
):
    me, rank = lax.axis_index(DP), lax.axis_index(TENSOR)
    ranks, count = lax.axis_size(TENSOR), lax.axis_size(DP)
    by_core, by_x, by_y = [(flip(me, bit), rank) for bit in (1, 2, 4)]

    def owner(k):
        other = me
        for bit in (1, 2, 4):
            other = flip(other, bit) if k & bit else other
        return other

    partners = [(owner(k), rank) for k in range(1, count)]
    beside = [(me, lax.rem(rank + r, ranks)) for r in range(1, ranks)]
    width = normed.shape[1]
    routed_width = down_out.shape[0]
    shared_pad = shared_low.shape[1]
    rows = hidden.shape[0]
    staged = {}
    for n, (key, src, dst) in enumerate(
        (
            (0, normed_in, normed),
            (1, query_grad_in, query_grad),
            (2, latent_columns_in, latent_columns),
            (2, hidden_in, hidden),
            (2, resid_grad_in, resid_grad),
            (3, attended_in, attended),
            (3, resid_in, resid),
            (4, latent_group_in, latent_group),
            (4, expand_grad_in, expand_grad),
            (5, residual_in, residual),
        )
    ):
        copy = pltpu.make_async_copy(src, dst, stage_sem.at[n])
        copy.start()
        staged.setdefault(key, []).append(copy)

    def ready(key):
        for copy in staged[key]:
            copy.wait()

    greet(partners + beside)

    def moe_step(step):
        src = moe_sums.at[1] if step == 0 else moe_out.at[step]
        return remote(src, moe_in.at[step], m_send.at[step], m_recv.at[step], beside[0])

    moe_loads = [
        pltpu.make_async_copy(moe_sums.at[0], moe_first, local_sem.at[4]),
        pltpu.make_async_copy(moe_sums.at[2], moe_out.at[1], local_sem.at[5]),
        pltpu.make_async_copy(moe_sums.at[3], moe_out.at[2], local_sem.at[6]),
    ]
    shared_load = pltpu.make_async_copy(shared_rows, shared_full, local_sem.at[7])
    for copy in moe_loads + [shared_load]:
        copy.start()

    def moe_next(step):
        moe_loads[step].wait()
        moe_step(step - 1).wait_recv()
        add_rows(moe_out.at[step], rows, moe_in.at[step - 1])
        moe_step(step).start()

    def moe_last():
        ready(5)
        moe_loads[0].wait()
        moe_step(ranks - 2).wait_recv()
        total = moe_first[...].astype(jnp.float32) + moe_in[ranks - 2].astype(jnp.float32)
        layer_out[...] = bfloat(residual[...] + total)

    values = own_latent[...]
    scale = lax.rsqrt(jnp.mean(values * values, axis=-1, keepdims=True) + epsilon)
    grad = latent_back[:, :LATENT]
    scaled_grad = grad * latent_gain[...]
    inner = jnp.mean(scaled_grad * values, axis=-1, keepdims=True)
    latent_in = scale * scaled_grad - values * (scale * scale * scale) * inner
    latent_own[:, :LATENT] = bfloat(latent_in)
    latent_own[:, LATENT:] = bfloat(
        turn(latent_back[:, LATENT:], cos_table[0:rows, :], -sin_table[0:rows, :])
    )
    gains[...] = jnp.zeros_like(gains)
    gains[2:3, :LATENT] = jnp.sum(grad * values * scale, axis=0, keepdims=True)
    gains[1:2, :] = mlp_grad[...]

    def first_norm():
        ready(2)
        lanes = latent_columns.shape[0]
        total = normed_back[...] + plain_dot(latent_own[:, :lanes], latent_columns[...])
        values = hidden[...].astype(jnp.float32)
        scale = lax.rsqrt(jnp.mean(values * values, axis=-1, keepdims=True) + epsilon)
        scaled_grad = total * attn_gain[...]
        inner = jnp.mean(scaled_grad * values, axis=-1, keepdims=True)
        through = scale * scaled_grad - values * (scale * scale * scale) * inner
        hidden_grad[...] = resid_grad[...] + through
        gains[0:1, :] = jnp.sum(total * values * scale, axis=0, keepdims=True)

    own_rows = pltpu.make_async_copy(latent_own, latent_rows.at[0], local_sem.at[0])
    own_rows.start()
    latent_sends = [
        remote(latent_own, latent_rows.at[r], lz_send.at[r - 1], lz_recv.at[r - 1], peer)
        for r, peer in enumerate(beside, 1)
    ]
    gains_sends = [
        remote(gains, gains_buf.at[me], gd_send.at[n], gd_recv.at[n], peer)
        for n, peer in enumerate(partners)
    ]
    for copy in latent_sends:
        copy.start()

    sets = (
        (query_full, core_q, far_q, x_q, y_q, query_out),
        (expand_full, core_e, far_e, x_e, y_e, expand_out),
        (output_full, core_o, far_o, x_o, y_o, output_out),
    )

    def copy_of(i, kind):
        whole, core, far, x_buf, y_buf, _ = sets[i]
        half = whole.shape[1] // 2
        first, last = pl.ds(0, half), pl.ds(half, half)
        at = whole.at
        n, src, dst, peer = {
            K_CORE_OWN: lambda: (0, at[owner(1)], core.at[0], by_core),
            K_CORE_X: lambda: (1, at[owner(3)], core.at[1], by_core),
            K_CORE_Y: lambda: (2, at[owner(5)], core.at[2], by_core),
            K_CORE_FAR: lambda: (3, at[owner(7)], core.at[3], by_core),
            K_FAR_X: lambda: (4, at[owner(6), first], far.at[0], by_x),
            K_FAR_Y: lambda: (5, at[owner(6), last], far.at[1], by_y),
            K_X_FIRST: lambda: (6, at[owner(2), first], x_buf.at[0], by_x),
            K_X_LAST: lambda: (7, at[owner(2), last], x_buf.at[1], by_x),
            K_Y_FIRST: lambda: (8, at[owner(4), first], y_buf.at[0], by_y),
            K_Y_LAST: lambda: (9, at[owner(4), last], y_buf.at[1], by_y),
        }[kind]()
        return remote(src, dst, s_send.at[i, n], s_recv.at[i, n], peer)

    def sums_start(i):
        for kind in (K_CORE_FAR, K_CORE_X, K_CORE_Y, K_CORE_OWN):
            copy_of(i, kind).start()

    def sums_first(i):
        whole, core, _, _, _, _ = sets[i]
        half = whole.shape[1] // 2
        first, last = pl.ds(0, half), pl.ds(half, half)
        copy_of(i, K_CORE_FAR).wait_recv()
        add_rows(whole.at[owner(6)], 2 * half, core.at[3])
        copy_of(i, K_FAR_X).start()
        copy_of(i, K_FAR_Y).start()
        copy_of(i, K_CORE_X).wait_recv()
        add_rows(whole.at[owner(2), first], half, core.at[1, first])
        copy_of(i, K_X_FIRST).start()
        copy_of(i, K_CORE_Y).wait_recv()
        add_rows(whole.at[owner(4), last], half, core.at[2, last])
        copy_of(i, K_Y_LAST).start()

    def sums_next(i):
        whole, core, far, _, _, _ = sets[i]
        half = whole.shape[1] // 2
        first, last = pl.ds(0, half), pl.ds(half, half)
        copy_of(i, K_FAR_X).wait_recv()
        add_rows(whole.at[owner(4), first], half, core.at[2, first], far.at[0])
        copy_of(i, K_Y_FIRST).start()
        copy_of(i, K_FAR_Y).wait_recv()
        add_rows(whole.at[owner(2), last], half, core.at[1, last], far.at[1])
        copy_of(i, K_X_LAST).start()

    def sums_last(i):
        whole, core, _, x_buf, y_buf, out = sets[i]
        half = whole.shape[1] // 2
        for kind in (K_CORE_OWN, K_X_FIRST, K_X_LAST, K_Y_FIRST, K_Y_LAST):
            copy_of(i, kind).wait_recv()
        for n in range(2):
            part = pl.ds(n * half, half)
            add_rows(
                whole.at[me, part],
                half,
                core.at[0, part],
                x_buf.at[n],
                y_buf.at[n],
                store=out.at[part],
            )

    q_rows, o_cols = query_full.shape[1], output_full.shape[2]
    ready(0)
    ready(1)
    for o in range(count):
        at = slice(o * q_rows, (o + 1) * q_rows)
        query_full[o] = bfloat(first_dot(normed[:, at], query_grad[...]))
    sums_start(0)

    part_width = latent_full.shape[2]
    latent_count = latent_full.shape[1]
    own_rows.wait()
    for copy in latent_sends:
        copy.wait_recv()
    columns = pl.ds(pl.multiple_of(rank * part_width, part_width), part_width)
    rows_low = latent_rows[...].reshape(-1, latent_rows.shape[2])
    latent_full[...] = bfloat(first_dot(rows_low, normed[:, columns])).reshape(latent_full.shape)
    dealt = [
        remote(
            latent_full.at[peer[0]], latent_buf.at[me], ld_send.at[n], ld_recv.at[n], peer
        )
        for n, peer in enumerate(partners)
    ]
    for copy in dealt:
        copy.start()
    moe_step(0).start()
    latent_buf[me] = latent_full[me]
    first_norm()
    for copy in gains_sends:
        copy.start()
    gains_buf[me] = gains[...]
    ready(3)
    for o in range(count):
        at = slice(o * o_cols, (o + 1) * o_cols)
        output_full[o] = bfloat(first_dot(attended[...], resid[:, at]))
    sums_start(2)
    ready(4)
    expanded = bfloat(first_dot(latent_group[...], expand_grad[...]))
    expand_full[...] = expanded.reshape(expand_full.shape)
    sums_start(1)

    def latent_at(o, columns=None):
        at = pl.ds(pl.multiple_of(o * latent_count, latent_count), latent_count)
        return latent_all.at[at] if columns is None else latent_all.at[at, columns]

    pieces = [
        remote(
            latent_piece, latent_at(me, columns), lp_send.at[r - 1], lp_recv.at[r - 1], peer
        )
        for r, peer in enumerate(beside, 1)
    ]
    own_piece = pltpu.make_async_copy(latent_piece, latent_at(me, columns), local_sem.at[1])

    def latent_sum():
        for copy in dealt:
            copy.wait_recv()
        total = latent_buf[0].astype(jnp.float32)
        for o in range(1, count):
            total = total + latent_buf[o].astype(jnp.float32)
        latent_piece[...] = bfloat(total)
        for copy in pieces + [own_piece]:
            copy.start()

    def latent_copy(kind):
        first, last = pl.ds(0, width // 2), pl.ds(width // 2, width // 2)
        n, block, peer = {
            K_X: lambda: (0, latent_at(me), by_x),
            K_Y: lambda: (1, latent_at(me), by_y),
            K_CORE: lambda: (2, latent_at(me), by_core),
            K_FAR_Y: lambda: (3, latent_at(owner(2), last), by_y),
            K_FAR_X: lambda: (4, latent_at(owner(4), first), by_x),
            K_CORE_X: lambda: (5, latent_at(owner(2)), by_core),
            K_CORE_Y: lambda: (6, latent_at(owner(4)), by_core),
            K_CORE_FAR: lambda: (7, latent_at(owner(6)), by_core),
        }[kind]()
        return remote(block, block, lc_send.at[n], lc_recv.at[n], peer)

    def latent_cube():
        own_piece.wait()
        for copy in pieces:
            copy.wait_recv()
        for kind in (K_X, K_Y, K_CORE):
            latent_copy(kind).start()

    def latent_forward():
        latent_copy(K_X).wait_recv()
        latent_copy(K_FAR_Y).start()
        latent_copy(K_CORE_X).start()
        latent_copy(K_Y).wait_recv()
        latent_copy(K_FAR_X).start()
        latent_copy(K_CORE_Y).start()

    def latent_far():
        latent_copy(K_FAR_X).wait_recv()
        latent_copy(K_FAR_Y).wait_recv()
        latent_copy(K_CORE_FAR).start()

    gains_beside = [
        remote(gains_sum, gains_rank.at[rank], gz_send.at[r - 1], gz_recv.at[r - 1], peer)
        for r, peer in enumerate(beside, 1)
    ]

    def gains_first():
        for copy in gains_sends:
            copy.wait_recv()
        total = gains_buf[0]
        for o in range(1, count):
            total = total + gains_buf[o]
        gains_sum[...] = total
        gains_rank[rank] = total
        for copy in gains_beside:
            copy.start()

    def gains_last():
        for copy in gains_beside:
            copy.wait_recv()
        total = gains_rank[0]
        for r in range(1, ranks):
            total = total + gains_rank[r]
        gains_out[...] = total

    chunk, columns = cotan_buf.shape[1:]
    chunks = cotan_all.shape[0] // chunk
    units = chunks * (width // columns)

    def loads(unit, parity):
        at = pl.ds(pl.multiple_of(lax.rem(unit, chunks) * chunk, chunk), chunk)
        part = pl.ds(pl.multiple_of(lax.div(unit, chunks) * columns, columns), columns)
        return (
            pltpu.make_async_copy(act_all.at[at], act_buf.at[parity], load_sem.at[parity, 0]),
            pltpu.make_async_copy(
                cotan_all.at[at, part], cotan_buf.at[parity], load_sem.at[parity, 1]
            ),
        )

    def acc_store(unit):
        part = pl.ds(pl.multiple_of(lax.div(unit, chunks) * columns, columns), columns)
        return pltpu.make_async_copy(
            acc.at[pl.ds(0, routed_width)], down_out.at[:, part], out_sem
        )

    def products(begin, end):
        def one(unit, carry):
            parity = lax.rem(unit, 2)

            @pl.when(unit + 1 < units)
            def _():
                for copy in loads(unit + 1, 1 - parity):
                    copy.start()

            for copy in loads(unit, parity):
                copy.wait()
            part = first_dot(act_buf[parity], cotan_buf[parity])
            place = lax.rem(unit, chunks)

            @pl.when(place == 0)
            def _():
                acc[...] = part

            @pl.when(place > 0)
            def _():
                acc[...] += part

            @pl.when(place == chunks - 1)
            def _():
                acc_store(unit).start()
                start = pl.multiple_of(lax.div(unit, chunks) * columns, columns)
                shared_low[2, :, pl.ds(start, columns)] = bfloat(
                    acc[routed_width : routed_width + shared_pad, :]
                )
                acc_store(unit).wait()

            return carry

        lax.fori_loop(begin, end, one, 0)

    def shared_copies(at, n):
        size = shared_back.shape[3]
        return [
            remote(
                shared_low.at[at, :, pl.ds(pl.multiple_of(peer[0] * size, size), size)],
                shared_back.at[me, at],
                h_send.at[n, m],
                h_recv.at[n, m],
                peer,
            )
            for m, peer in enumerate(partners)
        ]

    def own_shared(at, n):
        size = shared_back.shape[3]
        return pltpu.make_async_copy(
            shared_low.at[at, :, pl.ds(pl.multiple_of(me * size, size), size)],
            shared_back.at[me, at],
            local_sem.at[2 + n],
        )

    def shared_receive(at, n, outs):
        own_shared(at, n).wait()
        for copy in shared_copies(at, n):
            copy.wait_recv()
        for m, out in outs:
            size = out.shape[0] // count
            for o in range(count):
                out[o * size : (o + 1) * size, :] = shared_back[o, m, :size, :].astype(jnp.float32)

    for copy in loads(0, 0):
        copy.start()
    pair, single = pl.ds(0, 2), pl.ds(2, 1)
    sums_first(0)
    sums_first(2)
    sums_first(1)
    latent_sum()
    products(0, 3)
    moe_next(1)
    latent_cube()
    sums_next(0)
    sums_next(2)
    sums_next(1)
    gains_first()
    products(3, 5)
    latent_forward()
    moe_next(2)
    latent_far()
    shared_load.wait()
    shared_low[0:2] = bfloat(shared_full[...])
    for copy in shared_copies(pair, 0) + [own_shared(pair, 0)]:
        copy.start()
    products(5, 8)
    for i in (0, 2, 1):
        sums_last(i)
    gains_last()
    products(8, 16)
    for copy in shared_copies(single, 1) + [own_shared(single, 1)]:
        copy.start()
    moe_last()
    for kind in (K_CORE, K_CORE_X, K_CORE_Y, K_CORE_FAR):
        latent_copy(kind).wait_recv()
    shared_receive(pair, 0, ((0, shared_gate_out), (1, shared_up_out)))
    shared_receive(single, 1, ((2, shared_down_out),))

    for kind in (K_X, K_Y, K_CORE, K_FAR_Y, K_FAR_X, K_CORE_X, K_CORE_Y, K_CORE_FAR):
        latent_copy(kind).wait_send()
    for copy in latent_sends + gains_sends + dealt + pieces + gains_beside:
        copy.wait_send()
    for i in range(len(sets)):
        for kind in SUM_KINDS:
            copy_of(i, kind).wait_send()
    for step in range(ranks - 1):
        moe_step(step).wait_send()
    for at, n in ((pair, 0), (single, 1)):
        for copy in shared_copies(at, n):
            copy.wait_send()


def weight_pass(
    normed,
    latent_group,
    attended,
    resid,
    query_grad,
    expand_grad,
    normed_back,
    latent_back,
    own_latent,
    hidden,
    resid_grad,
    residual,
    cos_table,
    sin_table,
    attn_gain,
    latent_gain,
    mlp_grad,
    latent_columns,
    moe_sums,
    shared_rows,
    act_all,
    cotan_all,
    shared_width,
    routed_width,
):
    ranks, count = lax.axis_size(TENSOR), lax.axis_size(DP)
    rows, width = hidden.shape
    hidden_width = act_all.shape[1]
    shared_pad = shared_rows.shape[1]
    low, full = jnp.bfloat16, jnp.float32
    anywhere = pl.BlockSpec(memory_space=pl.ANY)
    in_vmem = pl.BlockSpec(memory_space=pltpu.VMEM)
    dma = pltpu.SemaphoreType.DMA
    chunk = cotan_all.shape[0] // 8
    latent_width = latent_back.shape[1]
    q_shape = (width // count, query_grad.shape[1])
    e_shape = (latent_group.shape[1] // count, expand_grad.shape[1])
    o_shape = (attended.shape[1], width // count)
    l_shape = (latent_width // count, width // ranks)
    g_shape = (8, width)
    shapes = (q_shape, e_shape, o_shape)

    def array(*shape):
        return jax.ShapeDtypeStruct(shape, full)

    def halves(n):
        return [pltpu.VMEM((n, shape[0] // 2, shape[1]), low) for shape in shapes]

    return pl.pallas_call(
        weight_kernel,
        out_shape=(
            jax.ShapeDtypeStruct((rows, width), low),
            array(rows, width),
            array(*q_shape),
            array(*e_shape),
            array(*o_shape),
            array(*g_shape),
            jax.ShapeDtypeStruct((latent_width, width), low),
            array(count * shared_width, width // count),
            array(count * shared_width, width // count),
            array(count * shared_width, width // count),
            array(routed_width, width),
        ),
        in_specs=[anywhere] * 6
        + [in_vmem] * 3
        + [anywhere] * 3
        + [in_vmem] * 5
        + [anywhere] * 5,
        out_specs=(in_vmem,) * 6 + (anywhere,) + (in_vmem,) * 3 + (anywhere,),
        scratch_shapes=[pltpu.VMEM((count,) + shape, low) for shape in shapes]
        + [pltpu.VMEM((4,) + shape, low) for shape in shapes]
        + halves(2)
        + halves(2)
        + halves(2)
        + [
            pltpu.VMEM(g_shape, full),
            pltpu.VMEM((rows, latent_width), low),
            pltpu.VMEM((ranks, rows, latent_width), low),
            pltpu.VMEM((count,) + l_shape, low),
            pltpu.VMEM((count,) + l_shape, low),
            pltpu.VMEM(l_shape, low),
            pltpu.VMEM((count,) + g_shape, full),
            pltpu.VMEM(g_shape, full),
            pltpu.VMEM((ranks,) + g_shape, full),
            pltpu.VMEM((2, chunk, hidden_width), low),
            pltpu.VMEM((2, chunk, width // 2), low),
            pltpu.VMEM((hidden_width, width // 2), full),
            pltpu.VMEM((2, shared_pad, width), full),
            pltpu.VMEM((3, shared_pad, width), low),
            pltpu.VMEM((count, 3, shared_pad, width // count), low),
            pltpu.VMEM((rows, width), low),
            pltpu.VMEM((ranks - 1, rows, width), low),
            pltpu.VMEM((ranks - 1, rows, width), low),
        ]
        + [
            pltpu.VMEM(values.shape, values.dtype)
            for values in (
                normed,
                attended,
                resid,
                query_grad,
                expand_grad,
                latent_group,
                hidden,
                resid_grad,
                residual,
                latent_columns,
            )
        ]
        + [
            dma((10,)),
            dma((2, 2)),
            dma((8,)),
            dma,
            dma((3, 10)),
            dma((3, 10)),
            dma((ranks - 1,)),
            dma((ranks - 1,)),
            dma((count - 1,)),
            dma((count - 1,)),
            dma((ranks - 1,)),
            dma((ranks - 1,)),
            dma((8,)),
            dma((8,)),
            dma((count - 1,)),
            dma((count - 1,)),
            dma((ranks - 1,)),
            dma((ranks - 1,)),
            dma((2, count - 1)),
            dma((2, count - 1)),
            dma((ranks - 1,)),
            dma((ranks - 1,)),
        ],
        compiler_params=pltpu.CompilerParams(
            collective_id=4, has_side_effects=True, vmem_limit_bytes=63 * 1024 * 1024
        ),
        name="weight_pass",
    )(
        normed,
        latent_group,
        attended,
        resid,
        query_grad,
        expand_grad,
        normed_back,
        latent_back,
        own_latent,
        hidden,
        resid_grad,
        residual,
        cos_table,
        sin_table,
        attn_gain,
        latent_gain,
        mlp_grad,
        latent_columns,
        moe_sums,
        shared_rows,
        act_all,
        cotan_all,
    )


def part_heads(values, heads):
    split = values.reshape(-1, heads, NOPE + ROPE)
    parts = (split[:, :, :NOPE], split[:, :, NOPE:])
    return jnp.concatenate([part.reshape(values.shape[0], -1) for part in parts], axis=1)


def join_heads(values, heads):
    plain = values[:, : heads * NOPE].reshape(-1, heads, NOPE)
    turned = values[:, heads * NOPE :].reshape(-1, heads, ROPE)
    return jnp.concatenate([plain, turned], axis=2).reshape(values.shape)


def cube_shards(
    hidden,
    cotangent,
    routes,
    route_gates,
    doc_lengths,
    attn_gain,
    query_weight,
    latent_weight,
    latent_gain,
    expand_weight,
    output_weight,
    mlp_gain,
    shared_gate,
    shared_up,
    shared_down,
    expert_gate,
    expert_up,
    expert_down,
):
    ranks = lax.axis_size(TENSOR)
    groups = lax.axis_size(DP)
    rows = hidden.shape[0]
    group_rows = rows * ranks
    width = hidden.shape[1]
    local_experts, _, expert_width = expert_gate.shape
    experts = local_experts * groups

    shared_width = shared_gate.shape[1] // groups
    shared_pad = -(-shared_width // 16) * 16
    shared_stack = jnp.stack(
        [
            jnp.pad(
                weight.reshape(groups, shared_width, weight.shape[1]),
                ((0, 0), (0, shared_pad - shared_width), (0, 0)),
            )
            for weight in (shared_gate.T, shared_up.T, shared_down)
        ],
        axis=1,
    )
    routed_width = local_experts * expert_width
    hidden_width = -(-(routed_width + shared_pad) // 128) * 128
    local_heads = query_weight.shape[1] // (NOPE + ROPE)
    latent_columns = latent_weight.T

    (
        normed_group,
        latent_group,
        own_latent,
        query_full,
        expand_full,
        output_full,
        q_cat,
        k_cat,
        value_all,
        probability,
        attended_low,
        cos_group,
        sin_group,
        residual,
        normed_two,
        shared_all,
        slot_gates,
        cotan_all,
        back_all,
    ) = front_pass(
        doc_lengths,
        hidden,
        cotangent,
        part_heads(query_weight, local_heads),
        expand_weight,
        output_weight,
        shared_stack,
        expert_down.reshape(-1, width),
        routes.T,
        route_gates.T,
        jnp.concatenate([latent_columns, latent_columns[LATENT:]], axis=0),
        attn_gain[None],
        latent_gain[None],
        mlp_gain[None],
        hidden_width,
        experts,
    )
    (
        row_all,
        act_all,
        gate_all,
        up_all,
        resid_grad,
        resid_low,
        mlpgain_part,
    ) = moe_pass(
        normed_two,
        back_all,
        slot_gates,
        expert_gate.transpose(0, 2, 1).reshape(-1, width),
        expert_up.transpose(0, 2, 1).reshape(-1, width),
        shared_all,
        residual,
        cotangent,
        mlp_gain[None],
        expert_width,
    )
    (
        resid_all,
        moe_sums,
        gate_wgrad,
        up_wgrad,
        shared_rows,
        normed_back,
        latent_back,
        qraw_grad,
        expand_rows,
    ) = back_pass(
        resid_low,
        act_all,
        expert_down.reshape(-1, width),
        shared_all,
        output_full,
        query_full,
        expand_full,
        q_cat,
        k_cat,
        value_all,
        probability,
        cos_group,
        sin_group,
        gate_all.reshape(-1, hidden_width),
        up_all.reshape(-1, hidden_width),
        row_all.reshape(-1, width),
    )
    (
        layer_out,
        hidden_grad,
        query_total,
        expand_total,
        output_total,
        small,
        latent_total,
        shared_gate_total,
        shared_up_total,
        shared_down_total,
        down_wgrad,
    ) = weight_pass(
        normed_group,
        latent_group,
        attended_low,
        resid_all.reshape(group_rows, width),
        qraw_grad,
        expand_rows,
        normed_back,
        latent_back,
        own_latent,
        hidden,
        resid_grad,
        residual,
        cos_group,
        sin_group,
        attn_gain[None],
        latent_gain[None],
        mlpgain_part,
        latent_columns,
        moe_sums,
        shared_rows,
        act_all.reshape(-1, hidden_width),
        cotan_all.reshape(-1, width),
        shared_width,
        routed_width,
    )

    def expert_part(values):
        return values.reshape(local_experts, expert_width, width)

    return (
        layer_out,
        hidden_grad,
        small[0],
        join_heads(query_total, local_heads),
        latent_total[: LATENT + ROPE].T.astype(jnp.float32),
        small[2, :LATENT],
        expand_total,
        output_total,
        small[1],
        shared_gate_total.T,
        shared_up_total.T,
        shared_down_total,
        expert_part(gate_wgrad).transpose(0, 2, 1),
        expert_part(up_wgrad).transpose(0, 2, 1),
        expert_part(down_wgrad),
    )


def solution(mesh):
    in_specs = (
        P((DP, TENSOR), None),
        P((DP, TENSOR), None),
        P(DP, None),
        P(DP, None),
        P(DP, None),
        P(),
        P(DP, TENSOR),
        P(),
        P(),
        P(DP, TENSOR),
        P(TENSOR, DP),
        P(),
        P(DP, TENSOR),
        P(DP, TENSOR),
        P(TENSOR, DP),
        P(DP, None, TENSOR),
        P(DP, None, TENSOR),
        P(DP, TENSOR, None),
    )
    out_specs = (
        P((DP, TENSOR), None),
        P((DP, TENSOR), None),
        P(),
        P(DP, TENSOR),
        P(),
        P(),
        P(DP, TENSOR),
        P(TENSOR, DP),
        P(),
        P(DP, TENSOR),
        P(DP, TENSOR),
        P(TENSOR, DP),
        P(DP, None, TENSOR),
        P(DP, None, TENSOR),
        P(DP, TENSOR, None),
    )
    cube = dict(mesh.shape) == {DP: 8, TENSOR: 4}
    shards = cube_shards if cube else general_shards
    return jax.shard_map(shards, mesh=mesh, in_specs=in_specs, out_specs=out_specs, check_vma=False)
```

```python
import functools
from types import SimpleNamespace

import jax
import jax.numpy as jnp
from jax import lax
from jax.experimental import pallas as pl
from jax.experimental.pallas import tpu as pltpu
from jax.sharding import PartitionSpec as P

DP = "dp"
TENSOR = "tensor"
NOPE = 128
ROPE = 64
VDIM = 128
LATENT = 512
TOPK = 6

(
    K_RING,
    K_X,
    K_Y,
    K_CORE,
    K_FAR_Y,
    K_FAR_X,
    K_CORE_X,
    K_CORE_Y,
    K_CORE_FAR,
    K_CORE_OWN,
    K_X_FIRST,
    K_X_LAST,
    K_Y_FIRST,
    K_Y_LAST,
    K_FAR_RING,
) = range(15)


epsilon = 1e-06
rope_base = 10000.0


def bfloat(values):
    return values.astype(jnp.bfloat16)


def plain_dot(left_op, right_op):
    return jnp.dot(left_op, right_op, preferred_element_type=jnp.float32)


def first_dot(left_op, right_op):
    return lax.dot_general(
        left_op, right_op, (((0,), (0,)), ((), ())), preferred_element_type=jnp.float32
    )


def last_dot(left_op, right_op):
    return lax.dot_general(
        left_op, right_op, (((1,), (1,)), ((), ())), preferred_element_type=jnp.float32
    )


def rms_scale(values):
    return lax.rsqrt(jnp.mean(values * values, axis=-1, keepdims=True) + epsilon)


def rms_back(grad_out, values, scaling, gain_vec):
    scaled_grad = grad_out * gain_vec
    inner_sum = jnp.mean(scaled_grad * values, axis=-1, keepdims=True)
    grad_in = scaling * scaled_grad - values * (scaling * scaling * scaling) * inner_sum
    return (grad_in, jnp.sum(grad_out * values * scaling, axis=0))


def silu_parts(values):
    sigmoid = jax.nn.sigmoid(values)
    return (values * sigmoid, sigmoid * (1.0 + values * (1.0 - sigmoid)))


def rope_tables(positions, rot_width):
    middle = rot_width // 2
    frequency = rope_base ** (-jnp.arange(middle, dtype=jnp.float32) * 2.0 / rot_width)
    angles = positions.astype(jnp.float32)[:, None] * frequency[None, :]
    return (jnp.cos(angles), jnp.sin(angles))


def rotate(values, cos_table, sin_table):
    middle = values.shape[-1] // 2
    first_half = values[..., :middle]
    second_half = values[..., middle:]
    return jnp.concatenate(
        [
            first_half * cos_table - second_half * sin_table,
            second_half * cos_table + first_half * sin_table,
        ],
        axis=-1,
    )


def doc_layout(lengths, row_count):
    doc_ends = jnp.cumsum(lengths)
    tok_index = jnp.arange(row_count, dtype=jnp.int32)
    before = (doc_ends[None, :] <= tok_index[:, None]).astype(jnp.int32)
    doc_ids = jnp.sum(before, axis=1)
    starts = jnp.sum(before * lengths[None, :], axis=1)
    return (doc_ids, tok_index - starts)


def slot_tables(routes, experts, capacity):
    row_count = routes.shape[0] * routes.shape[1]
    flat_routes = routes.reshape(row_count)
    onehot = (flat_routes[:, None] == jnp.arange(experts, dtype=jnp.int32)[None, :]).astype(
        jnp.int32
    )
    earlier = jnp.cumsum(onehot, axis=0) - onehot
    position = jnp.sum(earlier * onehot, axis=1)
    slot_ids = flat_routes * capacity + position
    tok_rows = jnp.arange(row_count, dtype=jnp.int32) // routes.shape[1]
    owner_tok = jnp.zeros((experts * capacity,), jnp.int32).at[slot_ids].set(tok_rows)
    return (slot_ids.reshape(routes.shape), owner_tok)


def slot_share(capacity):
    return (0, capacity)


def route_rows(outgoing, apply_fn):
    arrived = lax.all_to_all(outgoing, DP, split_axis=1, concat_axis=1, tiled=True)
    result, extra = apply_fn(arrived)
    back = lax.all_to_all(
        result.astype(jnp.bfloat16), DP, split_axis=1, concat_axis=1, tiled=True
    ).astype(result.dtype)
    return (back, extra)


def block_mask(doc_ids, row_start, block_rows):
    group_rows = doc_ids.shape[0]
    key_index = jnp.arange(group_rows, dtype=jnp.int32)
    query_index = row_start + jnp.arange(block_rows, dtype=jnp.int32)
    return (key_index[None, :] <= query_index[:, None]) & (doc_ids[None, :] == doc_ids[:, None])


def attend(query_all, key_all, value_all, doc_ids, scaling):
    group_rows = query_all.shape[0]
    block_rows = min(512, group_rows)
    block_count = group_rows // block_rows

    def one_block(block_id):
        row_start = block_id * block_rows
        allowed = block_mask(doc_ids, row_start, block_rows)
        scores = (
            jnp.einsum("qhd,khd->hqk", query_all, key_all, preferred_element_type=jnp.float32)
            * scaling
        )
        scores = jnp.where(allowed[None], scores, -jnp.inf)
        row_max = jnp.max(scores, axis=-1, keepdims=True)
        exp_scores = jnp.exp(scores - row_max)
        row_total = jnp.sum(exp_scores, axis=-1, keepdims=True)
        probability = bfloat(exp_scores / row_total)
        output = jnp.einsum(
            "hqk,khd->qhd", probability, value_all, preferred_element_type=jnp.float32
        )
        return (output, (row_max + jnp.log(row_total))[..., 0])

    outputs, log_total = lax.map(one_block, jnp.arange(block_count, dtype=jnp.int32))
    return (outputs.reshape(group_rows, outputs.shape[2], outputs.shape[3]), log_total)


def attend_back(query_all, key_all, value_all, doc_ids, scaling, log_total, grad_out):
    group_rows = query_all.shape[0]
    block_rows = min(512, group_rows)
    block_count = group_rows // block_rows

    def one_block(carried, inputs):
        key_grad, value_grad = carried
        block_id, block_lse = inputs
        row_start = block_id * block_rows
        allowed = block_mask(doc_ids, row_start, block_rows)
        scores = (
            jnp.einsum("qhd,khd->hqk", query_all, key_all, preferred_element_type=jnp.float32)
            * scaling
        )
        scores = jnp.where(allowed[None], scores, -jnp.inf)
        probability = jnp.exp(scores - block_lse[..., None])
        value_grad = value_grad + jnp.einsum(
            "hqk,qhd->khd", bfloat(probability), grad_out, preferred_element_type=jnp.float32
        )
        prob_grad = jnp.einsum(
            "qhd,khd->hqk", grad_out, value_all, preferred_element_type=jnp.float32
        )
        row_dot = jnp.sum(prob_grad * probability, axis=-1, keepdims=True)
        score_grad = bfloat(probability * (prob_grad - row_dot))
        query_grad = (
            jnp.einsum("hqk,khd->qhd", score_grad, key_all, preferred_element_type=jnp.float32)
            * scaling
        )
        key_grad = (
            key_grad
            + jnp.einsum("hqk,qhd->khd", score_grad, query_all, preferred_element_type=jnp.float32)
            * scaling
        )
        return ((key_grad, value_grad), query_grad)

    start_state = (jnp.zeros(key_all.shape, jnp.float32), jnp.zeros(value_all.shape, jnp.float32))
    (key_grad, value_grad), query_blocks = lax.scan(
        one_block, start_state, (jnp.arange(block_count, dtype=jnp.int32), log_total)
    )
    query_grad = query_blocks.reshape(group_rows, query_blocks.shape[2], query_blocks.shape[3])
    return (query_grad, key_grad, value_grad)


def forward_pass(
    hidden,
    cotangent,
    routes,
    route_gates,
    doc_lengths,
    attn_gain,
    query_weight,
    latent_weight,
    latent_gain,
    expand_weight,
    output_weight,
    mlp_gain,
    shared_gate,
    shared_up,
    shared_down,
    expert_gate,
    expert_up,
    expert_down,
):
    tensor_count = lax.axis_size(TENSOR)
    dp_count = lax.axis_size(DP)
    local_rows = hidden.shape[0]
    group_rows = local_rows * tensor_count
    query_full, expand_full, output_full, sgate_full, sup_full, sdown_full = (
        lax.all_gather(query_weight, DP, axis=0, tiled=True),
        lax.all_gather(expand_weight, DP, axis=0, tiled=True),
        lax.all_gather(output_weight, DP, axis=1, tiled=True),
        lax.all_gather(shared_gate, DP, axis=0, tiled=True),
        lax.all_gather(shared_up, DP, axis=0, tiled=True),
        lax.all_gather(shared_down, DP, axis=1, tiled=True),
    )
    hidden_f = hidden.astype(jnp.float32)
    scale_one = rms_scale(hidden_f)
    normed_one = bfloat(hidden_f * scale_one * attn_gain)
    latent_full = plain_dot(normed_one, latent_weight)
    latent_part = latent_full[:, :LATENT]
    scale_latent = rms_scale(latent_part)
    latent_norm = bfloat(latent_part * scale_latent * latent_gain)
    doc_ids, positions = doc_layout(doc_lengths[0], group_rows)
    cos_group, sin_group = rope_tables(positions, ROPE)
    local_start = lax.axis_index(TENSOR) * local_rows
    cos_local = lax.dynamic_slice_in_dim(cos_group, local_start, local_rows, 0)
    sin_local = lax.dynamic_slice_in_dim(sin_group, local_start, local_rows, 0)
    key_rot = bfloat(rotate(latent_full[:, LATENT:], cos_local, sin_local))
    normed_group, latent_group, keyrot_group = (
        lax.all_gather(normed_one, TENSOR, axis=0, tiled=True),
        lax.all_gather(latent_norm, TENSOR, axis=0, tiled=True),
        lax.all_gather(key_rot, TENSOR, axis=0, tiled=True),
    )
    local_heads = query_full.shape[1] // (NOPE + ROPE)
    query_raw = plain_dot(normed_group, query_full).reshape(group_rows, local_heads, NOPE + ROPE)
    query_rot = rotate(query_raw[..., NOPE:], cos_group[:, None, :], sin_group[:, None, :])
    query_all = bfloat(jnp.concatenate([query_raw[..., :NOPE], query_rot], axis=-1))
    expanded = plain_dot(latent_group, expand_full).reshape(group_rows, local_heads, NOPE + VDIM)
    key_shared = jnp.broadcast_to(keyrot_group[:, None, :], (group_rows, local_heads, ROPE))
    key_all = jnp.concatenate([bfloat(expanded[..., :NOPE]), key_shared], axis=-1)
    value_all = bfloat(expanded[..., NOPE:])
    scaling = (NOPE + ROPE) ** (-0.5)
    attended, log_total = attend(query_all, key_all, value_all, doc_ids, scaling)
    attended_low = bfloat(attended).reshape(group_rows, local_heads * VDIM)
    attn_local = lax.psum_scatter(
        plain_dot(attended_low, output_full), TENSOR, scatter_dimension=0, tiled=True
    )
    residual = hidden_f + attn_local
    scale_two = rms_scale(residual)
    normed_two = bfloat(residual * scale_two * mlp_gain)
    mlp_rows, cotan_rows = (
        lax.all_gather(normed_two, TENSOR, axis=0, tiled=True),
        lax.all_gather(cotangent, TENSOR, axis=0, tiled=True),
    )
    shared_gpre = plain_dot(mlp_rows, sgate_full)
    shared_upre = plain_dot(mlp_rows, sup_full)
    shared_silu, shared_dsilu = silu_parts(shared_gpre)
    shared_hidden = bfloat(shared_silu * shared_upre)
    shared_out = plain_dot(shared_hidden, sdown_full)
    local_experts = expert_gate.shape[0]
    experts = local_experts * dp_count
    capacity = group_rows * TOPK * 4 // (3 * experts)
    slot_ids, owner_tok = slot_tables(routes, experts, capacity)
    slot_start, slot_count = slot_share(capacity)
    all_tok = owner_tok.reshape(dp_count, local_experts, capacity).transpose(1, 0, 2)
    send_rows = mlp_rows[all_tok]

    def expert_apply(received):
        gate_pre = jnp.einsum(
            "jscd,jdf->jscf", received, expert_gate, preferred_element_type=jnp.float32
        )
        up_pre = jnp.einsum(
            "jscd,jdf->jscf", received, expert_up, preferred_element_type=jnp.float32
        )
        gate_silu, gate_dsilu = silu_parts(gate_pre)
        activated = bfloat(gate_silu * up_pre)
        result = jnp.einsum(
            "jscf,jfd->jscd", activated, expert_down, preferred_element_type=jnp.float32
        )
        return (result, (received, up_pre, gate_silu, gate_dsilu, activated))

    returned, expert_state = route_rows(send_rows, expert_apply)
    received, up_pre, gate_silu, gate_dsilu, activated = expert_state
    position = slot_ids % capacity - slot_start
    slot_mask = ((position >= 0) & (position < slot_count)).astype(jnp.float32)
    flat_index = (
        routes % local_experts * dp_count + routes // local_experts
    ) * slot_count + jnp.clip(position, 0, slot_count - 1)
    returned_flat = returned.reshape(local_experts * dp_count * slot_count, returned.shape[-1])
    routed = jnp.sum((route_gates * slot_mask)[:, :, None] * returned_flat[flat_index], axis=1)
    moe_local = lax.psum_scatter(
        (shared_out + routed).astype(jnp.bfloat16), TENSOR, scatter_dimension=0, tiled=True
    ).astype(jnp.float32)
    layer_out = bfloat(residual + moe_local)
    return SimpleNamespace(
        layer_out=layer_out,
        hidden_f=hidden_f,
        scale_one=scale_one,
        normed_one=normed_one,
        latent_part=latent_part,
        scale_latent=scale_latent,
        cos_local=cos_local,
        sin_local=sin_local,
        cos_group=cos_group,
        sin_group=sin_group,
        doc_ids=doc_ids,
        normed_group=normed_group,
        latent_group=latent_group,
        query_all=query_all,
        key_all=key_all,
        value_all=value_all,
        log_total=log_total,
        attended_low=attended_low,
        residual=residual,
        scale_two=scale_two,
        mlp_rows=mlp_rows,
        cotan_rows=cotan_rows,
        shared_upre=shared_upre,
        shared_silu=shared_silu,
        shared_dsilu=shared_dsilu,
        shared_hidden=shared_hidden,
        slot_ids=slot_ids,
        send_tok=all_tok,
        flat_index=flat_index,
        slot_mask=slot_mask,
        received=received,
        up_pre=up_pre,
        gate_silu=gate_silu,
        gate_dsilu=gate_dsilu,
        activated=activated,
        query_full=query_full,
        expand_full=expand_full,
        output_full=output_full,
        sgate_full=sgate_full,
        sup_full=sup_full,
        sdown_full=sdown_full,
    )


def general_shards(
    hidden,
    cotangent,
    routes,
    route_gates,
    doc_lengths,
    attn_gain,
    query_weight,
    latent_weight,
    latent_gain,
    expand_weight,
    output_weight,
    mlp_gain,
    shared_gate,
    shared_up,
    shared_down,
    expert_gate,
    expert_up,
    expert_down,
):
    kept_state = forward_pass(
        hidden,
        cotangent,
        routes,
        route_gates,
        doc_lengths,
        attn_gain,
        query_weight,
        latent_weight,
        latent_gain,
        expand_weight,
        output_weight,
        mlp_gain,
        shared_gate,
        shared_up,
        shared_down,
        expert_gate,
        expert_up,
        expert_down,
    )
    dp_count = lax.axis_size(DP)
    local_experts = expert_gate.shape[0]
    experts = local_experts * dp_count
    group_rows = kept_state.mlp_rows.shape[0]
    capacity = group_rows * TOPK * 4 // (3 * experts)
    cotan_rows = kept_state.cotan_rows
    mlp_rows = kept_state.mlp_rows
    sdown_wgrad = first_dot(kept_state.shared_hidden, cotan_rows)
    shared_hgrad = last_dot(cotan_rows, kept_state.sdown_full)
    sgate_pgrad = bfloat(shared_hgrad * kept_state.shared_upre * kept_state.shared_dsilu)
    sup_pgrad = bfloat(shared_hgrad * kept_state.shared_silu)
    sgate_wgrad = first_dot(mlp_rows, sgate_pgrad)
    sup_wgrad = first_dot(mlp_rows, sup_pgrad)
    mlp_partial = last_dot(sgate_pgrad, kept_state.sgate_full) + last_dot(
        sup_pgrad, kept_state.sup_full
    )
    slot_start, slot_count = slot_share(capacity)
    slot_gate = (
        jnp.zeros((experts * capacity,), jnp.float32)
        .at[kept_state.slot_ids.reshape(-1)]
        .set(route_gates.reshape(-1))
    )
    all_gate = slot_gate.reshape(dp_count, local_experts, capacity).transpose(1, 0, 2)
    grad_send = bfloat(all_gate[..., None] * cotan_rows[kept_state.send_tok].astype(jnp.float32))
    received = kept_state.received

    def expert_back(grad_recv):
        expert_down_partial = jnp.einsum(
            "jscf,jscd->jfd", kept_state.activated, grad_recv, preferred_element_type=jnp.float32
        )
        act_grad = jnp.einsum(
            "jscd,jfd->jscf", grad_recv, expert_down, preferred_element_type=jnp.float32
        )
        gate_pgrad = bfloat(act_grad * kept_state.up_pre * kept_state.gate_dsilu)
        up_pgrad = bfloat(act_grad * kept_state.gate_silu)
        row_gradient = jnp.einsum(
            "jscf,jdf->jscd", gate_pgrad, expert_gate, preferred_element_type=jnp.float32
        )
        row_gradient = row_gradient + jnp.einsum(
            "jscf,jdf->jscd", up_pgrad, expert_up, preferred_element_type=jnp.float32
        )
        expert_gate_partial = jnp.einsum(
            "jscd,jscf->jdf", received, gate_pgrad, preferred_element_type=jnp.float32
        )
        expert_up_partial = jnp.einsum(
            "jscd,jscf->jdf", received, up_pgrad, preferred_element_type=jnp.float32
        )
        return (row_gradient, (expert_gate_partial, expert_up_partial, expert_down_partial))

    rows_back, expert_weight_gradients = route_rows(grad_send, expert_back)
    expert_gate_weight_gradient, expert_up_weight_gradient, expert_down_weight_gradient = (
        expert_weight_gradients
    )
    back_flat = rows_back.reshape(local_experts * dp_count * slot_count, rows_back.shape[-1])
    mlp_partial = mlp_partial + jnp.sum(
        kept_state.slot_mask[:, :, None] * back_flat[kept_state.flat_index], axis=1
    )
    mlp_grad = lax.psum_scatter(mlp_partial, TENSOR, scatter_dimension=0, tiled=True)
    resid_from, mlpgain_part = rms_back(
        mlp_grad, kept_state.residual, kept_state.scale_two, mlp_gain
    )
    resid_grad = cotangent.astype(jnp.float32) + resid_from
    attn_rows = lax.all_gather(bfloat(resid_grad), TENSOR, axis=0, tiled=True)
    output_wgrad = first_dot(kept_state.attended_low, attn_rows)
    local_heads = kept_state.query_all.shape[1]
    attended_grad = bfloat(last_dot(attn_rows, kept_state.output_full)).reshape(
        group_rows, local_heads, VDIM
    )
    query_g, key_g, value_g = attend_back(
        kept_state.query_all,
        kept_state.key_all,
        kept_state.value_all,
        kept_state.doc_ids,
        (NOPE + ROPE) ** (-0.5),
        kept_state.log_total,
        attended_grad,
    )
    query_low = bfloat(query_g)
    key_low = bfloat(key_g)
    value_low = bfloat(value_g)
    query_unrot = rotate(
        query_low[..., NOPE:].astype(jnp.float32),
        kept_state.cos_group[:, None, :],
        -kept_state.sin_group[:, None, :],
    )
    qraw_grad = bfloat(
        jnp.concatenate([query_low[..., :NOPE].astype(jnp.float32), query_unrot], axis=-1)
    )
    qraw_grad = qraw_grad.reshape(group_rows, local_heads * (NOPE + ROPE))
    query_wgrad = first_dot(kept_state.normed_group, qraw_grad)
    normed_partial = last_dot(qraw_grad, kept_state.query_full)
    expand_rows = jnp.concatenate([key_low[..., :NOPE], value_low], axis=-1).reshape(
        group_rows, local_heads * (NOPE + VDIM)
    )
    expand_wgrad = first_dot(kept_state.latent_group, expand_rows)
    latent_partial = last_dot(expand_rows, kept_state.expand_full)
    keyrot_partial = jnp.sum(key_low[..., NOPE:].astype(jnp.float32), axis=1)
    normed_back, latent_back, keyrot_back = (
        lax.psum_scatter(
            normed_partial.astype(jnp.bfloat16), TENSOR, scatter_dimension=0, tiled=True
        ).astype(jnp.float32),
        lax.psum_scatter(
            latent_partial.astype(jnp.bfloat16), TENSOR, scatter_dimension=0, tiled=True
        ).astype(jnp.float32),
        lax.psum_scatter(
            keyrot_partial.astype(jnp.bfloat16), TENSOR, scatter_dimension=0, tiled=True
        ).astype(jnp.float32),
    )
    keyraw_back = rotate(keyrot_back, kept_state.cos_local, -kept_state.sin_local)
    latent_in, latgain_part = rms_back(
        latent_back, kept_state.latent_part, kept_state.scale_latent, latent_gain
    )
    latent_low = bfloat(jnp.concatenate([latent_in, keyraw_back], axis=-1))
    latent_wgrad = first_dot(kept_state.normed_one, latent_low)
    normed_total = normed_back + last_dot(latent_low, latent_weight)
    hidden_back, attngain_part = rms_back(
        normed_total, kept_state.hidden_f, kept_state.scale_one, attn_gain
    )
    hidden_grad = resid_grad + hidden_back
    fsdp_sums = (
        lax.psum_scatter(
            query_wgrad.astype(jnp.bfloat16), DP, scatter_dimension=0, tiled=True
        ).astype(jnp.float32),
        lax.psum_scatter(
            expand_wgrad.astype(jnp.bfloat16), DP, scatter_dimension=0, tiled=True
        ).astype(jnp.float32),
        lax.psum_scatter(
            output_wgrad.astype(jnp.bfloat16), DP, scatter_dimension=1, tiled=True
        ).astype(jnp.float32),
        lax.psum_scatter(
            sgate_wgrad.astype(jnp.bfloat16), DP, scatter_dimension=0, tiled=True
        ).astype(jnp.float32),
        lax.psum_scatter(
            sup_wgrad.astype(jnp.bfloat16), DP, scatter_dimension=0, tiled=True
        ).astype(jnp.float32),
        lax.psum_scatter(
            sdown_wgrad.astype(jnp.bfloat16), DP, scatter_dimension=1, tiled=True
        ).astype(jnp.float32),
    )
    small_sums = lax.psum(
        (latent_wgrad, attngain_part, mlpgain_part, latgain_part), (DP, TENSOR)
    )
    return (
        kept_state.layer_out,
        hidden_grad,
        small_sums[1],
        fsdp_sums[0],
        small_sums[0],
        small_sums[3],
        fsdp_sums[1],
        fsdp_sums[2],
        small_sums[2],
        fsdp_sums[3],
        fsdp_sums[4],
        fsdp_sums[5],
        expert_gate_weight_gradient,
        expert_up_weight_gradient,
        expert_down_weight_gradient,
    )


MESH = pl.DeviceIdType.MESH


def flip(index, bit):
    return index + bit - 2 * bit * ((index // bit) % 2)


def remote(src, dst, send_sem, recv_sem, peer):
    return pltpu.make_async_remote_copy(
        src_ref=src,
        dst_ref=dst,
        send_sem=send_sem,
        recv_sem=recv_sem,
        device_id=peer,
        device_id_type=MESH,
    )


def greet(peers):
    barrier = pltpu.get_barrier_semaphore()
    for peer in peers:
        pl.semaphore_signal(barrier, inc=1, device_id=peer, device_id_type=MESH)
    pl.semaphore_wait(barrier, len(peers))


def add_rows(target, size, *terms, store=None):
    step = 16
    while step * target.shape[1] < 65536 and size % (2 * step) == 0:
        step *= 2

    def one(i, carry):
        at = pl.ds(pl.multiple_of(i * step, step), step)
        total = target[at, :].astype(jnp.float32)
        for term in terms:
            total = total + term[at, :].astype(jnp.float32)
        to = target if store is None else store
        to[at, :] = total.astype(to.dtype)
        return carry

    lax.fori_loop(0, size // step, one, 0)


def sum_copies(blocks, core_buf, far_buf, x_buf, y_buf, sends, recvs, by_core, by_x, by_y):
    half = blocks.shape[2] // 2
    first, last = pl.ds(0, half), pl.ds(half, half)

    def copy(kind, j):
        at = blocks.at[lax.rem(j, 2)].at
        n, src, dst, peer = {
            K_CORE_OWN: lambda: (0, at[1], core_buf.at[j, 0], by_core),
            K_CORE_X: lambda: (1, at[4], core_buf.at[j, 1], by_core),
            K_CORE_Y: lambda: (2, at[5], core_buf.at[j, 2], by_core),
            K_CORE_FAR: lambda: (3, at[7], core_buf.at[j, 3], by_core),
            K_FAR_X: lambda: (4, at[6, first], far_buf.at[j, 0], by_x),
            K_FAR_Y: lambda: (5, at[6, last], far_buf.at[j, 1], by_y),
            K_X_FIRST: lambda: (6, at[2, first], x_buf.at[j, 0], by_x),
            K_X_LAST: lambda: (7, at[2, last], x_buf.at[j, 1], by_x),
            K_Y_FIRST: lambda: (8, at[3, first], y_buf.at[j, 0], by_y),
            K_Y_LAST: lambda: (9, at[3, last], y_buf.at[j, 1], by_y),
        }[kind]()
        return remote(src, dst, sends.at[n, j], recvs.at[n, j], peer)

    return copy


SUM_KINDS = (
    K_CORE_OWN,
    K_CORE_X,
    K_CORE_Y,
    K_CORE_FAR,
    K_FAR_X,
    K_FAR_Y,
    K_X_FIRST,
    K_X_LAST,
    K_Y_FIRST,
    K_Y_LAST,
)


SLOTS = (0, 1, 2, 4, 3, 5, 6, 7)


def moe_kernel(
    rows,
    back,
    gates,
    expert_gate,
    expert_up,
    shared_all,
    residual,
    cotangent,
    gain,
    rows_all,
    act_all,
    gpre_all,
    upre_all,
    resid_grad,
    resid_low,
    gain_grad,
    grad_out,
    gate_rows,
    up_rows,
    row_buf,
    back_buf,
    out_buf,
    blocks,
    core_buf,
    far_buf,
    x_buf,
    y_buf,
    ring_buf,
    ring_out,
    weight_sem,
    load_sem,
    back_sem,
    store_sem,
    ag_send,
    ag_recv,
    rs_send,
    rs_recv,
    ring_send,
    ring_recv,
    *,
    expert_width,
    routed_width,
):
    me, rank = lax.axis_index(DP), lax.axis_index(TENSOR)
    ranks = lax.axis_size(TENSOR)
    right = (me, lax.rem(rank + 1, ranks))
    left = (me, lax.rem(rank + ranks - 1, ranks))
    by_core, by_x, by_y = [(flip(me, bit), rank) for bit in (1, 2, 4)]
    count = rows.shape[0]
    half = count // 2
    first, last = pl.ds(0, half), pl.ds(half, half)
    hidden_width = gate_rows.shape[0]
    shared_pad = shared_all.shape[1]
    greet([by_core, by_x, by_y, right, left])

    def ag(kind, j, src, dst, peer):
        return remote(src, dst, ag_send.at[kind, j], ag_recv.at[kind, j], peer)

    def rs(kind, j, src, dst, peer):
        return remote(src, dst, rs_send.at[kind, j], rs_recv.at[kind, j], peer)

    def row_copy(kind, j):
        at = rows_all.at
        return {
            K_RING: lambda: ag(0, j, at[0, j - 1], at[0, j], right),
            K_X: lambda: ag(1, j, at[0, j], at[2, j], by_x),
            K_Y: lambda: ag(2, j, at[0, j], at[3, j], by_y),
            K_CORE: lambda: ag(3, j, at[0, j], at[1, j], by_core),
            K_FAR_Y: lambda: ag(4, j, at[2, j, last], at[6, j, last], by_y),
            K_FAR_X: lambda: ag(5, j, at[3, j, first], at[6, j, first], by_x),
            K_CORE_X: lambda: ag(6, j, at[2, j], at[4, j], by_core),
            K_CORE_Y: lambda: ag(7, j, at[3, j], at[5, j], by_core),
            K_CORE_FAR: lambda: ag(8, j, at[6, j], at[7, j], by_core),
            K_FAR_RING: lambda: ag(4, j, at[6, j - 1], at[6, j], right),
        }[kind]()

    def sum_copy(kind, j):
        at = blocks.at[lax.rem(j, 2)].at
        return {
            K_CORE_OWN: lambda: rs(0, j, at[1], core_buf.at[j, 0], by_core),
            K_CORE_X: lambda: rs(1, j, at[4], core_buf.at[j, 1], by_core),
            K_CORE_Y: lambda: rs(2, j, at[5], core_buf.at[j, 2], by_core),
            K_CORE_FAR: lambda: rs(3, j, at[7], core_buf.at[j, 3], by_core),
            K_FAR_X: lambda: rs(4, j, at[6, first], far_buf.at[j, 0], by_x),
            K_FAR_Y: lambda: rs(5, j, at[6, last], far_buf.at[j, 1], by_y),
            K_X_FIRST: lambda: rs(6, j, at[2, first], x_buf.at[j, 0], by_x),
            K_X_LAST: lambda: rs(7, j, at[2, last], x_buf.at[j, 1], by_x),
            K_Y_FIRST: lambda: rs(8, j, at[3, first], y_buf.at[j, 0], by_y),
            K_Y_LAST: lambda: rs(9, j, at[3, last], y_buf.at[j, 1], by_y),
        }[kind]()

    def ring_copy(step):
        return remote(
            ring_out.at[step], ring_buf.at[step], ring_send.at[step], ring_recv.at[step], right
        )

    def back_load(j, p, parity):
        return pltpu.make_async_copy(
            back.at[pl.ds(2 * p, 2), j], back_buf.at[parity], back_sem.at[parity]
        )

    def row_load(j, p, parity):
        return pltpu.make_async_copy(
            rows_all.at[pl.ds(2 * p, 2), j], row_buf.at[parity], load_sem.at[parity]
        )

    def stores(j, p, parity):
        return [
            pltpu.make_async_copy(
                out_buf.at[parity, n], to.at[pl.ds(2 * p, 2), j], store_sem.at[parity, n]
            )
            for n, to in enumerate((act_all, gpre_all, upre_all))
        ]

    def compute(j, p, place, following, used):
        parity = place % 2
        if following is not None:
            back_load(*following, 1 - parity).start()
        back_load(j, p, parity).wait()
        for copy in stores(*used, parity) if used is not None else ():
            copy.wait()
        row_load(j, p, parity).wait()
        wide = row_buf[parity].reshape(2 * count, row_buf.shape[3])
        gate_pre = last_dot(wide, gate_rows[...])
        up_pre = last_dot(wide, up_rows[...])
        column = lax.broadcasted_iota(jnp.int32, (1, hidden_width), 1)
        lanes = pl.ds(pl.multiple_of(j * count, count), count)
        gate = jnp.concatenate([gates[2 * p + i, :, lanes].T for i in range(2)], axis=0)
        scaled = jnp.where(
            column < expert_width,
            gate[:, 0:1],
            jnp.where(column < routed_width, gate[:, 1:2], 1.0),
        )
        sigmoid = 1.0 / (1.0 + jnp.exp(-gate_pre))
        silu = gate_pre * sigmoid
        dsilu = sigmoid * (1.0 + gate_pre * (1.0 - sigmoid))
        back_pre = back_buf[parity].reshape(2 * count, hidden_width).astype(jnp.float32) * scaled
        act = bfloat(silu * up_pre * scaled)
        gate_grad = bfloat(back_pre * up_pre * dsilu)
        up_grad = bfloat(back_pre * silu)
        out_buf[parity, 0] = act.reshape(2, count, hidden_width)
        out_buf[parity, 1] = gate_grad.reshape(2, count, hidden_width)
        out_buf[parity, 2] = up_grad.reshape(2, count, hidden_width)
        for copy in stores(j, p, parity):
            copy.start()
        grad = plain_dot(gate_grad, gate_rows[...]) + plain_dot(up_grad, up_rows[...])
        blocks[lax.rem(j, 2), pl.ds(2 * p, 2)] = bfloat(grad).reshape(2, count, grad.shape[1])

    own = pltpu.make_async_copy(rows, rows_all.at[0, 0], load_sem.at[0])
    own.start()
    assembled = []
    for n, (routed, target) in enumerate(((expert_gate, gate_rows), (expert_up, up_rows))):
        for i, (src, at) in enumerate(
            ((routed, pl.ds(0, routed_width)), (shared_all.at[n], pl.ds(routed_width, shared_pad)))
        ):
            copy = pltpu.make_async_copy(src, target.at[at], weight_sem.at[n, i])
            copy.start()
            assembled.append(copy)
        target[routed_width + shared_pad :] = jnp.zeros(
            (hidden_width - routed_width - shared_pad, target.shape[1]), jnp.bfloat16
        )
    back_load(0, 0, 0).start()
    own.wait()
    ring0 = row_copy(K_RING, 1)
    ring0.start()
    for kind in (K_X, K_Y, K_CORE):
        row_copy(kind, 0).start()
    for copy in assembled:
        copy.wait()

    def send_piece(j):
        for kind in (K_X, K_Y, K_CORE):
            row_copy(kind, j).start()

    def forward_piece(j):
        row_copy(K_X, j).wait_recv()
        row_copy(K_CORE_X, j).start()
        row_copy(K_Y, j).wait_recv()
        row_copy(K_CORE_Y, j).start()

    def sums_far(j):
        sum_copy(K_CORE_FAR, j).wait_recv()
        add_rows(blocks.at[lax.rem(j, 2), 6], count, core_buf.at[j, 3])
        sum_copy(K_FAR_X, j).start()
        sum_copy(K_FAR_Y, j).start()

    def sums_near(j):
        at = blocks.at[lax.rem(j, 2)].at
        sum_copy(K_CORE_X, j).wait_recv()
        add_rows(at[2, first], half, core_buf.at[j, 1, first])
        sum_copy(K_X_FIRST, j).start()
        sum_copy(K_CORE_Y, j).wait_recv()
        add_rows(at[3, last], half, core_buf.at[j, 2, last])
        sum_copy(K_Y_LAST, j).start()

    def sums_next(j):
        at = blocks.at[lax.rem(j, 2)].at
        sum_copy(K_FAR_X, j).wait_recv()
        add_rows(at[3, first], half, core_buf.at[j, 2, first], far_buf.at[j, 0])
        sum_copy(K_Y_FIRST, j).start()
        sum_copy(K_FAR_Y, j).wait_recv()
        add_rows(at[2, last], half, core_buf.at[j, 1, last], far_buf.at[j, 1])
        sum_copy(K_X_LAST, j).start()

    def sums_last(j):
        at = blocks.at[lax.rem(j, 2)].at
        for kind in (K_CORE_OWN, K_X_FIRST, K_X_LAST, K_Y_FIRST, K_Y_LAST):
            sum_copy(kind, j).wait_recv()
        terms = [
            (core_buf.at[j, 0, part], x_buf.at[j, n], y_buf.at[j, n])
            for n, part in enumerate((first, last))
        ]

        @pl.when(j == 0)
        def _():
            for part, more in zip((first, last), terms):
                add_rows(at[0, part], half, *more, store=grad_out.at[part])

        @pl.when(j == 1)
        def _():
            for part, more in zip((first, last), terms):
                add_rows(at[0, part], half, *more, store=ring_out.at[0, part])
            ring_copy(0).start()

        @pl.when(j > 1)
        def _():
            ring_copy(j - 2).wait_recv()
            for part, more in zip((first, last), terms):
                add_rows(
                    at[0, part],
                    half,
                    *more,
                    ring_buf.at[j - 2, part],
                    store=ring_out.at[j - 1, part],
                )
            ring_copy(j - 1).start()

        for kind in SUM_KINDS:
            sum_copy(kind, j).wait_send()

    row_copy(K_CORE, 0).wait_recv()
    row_load(0, 0, 0).start()
    compute(0, 0, 0, (0, 1), None)
    sum_copy(K_CORE_OWN, 0).start()
    row_copy(K_RING, 1).wait_recv()
    row_copy(K_RING, 2).start()
    send_piece(1)
    row_copy(K_X, 0).wait_recv()
    row_copy(K_FAR_Y, 0).start()
    row_copy(K_CORE_X, 0).start()
    row_copy(K_Y, 0).wait_recv()
    row_copy(K_FAR_X, 0).start()
    row_copy(K_CORE_Y, 0).start()
    row_load(0, 1, 1).start()
    compute(0, 1, 1, (0, 2), None)
    row_copy(K_RING, 2).wait_recv()
    row_copy(K_RING, 3).start()
    send_piece(2)
    row_copy(K_CORE_X, 0).wait_recv()
    row_copy(K_CORE_Y, 0).wait_recv()
    row_load(0, 2, 0).start()
    row_copy(K_FAR_X, 0).wait_recv()
    row_copy(K_FAR_Y, 0).wait_recv()
    row_copy(K_CORE_FAR, 0).start()
    row_copy(K_FAR_RING, 1).start()
    compute(0, 2, 0, (0, 3), (0, 0))
    sum_copy(K_CORE_X, 0).start()
    sum_copy(K_CORE_Y, 0).start()
    row_copy(K_CORE_FAR, 0).wait_recv()
    row_load(0, 3, 1).start()
    row_copy(K_RING, 3).wait_recv()
    send_piece(3)
    forward_piece(1)
    row_copy(K_CORE, 1).wait_recv()
    compute(0, 3, 1, (1, 3), (0, 1))
    sum_copy(K_CORE_FAR, 0).start()
    sums_near(0)
    sums_far(0)
    row_copy(K_FAR_RING, 1).wait_recv()
    row_copy(K_CORE_FAR, 1).start()
    row_copy(K_FAR_RING, 2).start()
    row_copy(K_CORE_FAR, 1).wait_recv()
    row_load(1, 3, 0).start()

    def body(j, carry):
        before = j - 1
        row_copy(K_CORE_X, j).wait_recv()
        row_copy(K_CORE_Y, j).wait_recv()
        row_load(j, 2, 1).start()

        @pl.when(j == 1)
        def _():
            for copy in stores(0, 2, 0):
                copy.wait()

        @pl.when(j > 1)
        def _():
            for copy in stores(before, 1, 0):
                copy.wait()

        compute(j, 3, 0, (j, 2), None)
        sum_copy(K_CORE_FAR, j).start()

        @pl.when(j == 1)
        def _():
            sums_next(0)
            for copy in stores(0, 3, 1):
                copy.wait()

        @pl.when(j > 1)
        def _():
            for copy in stores(before, 0, 1):
                copy.wait()

        row_load(j, 1, 0).start()
        compute(j, 2, 1, (j, 1), None)
        sum_copy(K_CORE_X, j).start()
        sum_copy(K_CORE_Y, j).start()
        sums_far(j)

        @pl.when(j < ranks - 1)
        def _():
            row_copy(K_FAR_RING, j + 1).wait_recv()
            row_copy(K_CORE_FAR, j + 1).start()

            @pl.when(j < ranks - 2)
            def _():
                row_copy(K_FAR_RING, j + 2).start()

        row_load(j, 0, 1).start()
        compute(j, 1, 0, (j, 0), (j, 3))
        sums_near(j)

        @pl.when(j < ranks - 1)
        def _():
            forward_piece(j + 1)
            row_copy(K_CORE, j + 1).wait_recv()
            row_copy(K_CORE_FAR, j + 1).wait_recv()
            row_load(j + 1, 3, 0).start()
            back_load(j + 1, 3, 0).start()

        compute(j, 0, 1, None, (j, 2))
        sum_copy(K_CORE_OWN, j).start()
        sums_last(before)
        sums_next(j)
        return carry

    lax.fori_loop(1, ranks, body, 0)
    sums_last(ranks - 1)
    ring_copy(ranks - 2).wait_recv()
    grad = grad_out[...] + ring_buf[ranks - 2].astype(jnp.float32)
    values = residual[...]
    scale = lax.rsqrt(jnp.mean(values * values, axis=-1, keepdims=True) + epsilon)
    scaled_grad = grad * gain[...]
    inner = jnp.mean(scaled_grad * values, axis=-1, keepdims=True)
    through = scale * scaled_grad - values * (scale * scale * scale) * inner
    total = cotangent[...].astype(jnp.float32) + through
    resid_grad[...] = total
    resid_low[...] = bfloat(total)
    gain_grad[...] = jnp.sum(grad * values * scale, axis=0, keepdims=True)
    for step in range(ranks - 1):
        ring_copy(step).wait_send()
        row_copy(K_RING, step + 1).wait_send()
    for p in (1, 0):
        for copy in stores(ranks - 1, p, 1 - p):
            copy.wait()

    def drain(j, carry):
        for kind in (K_X, K_Y, K_CORE, K_CORE_X, K_CORE_Y, K_CORE_FAR):
            row_copy(kind, j).wait_send()
        return carry

    row_copy(K_FAR_X, 0).wait_send()
    row_copy(K_FAR_Y, 0).wait_send()
    for j in range(1, ranks):
        row_copy(K_FAR_RING, j).wait_send()
    lax.fori_loop(0, ranks, drain, 0)


def moe_pass(
    rows,
    back,
    gates,
    expert_gate,
    expert_up,
    shared_all,
    residual,
    cotangent,
    gain,
    expert_width,
):
    ranks = lax.axis_size(TENSOR)
    groups = lax.axis_size(DP)
    count, width = rows.shape
    hidden_width = back.shape[-1]
    anywhere = pl.BlockSpec(memory_space=pl.ANY)
    in_vmem = pl.BlockSpec(memory_space=pltpu.VMEM)
    low = jnp.bfloat16
    hidden_shape = jax.ShapeDtypeStruct((groups, ranks, count, hidden_width), low)
    dma = pltpu.SemaphoreType.DMA
    return pl.pallas_call(
        functools.partial(
            moe_kernel, expert_width=expert_width, routed_width=expert_gate.shape[0]
        ),
        out_shape=(
            jax.ShapeDtypeStruct((groups, ranks, count, width), low),
            hidden_shape,
            hidden_shape,
            hidden_shape,
            jax.ShapeDtypeStruct((count, width), jnp.float32),
            jax.ShapeDtypeStruct((count, width), low),
            jax.ShapeDtypeStruct((1, width), jnp.float32),
        ),
        in_specs=[anywhere, anywhere, in_vmem] + [anywhere] * 3 + [in_vmem] * 3,
        out_specs=(anywhere,) * 4 + (in_vmem,) * 3,
        scratch_shapes=[
            pltpu.VMEM((count, width), jnp.float32),
            pltpu.VMEM((hidden_width, width), low),
            pltpu.VMEM((hidden_width, width), low),
            pltpu.VMEM((2, 2, count, width), low),
            pltpu.VMEM((2, 2, count, hidden_width), low),
            pltpu.VMEM((2, 3, 2, count, hidden_width), low),
            pltpu.VMEM((2, groups, count, width), low),
            pltpu.VMEM((ranks, 4, count, width), low),
            pltpu.VMEM((ranks, 2, count // 2, width), low),
            pltpu.VMEM((ranks, 2, count // 2, width), low),
            pltpu.VMEM((ranks, 2, count // 2, width), low),
            pltpu.VMEM((ranks - 1, count, width), low),
            pltpu.VMEM((ranks - 1, count, width), low),
            dma((2, 2)),
            dma((2,)),
            dma((2,)),
            dma((2, 3)),
            dma((9, ranks)),
            dma((9, ranks)),
            dma((10, ranks)),
            dma((10, ranks)),
            dma((ranks - 1,)),
            dma((ranks - 1,)),
        ],
        compiler_params=pltpu.CompilerParams(
            collective_id=2, has_side_effects=True, vmem_limit_bytes=60 * 1024 * 1024
        ),
        name="moe_pass",
    )(
        rows,
        back,
        gates,
        expert_gate,
        expert_up,
        shared_all,
        residual,
        cotangent,
        gain,
    )


def cube_copies(gathered, sends, recvs, by_core, by_x, by_y):
    half = gathered.shape[2] // 2
    first, last = pl.ds(0, half), pl.ds(half, half)
    at = gathered.at

    def copy(kind, j):
        src, dst, peer = {
            K_X: lambda: (at[0, j], at[2, j], by_x),
            K_Y: lambda: (at[0, j], at[3, j], by_y),
            K_CORE: lambda: (at[0, j], at[1, j], by_core),
            K_FAR_Y: lambda: (at[2, j, last], at[6, j, last], by_y),
            K_FAR_X: lambda: (at[3, j, first], at[6, j, first], by_x),
            K_CORE_X: lambda: (at[2, j], at[4, j], by_core),
            K_CORE_Y: lambda: (at[3, j], at[5, j], by_core),
            K_CORE_FAR: lambda: (at[6, j], at[7, j], by_core),
        }[kind]()
        return remote(src, dst, sends.at[kind, j], recvs.at[kind, j], peer)

    return copy


def swap_halves(values):
    lane = lax.broadcasted_iota(jnp.int32, values.shape, 1)
    middle = ROPE // 2
    lanes = values.shape[1]
    ahead, behind = pltpu.roll(values, lanes - middle, 1), pltpu.roll(values, middle, 1)
    return jnp.where((lane // middle) % 2 == 0, ahead, behind)


def turn(values, cos_table, sin_table):
    return values * cos_table + swap_halves(values) * sin_table


def front_kernel(
    lengths,
    hidden,
    cotangent,
    query,
    expand,
    output,
    shared,
    expert_down,
    routes,
    route_gates,
    latent_columns,
    attn_gain,
    latent_gain,
    mlp_gain,
    frequency,
    normed_out,
    latent_out,
    own_latent,
    query_out,
    expand_out,
    output_out,
    qcat_out,
    kcat_out,
    value_out,
    prob_out,
    attended_out,
    cos_out,
    sin_out,
    residual_out,
    normed_two,
    shared_all,
    gates_all,
    cotan_all,
    back_all,
    hidden_all,
    query_all,
    expand_all,
    output_all,
    down_rows,
    latent_rows,
    normed,
    latent_low,
    q_cat,
    k_cat,
    value,
    mask,
    prob,
    attended,
    gate_abs,
    gate_rel,
    gate_send,
    row_buf,
    back_buf,
    ring_out,
    ring_buf,
    local_sem,
    prob_sem,
    row_sem,
    back_sem,
    ring_send,
    ring_recv,
    w_send,
    w_recv,
    deal_send,
    deal_recv,
    gates_send,
    gates_recv,
    cring_send,
    cring_recv,
    c_send,
    c_recv,
    sum_send,
    sum_recv,
):
    me, rank = lax.axis_index(DP), lax.axis_index(TENSOR)
    ranks, count = lax.axis_size(TENSOR), lax.axis_size(DP)
    right = (me, lax.rem(rank + 1, ranks))
    left = (me, lax.rem(rank + ranks - 1, ranks))
    by_core, by_x, by_y = [(flip(me, bit), rank) for bit in (1, 2, 4)]
    partners = []
    for k in range(1, count):
        other = me
        for bit in (1, 2, 4):
            other = flip(other, bit) if k & bit else other
        partners.append((k, (other, rank)))
    rows, width = hidden.shape
    group_rows = rows * ranks
    heads = q_cat.shape[0]
    local_experts = gate_abs.shape[0] // count
    q_rows, e_rows, o_cols = query.shape[0], expand.shape[0], output.shape[1]
    routed_width = expert_down.shape[0]
    shared_pad = shared.shape[2]
    piece = shared.shape[3]

    def query_at(owner, half=None):
        size = q_rows if half is None else q_rows // 2
        start = owner * q_rows + (0 if half is None else half * size)
        return query_all.at[pl.ds(pl.multiple_of(start, size), size)]

    def expand_at(owner, half=None):
        size = e_rows if half is None else e_rows // 2
        start = owner * e_rows + (0 if half is None else half * size)
        return expand_all.at[pl.ds(pl.multiple_of(start, size), size)]

    def output_at(owner, half=None):
        size = output.shape[0] if half is None else output.shape[0] // 2
        start = 0 if half is None else half * size
        return output_all.at[
            pl.ds(start, size), pl.ds(pl.multiple_of(owner * o_cols, o_cols), o_cols)
        ]

    greet([peer for _, peer in partners] + [right, left])

    ring = {}

    def ring_step(step):
        src = hidden if step == 0 else hidden_all.at[step]
        ring[step] = remote(
            src, hidden_all.at[step + 1], ring_send.at[step], ring_recv.at[step], right
        )
        ring[step].start()

    weights = ((query, query_at), (expand, expand_at), (output, output_at))
    copies = {}

    def send(i, kind, src, dst, peer):
        copies[i, kind] = remote(src, dst, w_send.at[i, kind], w_recv.at[i, kind], peer)
        copies[i, kind].start()

    def weight_first(i):
        own, at = weights[i]
        send(i, 0, own, at(me), by_x)
        send(i, 1, own, at(me), by_y)
        send(i, 2, own, at(me), by_core)

    def weight_forward(i):
        _, at = weights[i]
        copies[i, 0].wait_recv()
        send(i, 3, at(flip(me, 2), 1), at(flip(me, 2), 1), by_y)
        send(i, 4, at(flip(me, 2)), at(flip(me, 2)), by_core)
        copies[i, 1].wait_recv()
        send(i, 5, at(flip(me, 4), 0), at(flip(me, 4), 0), by_x)
        send(i, 6, at(flip(me, 4)), at(flip(me, 4)), by_core)

    def weight_far(i):
        _, at = weights[i]
        far = flip(flip(me, 2), 4)
        copies[i, 3].wait_recv()
        copies[i, 5].wait_recv()
        send(i, 7, at(far), at(far), by_core)

    def weight_last(i):
        for kind in (2, 4, 6, 7):
            copies[i, kind].wait_recv()

    cube = cube_copies(cotan_all, c_send, c_recv, by_core, by_x, by_y)

    def cotan_ring(j):
        src = cotan_all.at[0, j - 1]
        return remote(src, cotan_all.at[0, j], cring_send.at[j - 1], cring_recv.at[j - 1], right)

    def cotan_send(j):
        for kind in (K_X, K_Y, K_CORE):
            cube(kind, j).start()

    def cotan_forward(j):
        cube(K_X, j).wait_recv()
        cube(K_FAR_Y, j).start()
        cube(K_CORE_X, j).start()
        cube(K_Y, j).wait_recv()
        cube(K_FAR_X, j).start()
        cube(K_CORE_Y, j).start()

    def cotan_far(j):
        cube(K_FAR_X, j).wait_recv()
        cube(K_FAR_Y, j).wait_recv()
        cube(K_CORE_FAR, j).start()

    def cotan_next(j):
        cotan_ring(j).wait_recv()
        if j + 1 < ranks:
            cotan_ring(j + 1).start()
        cotan_send(j)

    def down_back(j, begin=0, end=4):
        needs = ((K_CORE,), (), (K_CORE_X, K_CORE_Y), (K_CORE_FAR,))
        for p in range(begin, end):
            for kind in needs[p]:
                cube(kind, j).wait_recv()

        def load(p, parity):
            return pltpu.make_async_copy(
                cotan_all.at[pl.ds(2 * p, 2), j], row_buf.at[parity], row_sem.at[parity]
            )

        def store(p, parity):
            return pltpu.make_async_copy(
                back_buf.at[parity], back_all.at[pl.ds(2 * p, 2), j], back_sem.at[parity]
            )

        load(begin, begin % 2).start()

        def one(p, carry):
            parity = lax.rem(p, 2)
            load(p, parity).wait()

            @pl.when(p + 1 < end)
            def _():
                load(p + 1, 1 - parity).start()

            @pl.when(p > begin + 1)
            def _():
                store(p - 2, parity).wait()

            wide = row_buf[parity].reshape(2 * rows, width)
            back = bfloat(last_dot(wide, down_rows[...]))
            back_buf[parity] = back.reshape(2, rows, back.shape[1])
            store(p, parity).start()
            return carry

        lax.fori_loop(begin, end, one, 0)
        for p in range(max(begin, end - 2), end):
            store(p, p % 2).wait()

    ring_step(0)
    weight_first(0)
    weight_first(1)
    dealt = []
    for n, (k, peer) in enumerate(partners):
        copy = remote(
            shared.at[peer[0]],
            shared_all.at[:, :, pl.ds(pl.multiple_of(me * piece, piece), piece)],
            deal_send.at[n],
            deal_recv.at[n],
            peer,
        )
        dealt.append(copy)
    local = [
        pltpu.make_async_copy(hidden, hidden_all.at[0], local_sem.at[0]),
        pltpu.make_async_copy(query, query_at(me), local_sem.at[1]),
        pltpu.make_async_copy(expand, expand_at(me), local_sem.at[2]),
        pltpu.make_async_copy(output, output_at(me), local_sem.at[3]),
        pltpu.make_async_copy(
            shared.at[me],
            shared_all.at[:, :, pl.ds(pl.multiple_of(me * piece, piece), piece)],
            local_sem.at[4],
        ),
        pltpu.make_async_copy(cotangent, cotan_all.at[0, 0], local_sem.at[5]),
        pltpu.make_async_copy(expert_down, down_rows.at[pl.ds(0, routed_width)], local_sem.at[6]),
        pltpu.make_async_copy(
            latent_columns, latent_rows.at[pl.ds(0, LATENT + ROPE)], local_sem.at[18]
        ),
        pltpu.make_async_copy(
            latent_columns.at[pl.ds(LATENT, ROPE)],
            latent_rows.at[pl.ds(LATENT + ROPE, ROPE)],
            local_sem.at[19],
        ),
    ]
    for copy in local:
        copy.start()

    def absolute(index):
        block = index // rows
        return ((rank + ranks - block) % ranks) * rows + index % rows

    def starts_of(token):
        start, total = jnp.zeros_like(token), 0
        for n in range(lengths.shape[1]):
            total = total + lengths[0, n]
            start = jnp.where(token >= total, total, start)
        return start

    token = absolute(lax.broadcasted_iota(jnp.int32, (group_rows, cos_out.shape[1]), 0))
    angle = (token - starts_of(token)).astype(jnp.float32) * frequency[...]
    lane = lax.broadcasted_iota(jnp.int32, angle.shape, 1)
    cos_out[...] = jnp.cos(angle)
    sine = jnp.sin(angle)
    sin_out[...] = jnp.where((lane // (ROPE // 2)) % 2 == 0, -sine, sine)
    row_token = absolute(lax.broadcasted_iota(jnp.int32, mask.shape, 0))
    column_token = absolute(lax.broadcasted_iota(jnp.int32, mask.shape, 1))
    allowed = (column_token <= row_token) & (column_token >= starts_of(row_token))
    mask[...] = jnp.where(allowed, 0.0, -jnp.inf)

    expert = lax.broadcasted_iota(jnp.int32, gate_abs.shape, 0)
    dense = jnp.zeros(gate_abs.shape, jnp.float32)
    for k in range(routes.shape[0]):
        dense = dense + jnp.where(routes[k : k + 1, :] == expert, route_gates[k : k + 1, :], 0.0)
    gate_abs[...] = dense
    for r in range(ranks):
        start = pl.multiple_of(((rank + ranks - r) % ranks) * rows, rows)
        gate_rel[:, r * rows : (r + 1) * rows] = gate_abs[:, pl.ds(start, rows)]
    gate_send[...] = jnp.zeros_like(gate_send)
    for p in range(count):
        gate_send[p, 0:local_experts] = gate_rel[p * local_experts : (p + 1) * local_experts]
    down_rows[routed_width + shared_pad :] = jnp.zeros(
        (down_rows.shape[0] - routed_width - shared_pad, width), jnp.bfloat16
    )
    gate_copies = []
    for n, (k, peer) in enumerate(partners):
        gate_copies.append(
            remote(
                gate_send.at[peer[0]],
                gates_all.at[SLOTS.index(k)],
                gates_send.at[n],
                gates_recv.at[n],
                peer,
            )
        )
    own_gates = pltpu.make_async_copy(gate_send.at[me], gates_all.at[0], local_sem.at[7])
    own_gates.start()

    def norm_piece(r):
        at = pl.ds(r * rows, rows)
        values = hidden_all[r].astype(jnp.float32)
        scale = lax.rsqrt(jnp.mean(values * values, axis=-1, keepdims=True) + epsilon)
        normed[at, :] = bfloat(values * scale * attn_gain[...])

    def project_piece(r):
        at = pl.ds(r * rows, rows)
        values = normed[at, :]
        cos_table, sin_table = cos_out[at, :], sin_out[at, :]
        lanes = cos_table.shape[1]
        raw = plain_dot(values, query_all[...])
        for h in range(heads):
            q_cat[h, at, 0:NOPE] = bfloat(raw[:, h * NOPE : (h + 1) * NOPE])
        for pair in range(heads // 2):
            start = heads * NOPE + pair * lanes
            turned = bfloat(turn(raw[:, start : start + lanes], cos_table, sin_table))
            q_cat[2 * pair, at, NOPE : NOPE + lanes] = turned
            q_cat[2 * pair + 1, at, NOPE : NOPE + lanes] = turned
        latent = last_dot(values, latent_rows[...])
        part = latent[:, :LATENT]
        if r == 0:
            own_latent[...] = part
        scale = lax.rsqrt(jnp.mean(part * part, axis=-1, keepdims=True) + epsilon)
        low_part = bfloat(part * scale * latent_gain[...])
        latent_low[at, :] = low_part
        turned = turn(latent[:, LATENT:], cos_table, sin_table)
        lane = lax.broadcasted_iota(jnp.int32, turned.shape, 1)
        even = bfloat(jnp.where(lane < ROPE, turned, 0.0))
        odd = bfloat(jnp.where(lane < ROPE, 0.0, turned))
        expanded = plain_dot(low_part, expand_all[...])
        step = NOPE + VDIM
        for h in range(heads):
            k_cat[h, at, 0:NOPE] = bfloat(expanded[:, h * step : h * step + NOPE])
            k_cat[h, at, NOPE : NOPE + lanes] = even if h % 2 == 0 else odd
            value[h, at, :] = bfloat(expanded[:, h * step + NOPE : (h + 1) * step])

    def prob_store(h, parity):
        return pltpu.make_async_copy(prob.at[parity], prob_out.at[h], prob_sem.at[parity])

    def head(h):
        parity = h % 2
        if h >= 2:
            prob_store(h - 2, parity).wait()
        scores = last_dot(q_cat[h], k_cat[h]) * (NOPE + ROPE) ** (-0.5) + mask[...]
        exp_scores = jnp.exp(scores - jnp.max(scores, axis=-1, keepdims=True))
        ratio = exp_scores / jnp.sum(exp_scores, axis=-1, keepdims=True)
        prob[parity] = ratio
        prob_store(h, parity).start()
        attended[:, h * VDIM : (h + 1) * VDIM] = bfloat(plain_dot(bfloat(ratio), value[h]))

    norm_piece_wait = [local[0].wait] + [lambda s=s: ring[s].wait_recv() for s in range(ranks - 1)]
    norm_piece_wait[0]()
    norm_piece(0)
    weight_first(2)
    weight_forward(0)
    norm_piece_wait[1]()
    ring_step(1)
    weight_forward(1)
    norm_piece(1)
    weight_far(0)
    weight_far(1)
    local[5].wait()
    cotan_send(0)
    norm_piece_wait[2]()
    ring_step(2)
    cotan_ring(1).start()
    norm_piece(2)
    weight_forward(2)
    weight_last(0)
    weight_last(1)
    local[1].wait()
    local[2].wait()
    local[7].wait()
    local[8].wait()
    project_piece(0)
    project_piece(1)
    weight_far(2)
    project_piece(2)
    norm_piece_wait[3]()
    norm_piece(3)
    cotan_forward(0)
    for copy in gate_copies:
        copy.start()
    for copy in dealt:
        copy.start()
    project_piece(3)
    cotan_next(1)
    for h in range(heads):
        head(h)
    weight_last(2)
    local[3].wait()

    def attn_block(r):
        return plain_dot(attended[r * rows : (r + 1) * rows, :], output_all[...])

    def sum_step(step):
        return remote(
            ring_out.at[step], ring_buf.at[step], sum_send.at[step], sum_recv.at[step], right
        )

    ring_out[0] = bfloat(attn_block(1))
    sum_step(0).start()
    cotan_far(0)
    for copy in dealt:
        copy.wait_recv()
    local[4].wait()
    local[6].wait()
    shared_down = pltpu.make_async_copy(
        shared_all.at[2], down_rows.at[pl.ds(routed_width, shared_pad)], local_sem.at[8]
    )
    shared_down.start()
    shared_down.wait()
    down_back(0)
    cotan_next(2)
    sum_step(0).wait_recv()
    ring_out[1] = bfloat(attn_block(2) + ring_buf[0].astype(jnp.float32))
    sum_step(1).start()
    outs = [
        pltpu.make_async_copy(src, dst, local_sem.at[9 + n])
        for n, (src, dst) in enumerate(
            (
                (normed, normed_out),
                (latent_low, latent_out),
                (query_all, query_out),
                (expand_all, expand_out),
                (output_all, output_out),
                (q_cat, qcat_out),
                (k_cat, kcat_out),
                (value, value_out),
                (attended, attended_out),
            )
        )
    ]
    for copy in outs:
        copy.start()
    cotan_forward(1)
    cotan_far(1)
    cotan_next(3)
    sum_step(1).wait_recv()
    ring_out[2] = bfloat(attn_block(3) + ring_buf[1].astype(jnp.float32))
    sum_step(2).start()
    down_back(1)
    cotan_forward(2)
    cotan_far(2)
    cotan_forward(3)
    sum_step(2).wait_recv()
    residual = (
        hidden_all[0].astype(jnp.float32) + attn_block(0) + ring_buf[2].astype(jnp.float32)
    )
    residual_out[...] = residual
    scale = lax.rsqrt(jnp.mean(residual * residual, axis=-1, keepdims=True) + epsilon)
    normed_two[...] = bfloat(residual * scale * mlp_gain[...])
    down_back(2)
    cotan_far(3)
    down_back(3, 0, 3)
    down_back(3, 3, 4)

    for h in (heads - 2, heads - 1):
        prob_store(h, h % 2).wait()
    for copy in outs:
        copy.wait()
    own_gates.wait()
    for copy in gate_copies:
        copy.wait()
    for copy in dealt:
        copy.wait_send()
    for i in range(len(weights)):
        for kind in range(8):
            copies[i, kind].wait_send()
    for step in range(ranks - 1):
        ring[step].wait_send()
        cotan_ring(step + 1).wait_send()
        sum_step(step).wait_send()
    for j in range(ranks):
        for kind in (
            K_X,
            K_Y,
            K_CORE,
            K_FAR_Y,
            K_FAR_X,
            K_CORE_X,
            K_CORE_Y,
            K_CORE_FAR,
        ):
            cube(kind, j).wait_send()


def front_pass(
    lengths,
    hidden,
    cotangent,
    query,
    expand,
    output,
    shared,
    expert_down,
    routes,
    route_gates,
    latent_columns,
    attn_gain,
    latent_gain,
    mlp_gain,
    hidden_width,
    experts,
):
    count, ranks = lax.axis_size(DP), lax.axis_size(TENSOR)
    rows, width = hidden.shape
    group_rows = rows * ranks
    heads = query.shape[1] // (NOPE + ROPE)
    lanes = 2 * ROPE
    low, full = jnp.bfloat16, jnp.float32
    frequency = rope_base ** (-jnp.arange(ROPE // 2, dtype=full) * 2.0 / ROPE)
    frequency = jnp.tile(frequency, lanes // (ROPE // 2))[None, :]
    anywhere = pl.BlockSpec(memory_space=pl.ANY)
    in_vmem = pl.BlockSpec(memory_space=pltpu.VMEM)
    dma = pltpu.SemaphoreType.DMA
    by_slot = (count, ranks, rows)

    def array(*shape, dtype=low):
        return jax.ShapeDtypeStruct(shape, dtype)

    def full_query():
        return (count * query.shape[0], query.shape[1])

    def full_expand():
        return (count * expand.shape[0], expand.shape[1])

    def full_output():
        return (output.shape[0], count * output.shape[1])

    return pl.pallas_call(
        front_kernel,
        out_shape=(
            array(group_rows, width),
            array(group_rows, LATENT),
            array(rows, LATENT, dtype=full),
            array(*full_query()),
            array(*full_expand()),
            array(*full_output()),
            array(heads, group_rows, NOPE + lanes),
            array(heads, group_rows, NOPE + lanes),
            array(heads, group_rows, VDIM),
            array(heads, group_rows, group_rows, dtype=full),
            array(group_rows, heads * VDIM),
            array(group_rows, lanes, dtype=full),
            array(group_rows, lanes, dtype=full),
            array(rows, width, dtype=full),
            array(rows, width),
            array(*shared.shape[1:3], count * shared.shape[3]),
            array(count, 8, group_rows, dtype=full),
            array(*by_slot, width),
            array(*by_slot, hidden_width),
        ),
        in_specs=[pl.BlockSpec(memory_space=pltpu.SMEM)] + [anywhere] * 7
        + [in_vmem] * 2 + [anywhere] + [in_vmem] * 4,
        out_specs=(anywhere, anywhere, in_vmem)
        + (anywhere,) * 8
        + (in_vmem,) * 4
        + (anywhere,) * 4,
        scratch_shapes=[
            pltpu.VMEM((ranks, rows, width), low),
            pltpu.VMEM(full_query(), low),
            pltpu.VMEM(full_expand(), low),
            pltpu.VMEM(full_output(), low),
            pltpu.VMEM((hidden_width, width), low),
            pltpu.VMEM((LATENT + 2 * ROPE, width), low),
            pltpu.VMEM((group_rows, width), low),
            pltpu.VMEM((group_rows, LATENT), low),
            pltpu.VMEM((heads, group_rows, NOPE + lanes), low),
            pltpu.VMEM((heads, group_rows, NOPE + lanes), low),
            pltpu.VMEM((heads, group_rows, VDIM), low),
            pltpu.VMEM((group_rows, group_rows), full),
            pltpu.VMEM((2, group_rows, group_rows), full),
            pltpu.VMEM((group_rows, heads * VDIM), low),
            pltpu.VMEM((experts, group_rows), full),
            pltpu.VMEM((experts, group_rows), full),
            pltpu.VMEM((count, 8, group_rows), full),
            pltpu.VMEM((2, 2, rows, width), low),
            pltpu.VMEM((2, 2, rows, hidden_width), low),
            pltpu.VMEM((ranks - 1, rows, width), low),
            pltpu.VMEM((ranks - 1, rows, width), low),
            dma((20,)),
            dma((2,)),
            dma((2,)),
            dma((2,)),
            dma((ranks - 1,)),
            dma((ranks - 1,)),
            dma((3, 8)),
            dma((3, 8)),
            dma((count - 1,)),
            dma((count - 1,)),
            dma((count - 1,)),
            dma((count - 1,)),
            dma((ranks - 1,)),
            dma((ranks - 1,)),
            dma((9, ranks)),
            dma((9, ranks)),
            dma((ranks - 1,)),
            dma((ranks - 1,)),
        ],
        compiler_params=pltpu.CompilerParams(
            collective_id=1, has_side_effects=True, vmem_limit_bytes=60 * 1024 * 1024
        ),
        name="front_pass",
    )(
        lengths,
        hidden,
        cotangent,
        query,
        expand,
        output,
        shared,
        expert_down,
        routes,
        route_gates,
        latent_columns,
        attn_gain,
        latent_gain,
        mlp_gain,
        frequency,
    )


def back_kernel(
    resid,
    acts,
    expert_down,
    shared_all,
    output,
    query,
    expand,
    q_cat,
    k_cat,
    value,
    prob_all,
    cos_table,
    sin_table,
    gate_all,
    up_all,
    row_all,
    resid_all,
    moe_sums,
    gate_out,
    up_out,
    shared_rows,
    normed_back,
    latent_back,
    query_grad,
    expand_grad,
    down_rows,
    act_buf,
    resid_buf,
    attended_grad,
    prob,
    pair,
    key_rot,
    blocks,
    core_buf,
    far_buf,
    x_buf,
    y_buf,
    ring_out,
    ring_buf,
    left_buf,
    right_buf,
    acc,
    local_sem,
    act_sem,
    prob_sem,
    sums_sem,
    load_sem,
    acc_sem,
    resid_send,
    resid_recv,
    s_send,
    s_recv,
    ring_send,
    ring_recv,
):
    me, rank = lax.axis_index(DP), lax.axis_index(TENSOR)
    ranks = lax.axis_size(TENSOR)
    right = (me, lax.rem(rank + 1, ranks))
    left = (me, lax.rem(rank + ranks - 1, ranks))
    by_core, by_x, by_y = [(flip(me, bit), rank) for bit in (1, 2, 4)]
    rows, width = resid.shape
    half = rows // 2
    first, last = pl.ds(0, half), pl.ds(half, half)
    heads = q_cat.shape[0]
    lanes = cos_table.shape[1]
    routed_width, shared_pad = expert_down.shape[0], shared_all.shape[1]
    scaling = (NOPE + ROPE) ** (-0.5)
    greet([by_core, by_x, by_y, right, left])

    local = [
        pltpu.make_async_copy(resid, resid_buf.at[0], local_sem.at[0]),
        pltpu.make_async_copy(expert_down, down_rows.at[pl.ds(0, routed_width)], local_sem.at[1]),
        pltpu.make_async_copy(
            shared_all.at[2], down_rows.at[pl.ds(routed_width, shared_pad)], local_sem.at[2]
        ),
    ]

    def resid_step(step):
        src = resid if step == 0 else resid_buf.at[step]
        return remote(
            src, resid_buf.at[step + 1], resid_send.at[step], resid_recv.at[step], right
        )

    resid_step(0).start()
    for copy in local:
        copy.start()
    down_rows[routed_width + shared_pad :] = jnp.zeros(
        (down_rows.shape[0] - routed_width - shared_pad, width), jnp.bfloat16
    )
    key_rot[...] = jnp.zeros_like(key_rot)

    copy_of = sum_copies(
        blocks, core_buf, far_buf, x_buf, y_buf, s_send, s_recv, by_core, by_x, by_y
    )

    def act_load(j, p, parity):
        return pltpu.make_async_copy(
            acts.at[pl.ds(2 * p, 2), j], act_buf.at[parity], act_sem.at[parity]
        )

    def outputs(j):
        if j == 0:
            act_load(0, 0, 0).start()

        def one(p, carry):
            parity = lax.rem(p, 2)
            act_load(j, p, parity).wait()

            @pl.when(p < 3)
            def _():
                act_load(j, p + 1, 1 - parity).start()

            if j + 1 < ranks:

                @pl.when(p == 3)
                def _():
                    act_load(j + 1, 0, 0).start()

            wide = act_buf[parity].reshape(2 * rows, act_buf.shape[3])
            out = plain_dot(wide, down_rows[...])
            blocks[j % 2, pl.ds(2 * p, 2)] = bfloat(out).reshape(2, rows, width)
            return carry

        lax.fori_loop(0, 4, one, 0)
        for kind in (K_CORE_FAR, K_CORE_X, K_CORE_Y, K_CORE_OWN):
            copy_of(kind, j).start()

    def sums_first(j):
        at = blocks.at[j % 2].at
        copy_of(K_CORE_FAR, j).wait_recv()
        add_rows(at[6], rows, core_buf.at[j, 3])
        copy_of(K_FAR_X, j).start()
        copy_of(K_FAR_Y, j).start()
        copy_of(K_CORE_X, j).wait_recv()
        add_rows(at[2, first], half, core_buf.at[j, 1, first])
        copy_of(K_X_FIRST, j).start()
        copy_of(K_CORE_Y, j).wait_recv()
        add_rows(at[3, last], half, core_buf.at[j, 2, last])
        copy_of(K_Y_LAST, j).start()

    def sums_next(j):
        at = blocks.at[j % 2].at
        copy_of(K_FAR_X, j).wait_recv()
        add_rows(at[3, first], half, core_buf.at[j, 2, first], far_buf.at[j, 0])
        copy_of(K_Y_FIRST, j).start()
        copy_of(K_FAR_Y, j).wait_recv()
        add_rows(at[2, last], half, core_buf.at[j, 1, last], far_buf.at[j, 1])
        copy_of(K_X_LAST, j).start()

    def sums_store(j):
        return pltpu.make_async_copy(
            blocks.at[j % 2, 0], moe_sums.at[j], sums_sem.at[j % 2]
        )

    def sums_last(j):
        at = blocks.at[j % 2].at
        for kind in (K_CORE_OWN, K_X_FIRST, K_X_LAST, K_Y_FIRST, K_Y_LAST):
            copy_of(kind, j).wait_recv()
        for n, part in enumerate((first, last)):
            add_rows(at[0, part], half, core_buf.at[j, 0, part], x_buf.at[j, n], y_buf.at[j, n])
        sums_store(j).start()
        for kind in SUM_KINDS:
            copy_of(kind, j).wait_send()
        sums_store(j).wait()

    chunk, columns = right_buf.shape[1:]
    chunks, parts = row_all.shape[0] // chunk, width // columns
    kinds = ((gate_all, gate_out), (up_all, up_out))

    def chunk_loads(w, unit, parity):
        at = pl.ds(pl.multiple_of(lax.rem(unit, chunks) * chunk, chunk), chunk)
        part = pl.ds(pl.multiple_of(lax.div(unit, chunks) * columns, columns), columns)
        return (
            pltpu.make_async_copy(kinds[w][0].at[at], left_buf.at[parity], load_sem.at[parity, 0]),
            pltpu.make_async_copy(
                row_all.at[at, part], right_buf.at[parity], load_sem.at[parity, 1]
            ),
        )

    def acc_store(w, unit):
        part = pl.ds(pl.multiple_of(lax.div(unit, chunks) * columns, columns), columns)
        return (
            pltpu.make_async_copy(
                acc.at[pl.ds(0, routed_width)], kinds[w][1].at[:, part], acc_sem.at[0]
            ),
            pltpu.make_async_copy(
                acc.at[pl.ds(routed_width, shared_pad)], shared_rows.at[w, :, part], acc_sem.at[1]
            ),
        )

    units = chunks * parts

    def products(w, begin, end):
        def one(unit, carry):
            parity = lax.rem(unit, 2)

            @pl.when(unit + 1 < units)
            def _():
                for copy in chunk_loads(w, unit + 1, 1 - parity):
                    copy.start()

            if w + 1 < len(kinds):

                @pl.when(unit + 1 == units)
                def _():
                    for copy in chunk_loads(w + 1, 0, 0):
                        copy.start()

            for copy in chunk_loads(w, unit, parity):
                copy.wait()
            part = first_dot(left_buf[parity], right_buf[parity])
            place = lax.rem(unit, chunks)

            @pl.when(place == 0)
            def _():
                acc[...] = part

            @pl.when(place > 0)
            def _():
                acc[...] += part

            @pl.when(place == chunks - 1)
            def _():
                for copy in acc_store(w, unit):
                    copy.start()
                for copy in acc_store(w, unit):
                    copy.wait()

            return carry

        lax.fori_loop(begin, end, one, 0)

    def attended_piece(r):
        attended_grad[r * rows : (r + 1) * rows, :] = bfloat(
            last_dot(resid_buf[r], output[...])
        )

    def prob_load(h):
        return pltpu.make_async_copy(prob_all.at[h], prob.at[h % 2], prob_sem.at[h % 2])

    def head(h):
        prob_load(h).wait()
        ratio = prob[h % 2]
        back = attended_grad[:, h * VDIM : (h + 1) * VDIM]
        prob_back = last_dot(back, value[h])
        row_dot = jnp.sum(prob_back * ratio, axis=-1, keepdims=True)
        score_back = bfloat(ratio * (prob_back - row_dot))
        value_back = first_dot(bfloat(ratio), back)
        query_back = bfloat(plain_dot(score_back, k_cat[h]) * scaling)
        key_back = bfloat(first_dot(score_back, q_cat[h]) * scaling)
        step = NOPE + VDIM
        expand_grad[:, h * step : h * step + NOPE] = key_back[:, :NOPE]
        expand_grad[:, h * step + NOPE : (h + 1) * step] = bfloat(value_back)
        query_grad[:, h * NOPE : (h + 1) * NOPE] = query_back[:, :NOPE]
        turned = key_back[:, NOPE:].astype(jnp.float32)
        lane = lax.broadcasted_iota(jnp.int32, turned.shape, 1)
        own = (lane < ROPE) if h % 2 == 0 else (lane >= ROPE)
        key_rot[...] += jnp.where(own, turned, 0.0)
        rope_part = query_back[:, NOPE:].astype(jnp.float32)
        if h % 2 == 0:
            pair[...] = rope_part
        else:
            whole = pair[...] + rope_part
            start = heads * NOPE + h // 2 * lanes
            query_grad[:, start : start + lanes] = bfloat(
                turn(whole, cos_table[...], -sin_table[...])
            )
        if h + 2 < heads:
            prob_load(h + 2).start()

    prob_load(0).start()
    prob_load(1).start()
    for copy in chunk_loads(0, 0, 0):
        copy.start()
    for copy in local[1:]:
        copy.wait()
    outputs(0)
    local[0].wait()
    attended_piece(0)
    sums_first(0)
    resid_step(0).wait_recv()
    resid_step(1).start()
    attended_piece(1)
    outputs(1)
    sums_next(0)
    sums_first(1)
    products(0, 0, 4)
    resid_step(1).wait_recv()
    resid_step(2).start()
    attended_piece(2)
    sums_last(0)
    outputs(2)
    sums_next(1)
    sums_first(2)
    products(0, 4, 6)
    resid_step(2).wait_recv()
    save = pltpu.make_async_copy(resid_buf, resid_all, local_sem.at[3])
    save.start()
    attended_piece(3)
    for h in range(heads):
        head(h)

    folded = key_rot[...] + pltpu.roll(key_rot[...], ROPE, 1)
    key_rot[...] = folded

    def partial(r):
        at = slice(r * rows, (r + 1) * rows)
        latent = last_dot(expand_grad[at, :], expand[...])
        normed = last_dot(query_grad[at, :], query[...])
        return normed, latent, key_rot[at, :]

    splits = ((0, width), (width, width + LATENT), (width + LATENT, width + LATENT + lanes))

    def ring_step(step):
        return remote(
            ring_out.at[step], ring_buf.at[step], ring_send.at[step], ring_recv.at[step], right
        )

    def between_0():
        sums_last(1)
        outputs(3)
        sums_next(2)
        sums_first(3)
        products(0, 6, 12)

    def between_1():
        sums_last(2)
        sums_next(3)
        products(0, 12, 16)
        products(1, 0, 6)

    def between_2():
        sums_last(3)
        products(1, 6, 16)

    for step, between in enumerate((between_0, between_1, between_2)):
        values = partial(step + 1)
        if step:
            ring_step(step - 1).wait_recv()
        for (start, stop), part in zip(splits, values):
            if step:
                part = part + ring_buf[step - 1, :, start:stop].astype(jnp.float32)
            ring_out[step, :, start:stop] = bfloat(part)
        ring_step(step).start()
        between()
    parts = partial(0)
    ring_step(ranks - 2).wait_recv()
    normed_back[...] = parts[0] + ring_buf[ranks - 2, :, :width].astype(jnp.float32)
    latent_back[:, :LATENT] = parts[1] + ring_buf[
        ranks - 2, :, width : width + LATENT
    ].astype(jnp.float32)
    latent_back[:, LATENT:] = parts[2] + ring_buf[ranks - 2, :, width + LATENT :].astype(
        jnp.float32
    )
    save.wait()
    for step in range(ranks - 1):
        resid_step(step).wait_send()
        ring_step(step).wait_send()


def back_pass(
    resid,
    acts,
    expert_down,
    shared_all,
    output,
    query,
    expand,
    q_cat,
    k_cat,
    value,
    prob_all,
    cos_table,
    sin_table,
    gate_all,
    up_all,
    row_all,
):
    ranks, groups = lax.axis_size(TENSOR), lax.axis_size(DP)
    rows, width = resid.shape
    group_rows = rows * ranks
    heads = q_cat.shape[0]
    lanes = cos_table.shape[1]
    hidden_width = acts.shape[-1]
    low, full = jnp.bfloat16, jnp.float32
    anywhere = pl.BlockSpec(memory_space=pl.ANY)
    in_vmem = pl.BlockSpec(memory_space=pltpu.VMEM)
    dma = pltpu.SemaphoreType.DMA

    def array(*shape, dtype=low):
        return jax.ShapeDtypeStruct(shape, dtype)

    return pl.pallas_call(
        back_kernel,
        out_shape=(
            array(ranks, rows, width),
            array(ranks, rows, width),
            array(expert_down.shape[0], width, dtype=full),
            array(expert_down.shape[0], width, dtype=full),
            array(2, shared_all.shape[1], width, dtype=full),
            array(rows, width, dtype=full),
            array(rows, LATENT + lanes, dtype=full),
            array(group_rows, query.shape[1]),
            array(group_rows, expand.shape[1]),
        ),
        in_specs=[anywhere] * 4 + [in_vmem] * 6 + [anywhere] + [in_vmem] * 2 + [anywhere] * 3,
        out_specs=(anywhere,) * 5 + (in_vmem,) * 4,
        scratch_shapes=[
            pltpu.VMEM((hidden_width, width), low),
            pltpu.VMEM((2, 2, rows, hidden_width), low),
            pltpu.VMEM((ranks, rows, width), low),
            pltpu.VMEM((group_rows, heads * VDIM), low),
            pltpu.VMEM((2, group_rows, group_rows), full),
            pltpu.VMEM((group_rows, lanes), full),
            pltpu.VMEM((group_rows, lanes), full),
            pltpu.VMEM((2, groups, rows, width), low),
            pltpu.VMEM((ranks, 4, rows, width), low),
            pltpu.VMEM((ranks, 2, rows // 2, width), low),
            pltpu.VMEM((ranks, 2, rows // 2, width), low),
            pltpu.VMEM((ranks, 2, rows // 2, width), low),
            pltpu.VMEM((ranks - 1, rows, width + LATENT + lanes), low),
            pltpu.VMEM((ranks - 1, rows, width + LATENT + lanes), low),
            pltpu.VMEM((2, 512, hidden_width), low),
            pltpu.VMEM((2, 512, width // 2), low),
            pltpu.VMEM((hidden_width, width // 2), full),
            dma((4,)),
            dma((2,)),
            dma((2,)),
            dma((2,)),
            dma((2, 2)),
            dma((2,)),
            dma((ranks - 1,)),
            dma((ranks - 1,)),
            dma((10, ranks)),
            dma((10, ranks)),
            dma((ranks - 1,)),
            dma((ranks - 1,)),
        ],
        compiler_params=pltpu.CompilerParams(
            collective_id=3, has_side_effects=True, vmem_limit_bytes=63 * 1024 * 1024
        ),
        name="back_pass",
    )(
        resid,
        acts,
        expert_down,
        shared_all,
        output,
        query,
        expand,
        q_cat,
        k_cat,
        value,
        prob_all,
        cos_table,
        sin_table,
        gate_all,
        up_all,
        row_all,
    )


def weight_kernel(
    normed_in,
    latent_group_in,
    attended_in,
    resid_in,
    query_grad_in,
    expand_grad_in,
    normed_back,
    latent_back,
    own_latent,
    hidden_in,
    resid_grad_in,
    residual_in,
    cos_table,
    sin_table,
    attn_gain,
    latent_gain,
    mlp_grad,
    latent_columns_in,
    moe_sums,
    shared_rows,
    act_all,
    cotan_all,
    layer_out,
    hidden_grad,
    query_out,
    expand_out,
    output_out,
    gains_out,
    latent_all,
    shared_gate_out,
    shared_up_out,
    shared_down_out,
    down_out,
    query_full,
    expand_full,
    output_full,
    core_q,
    core_e,
    core_o,
    far_q,
    far_e,
    far_o,
    x_q,
    x_e,
    x_o,
    y_q,
    y_e,
    y_o,
    gains,
    latent_own,
    latent_rows,
    latent_full,
    latent_buf,
    latent_piece,
    gains_buf,
    gains_sum,
    gains_rank,
    act_buf,
    cotan_buf,
    acc,
    shared_full,
    shared_low,
    shared_back,
    moe_first,
    moe_out,
    moe_in,
    normed,
    attended,
    resid,
    query_grad,
    expand_grad,
    latent_group,
    hidden,
    resid_grad,
    residual,
    latent_columns,
    stage_sem,
    load_sem,
    local_sem,
    out_sem,
    s_send,
    s_recv,
    lz_send,
    lz_recv,
    ld_send,
    ld_recv,
    lp_send,
    lp_recv,
    lc_send,
    lc_recv,
    gd_send,
    gd_recv,
    gz_send,
    gz_recv,
    h_send,
    h_recv,
    m_send,
    m_recv,
):
    me, rank = lax.axis_index(DP), lax.axis_index(TENSOR)
    ranks, count = lax.axis_size(TENSOR), lax.axis_size(DP)
    by_core, by_x, by_y = [(flip(me, bit), rank) for bit in (1, 2, 4)]

    def owner(k):
        other = me
        for bit in (1, 2, 4):
            other = flip(other, bit) if k & bit else other
        return other

    partners = [(owner(k), rank) for k in range(1, count)]
    beside = [(me, lax.rem(rank + r, ranks)) for r in range(1, ranks)]
    width = normed.shape[1]
    routed_width = down_out.shape[0]
    shared_pad = shared_low.shape[1]
    rows = hidden.shape[0]
    staged = {}
    for n, (key, src, dst) in enumerate(
        (
            (0, normed_in, normed),
            (1, query_grad_in, query_grad),
            (2, latent_columns_in, latent_columns),
            (2, hidden_in, hidden),
            (2, resid_grad_in, resid_grad),
            (3, attended_in, attended),
            (3, resid_in, resid),
            (4, latent_group_in, latent_group),
            (4, expand_grad_in, expand_grad),
            (5, residual_in, residual),
        )
    ):
        copy = pltpu.make_async_copy(src, dst, stage_sem.at[n])
        copy.start()
        staged.setdefault(key, []).append(copy)

    def ready(key):
        for copy in staged[key]:
            copy.wait()

    greet(partners + beside)

    def moe_step(step):
        src = moe_sums.at[1] if step == 0 else moe_out.at[step]
        return remote(src, moe_in.at[step], m_send.at[step], m_recv.at[step], beside[0])

    moe_loads = [
        pltpu.make_async_copy(moe_sums.at[0], moe_first, local_sem.at[4]),
        pltpu.make_async_copy(moe_sums.at[2], moe_out.at[1], local_sem.at[5]),
        pltpu.make_async_copy(moe_sums.at[3], moe_out.at[2], local_sem.at[6]),
    ]
    shared_load = pltpu.make_async_copy(shared_rows, shared_full, local_sem.at[7])
    for copy in moe_loads + [shared_load]:
        copy.start()

    def moe_next(step):
        moe_loads[step].wait()
        moe_step(step - 1).wait_recv()
        add_rows(moe_out.at[step], rows, moe_in.at[step - 1])
        moe_step(step).start()

    def moe_last():
        ready(5)
        moe_loads[0].wait()
        moe_step(ranks - 2).wait_recv()
        total = moe_first[...].astype(jnp.float32) + moe_in[ranks - 2].astype(jnp.float32)
        layer_out[...] = bfloat(residual[...] + total)

    values = own_latent[...]
    scale = lax.rsqrt(jnp.mean(values * values, axis=-1, keepdims=True) + epsilon)
    grad = latent_back[:, :LATENT]
    scaled_grad = grad * latent_gain[...]
    inner = jnp.mean(scaled_grad * values, axis=-1, keepdims=True)
    latent_in = scale * scaled_grad - values * (scale * scale * scale) * inner
    latent_own[:, :LATENT] = bfloat(latent_in)
    latent_own[:, LATENT:] = bfloat(
        turn(latent_back[:, LATENT:], cos_table[0:rows, :], -sin_table[0:rows, :])
    )
    gains[...] = jnp.zeros_like(gains)
    gains[2:3, :LATENT] = jnp.sum(grad * values * scale, axis=0, keepdims=True)
    gains[1:2, :] = mlp_grad[...]

    def first_norm():
        ready(2)
        lanes = latent_columns.shape[0]
        total = normed_back[...] + plain_dot(latent_own[:, :lanes], latent_columns[...])
        values = hidden[...].astype(jnp.float32)
        scale = lax.rsqrt(jnp.mean(values * values, axis=-1, keepdims=True) + epsilon)
        scaled_grad = total * attn_gain[...]
        inner = jnp.mean(scaled_grad * values, axis=-1, keepdims=True)
        through = scale * scaled_grad - values * (scale * scale * scale) * inner
        hidden_grad[...] = resid_grad[...] + through
        gains[0:1, :] = jnp.sum(total * values * scale, axis=0, keepdims=True)

    own_rows = pltpu.make_async_copy(latent_own, latent_rows.at[0], local_sem.at[0])
    own_rows.start()
    latent_sends = [
        remote(latent_own, latent_rows.at[r], lz_send.at[r - 1], lz_recv.at[r - 1], peer)
        for r, peer in enumerate(beside, 1)
    ]
    gains_sends = [
        remote(gains, gains_buf.at[me], gd_send.at[n], gd_recv.at[n], peer)
        for n, peer in enumerate(partners)
    ]
    for copy in latent_sends:
        copy.start()

    sets = (
        (query_full, core_q, far_q, x_q, y_q, query_out),
        (expand_full, core_e, far_e, x_e, y_e, expand_out),
        (output_full, core_o, far_o, x_o, y_o, output_out),
    )

    def copy_of(i, kind):
        whole, core, far, x_buf, y_buf, _ = sets[i]
        half = whole.shape[1] // 2
        first, last = pl.ds(0, half), pl.ds(half, half)
        at = whole.at
        n, src, dst, peer = {
            K_CORE_OWN: lambda: (0, at[owner(1)], core.at[0], by_core),
            K_CORE_X: lambda: (1, at[owner(3)], core.at[1], by_core),
            K_CORE_Y: lambda: (2, at[owner(5)], core.at[2], by_core),
            K_CORE_FAR: lambda: (3, at[owner(7)], core.at[3], by_core),
            K_FAR_X: lambda: (4, at[owner(6), first], far.at[0], by_x),
            K_FAR_Y: lambda: (5, at[owner(6), last], far.at[1], by_y),
            K_X_FIRST: lambda: (6, at[owner(2), first], x_buf.at[0], by_x),
            K_X_LAST: lambda: (7, at[owner(2), last], x_buf.at[1], by_x),
            K_Y_FIRST: lambda: (8, at[owner(4), first], y_buf.at[0], by_y),
            K_Y_LAST: lambda: (9, at[owner(4), last], y_buf.at[1], by_y),
        }[kind]()
        return remote(src, dst, s_send.at[i, n], s_recv.at[i, n], peer)

    def sums_start(i):
        for kind in (K_CORE_FAR, K_CORE_X, K_CORE_Y, K_CORE_OWN):
            copy_of(i, kind).start()

    def sums_first(i):
        whole, core, _, _, _, _ = sets[i]
        half = whole.shape[1] // 2
        first, last = pl.ds(0, half), pl.ds(half, half)
        copy_of(i, K_CORE_FAR).wait_recv()
        add_rows(whole.at[owner(6)], 2 * half, core.at[3])
        copy_of(i, K_FAR_X).start()
        copy_of(i, K_FAR_Y).start()
        copy_of(i, K_CORE_X).wait_recv()
        add_rows(whole.at[owner(2), first], half, core.at[1, first])
        copy_of(i, K_X_FIRST).start()
        copy_of(i, K_CORE_Y).wait_recv()
        add_rows(whole.at[owner(4), last], half, core.at[2, last])
        copy_of(i, K_Y_LAST).start()

    def sums_next(i):
        whole, core, far, _, _, _ = sets[i]
        half = whole.shape[1] // 2
        first, last = pl.ds(0, half), pl.ds(half, half)
        copy_of(i, K_FAR_X).wait_recv()
        add_rows(whole.at[owner(4), first], half, core.at[2, first], far.at[0])
        copy_of(i, K_Y_FIRST).start()
        copy_of(i, K_FAR_Y).wait_recv()
        add_rows(whole.at[owner(2), last], half, core.at[1, last], far.at[1])
        copy_of(i, K_X_LAST).start()

    def sums_last(i):
        whole, core, _, x_buf, y_buf, out = sets[i]
        half = whole.shape[1] // 2
        for kind in (K_CORE_OWN, K_X_FIRST, K_X_LAST, K_Y_FIRST, K_Y_LAST):
            copy_of(i, kind).wait_recv()
        for n in range(2):
            part = pl.ds(n * half, half)
            add_rows(
                whole.at[me, part],
                half,
                core.at[0, part],
                x_buf.at[n],
                y_buf.at[n],
                store=out.at[part],
            )

    q_rows, o_cols = query_full.shape[1], output_full.shape[2]
    ready(0)
    ready(1)
    for o in range(count):
        at = slice(o * q_rows, (o + 1) * q_rows)
        query_full[o] = bfloat(first_dot(normed[:, at], query_grad[...]))
    sums_start(0)

    part_width = latent_full.shape[2]
    latent_count = latent_full.shape[1]
    own_rows.wait()
    for copy in latent_sends:
        copy.wait_recv()
    columns = pl.ds(pl.multiple_of(rank * part_width, part_width), part_width)
    rows_low = latent_rows[...].reshape(-1, latent_rows.shape[2])
    latent_full[...] = bfloat(first_dot(rows_low, normed[:, columns])).reshape(latent_full.shape)
    dealt = [
        remote(
            latent_full.at[peer[0]], latent_buf.at[me], ld_send.at[n], ld_recv.at[n], peer
        )
        for n, peer in enumerate(partners)
    ]
    for copy in dealt:
        copy.start()
    moe_step(0).start()
    latent_buf[me] = latent_full[me]
    first_norm()
    for copy in gains_sends:
        copy.start()
    gains_buf[me] = gains[...]
    ready(3)
    for o in range(count):
        at = slice(o * o_cols, (o + 1) * o_cols)
        output_full[o] = bfloat(first_dot(attended[...], resid[:, at]))
    sums_start(2)
    ready(4)
    expanded = bfloat(first_dot(latent_group[...], expand_grad[...]))
    expand_full[...] = expanded.reshape(expand_full.shape)
    sums_start(1)

    def latent_at(o, columns=None):
        at = pl.ds(pl.multiple_of(o * latent_count, latent_count), latent_count)
        return latent_all.at[at] if columns is None else latent_all.at[at, columns]

    pieces = [
        remote(
            latent_piece, latent_at(me, columns), lp_send.at[r - 1], lp_recv.at[r - 1], peer
        )
        for r, peer in enumerate(beside, 1)
    ]
    own_piece = pltpu.make_async_copy(latent_piece, latent_at(me, columns), local_sem.at[1])

    def latent_sum():
        for copy in dealt:
            copy.wait_recv()
        total = latent_buf[0].astype(jnp.float32)
        for o in range(1, count):
            total = total + latent_buf[o].astype(jnp.float32)
        latent_piece[...] = bfloat(total)
        for copy in pieces + [own_piece]:
            copy.start()

    def latent_copy(kind):
        first, last = pl.ds(0, width // 2), pl.ds(width // 2, width // 2)
        n, block, peer = {
            K_X: lambda: (0, latent_at(me), by_x),
            K_Y: lambda: (1, latent_at(me), by_y),
            K_CORE: lambda: (2, latent_at(me), by_core),
            K_FAR_Y: lambda: (3, latent_at(owner(2), last), by_y),
            K_FAR_X: lambda: (4, latent_at(owner(4), first), by_x),
            K_CORE_X: lambda: (5, latent_at(owner(2)), by_core),
            K_CORE_Y: lambda: (6, latent_at(owner(4)), by_core),
            K_CORE_FAR: lambda: (7, latent_at(owner(6)), by_core),
        }[kind]()
        return remote(block, block, lc_send.at[n], lc_recv.at[n], peer)

    def latent_cube():
        own_piece.wait()
        for copy in pieces:
            copy.wait_recv()
        for kind in (K_X, K_Y, K_CORE):
            latent_copy(kind).start()

    def latent_forward():
        latent_copy(K_X).wait_recv()
        latent_copy(K_FAR_Y).start()
        latent_copy(K_CORE_X).start()
        latent_copy(K_Y).wait_recv()
        latent_copy(K_FAR_X).start()
        latent_copy(K_CORE_Y).start()

    def latent_far():
        latent_copy(K_FAR_X).wait_recv()
        latent_copy(K_FAR_Y).wait_recv()
        latent_copy(K_CORE_FAR).start()

    gains_beside = [
        remote(gains_sum, gains_rank.at[rank], gz_send.at[r - 1], gz_recv.at[r - 1], peer)
        for r, peer in enumerate(beside, 1)
    ]

    def gains_first():
        for copy in gains_sends:
            copy.wait_recv()
        total = gains_buf[0]
        for o in range(1, count):
            total = total + gains_buf[o]
        gains_sum[...] = total
        gains_rank[rank] = total
        for copy in gains_beside:
            copy.start()

    def gains_last():
        for copy in gains_beside:
            copy.wait_recv()
        total = gains_rank[0]
        for r in range(1, ranks):
            total = total + gains_rank[r]
        gains_out[...] = total

    chunk, columns = cotan_buf.shape[1:]
    chunks = cotan_all.shape[0] // chunk
    units = chunks * (width // columns)

    def loads(unit, parity):
        at = pl.ds(pl.multiple_of(lax.rem(unit, chunks) * chunk, chunk), chunk)
        part = pl.ds(pl.multiple_of(lax.div(unit, chunks) * columns, columns), columns)
        return (
            pltpu.make_async_copy(act_all.at[at], act_buf.at[parity], load_sem.at[parity, 0]),
            pltpu.make_async_copy(
                cotan_all.at[at, part], cotan_buf.at[parity], load_sem.at[parity, 1]
            ),
        )

    def acc_store(unit):
        part = pl.ds(pl.multiple_of(lax.div(unit, chunks) * columns, columns), columns)
        return pltpu.make_async_copy(
            acc.at[pl.ds(0, routed_width)], down_out.at[:, part], out_sem
        )

    def products(begin, end):
        def one(unit, carry):
            parity = lax.rem(unit, 2)

            @pl.when(unit + 1 < units)
            def _():
                for copy in loads(unit + 1, 1 - parity):
                    copy.start()

            for copy in loads(unit, parity):
                copy.wait()
            part = first_dot(act_buf[parity], cotan_buf[parity])
            place = lax.rem(unit, chunks)

            @pl.when(place == 0)
            def _():
                acc[...] = part

            @pl.when(place > 0)
            def _():
                acc[...] += part

            @pl.when(place == chunks - 1)
            def _():
                acc_store(unit).start()
                start = pl.multiple_of(lax.div(unit, chunks) * columns, columns)
                shared_low[2, :, pl.ds(start, columns)] = bfloat(
                    acc[routed_width : routed_width + shared_pad, :]
                )
                acc_store(unit).wait()

            return carry

        lax.fori_loop(begin, end, one, 0)

    def shared_copies(at, n):
        size = shared_back.shape[3]
        return [
            remote(
                shared_low.at[at, :, pl.ds(pl.multiple_of(peer[0] * size, size), size)],
                shared_back.at[me, at],
                h_send.at[n, m],
                h_recv.at[n, m],
                peer,
            )
            for m, peer in enumerate(partners)
        ]

    def own_shared(at, n):
        size = shared_back.shape[3]
        return pltpu.make_async_copy(
            shared_low.at[at, :, pl.ds(pl.multiple_of(me * size, size), size)],
            shared_back.at[me, at],
            local_sem.at[2 + n],
        )

    def shared_receive(at, n, outs):
        own_shared(at, n).wait()
        for copy in shared_copies(at, n):
            copy.wait_recv()
        for m, out in outs:
            size = out.shape[0] // count
            for o in range(count):
                out[o * size : (o + 1) * size, :] = shared_back[o, m, :size, :].astype(jnp.float32)

    for copy in loads(0, 0):
        copy.start()
    pair, single = pl.ds(0, 2), pl.ds(2, 1)
    sums_first(0)
    sums_first(2)
    sums_first(1)
    latent_sum()
    products(0, 6)
    moe_next(1)
    latent_cube()
    sums_next(0)
    sums_next(2)
    sums_next(1)
    gains_first()
    products(6, 12)
    latent_forward()
    moe_next(2)
    latent_far()
    shared_load.wait()
    shared_low[0:2] = bfloat(shared_full[...])
    for copy in shared_copies(pair, 0) + [own_shared(pair, 0)]:
        copy.start()
    products(12, 16)
    for i in (0, 2, 1):
        sums_last(i)
    gains_last()
    for copy in shared_copies(single, 1) + [own_shared(single, 1)]:
        copy.start()
    moe_last()
    for kind in (K_CORE, K_CORE_X, K_CORE_Y, K_CORE_FAR):
        latent_copy(kind).wait_recv()
    shared_receive(pair, 0, ((0, shared_gate_out), (1, shared_up_out)))
    shared_receive(single, 1, ((2, shared_down_out),))

    for kind in (K_X, K_Y, K_CORE, K_FAR_Y, K_FAR_X, K_CORE_X, K_CORE_Y, K_CORE_FAR):
        latent_copy(kind).wait_send()
    for copy in latent_sends + gains_sends + dealt + pieces + gains_beside:
        copy.wait_send()
    for i in range(len(sets)):
        for kind in SUM_KINDS:
            copy_of(i, kind).wait_send()
    for step in range(ranks - 1):
        moe_step(step).wait_send()
    for at, n in ((pair, 0), (single, 1)):
        for copy in shared_copies(at, n):
            copy.wait_send()


def weight_pass(
    normed,
    latent_group,
    attended,
    resid,
    query_grad,
    expand_grad,
    normed_back,
    latent_back,
    own_latent,
    hidden,
    resid_grad,
    residual,
    cos_table,
    sin_table,
    attn_gain,
    latent_gain,
    mlp_grad,
    latent_columns,
    moe_sums,
    shared_rows,
    act_all,
    cotan_all,
    shared_width,
    routed_width,
):
    ranks, count = lax.axis_size(TENSOR), lax.axis_size(DP)
    rows, width = hidden.shape
    hidden_width = act_all.shape[1]
    shared_pad = shared_rows.shape[1]
    low, full = jnp.bfloat16, jnp.float32
    anywhere = pl.BlockSpec(memory_space=pl.ANY)
    in_vmem = pl.BlockSpec(memory_space=pltpu.VMEM)
    dma = pltpu.SemaphoreType.DMA
    chunk = cotan_all.shape[0] // 8
    latent_width = latent_back.shape[1]
    q_shape = (width // count, query_grad.shape[1])
    e_shape = (latent_group.shape[1] // count, expand_grad.shape[1])
    o_shape = (attended.shape[1], width // count)
    l_shape = (latent_width // count, width // ranks)
    g_shape = (8, width)
    shapes = (q_shape, e_shape, o_shape)

    def array(*shape):
        return jax.ShapeDtypeStruct(shape, full)

    def halves(n):
        return [pltpu.VMEM((n, shape[0] // 2, shape[1]), low) for shape in shapes]

    return pl.pallas_call(
        weight_kernel,
        out_shape=(
            jax.ShapeDtypeStruct((rows, width), low),
            array(rows, width),
            array(*q_shape),
            array(*e_shape),
            array(*o_shape),
            array(*g_shape),
            jax.ShapeDtypeStruct((latent_width, width), low),
            array(count * shared_width, width // count),
            array(count * shared_width, width // count),
            array(count * shared_width, width // count),
            array(routed_width, width),
        ),
        in_specs=[anywhere] * 6
        + [in_vmem] * 3
        + [anywhere] * 3
        + [in_vmem] * 5
        + [anywhere] * 5,
        out_specs=(in_vmem,) * 6 + (anywhere,) + (in_vmem,) * 3 + (anywhere,),
        scratch_shapes=[pltpu.VMEM((count,) + shape, low) for shape in shapes]
        + [pltpu.VMEM((4,) + shape, low) for shape in shapes]
        + halves(2)
        + halves(2)
        + halves(2)
        + [
            pltpu.VMEM(g_shape, full),
            pltpu.VMEM((rows, latent_width), low),
            pltpu.VMEM((ranks, rows, latent_width), low),
            pltpu.VMEM((count,) + l_shape, low),
            pltpu.VMEM((count,) + l_shape, low),
            pltpu.VMEM(l_shape, low),
            pltpu.VMEM((count,) + g_shape, full),
            pltpu.VMEM(g_shape, full),
            pltpu.VMEM((ranks,) + g_shape, full),
            pltpu.VMEM((2, chunk, hidden_width), low),
            pltpu.VMEM((2, chunk, width // 2), low),
            pltpu.VMEM((hidden_width, width // 2), full),
            pltpu.VMEM((2, shared_pad, width), full),
            pltpu.VMEM((3, shared_pad, width), low),
            pltpu.VMEM((count, 3, shared_pad, width // count), low),
            pltpu.VMEM((rows, width), low),
            pltpu.VMEM((ranks - 1, rows, width), low),
            pltpu.VMEM((ranks - 1, rows, width), low),
        ]
        + [
            pltpu.VMEM(values.shape, values.dtype)
            for values in (
                normed,
                attended,
                resid,
                query_grad,
                expand_grad,
                latent_group,
                hidden,
                resid_grad,
                residual,
                latent_columns,
            )
        ]
        + [
            dma((10,)),
            dma((2, 2)),
            dma((8,)),
            dma,
            dma((3, 10)),
            dma((3, 10)),
            dma((ranks - 1,)),
            dma((ranks - 1,)),
            dma((count - 1,)),
            dma((count - 1,)),
            dma((ranks - 1,)),
            dma((ranks - 1,)),
            dma((8,)),
            dma((8,)),
            dma((count - 1,)),
            dma((count - 1,)),
            dma((ranks - 1,)),
            dma((ranks - 1,)),
            dma((2, count - 1)),
            dma((2, count - 1)),
            dma((ranks - 1,)),
            dma((ranks - 1,)),
        ],
        compiler_params=pltpu.CompilerParams(
            collective_id=4, has_side_effects=True, vmem_limit_bytes=63 * 1024 * 1024
        ),
        name="weight_pass",
    )(
        normed,
        latent_group,
        attended,
        resid,
        query_grad,
        expand_grad,
        normed_back,
        latent_back,
        own_latent,
        hidden,
        resid_grad,
        residual,
        cos_table,
        sin_table,
        attn_gain,
        latent_gain,
        mlp_grad,
        latent_columns,
        moe_sums,
        shared_rows,
        act_all,
        cotan_all,
    )


def part_heads(values, heads):
    split = values.reshape(-1, heads, NOPE + ROPE)
    parts = (split[:, :, :NOPE], split[:, :, NOPE:])
    return jnp.concatenate([part.reshape(values.shape[0], -1) for part in parts], axis=1)


def join_heads(values, heads):
    plain = values[:, : heads * NOPE].reshape(-1, heads, NOPE)
    turned = values[:, heads * NOPE :].reshape(-1, heads, ROPE)
    return jnp.concatenate([plain, turned], axis=2).reshape(values.shape)


def cube_shards(
    hidden,
    cotangent,
    routes,
    route_gates,
    doc_lengths,
    attn_gain,
    query_weight,
    latent_weight,
    latent_gain,
    expand_weight,
    output_weight,
    mlp_gain,
    shared_gate,
    shared_up,
    shared_down,
    expert_gate,
    expert_up,
    expert_down,
):
    ranks = lax.axis_size(TENSOR)
    groups = lax.axis_size(DP)
    rows = hidden.shape[0]
    group_rows = rows * ranks
    width = hidden.shape[1]
    local_experts, _, expert_width = expert_gate.shape
    experts = local_experts * groups

    shared_width = shared_gate.shape[1] // groups
    shared_pad = -(-shared_width // 16) * 16
    shared_stack = jnp.stack(
        [
            jnp.pad(
                weight.reshape(groups, shared_width, weight.shape[1]),
                ((0, 0), (0, shared_pad - shared_width), (0, 0)),
            )
            for weight in (shared_gate.T, shared_up.T, shared_down)
        ],
        axis=1,
    )
    routed_width = local_experts * expert_width
    hidden_width = -(-(routed_width + shared_pad) // 128) * 128
    local_heads = query_weight.shape[1] // (NOPE + ROPE)
    latent_columns = latent_weight.T

    (
        normed_group,
        latent_group,
        own_latent,
        query_full,
        expand_full,
        output_full,
        q_cat,
        k_cat,
        value_all,
        probability,
        attended_low,
        cos_group,
        sin_group,
        residual,
        normed_two,
        shared_all,
        slot_gates,
        cotan_all,
        back_all,
    ) = front_pass(
        doc_lengths,
        hidden,
        cotangent,
        part_heads(query_weight, local_heads),
        expand_weight,
        output_weight,
        shared_stack,
        expert_down.reshape(-1, width),
        routes.T,
        route_gates.T,
        latent_columns,
        attn_gain[None],
        latent_gain[None],
        mlp_gain[None],
        hidden_width,
        experts,
    )
    (
        row_all,
        act_all,
        gate_all,
        up_all,
        resid_grad,
        resid_low,
        mlpgain_part,
    ) = moe_pass(
        normed_two,
        back_all,
        slot_gates,
        expert_gate.transpose(0, 2, 1).reshape(-1, width),
        expert_up.transpose(0, 2, 1).reshape(-1, width),
        shared_all,
        residual,
        cotangent,
        mlp_gain[None],
        expert_width,
    )
    (
        resid_all,
        moe_sums,
        gate_wgrad,
        up_wgrad,
        shared_rows,
        normed_back,
        latent_back,
        qraw_grad,
        expand_rows,
    ) = back_pass(
        resid_low,
        act_all,
        expert_down.reshape(-1, width),
        shared_all,
        output_full,
        query_full,
        expand_full,
        q_cat,
        k_cat,
        value_all,
        probability,
        cos_group,
        sin_group,
        gate_all.reshape(-1, hidden_width),
        up_all.reshape(-1, hidden_width),
        row_all.reshape(-1, width),
    )
    (
        layer_out,
        hidden_grad,
        query_total,
        expand_total,
        output_total,
        small,
        latent_total,
        shared_gate_total,
        shared_up_total,
        shared_down_total,
        down_wgrad,
    ) = weight_pass(
        normed_group,
        latent_group,
        attended_low,
        resid_all.reshape(group_rows, width),
        qraw_grad,
        expand_rows,
        normed_back,
        latent_back,
        own_latent,
        hidden,
        resid_grad,
        residual,
        cos_group,
        sin_group,
        attn_gain[None],
        latent_gain[None],
        mlpgain_part,
        latent_columns,
        moe_sums,
        shared_rows,
        act_all.reshape(-1, hidden_width),
        cotan_all.reshape(-1, width),
        shared_width,
        routed_width,
    )

    def expert_part(values):
        return values.reshape(local_experts, expert_width, width)

    return (
        layer_out,
        hidden_grad,
        small[0],
        join_heads(query_total, local_heads),
        latent_total[: LATENT + ROPE].T.astype(jnp.float32),
        small[2, :LATENT],
        expand_total,
        output_total,
        small[1],
        shared_gate_total.T,
        shared_up_total.T,
        shared_down_total,
        expert_part(gate_wgrad).transpose(0, 2, 1),
        expert_part(up_wgrad).transpose(0, 2, 1),
        expert_part(down_wgrad),
    )


def solution(mesh):
    in_specs = (
        P((DP, TENSOR), None),
        P((DP, TENSOR), None),
        P(DP, None),
        P(DP, None),
        P(DP, None),
        P(),
        P(DP, TENSOR),
        P(),
        P(),
        P(DP, TENSOR),
        P(TENSOR, DP),
        P(),
        P(DP, TENSOR),
        P(DP, TENSOR),
        P(TENSOR, DP),
        P(DP, None, TENSOR),
        P(DP, None, TENSOR),
        P(DP, TENSOR, None),
    )
    out_specs = (
        P((DP, TENSOR), None),
        P((DP, TENSOR), None),
        P(),
        P(DP, TENSOR),
        P(),
        P(),
        P(DP, TENSOR),
        P(TENSOR, DP),
        P(),
        P(DP, TENSOR),
        P(DP, TENSOR),
        P(TENSOR, DP),
        P(DP, None, TENSOR),
        P(DP, None, TENSOR),
        P(DP, TENSOR, None),
    )
    cube = dict(mesh.shape) == {DP: 8, TENSOR: 4}
    shards = cube_shards if cube else general_shards
    return jax.shard_map(shards, mesh=mesh, in_specs=in_specs, out_specs=out_specs, check_vma=False)
```
